128 devices in a mesh: dp: 32 (over x, z_lo, y), seq: 4 (over z_hi, core).
Axes of the slice: x: 4, y: 4, z: 4 (z_hi: 2, z_lo: 2; z = z_hi * 2 + z_lo), core: 2. Of those that a mesh axis runs over, the one named last changes fastest.
Arguments:
- latents: bfloat16 [64, 32, 32, 768], P('dp', 'seq'), may hold values from -6 to 6
- conditioning: bfloat16 [64, 768], P('dp'), may hold values from -6 to 6
- timesteps: int32 [64], P('dp'), may hold values from 0 to 999
- item_counts: int32 [32], P('dp'), may hold values from 1 to 2, as said below
- cotangent: bfloat16 [64, 32, 32, 768], P('dp', 'seq'), may hold values from -6 to 6
- time_table: bfloat16 [1000, 768], replicated, may hold values from -3 to 3
- mod_weight: bfloat16 [768, 4608], replicated, may hold values from -0.21875 to 0.21875
- mod_bias: bfloat16 [4608], replicated, may hold values from -1.796875 to 1.796875
- conv_attn_weight: bfloat16 [9, 768], replicated, may hold values from -2 to 2
- conv_attn_bias: bfloat16 [768], replicated, may hold values from -3 to 3
- qkv_weight: bfloat16 [768, 2304], replicated, may hold values from -0.21875 to 0.21875
- query_bias: bfloat16 [768], replicated, may hold values from -3 to 3
- value_bias: bfloat16 [768], replicated, may hold values from -3 to 3
- out_weight: bfloat16 [768, 768], replicated, may hold values from -3.5 to 3.5
- out_bias: bfloat16 [768], replicated, may hold values from -1.796875 to 1.796875
- fc1_weight: bfloat16 [768, 3072], replicated, may hold values from -0.21875 to 0.21875
- fc1_bias: bfloat16 [3072], replicated, may hold values from -3 to 3
- conv_ffn_weight: bfloat16 [9, 3072], replicated, may hold values from -2 to 2
- conv_ffn_bias: bfloat16 [3072], replicated, may hold values from -3 to 3
- fc2_weight: bfloat16 [3072, 768], replicated, may hold values from -0.109375 to 0.109375
- fc2_bias: bfloat16 [768], replicated, may hold values from -1.796875 to 1.796875
Outputs:
- output: bfloat16 [64, 32, 32, 768], P('dp', 'seq')
- input_grad: float32 [64, 32, 32, 768], P('dp', 'seq')
- conditioning_grad: float32 [64, 768], P('dp')
- time_table_grad: float32 [1000, 768], P(None, ('dp', 'seq'))
- mod_weight_grad: float32 [768, 4608], P(('dp', 'seq'))
- mod_bias_grad: float32 [4608], P(('dp', 'seq'))
- conv_attn_weight_grad: float32 [9, 768], P(None, ('dp', 'seq'))
- conv_attn_bias_grad: float32 [768], P(('dp', 'seq'))
- qkv_weight_grad: float32 [768, 2304], P(('dp', 'seq'))
- query_bias_grad: float32 [768], P(('dp', 'seq'))
- value_bias_grad: float32 [768], P(('dp', 'seq'))
- out_weight_grad: float32 [768, 768], P(('dp', 'seq'))
- out_bias_grad: float32 [768], P(('dp', 'seq'))
- fc1_weight_grad: float32 [768, 3072], P(('dp', 'seq'))
- fc1_bias_grad: float32 [3072], P(('dp', 'seq'))
- conv_ffn_weight_grad: float32 [9, 3072], P(None, ('dp', 'seq'))
- conv_ffn_bias_grad: float32 [3072], P(('dp', 'seq'))
- fc2_weight_grad: float32 [3072, 768], P(('dp', 'seq'))
- fc2_bias_grad: float32 [768], P(('dp', 'seq'))
The draws below stay inside these ranges and needn't reach their ends.
Inputs may be any that keep to these rules, and one draw needn't show every extreme that they name: Item j of index i of dp is live when j < item_counts[i]; some index has 2 live items and some index one.
All inputs are finite; a program needn't handle non-finite values.
Results may differ from the reference program's by a relative error of at most 0.023.
Values may be sent and summed in bfloat16 or wider, within the bound.
A program may use at most 256 MiB of HBM per device.

```python
import math
import jax
import jax.numpy as jnp
from jax import lax

D = 768
HEADS = 12
HEAD_DIM = 64
FF = 3072
NT = 1000
GRID = 32
SLOTS = 2
ITEMS = 64
N_DP = 32


def draw_item_counts(key, part):
    key = jax.random.fold_in(key, 11)
    first_key, second_key = jax.random.split(key)
    counted = jax.random.randint(first_key, (N_DP,), 1, SLOTS + 1)
    order = jax.random.permutation(second_key, N_DP)
    counted = counted.at[order[0]].set(SLOTS)
    counted = counted.at[order[1]].set(1)
    return counted.astype(jnp.int32)


def with_ends(values, rng, least, high):
    longest = values.shape.index(max(values.shape))
    spots = []
    for shift in (0, 1):
        where = [jax.random.randint(jax.random.fold_in(rng, axis), (), 0, length) for axis, length in enumerate(values.shape)]
        where[longest] = (where[longest] + shift) % values.shape[longest]
        spots.append(tuple(where))
    return values.at[spots[0]].set(least).at[spots[1]].set(high)


def shard_levels(stream_key, dims, cuts, low, high):
    def one(axis_at, blocks):
        heights = jax.random.uniform(jax.random.fold_in(jax.random.fold_in(stream_key, 6), axis_at), (blocks,), jnp.float32, low / len(cuts), high / len(cuts))
        return jnp.repeat(jnp.exp(heights), dims[axis_at] // blocks).reshape((-1,) + (1,) * (len(dims) - axis_at - 1))

    loudness = one(*cuts[0])
    for cut in cuts[1:]:
        loudness = loudness * one(*cut)
    return loudness


def scatter_about(own_key, shape, deviation, limit, cuts=(), held_as=jnp.bfloat16):
    values = deviation * jax.random.normal(own_key, shape, jnp.float32)
    if cuts:
        values = values * shard_levels(own_key, shape, cuts, -0.22, 0.18)
    return jnp.clip(values, -limit, limit).astype(held_as)


def setup_inputs(seed: int = 0) -> dict:
    key_of = jax.random.split(jax.random.key(seed), 22)
    return {
        "latents": scatter_about(key_of[0], (ITEMS, GRID, GRID, D), 1.0, 6.0, ((0, 32), (1, 4))),
        "conditioning": scatter_about(key_of[1], (ITEMS, D), 1.0, 6.0, ((0, 32),)),
        "timesteps": with_ends(jax.random.randint(key_of[2], (ITEMS,), 0, NT), jax.random.fold_in(key_of[2], 1), 0, NT - 1).astype(jnp.int32),
        "item_counts": draw_item_counts(jax.random.fold_in(key_of[21], 71), 0),
        "cotangent": scatter_about(key_of[4], (ITEMS, GRID, GRID, D), 1.0, 6.0, ((0, 32), (1, 4))),
        "time_table": scatter_about(key_of[5], (NT, D), 0.5, 3.0),
        "mod_weight": scatter_about(key_of[6], (D, 6 * D), D ** -0.5, 0.21875),
        "mod_bias": scatter_about(key_of[7], (6 * D,), 0.3, 1.796875),
        "conv_attn_weight": scatter_about(key_of[8], (9, D), 9 ** -0.5, 2.0),
        "conv_attn_bias": scatter_about(key_of[9], (D,), 0.5, 3.0),
        "qkv_weight": scatter_about(key_of[10], (D, 3 * D), D ** -0.5, 0.21875),
        "query_bias": scatter_about(key_of[11], (D,), 0.5, 3.0),
        "value_bias": scatter_about(key_of[12], (D,), 0.5, 3.0),
        "out_weight": scatter_about(key_of[13], (D, D), (max(1, 4 * D // (GRID * GRID))) ** -0.5, 3.5),
        "out_bias": scatter_about(key_of[14], (D,), 0.3, 1.796875),
        "fc1_weight": scatter_about(key_of[15], (D, FF), D ** -0.5, 0.21875),
        "fc1_bias": scatter_about(key_of[16], (FF,), 0.5, 3.0),
        "conv_ffn_weight": scatter_about(key_of[17], (9, FF), 9 ** -0.5, 2.0),
        "conv_ffn_bias": scatter_about(key_of[18], (FF,), 0.5, 3.0),
        "fc2_weight": scatter_about(key_of[19], (FF, D), FF ** -0.5, 0.109375),
        "fc2_bias": scatter_about(key_of[20], (D,), 0.3, 1.796875),
    }


@jax.custom_vjp
def low(v):
    return lax.optimization_barrier(v.astype(jnp.bfloat16)).astype(jnp.float32)

@jax.custom_vjp
def low_back(v):
    return v

def low_keep(v):
    return (low(v), None)

def low_pass(kept, grad):
    return (grad,)

def back_keep(v):
    return (v, None)

def back_low(kept, grad):
    return (low(grad),)
low.defvjp(low_keep, low_pass)
low_back.defvjp(back_keep, back_low)

def layer_norm(values):
    center = values - lax.optimization_barrier(jnp.mean(values, axis=-1, keepdims=True))
    spread = lax.optimization_barrier(jnp.mean(center * center, axis=-1, keepdims=True))
    return center * lax.rsqrt(spread + 1e-06)

def depthwise(values, taps, offset):
    grid_rows = values.shape[1]
    grid_cols = values.shape[2]
    padded = jnp.pad(values, ((0, 0), (1, 1), (1, 1), (0, 0)))
    total = jnp.zeros_like(values) + offset
    for row_tap in range(3):
        for col_tap in range(3):
            total = total + taps[row_tap * 3 + col_tap] * padded[:, row_tap:row_tap + grid_rows, col_tap:col_tap + grid_cols, :]
    return total

def to_groups(values):
    extent = values.shape
    halved = values.reshape(extent[0], extent[1] // 2, 2, extent[2] // 2, 2, extent[3])
    return halved.transpose(0, 2, 4, 1, 3, 5).reshape(extent[0], 4, extent[1] // 2, extent[2] // 2, extent[3])

def from_groups(values):
    extent = values.shape
    halved = values.reshape(extent[0], 2, 2, extent[2], extent[3], extent[4])
    return halved.transpose(0, 3, 1, 4, 2, 5).reshape(extent[0], 2 * extent[2], 2 * extent[3], extent[4])

def project(values, matrix):
    return jnp.einsum('...c,cd->...d', values, matrix, precision=lax.Precision.HIGHEST)

def layer(params, inputs, conditioning, time_ids, alive_rows):
    width = inputs.shape[-1]
    item_count = inputs.shape[0]
    cond_full = conditioning + params['time_table'][time_ids]
    silu_cond = low(jax.nn.silu(cond_full))
    modulation = low_back(jnp.dot(silu_cond, params['mod_weight'], precision=lax.Precision.HIGHEST) + params['mod_bias'])
    pieces = [modulation[:, index * width:(index + 1) * width][:, None, None, :] for index in range(6)]
    shift_one, scale_one, gate_one, shift_two, scale_two, gate_two = pieces
    normed = low(layer_norm(inputs) * (1.0 + scale_one) + shift_one)
    mixed_in = low(low_back(depthwise(normed, params['conv_attn_weight'], params['conv_attn_bias'])))
    qkv_bias = jnp.concatenate((params['query_bias'], jnp.zeros_like(params['query_bias']), params['value_bias']))
    qkv_all = low(low_back(project(mixed_in, params['qkv_weight']) + qkv_bias))

    def split_heads(values):
        return to_groups(values).reshape(item_count, 4, -1, HEADS, HEAD_DIM)
    queries = split_heads(qkv_all[..., :width])
    keys_grp = split_heads(qkv_all[..., width:2 * width])
    values_grp = split_heads(qkv_all[..., 2 * width:])
    scores = low_back(0.125 * jnp.einsum('bgqhd,bgkhd->bghqk', queries, keys_grp, precision=lax.Precision.HIGHEST))
    probs = jax.nn.softmax(scores, axis=-1)
    attended = jnp.einsum('bghqk,bgkhd->bgqhd', low(probs), values_grp, precision=lax.Precision.HIGHEST)
    attended = from_groups(attended.reshape(item_count, 4, GRID // 2, GRID // 2, width))
    attended = low(low_back(attended))
    branch = low_back(project(attended, params['out_weight']) + params['out_bias'])
    hidden_one = inputs + gate_one * branch
    normed_two = low(layer_norm(hidden_one) * (1.0 + scale_two) + shift_two)
    expanded = low(low_back(project(normed_two, params['fc1_weight']) + params['fc1_bias']))
    mixed_ffn = low_back(depthwise(expanded, params['conv_ffn_weight'], params['conv_ffn_bias']))
    activated = low(jax.nn.gelu(mixed_ffn, approximate=False))
    ffn_out = low_back(project(activated, params['fc2_weight']) + params['fc2_bias'])
    hidden_two = hidden_one + gate_two * ffn_out
    return hidden_two * alive_rows[:, None, None, None]

def reference(latents, conditioning, timesteps, item_counts, cotangent, time_table, mod_weight, mod_bias, conv_attn_weight, conv_attn_bias, qkv_weight, query_bias, value_bias, out_weight, out_bias, fc1_weight, fc1_bias, conv_ffn_weight, conv_ffn_bias, fc2_weight, fc2_bias):
    alive_all = (jnp.arange(SLOTS)[None, :] < item_counts[:, None]).reshape(-1).astype(jnp.float32)
    params = {'time_table': time_table.astype(jnp.float32), 'mod_weight': mod_weight.astype(jnp.float32), 'mod_bias': mod_bias.astype(jnp.float32), 'conv_attn_weight': conv_attn_weight.astype(jnp.float32), 'conv_attn_bias': conv_attn_bias.astype(jnp.float32), 'qkv_weight': qkv_weight.astype(jnp.float32), 'query_bias': query_bias.astype(jnp.float32), 'value_bias': value_bias.astype(jnp.float32), 'out_weight': out_weight.astype(jnp.float32), 'out_bias': out_bias.astype(jnp.float32), 'fc1_weight': fc1_weight.astype(jnp.float32), 'fc1_bias': fc1_bias.astype(jnp.float32), 'conv_ffn_weight': conv_ffn_weight.astype(jnp.float32), 'conv_ffn_bias': conv_ffn_bias.astype(jnp.float32), 'fc2_weight': fc2_weight.astype(jnp.float32), 'fc2_bias': fc2_bias.astype(jnp.float32)}
    block_size = math.gcd(ITEMS, 4)
    block_count = ITEMS // block_size

    def regroup(values):
        return values.reshape((block_count, block_size) + values.shape[1:])
    zero_grads = jax.tree.map(jnp.zeros_like, params)

    def step(totals, slab):
        inputs, conds, time_ids, alive_rows, cotangent_blk = slab

        def forward(weights, inputs_in, conds_in):
            return layer(weights, inputs_in, conds_in, time_ids, alive_rows)
        result, backward = jax.vjp(forward, params, inputs, conds)
        grads, input_grad, cond_grad = backward(cotangent_blk)
        totals = jax.tree.map(lambda total, extra: total + extra, totals, grads)
        return (totals, (result.astype(jnp.bfloat16), input_grad, cond_grad))
    slabs = (regroup(latents.astype(jnp.float32)), regroup(conditioning.astype(jnp.float32)), regroup(timesteps.astype(jnp.int32)), regroup(alive_all), regroup(cotangent.astype(jnp.float32)))
    totals, (output, input_grad, cond_grad) = lax.scan(step, zero_grads, slabs)
    output = output.reshape(latents.shape)
    input_grad = input_grad.reshape(latents.shape)
    cond_grad = cond_grad.reshape(conditioning.shape)
    return (output, input_grad, cond_grad, totals['time_table'], totals['mod_weight'], totals['mod_bias'], totals['conv_attn_weight'], totals['conv_attn_bias'], totals['qkv_weight'], totals['query_bias'], totals['value_bias'], totals['out_weight'], totals['out_bias'], totals['fc1_weight'], totals['fc1_bias'], totals['conv_ffn_weight'], totals['conv_ffn_bias'], totals['fc2_weight'], totals['fc2_bias'])
```

```python
import functools

import jax
import jax.numpy as jnp
import numpy as np
from jax import lax
from jax.experimental import pallas as pl
from jax.experimental.pallas import tpu as pltpu
from jax.sharding import PartitionSpec as P

F32 = jnp.float32
BF16 = jnp.bfloat16
D = 768
FF = 3072
FC = 768
NFC = FF // FC
EPS = 1e-6


def mm(a, b):
    return lax.dot_general(a, b, (((1,), (0,)), ((), ())), preferred_element_type=F32)


def mm_nt(a, b):
    return lax.dot_general(a, b, (((1,), (1,)), ((), ())), preferred_element_type=F32)


def mm_tn(a, b):
    return lax.dot_general(a, b, (((0,), (0,)), ((), ())), preferred_element_type=F32)


def fold8(v):
    total = v[0:8]
    for at in range(8, v.shape[0], 8):
        total = total + v[at : at + 8]
    return total


def norm_parts(v):
    center = v - jnp.mean(v, axis=-1, keepdims=True)
    rs = lax.rsqrt(jnp.mean(center * center, axis=-1, keepdims=True) + EPS)
    return center * rs, rs


def by_core(taps, at, core):
    return jnp.where(core == 1, taps[3 * (2 - at // 3) + at % 3], taps[at])


def gelu_pair(v):
    z = jnp.abs(v) * 0.7071067811865476
    t = 1.0 / (1.0 + 0.3275911 * z)
    e = jnp.exp(-0.5 * (v * v))
    poly = t * (
        0.127414796
        + t * (-0.142248368 + t * (0.7107068705 + t * (-0.7265760135 + t * 0.5307027145)))
    )
    tail = poly * e
    cdf = jnp.where(v >= 0, 1.0 - tail, tail)
    return v * cdf, cdf + v * (e * 0.3989422804014327)


def side_masks():
    place = lax.broadcasted_iota(jnp.int32, (16, 128), 0)
    return place == 0, place == 15


def with_sides(even, odd, masks):
    left = jnp.where(masks[0], 0.0, pltpu.roll(odd, 1, 0))
    right = jnp.where(masks[1], 0.0, pltpu.roll(even, 15, 0))
    return even, odd, left, right


def conv_row(rows, taps):
    even = odd = None
    for a in range(3):
        if rows[a] is None:
            continue
        ev, od, left, right = rows[a]
        for tap, ce, co in ((3 * a, left, ev), (3 * a + 1, ev, od), (3 * a + 2, od, right)):
            even = taps[tap] * ce if even is None else even + taps[tap] * ce
            odd = taps[tap] * co if odd is None else odd + taps[tap] * co
    return even, odd


def tap_products(sums, rows, d_even, d_odd):
    for a in range(3):
        if rows[a] is None:
            continue
        ev, od, left, right = rows[a]
        for tap, ce, co in ((3 * a, left, ev), (3 * a + 1, ev, od), (3 * a + 2, od, right)):
            term = fold8(d_even * ce + d_odd * co)
            sums[tap] = term if sums[tap] is None else sums[tap] + term


def ffn_kernel(
    x_ref, at_ref, ct_ref, mod_ref, alive_ref, perm_ref, ow_ref, ob_ref, f1_ref, f1b_ref,
    tap_ref, cb_ref, f2_ref, f2b_ref,
    out_ref, fg_ref, go_ref, da_ref, dx_ref, s2_ref, sm_ref,
    x1_s, br_s, h2_s, h2t_s, dffn_s, u_s, duc_s, act_s, du_s, dact_s, ffn_s, dh2_s, acc_s,
    fg_s, fg_sem,
):
    step = pl.program_id(0)
    core = lax.axis_index("seq") % 2
    alive = alive_ref[0]

    @pl.when(step == 0)
    def _():
        br_s[...] = mm(at_ref[...], ow_ref[...]) + ob_ref[...].astype(F32)
        shift2, scale2, gate1, gate2 = (mod_ref[i : i + 1, :] for i in (3, 4, 2, 5))

        def rows_a(r, _):
            at = pl.ds(pl.multiple_of(r * 32, 32), 32)
            x1 = x_ref[at, :].astype(F32) + gate1 * br_s[at, :]
            x1_s[at, :] = x1
            n2, _unused = norm_parts(x1)
            h2_s[at, :] = (n2 * (1.0 + scale2) + shift2).astype(BF16)
            return 0

        lax.fori_loop(0, 18, rows_a, 0)

        def rows_b(r, _):
            at = pl.ds(pl.multiple_of(r * 32, 32), 32)
            dffn_s[at, :] = (ct_ref[at, :].astype(F32) * alive * gate2).astype(BF16)
            return 0

        lax.fori_loop(0, 17, rows_b, 0)
        for p in range(3):
            h2t_s[p] = mm_nt(perm_ref[p], h2_s[0:512, :]).astype(BF16)
        ffn_s[...] = jnp.zeros_like(ffn_s)
        dh2_s[...] = jnp.zeros_like(dh2_s)

    for j in range(3):
        cols = slice(256 * j, 256 * j + 256)
        u_s[:, cols] = (mm(h2_s[...], f1_ref[:, cols]) + f1b_ref[:, cols].astype(F32)).astype(BF16)
        dact_s[:, cols] = mm_nt(dffn_s[...], f2_ref[cols, :])

    masks = side_masks()

    def lanes(j, _):
        cols = pl.ds(pl.multiple_of(j * 128, 128), 128)
        taps = [tap_ref[t : t + 1, cols] for t in range(9)]
        taps = [by_core(taps, t, core) for t in range(9)]
        offset = cb_ref[:, cols].astype(F32)

        def sided(ref, l):
            return with_sides(
                ref[32 * l : 32 * l + 16, cols].astype(F32),
                ref[32 * l + 16 : 32 * l + 32, cols].astype(F32),
                masks,
            )

        rows = [None, sided(u_s, 0), sided(u_s, 1)]
        sums = [None] * 9
        bias_sum = None
        for l in range(17):
            ce, co = conv_row(rows, taps)
            ae, ge = gelu_pair(ce + offset)
            ao, go = gelu_pair(co + offset)
            de = (ge * dact_s[32 * l : 32 * l + 16, cols]).astype(BF16)
            do = (go * dact_s[32 * l + 16 : 32 * l + 32, cols]).astype(BF16)
            duc_s[32 * l : 32 * l + 16, cols] = de
            duc_s[32 * l + 16 : 32 * l + 32, cols] = do
            if l < 16:
                act_s[32 * l : 32 * l + 16, cols] = ae.astype(BF16)
                act_s[32 * l + 16 : 32 * l + 32, cols] = ao.astype(BF16)
                de, do = de.astype(F32), do.astype(F32)
                tap_products(sums, rows, de, do)
                term = fold8(de + do)
                bias_sum = term if bias_sum is None else bias_sum + term
                rows = [rows[1], rows[2], sided(u_s, l + 2) if l + 2 < 18 else None]
        for t in range(9):
            s2_ref[t : t + 1, cols] = jnp.sum(by_core(sums, t, core), axis=0, keepdims=True)
        s2_ref[9:10, cols] = jnp.sum(bias_sum, axis=0, keepdims=True)
        back = [taps[8 - t] for t in range(9)]
        rows = [None, sided(duc_s, 0), sided(duc_s, 1)]
        bias_sum = None
        for l in range(16):
            ue, uo = conv_row(rows, back)
            ue, uo = ue.astype(BF16), uo.astype(BF16)
            du_s[32 * l : 32 * l + 16, cols] = ue
            du_s[32 * l + 16 : 32 * l + 32, cols] = uo
            term = fold8(ue.astype(F32) + uo.astype(F32))
            bias_sum = term if bias_sum is None else bias_sum + term
            rows = [rows[1], rows[2], sided(duc_s, l + 2) if l + 2 < 17 else None]
        s2_ref[10:11, cols] = jnp.sum(bias_sum, axis=0, keepdims=True)
        return 0

    lax.fori_loop(0, FC // 128, lanes, 0)

    ffn_s[...] += mm(act_s[...], f2_ref[...])
    dh2_s[...] += mm_nt(du_s[...], f1_ref[...])
    for j in range(3):
        cols = slice(256 * j, 256 * j + 256)
        fg_s[0, j, step] = mm(h2t_s[j], du_s[:, cols]).astype(BF16).reshape(4, 4, 48, 256)
    for part in range(3):
        grad = mm_tn(act_s[...], dffn_s[0:512, 256 * part : 256 * part + 256]).astype(BF16)
        for zl in range(2):
            for y in range(4):
                for zh in range(2):
                    at = ((zl * 4 + y) * 2 + zh) * 48
                    z = zh * 2 + zl
                    rows = grad[at : at + 48, :]
                    if part == 0:
                        fg_s[1, 0, z, step, y] = rows
                    elif part == 1:
                        fg_s[1, 1, step, y, z] = rows
                    else:
                        fg_s[1, 2, y, z, step] = rows

    def moved(at, i):
        spots = (
            lambda ref: ref.at[0, :, at],
            lambda ref: ref.at[1, 0, :, at],
            lambda ref: ref.at[1, 1, at],
            lambda ref: ref.at[1, 2, :, :, at],
        )
        return pltpu.make_async_copy(spots[i](fg_s), spots[i](fg_ref), fg_sem.at[at, i])

    for i in range(4):
        moved(step, i).start()

    @pl.when(step == NFC - 1)
    def _():
        shift2, scale2, gate1, gate2 = (mod_ref[i : i + 1, :] for i in (3, 4, 2, 5))
        acc_s[...] = jnp.zeros_like(acc_s)
        f2b = f2b_ref[...].astype(F32)

        def rows_c(r, _):
            at = pl.ds(pl.multiple_of(r * 32, 32), 32)
            x1 = x1_s[at, :]
            ffn = ffn_s[at, :] + f2b
            dy = ct_ref[at, :].astype(F32) * alive
            out_ref[at, :] = (alive * (x1 + gate2 * ffn)).astype(BF16)
            n2, rs = norm_parts(x1)
            dh2 = dh2_s[at, :]
            g2 = dh2 * (1.0 + scale2)
            dx1 = dy + rs * (
                g2
                - jnp.mean(g2, axis=-1, keepdims=True)
                - n2 * jnp.mean(g2 * n2, axis=-1, keepdims=True)
            )
            dx_ref[at, :] = dx1
            dbr = (dx1 * gate1).astype(BF16)
            da_ref[at, :] = dbr
            acc_s[0] += fold8(dx1 * br_s[at, :])
            acc_s[1] += fold8(dh2)
            acc_s[2] += fold8(dh2 * n2)
            acc_s[3] += fold8(dy * ffn)
            acc_s[4] += fold8(dbr.astype(F32))
            acc_s[5] += fold8(dffn_s[at, :].astype(F32))
            return 0

        lax.fori_loop(0, 16, rows_c, 0)
        for i in range(6):
            sm_ref[i : i + 1, :] = jnp.sum(acc_s[i], axis=0, keepdims=True)
        for p in range(3):
            h2t_s[p] = mm_nt(perm_ref[p], at_ref[0:512, :]).astype(BF16)
            go_ref[p] = mm(h2t_s[p], da_ref[:, 256 * p : 256 * p + 256]).astype(BF16)
        da_ref[...] = mm_nt(da_ref[...], ow_ref[...]).astype(BF16)
        for at in range(NFC):
            for i in range(4):
                moved(at, i).wait()


def ffn_call(x, at, ct, mod, alive, perm, ow, ob, f1, f1b, taps, cb, f2, f2b):
    whole = lambda s: pl.BlockSpec(s, lambda i: (0,) * len(s))
    return pl.pallas_call(
        ffn_kernel,
        grid=(NFC,),
        in_specs=[
            whole((576, D)), whole((576, D)), whole((576, D)), whole((8, D)),
            pl.BlockSpec(memory_space=pltpu.SMEM),
            whole((3, D, D)), whole((D, D)), whole((1, D)),
            pl.BlockSpec((D, FC), lambda i: (0, i)),
            pl.BlockSpec((1, FC), lambda i: (0, i)),
            pl.BlockSpec((16, FC), lambda i: (0, i)),
            pl.BlockSpec((1, FC), lambda i: (0, i)),
            pl.BlockSpec((FC, D), lambda i: (i, 0)),
            whole((1, D)),
        ],
        out_specs=[
            whole((512, D)),
            pl.BlockSpec(memory_space=pl.ANY),
            whole((3, D, 256)),
            whole((512, D)), whole((512, D)),
            pl.BlockSpec((16, FC), lambda i: (0, i)),
            whole((8, D)),
        ],
        out_shape=[
            jax.ShapeDtypeStruct((512, D), BF16),
            jax.ShapeDtypeStruct((2, 3, 4, 4, 4, 48, 256), BF16),
            jax.ShapeDtypeStruct((3, D, 256), BF16),
            jax.ShapeDtypeStruct((512, D), BF16),
            jax.ShapeDtypeStruct((512, D), F32),
            jax.ShapeDtypeStruct((16, FF), F32),
            jax.ShapeDtypeStruct((8, D), F32),
        ],
        scratch_shapes=[
            pltpu.VMEM((576, D), F32), pltpu.VMEM((576, D), F32), pltpu.VMEM((576, D), BF16),
            pltpu.VMEM((3, D, 512), BF16), pltpu.VMEM((544, D), BF16),
            pltpu.VMEM((576, FC), BF16), pltpu.VMEM((544, FC), BF16), pltpu.VMEM((512, FC), BF16),
            pltpu.VMEM((512, FC), BF16), pltpu.VMEM((544, FC), F32),
            pltpu.VMEM((512, D), F32), pltpu.VMEM((512, D), F32), pltpu.VMEM((6, 8, D), F32),
            pltpu.VMEM((2, 3, 4, 4, 4, 48, 256), BF16), pltpu.SemaphoreType.DMA((NFC, 4)),
        ],
        compiler_params=pltpu.CompilerParams(
            dimension_semantics=("arbitrary",), vmem_limit_bytes=60 * 2**20
        ),
        name="ffn",
    )(x, at, ct, mod, alive, perm, ow, ob, f1, f1b, taps, cb, f2, f2b)


MESH = pl.DeviceIdType.MESH


def spot():
    dp = lax.axis_index("dp")
    seq = lax.axis_index("seq")
    return dict(dp=dp, seq=seq, x=dp // 8, zl=(dp // 4) % 2, y=dp % 4, zh=seq // 2, core=seq % 2)


def seq_peer(me, zh, core):
    return (me["dp"], zh * 2 + core)


def axis_peer(me, axis, offset):
    x, y, z = me["x"], me["y"], me["zh"] * 2 + me["zl"]
    if axis == "x":
        x = (x + offset) % 4
    elif axis == "y":
        y = (y + offset) % 4
    else:
        z = (z + offset) % 4
    return ((x * 2 + z % 2) * 4 + y, (z // 2) * 2 + me["core"])


def remote(src, dst, send, recv, device):
    return pltpu.make_async_remote_copy(
        src_ref=src, dst_ref=dst, send_sem=send, recv_sem=recv, device_id=device,
        device_id_type=MESH,
    )


def arrived(ref, sem):
    pltpu.make_async_copy(ref, ref, sem).wait()


def place_matrix(count, flip, inverse):
    rows = count // 32
    out = lax.broadcasted_iota(jnp.int32, (count, count), 0)
    at = lax.broadcasted_iota(jnp.int32, (count, count), 1)
    row = out // 32
    row = jnp.where(flip, rows - 1 - row, row)
    low = out % 32
    if inverse:
        low = (low % 2) * 16 + low // 2
    else:
        low = (low % 16) * 2 + low // 16
    return jnp.where(at == row * 32 + low, 1.0, 0.0).astype(BF16)


def head_lanes(values, half):
    lane = lax.broadcasted_iota(jnp.int32, values.shape, 1)
    return jnp.where((lane // 64) == half, values, jnp.zeros_like(values))


def attn_kernel(
    lat_ref, ct_ref, mod_ref, w_ref, qb_ref, tap_ref, cb_ref,
    x_out, ct_out, h_out, hcg_out, qkv_out, p_out, at_out,
    xr_s, xh_s, x_s, c_s, h_s, hcg_s, sb_s, w_s, qkv_s, p_s, ag_s, at_s,
    send0, recv0, sem_pair, sem_loc,
):
    me = spot()
    zh, core, seq = me["zh"], me["core"], me["seq"]
    other = seq_peer(me, zh, 1 - core)
    w_load = pltpu.make_async_copy(w_ref, w_s, sem_loc.at[0])
    w_load.start()

    barrier = pltpu.get_barrier_semaphore()
    for dz, dc in ((0, 1), (1, 0), (1, 1)):
        pl.semaphore_signal(
            barrier, inc=1, device_id=seq_peer(me, (zh + dz) % 2, (core + dc) % 2),
            device_id_type=MESH,
        )
    pl.semaphore_wait(barrier, 3)

    slot = jnp.where(zh == 0, core, 1 - core)
    inner = jnp.logical_or(seq == 1, seq == 2)
    halo_core = jnp.where(seq == 1, 1, 0)
    halo_at = pl.multiple_of(jnp.where(seq == 1, 192, 0), 64)

    def sends(act):
        for a, ref in enumerate((lat_ref, ct_ref)):
            for j in range(2):
                own = jnp.logical_and(zh == j, core == zh)
                main = (ref.at[j], xr_s.at[a, slot])
                halo = (ref.at[j, pl.ds(halo_at, 64)], xh_s.at[a])

                @pl.when(own)
                def _():
                    act(lambda: pltpu.make_async_copy(*main, recv0.at[a, slot]), True)

                @pl.when(jnp.logical_not(own))
                def _():
                    act(
                        lambda: remote(*main, send0.at[a, j, 0], recv0.at[a, slot], seq_peer(me, j, zh)),
                        False,
                    )

                @pl.when(jnp.logical_and(inner, zh == j))
                def _():
                    act(lambda: pltpu.make_async_copy(*halo, recv0.at[a, 2]), True)

                @pl.when(jnp.logical_and(inner, zh != j))
                def _():
                    act(
                        lambda: remote(
                            *halo, send0.at[a, j, 1], recv0.at[a, 2], seq_peer(me, j, halo_core)
                        ),
                        False,
                    )

    sends(lambda make, local: make().start())

    flip = core == 1
    big = place_matrix(256, flip, False)
    small = place_matrix(64, flip, False)
    shift1, scale1 = mod_ref[0:1, :], mod_ref[1:2, :]

    def placed(a, into):
        for b in range(2):
            arrived(xr_s.at[a, b], recv0.at[a, b])
            into[256 * b : 256 * b + 256, :] = mm(big, xr_s[a, b]).astype(BF16)
        arrived(xh_s.at[a], recv0.at[a, 2])
        into[512:576, :] = mm(small, xh_s[a]).astype(BF16)

    placed(0, x_s)

    def rows_a(r, _):
        at = pl.ds(pl.multiple_of(r * 32, 32), 32)
        n1, _unused = norm_parts(x_s[at, :].astype(F32))
        h_s[at, :] = (n1 * (1.0 + scale1) + shift1).astype(BF16)
        return 0

    lax.fori_loop(0, 18, rows_a, 0)
    outs = [
        pltpu.make_async_copy(x_s, x_out, sem_loc.at[1]),
        pltpu.make_async_copy(h_s, h_out, sem_loc.at[2]),
    ]
    for copy in outs:
        copy.start()
    masks = side_masks()

    def lanes(j, _):
        cols = pl.ds(pl.multiple_of(j * 128, 128), 128)
        taps = [tap_ref[t : t + 1, cols] for t in range(9)]
        taps = [by_core(taps, t, core) for t in range(9)]
        offset = cb_ref[:, cols].astype(F32)

        def sided(l):
            return with_sides(
                h_s[32 * l : 32 * l + 16, cols].astype(F32),
                h_s[32 * l + 16 : 32 * l + 32, cols].astype(F32),
                masks,
            )

        rows = [None, sided(0), sided(1)]
        for l in range(16):
            ce, co = conv_row(rows, taps)
            ce, co = (ce + offset).astype(BF16), (co + offset).astype(BF16)
            if l % 2 == 0:
                hcg_s[0, l // 2, 0, :, cols] = ce
                hcg_s[0, l // 2, 1, :, cols] = co
            else:
                sb_s[l // 2, 0, :, cols] = ce
                sb_s[l // 2, 1, :, cols] = co
            rows = [rows[1], rows[2], sided(l + 2) if l < 15 else None]
        return 0

    lax.fori_loop(0, D // 128, lanes, 0)
    hc_copy = remote(sb_s, hcg_s.at[1], sem_pair.at[0], sem_pair.at[1], other)
    hc_copy.start()
    w_load.wait()

    def project(half):
        got = mm(hcg_s[half].reshape(256, D), w_s[...]) + qb_ref[...]
        qkv_s[half] = got.astype(BF16).reshape(8, 2, 16, 3 * D)

    project(0)
    hc_copy.wait()
    outs.append(pltpu.make_async_copy(hcg_s, hcg_out, sem_loc.at[3]))
    outs[-1].start()
    project(1)
    outs.append(pltpu.make_async_copy(qkv_s, qkv_out, sem_loc.at[4]))
    outs[-1].start()

    def attend(i, _):
        pc, pair = i // 6, i % 6

        def part(which):
            cols = pl.ds(pl.multiple_of(which * D + pair * 128, 128), 128)
            return jnp.concatenate(
                [qkv_s[half, :, pc, :, cols].reshape(128, 128) for half in range(2)], axis=0
            )

        q, k, v = part(0), part(1), part(2)
        v_t = v.T
        got = []
        for half in range(2):
            scores = mm_nt(k, head_lanes(q, half)) * 0.125
            e = jnp.exp(scores - jnp.max(scores, axis=0, keepdims=True))
            low = (e * (1.0 / jnp.sum(e, axis=0, keepdims=True))).astype(BF16)
            p_s[2 * i + half] = low
            got.append(mm(v_t[64 * half : 64 * half + 64], low))
        o = jnp.concatenate(got, axis=0).T.astype(BF16)
        cols = pl.ds(pl.multiple_of(pair * 128, 128), 128)
        for half in range(2):
            ag_s[half, :, pc, :, cols] = o[128 * half : 128 * half + 128].reshape(8, 16, 128)
        return 0

    lax.fori_loop(0, 12, attend, 0)
    back = [
        remote(ag_s.at[1], at_s.at[pl.ds(0, 8), 1], sem_pair.at[2], sem_pair.at[3], other),
        remote(ag_s.at[0, 7], at_s.at[8, 1], sem_pair.at[4], sem_pair.at[5], other),
        pltpu.make_async_copy(ag_s.at[0], at_s.at[pl.ds(0, 8), 0], sem_loc.at[5]),
        pltpu.make_async_copy(ag_s.at[1, 7], at_s.at[8, 0], sem_loc.at[6]),
    ]
    for copy in back:
        copy.start()
    outs.append(pltpu.make_async_copy(p_s, p_out, sem_loc.at[7]))
    outs[-1].start()
    placed(1, c_s)
    outs.append(pltpu.make_async_copy(c_s, ct_out, sem_loc.at[8]))
    outs[-1].start()
    for copy in back:
        copy.wait()
    outs.append(pltpu.make_async_copy(at_s, at_out, sem_loc.at[9]))
    outs[-1].start()
    for copy in outs:
        copy.wait()

    def finish(make, local):
        if not local:
            make().wait_send()

    sends(finish)


VMEM_SPEC = pl.BlockSpec(memory_space=pltpu.VMEM)
ANY_SPEC = pl.BlockSpec(memory_space=pl.ANY)


def attn_call(lat, ct, mod, w, qb, taps, cb):
    G = (2, 8, 2, 16)
    shape = jax.ShapeDtypeStruct
    return pl.pallas_call(
        attn_kernel,
        in_specs=[ANY_SPEC, ANY_SPEC, VMEM_SPEC, ANY_SPEC, VMEM_SPEC, VMEM_SPEC, VMEM_SPEC],
        out_specs=[ANY_SPEC] * 7,
        out_shape=[
            shape((576, D), BF16), shape((576, D), BF16), shape((576, D), BF16),
            shape(G + (D,), BF16), shape(G + (3 * D,), BF16), shape((24, 256, 256), BF16),
            shape((9, 2, 2, 16, D), BF16),
        ],
        scratch_shapes=[
            pltpu.VMEM((2, 2, 256, D), BF16), pltpu.VMEM((2, 64, D), BF16),
            pltpu.VMEM((576, D), BF16), pltpu.VMEM((576, D), BF16), pltpu.VMEM((576, D), BF16),
            pltpu.VMEM(G + (D,), BF16), pltpu.VMEM((8, 2, 16, D), BF16),
            pltpu.VMEM((D, 3 * D), BF16), pltpu.VMEM(G + (3 * D,), BF16),
            pltpu.VMEM((24, 256, 256), BF16), pltpu.VMEM(G + (D,), BF16),
            pltpu.VMEM((9, 2, 2, 16, D), BF16),
            pltpu.SemaphoreType.DMA((2, 2, 2)), pltpu.SemaphoreType.DMA((2, 3)),
            pltpu.SemaphoreType.DMA((6,)), pltpu.SemaphoreType.DMA((10,)),
        ],
        compiler_params=pltpu.CompilerParams(
            collective_id=1, has_side_effects=True, vmem_limit_bytes=56 * 2**20
        ),
        name="attend",
    )(lat, ct, mod, w, qb, taps, cb)


ORDERS = (("x", "y", "z"), ("y", "z", "x"), ("z", "x", "y"))


def axis_spot(me, axis):
    return me["zh"] * 2 + me["zl"] if axis == "z" else me[axis]


def back_kernel(
    da_ref, qkv_ref, p_ref, hcg_ref, h_ref, x_ref, dx_ref, mod_ref, w_ref, tap_ref, perm_ref,
    o_ref, fg_ref, go_ref, s2_ref, sb_ref,
    oret_out, iret_out, fe_out, fl_out, sm_out, dm_out,
    qkv_s, p_s, w_s, perm_s, dag_s, dqkv_s, hct_s, dhc_s, dh_s, gh_s, ig_s, os_s, is_s,
    own_s, pre_s, lg_s, prl_s, r1e, r1l, s1e, s1l, r2e, r2l, t3e, t3l, r3e, r3l, fe_s, fl_s,
    acc_s, sv_s, sp_s, sr_s, sx_s, mp_s, mr_s, dm_s, smf_s,
    loc, pair_sem, ret_send, ret_recv, st_send, st_recv, sx_send, sx_recv, dm_send, dm_recv,
):
    me = spot()
    zh, core = me["zh"], me["core"]
    other = seq_peer(me, zh, 1 - core)
    loads = [
        pltpu.make_async_copy(qkv_ref, qkv_s, loc.at[0]),
        pltpu.make_async_copy(p_ref, p_s, loc.at[1]),
        pltpu.make_async_copy(w_ref, w_s, loc.at[2]),
        pltpu.make_async_copy(perm_ref, perm_s, loc.at[3]),
        pltpu.make_async_copy(da_ref.at[:, 0], dag_s.at[0], loc.at[4]),
        pltpu.make_async_copy(fg_ref.at[core], own_s, loc.at[5]),
        pltpu.make_async_copy(go_ref, lg_s.at[1, :, 0], loc.at[6]),
    ]
    for at in (4, 0, 1, 2, 3, 5, 6):
        loads[at].start()
    barrier = pltpu.get_barrier_semaphore()
    peers = [axis_peer(me, axis, o) for axis in "xyz" for o in (1, 2, 3)]
    peers += [other, seq_peer(me, 1 - zh, 1 - core)]
    for peer in peers:
        pl.semaphore_signal(barrier, inc=1, device_id=peer, device_id_type=MESH)
    pl.semaphore_wait(barrier, len(peers))

    da_copy = remote(da_ref.at[:, 1], dag_s.at[1], pair_sem.at[0, 0], pair_sem.at[0, 1], other)
    da_copy.start()
    early = [
        remote(fg_ref.at[1 - core, p], pre_s.at[p], pair_sem.at[1 + p, 0], pair_sem.at[1 + p, 1], other)
        for p in range(3)
    ]
    for copy in early:
        copy.start()

    home = place_matrix(256, core == 1, True)

    def give_back(which, act):
        ref, out = ((os_s, oret_out), (is_s, iret_out))[which]
        for b in range(2):
            to_core = jnp.where(core == 0, b, 1 - b)
            own = jnp.logical_and(zh == core, b == 0)

            @pl.when(own)
            def _():
                act(lambda: pltpu.make_async_copy(ref.at[b], out.at[zh], ret_recv.at[which, zh]), True)

            @pl.when(jnp.logical_not(own))
            def _():
                act(
                    lambda: remote(
                        ref.at[b], out.at[zh], ret_send.at[which, b], ret_recv.at[which, zh],
                        seq_peer(me, core, to_core),
                    ),
                    False,
                )

    for b in range(2):
        os_s[b] = mm(home, o_ref[256 * b : 256 * b + 256, :]).astype(BF16)
    give_back(0, lambda make, local: make().start())

    loads[3].wait()
    for p in range(3):
        hct_s[p] = mm_nt(perm_s[p], hcg_ref[...]).astype(BF16)
    loads[4].wait()
    loads[0].wait()
    loads[1].wait()
    da_copy.wait()

    def attend_back(i, _):
        pc, pair = i // 6, i % 6
        lanes_at = [
            pl.ds(pl.multiple_of(which * D + pair * 128, 128), 128) for which in range(3)
        ]

        def part(ref, cols):
            return jnp.concatenate(
                [ref[half, :, pc, :, cols].reshape(128, 128) for half in range(2)], axis=0
            )

        q, k, v = (part(qkv_s, cols) for cols in lanes_at)
        do = part(dag_s, lanes_at[0])
        k_t = k.T
        dq_t, dk, dv = [], None, None
        for half in range(2):
            dom, qm = head_lanes(do, half), head_lanes(q, half)
            low = p_s[2 * i + half]
            probs = low.astype(F32)
            dp = mm_nt(v, dom)
            ds = (probs * (dp - jnp.sum(probs * dp, axis=0, keepdims=True))).astype(BF16)
            dq_t.append(mm(k_t[64 * half : 64 * half + 64], ds))
            dk_h, dv_h = mm(ds, qm), mm(low, dom)
            dk = dk_h if dk is None else dk + dk_h
            dv = dv_h if dv is None else dv + dv_h
        dq = jnp.concatenate(dq_t, axis=0).T
        for cols, got in zip(lanes_at, (0.125 * dq, 0.125 * dk, dv)):
            got = got.astype(BF16)
            for half in range(2):
                dqkv_s[half, :, pc, :, cols] = got[128 * half : 128 * half + 128].reshape(8, 16, 128)
        return 0

    def stage_sends(stage, bufs, panels, late):
        out = []
        for p in range(3):
            axis = ORDERS[p][stage]
            here = axis_spot(me, axis)
            for o in (1, 2, 3):
                there = (here + o) % 4
                src, dst = bufs(p, o, there)
                copy = remote(
                    src, dst, st_send.at[late, stage, p, o - 1], st_recv.at[late, stage, p, o - 1],
                    axis_peer(me, axis, o),
                )
                copy.start()
                out.append(copy)
        return out

    def chunk(there, rows):
        return pl.ds(pl.multiple_of(there * rows, 16), rows)

    lax.fori_loop(0, 6, attend_back, 0)
    loads[5].wait()
    for p in range(3):
        early[p].wait()

        def add_early(k, _):
            own_s[p, k] = own_s[p, k] + pre_s[p, k]
            return 0

        lax.fori_loop(0, 4, add_early, 0)
    st1e = stage_sends(
        0, lambda p, o, a: (own_s.at[p, :, chunk(a, 192)], r1e.at[o - 1, p]), 4, 0
    )
    lax.fori_loop(6, 12, attend_back, 0)

    loads[2].wait()
    for half in (1, 0):
        got = mm_nt(dqkv_s[half].reshape(256, 3 * D), w_s[...]).astype(BF16)
        dhc_s[half] = got.reshape(8, 2, 16, D)
        if half == 1:
            dhc_copy = remote(
                dhc_s.at[1], dh_s.at[pl.ds(0, 8), 1], pair_sem.at[4, 0], pair_sem.at[4, 1], other
            )
            dhc_copy.start()
    near = [
        pltpu.make_async_copy(dhc_s.at[0], dh_s.at[pl.ds(0, 8), 0], loc.at[7]),
        pltpu.make_async_copy(dhc_s.at[1, 7], dh_s.at[8, 0], loc.at[8]),
    ]
    for copy in near:
        copy.start()
    loads[6].wait()
    for p in range(3):
        for at, to in (
            (512 * p, (0, p, 0)), (512 * p + 256, (0, p, 1)), (1536 + 256 * p, (1, p, 1))
        ):
            lg_s[to] = mm(
                hct_s[p], dqkv_s[:, :, :, :, at : at + 256].reshape(512, 256)
            ).astype(BF16)
    late = [
        remote(lg_s.at[1 - core, p], prl_s.at[p], pair_sem.at[5 + p, 0], pair_sem.at[5 + p, 1], other)
        for p in range(3)
    ]
    for copy in late:
        copy.start()
    ones = jnp.ones((8, 512), BF16)
    sv_s[64:96, :] = jnp.zeros((32, D), F32)
    for row, at in ((74, 0), (75, 2 * D)):
        sums = mm(ones, dqkv_s[:, :, :, :, at : at + D].reshape(512, D))
        sv_s[row : row + 1, :] = sums[0:1]
    sv_s[76:78, :] = sb_ref[4:6, :]
    for q in range(4):
        sv_s[16 * q : 16 * q + 16, :] = s2_ref[:, D * q : D * q + D]

    dhc_copy.wait()
    for copy in near:
        copy.wait()
    masks = side_masks()

    def lanes(j, _):
        cols = pl.ds(pl.multiple_of(j * 128, 128), 128)
        taps = [tap_ref[t : t + 1, cols] for t in range(9)]
        back = [by_core(taps, 8 - t, core) for t in range(9)]

        def sided_d(l):
            return with_sides(
                dh_s[l // 2, l % 2, 0, :, cols].astype(F32),
                dh_s[l // 2, l % 2, 1, :, cols].astype(F32),
                masks,
            )

        def sided_h(l):
            return with_sides(
                h_ref[32 * l : 32 * l + 16, cols].astype(F32),
                h_ref[32 * l + 16 : 32 * l + 32, cols].astype(F32),
                masks,
            )

        rows = [None, sided_d(0), sided_d(1)]
        rows_h = [None, sided_h(0), sided_h(1)]
        sums = [None] * 9
        bias_sum = None
        for l in range(16):
            ge, go = conv_row(rows, back)
            gh_s[32 * l : 32 * l + 16, cols] = ge
            gh_s[32 * l + 16 : 32 * l + 32, cols] = go
            de, do = rows[1][0], rows[1][1]
            tap_products(sums, rows_h, de, do)
            term = fold8(de + do)
            bias_sum = term if bias_sum is None else bias_sum + term
            if l < 15:
                rows = [rows[1], rows[2], sided_d(l + 2)]
                rows_h = [rows_h[1], rows_h[2], sided_h(l + 2)]
        for t in range(9):
            total = jnp.sum(by_core(sums, t, core), axis=0, keepdims=True)
            sv_s[64 + t : 65 + t, cols] = total
        sv_s[73:74, cols] = jnp.sum(bias_sum, axis=0, keepdims=True)
        return 0

    lax.fori_loop(0, D // 128, lanes, 0)
    scale1 = mod_ref[1:2, :]
    acc_s[...] = jnp.zeros_like(acc_s)

    def rows_n(r, _):
        at = pl.ds(pl.multiple_of(r * 32, 32), 32)
        n1, rs = norm_parts(x_ref[at, :].astype(F32))
        dh = gh_s[at, :]
        g1 = dh * (1.0 + scale1)
        got = dx_ref[at, :] + rs * (
            g1
            - jnp.mean(g1, axis=-1, keepdims=True)
            - n1 * jnp.mean(g1 * n1, axis=-1, keepdims=True)
        )
        ig_s[at, :] = got.astype(BF16)
        acc_s[0] += fold8(dh)
        acc_s[1] += fold8(dh * n1)
        return 0

    lax.fori_loop(0, 16, rows_n, 0)
    for i in range(2):
        mp_s[i : i + 1, :] = jnp.sum(acc_s[i], axis=0, keepdims=True)
    mp_s[2:6, :] = sb_ref[0:4, :]
    mp_s[6:8, :] = jnp.zeros((2, D), F32)
    mp_copy = remote(mp_s, mr_s, pair_sem.at[8, 0], pair_sem.at[8, 1], other)
    mp_copy.start()
    for half in range(2):
        sp_s[half] = sv_s[48 * half : 48 * half + 48, :].astype(BF16)
    sp_copy = remote(sp_s.at[1 - core], sr_s, pair_sem.at[9, 0], pair_sem.at[9, 1], other)
    sp_copy.start()
    for b in range(2):
        is_s[b] = mm(home, ig_s[256 * b : 256 * b + 256, :]).astype(BF16)
    give_back(1, lambda make, local: make().start())

    for copy in late:
        copy.wait()
    for p in range(3):
        for k in range(2):
            lg_s[core, p, k] = lg_s[core, p, k] + prl_s[p, k]
    st1l = stage_sends(
        0, lambda p, o, a: (lg_s.at[core, p, :, chunk(a, 192)], r1l.at[o - 1, p]), 2, 1
    )

    mp_copy.wait()
    item = (mp_s[...] + mr_s[...]).astype(BF16).astype(F32)
    dm_rows = [item[i : i + 1, 128 * l : 128 * l + 128] for i in range(6) for l in range(6)]
    z_me = axis_spot(me, "z")
    dm_s[z_me, me["y"], me["x"]] = jnp.concatenate(
        dm_rows + [jnp.zeros((12, 128), F32)], axis=0
    ).astype(BF16)
    sp_copy.wait()
    sx_s[0] = (sp_s[core].astype(F32) + sr_s[...].astype(F32)).astype(BF16)

    def small_stage(stage):
        axis = "xyz"[stage]
        view = (
            lambda ref: ref.at[z_me, me["y"], me["x"]],
            lambda ref: ref.at[z_me, me["y"]],
            lambda ref: ref.at[z_me],
        )[stage]
        out = []
        for o in (1, 2, 3):
            out.append(
                remote(
                    sx_s.at[4 * stage], sx_s.at[4 * stage + o], sx_send.at[stage, o - 1],
                    sx_recv.at[stage, o - 1], axis_peer(me, axis, o),
                )
            )
            out.append(
                remote(
                    view(dm_s), view(dm_s), dm_send.at[stage, o - 1], dm_recv.at[stage, o - 1],
                    axis_peer(me, axis, o),
                )
            )
        for copy in out:
            copy.start()
        return out

    def small_take(stage, copies):
        axis = "xyz"[stage]
        here = axis_spot(me, axis)
        for copy in copies:
            copy.wait_send()
        for o in (1, 2, 3):
            arrived(sx_s.at[4 * stage + o], sx_recv.at[stage, o - 1])
            there = (here + 4 - o) % 4
            view = (
                lambda: dm_s.at[z_me, me["y"], there],
                lambda: dm_s.at[z_me, there],
                lambda: dm_s.at[there],
            )[stage]
            arrived(view(), dm_recv.at[stage, o - 1])
        total = sx_s[4 * stage].astype(F32)
        for o in (1, 2, 3):
            total = total + sx_s[4 * stage + o].astype(F32)
        if stage < 2:
            sx_s[4 * stage + 4] = total.astype(BF16)
        else:
            smf_s[...] = total

    def take(copies):
        for copy in copies:
            copy.wait()

    def sum_one(own, recv, into, panels, p):
        def body(k, _):
            total = own(k).astype(F32)
            for o in range(3):
                total = total + recv[o, p, k].astype(F32)
            into[p, k] = total.astype(BF16)
            return 0

        lax.fori_loop(0, panels, body, 0)

    small = small_stage(0)
    take(st1e)
    for p in range(3):
        here = axis_spot(me, ORDERS[p][0])
        sum_one(lambda k: own_s[p, k, chunk(here, 192), :], r1e, s1e, 4, p)
    st2e = stage_sends(1, lambda p, o, b: (s1e.at[p, :, chunk(b, 48)], r2e.at[o - 1, p]), 4, 0)
    small_take(0, small)
    small = small_stage(1)
    take(st1l)
    for p in range(3):
        here = axis_spot(me, ORDERS[p][0])
        sum_one(lambda k: lg_s[core, p, k, chunk(here, 192), :], r1l, s1l, 2, p)
    st2l = stage_sends(1, lambda p, o, b: (s1l.at[p, :, chunk(b, 48)], r2l.at[o - 1, p]), 2, 1)

    def second(own, recv, panels, p):
        here = axis_spot(me, ORDERS[p][1])
        out = []
        for k in range(panels):
            total = own[p, k, chunk(here, 48), :].astype(F32)
            for o in range(3):
                total = total + recv[o, p, k].astype(F32)
            out.append(total)
        return out

    take(st2e)
    for p in range(3):
        got = second(s1e, r2e, 4, p)

        @pl.when(core == 0)
        def _():
            for c in range(4):
                t3e[p, c] = jnp.concatenate(
                    [got[k][12 * c : 12 * c + 12] for k in range(4)], axis=0
                ).astype(BF16)

        @pl.when(core == 1)
        def _():
            for c in range(4):
                t3e[p, c] = got[c].astype(BF16)

    st3e = stage_sends(2, lambda p, o, c: (t3e.at[p, c], r3e.at[o - 1, p]), 4, 0)
    small_take(1, small)
    small = small_stage(2)
    take(st2l)
    for p in range(3):
        got = second(s1l, r2l, 2, p)
        for c in range(4):
            t3l[p, c] = jnp.concatenate(
                [got[0][12 * c : 12 * c + 12], got[1][12 * c : 12 * c + 12], jnp.zeros((8, 256), F32)],
                axis=0,
            ).astype(BF16)
    st3l = stage_sends(2, lambda p, o, c: (t3l.at[p, c], r3l.at[o - 1, p]), 2, 1)

    ends = []

    def finish(copies, own, recv, done, out, at):
        take(copies)
        for p in range(3):
            total = own[p, axis_spot(me, ORDERS[p][2])].astype(F32)
            for o in range(3):
                total = total + recv[o, p].astype(F32)
            done[p] = total
        spread(done, out, at)

    def spread(done, out, at):
        ends.append(pltpu.make_async_copy(done, out.at[core], loc.at[at]))
        ends.append(
            remote(done, out.at[core], pair_sem.at[at, 0], pair_sem.at[at, 1], other)
        )
        ends[-1].start()
        ends[-2].start()

    finish(st3e, t3e, r3e, fe_s, fe_out, 10)
    small_take(2, small)
    spread(smf_s, sm_out, 11)
    ends.append(pltpu.make_async_copy(dm_s, dm_out, loc.at[9]))
    ends[-1].start()
    finish(st3l, t3l, r3l, fl_s, fl_out, 12)
    for which in range(2):
        give_back(which, lambda make, local: None if local else make().wait_send())
        for item_slot in range(2):
            out = (oret_out, iret_out)[which]
            arrived(out.at[item_slot], ret_recv.at[which, item_slot])
    for copy in ends:
        copy.wait()


def back_call(da, qkv, p, hcg, h, x, dx, mod, w, taps, perm, o, fg, go, s2, sb):
    G = (2, 8, 2, 16)
    shape = jax.ShapeDtypeStruct
    V = pltpu.VMEM
    return pl.pallas_call(
        back_kernel,
        in_specs=[
            ANY_SPEC, ANY_SPEC, ANY_SPEC, VMEM_SPEC, VMEM_SPEC, VMEM_SPEC, VMEM_SPEC, VMEM_SPEC,
            ANY_SPEC, VMEM_SPEC, ANY_SPEC, VMEM_SPEC, ANY_SPEC, ANY_SPEC, VMEM_SPEC, VMEM_SPEC,
        ],
        out_specs=[ANY_SPEC] * 6,
        out_shape=[
            shape((2, 256, D), BF16), shape((2, 256, D), BF16),
            shape((2, 3, 48, 256), F32), shape((2, 3, 32, 256), F32),
            shape((2, 48, D), F32), shape((4, 4, 4, 48, 128), BF16),
        ],
        scratch_shapes=[
            V(G + (3 * D,), BF16), V((24, 256, 256), BF16), V((D, 3 * D), BF16),
            V((3, D, D), BF16), V(G + (D,), BF16), V(G + (3 * D,), BF16), V((3, D, 512), BF16),
            V(G + (D,), BF16), V((9, 2, 2, 16, D), BF16), V((512, D), F32), V((512, D), BF16),
            V((2, 256, D), BF16), V((2, 256, D), BF16),
            V((3, 4, D, 256), BF16), V((3, 4, D, 256), BF16), V((2, 3, 2, D, 256), BF16),
            V((3, 2, D, 256), BF16),
            V((3, 3, 4, 192, 256), BF16), V((3, 3, 2, 192, 256), BF16),
            V((3, 4, 192, 256), BF16), V((3, 2, 192, 256), BF16),
            V((3, 3, 4, 48, 256), BF16), V((3, 3, 2, 48, 256), BF16),
            V((3, 4, 48, 256), BF16), V((3, 4, 32, 256), BF16),
            V((3, 3, 48, 256), BF16), V((3, 3, 32, 256), BF16),
            V((3, 48, 256), F32), V((3, 32, 256), F32),
            V((2, 8, D), F32), V((96, D), F32), V((2, 48, D), BF16), V((48, D), BF16),
            V((12, 48, D), BF16), V((8, D), F32), V((8, D), F32), V((4, 4, 4, 48, 128), BF16),
            V((48, D), F32),
            pltpu.SemaphoreType.DMA((13,)), pltpu.SemaphoreType.DMA((13, 2)),
            pltpu.SemaphoreType.DMA((2, 2)), pltpu.SemaphoreType.DMA((2, 2)),
            pltpu.SemaphoreType.DMA((2, 3, 3, 3)), pltpu.SemaphoreType.DMA((2, 3, 3, 3)),
            pltpu.SemaphoreType.DMA((3, 3)), pltpu.SemaphoreType.DMA((3, 3)),
            pltpu.SemaphoreType.DMA((3, 3)), pltpu.SemaphoreType.DMA((3, 3)),
        ],
        compiler_params=pltpu.CompilerParams(
            collective_id=2, has_side_effects=True, vmem_limit_bytes=62 * 2**20
        ),
        name="back",
    )(da, qkv, p, hcg, h, x, dx, mod, w, taps, perm, o, fg, go, s2, sb)


def perm_matrices():
    at = np.arange(D)
    rows = []
    for order in ORDERS:
        spots = dict(zip(order, (at // 192, at // 48 % 4, at // 12 % 4)))
        x, y, z = spots["x"], spots["y"], spots["z"]
        rows.append((((x * 2 + z % 2) * 4 + y) * 2 + z // 2) * 12 + at % 12)
    return np.stack(rows).astype(np.int32)


def local(
    latents, conditioning, timesteps, item_counts, cotangent, time_table, mod_weight, mod_bias,
    conv_attn_weight, conv_attn_bias, qkv_weight, query_bias, value_bias, out_weight, out_bias,
    fc1_weight, fc1_bias, conv_ffn_weight, conv_ffn_bias, fc2_weight, fc2_bias,
):
    core = lax.axis_index("seq") % 2
    shard = lax.axis_index("dp") * 4 + lax.axis_index("seq")
    all_cond = lax.all_gather(conditioning, "dp", axis=0, tiled=True)
    all_times = lax.all_gather(timesteps, "dp", axis=0, tiled=True)
    alive = (lax.axis_index("seq") // 2 < item_counts).astype(F32)
    perm = (perm_matrices()[:, :, None] == np.arange(D)[None, None, :]).astype(BF16)
    cond = conditioning.astype(F32) + time_table[timesteps].astype(F32)
    silu_cond = jax.nn.silu(cond).astype(BF16)
    mod = jnp.dot(silu_cond, mod_weight, preferred_element_type=F32) + mod_bias.astype(F32)
    mod = jnp.pad(mod.reshape(2, 6, D), ((0, 0), (0, 2), (0, 0)))
    mod = lax.dynamic_index_in_dim(mod, lax.axis_index("seq") // 2, 0, False)
    taps_attn = jnp.pad(conv_attn_weight.astype(F32), ((0, 7), (0, 0)))
    taps_ffn = jnp.pad(conv_ffn_weight.astype(F32), ((0, 7), (0, 0)))
    qkv_bias = jnp.concatenate(
        (query_bias.astype(F32), jnp.zeros((D,), F32), value_bias.astype(F32))
    )[None]
    x, ct, h, hcg, qkv, p, at = attn_call(
        latents.reshape(2, 256, D), cotangent.reshape(2, 256, D), mod, qkv_weight, qkv_bias,
        taps_attn, conv_attn_bias[None],
    )
    out, fg, go, da, dx, s2, sb = ffn_call(
        x, at.reshape(576, D), ct, mod, alive, perm, out_weight, out_bias[None], fc1_weight,
        fc1_bias[None], taps_ffn, conv_ffn_bias[None], fc2_weight, fc2_bias[None],
    )
    out, ig, fe, fl, sm, dm = back_call(
        da.reshape(8, 2, 2, 16, D), qkv, p, hcg.reshape(512, D), h, x, dx, mod, qkv_weight,
        taps_attn, perm, out, fg.reshape(2, 3, 4, D, 256), go, s2, sb,
    )
    output = out.reshape(2, 8, 32, D)
    input_grad = ig.reshape(2, 8, 32, D).astype(F32)
    d_mod = dm.reshape(2, 2, 4, 4, 48, 128)[:, :, :, :, :36].transpose(3, 1, 2, 0, 4, 5)
    d_mod = d_mod.reshape(64, 6 * D)
    all_cond = all_cond.astype(F32) + time_table[all_times].astype(F32)
    my_cond = lax.dynamic_slice_in_dim(all_cond, shard * 6, 6, axis=1)
    my_silu = jax.nn.silu(my_cond).astype(BF16)
    mod_grad = lax.dot_general(
        my_silu, d_mod, (((0,), (0,)), ((), ())), preferred_element_type=F32
    )
    mod_bias_grad = jnp.sum(
        lax.dynamic_slice_in_dim(d_mod, shard * 36, 36, axis=1).astype(F32), axis=0
    )

    def silu_slope(v):
        s = jax.nn.sigmoid(v)
        return s * (1.0 + v * (1.0 - s))

    own_d_mod = lax.dynamic_slice_in_dim(d_mod, lax.axis_index("dp") * 2, 2, axis=0)
    cond_grad = silu_slope(cond) * mm_nt(own_d_mod, mod_weight)
    my_rows = lax.dynamic_slice_in_dim(mod_weight, shard * 6, 6, axis=0)
    my_cond_grad = silu_slope(my_cond) * mm_nt(d_mod, my_rows)
    table_grad = jnp.dot(
        (jnp.arange(1000)[:, None] == all_times[None, :]).astype(F32), my_cond_grad,
        precision=lax.Precision.HIGHEST,
    )
    six = lambda v: lax.dynamic_slice_in_dim(v, core * 6, 6, axis=-2)
    fc1_grad = six(fe[0].reshape(3, 4, 12, 256)).transpose(2, 1, 0, 3).reshape(6, FF)
    fc2_grad = lax.dynamic_slice_in_dim(fe[1], core * 24, 24, axis=1).transpose(1, 0, 2)
    late = six(fl[:, :, :24].reshape(2, 3, 2, 12, 256))
    qkv_grad = jnp.concatenate(
        (
            late[0].transpose(2, 0, 1, 3).reshape(6, 1536),
            late[1, :, 1].transpose(1, 0, 2).reshape(6, D),
        ),
        axis=1,
    )
    out_grad = late[1, :, 0].transpose(1, 0, 2).reshape(6, D)
    sums = sm.reshape(96, D)
    wide = sums[:64].reshape(4, 16, D).transpose(1, 0, 2).reshape(16, FF)
    wide = lax.dynamic_slice_in_dim(wide, shard * 24, 24, axis=1)
    slim = lax.dynamic_slice_in_dim(sums[64:80], shard * 6, 6, axis=1)
    return (
        output, input_grad, cond_grad, table_grad, mod_grad, mod_bias_grad, slim[:9], slim[9],
        qkv_grad, slim[10], slim[11], out_grad, slim[12], fc1_grad, wide[10], wide[:9], wide[9],
        fc2_grad.reshape(24, D), slim[13],
    )


def solution(mesh):
    return jax.shard_map(
        local,
        mesh=mesh,
        in_specs=(
            P("dp", "seq", None, None),
            P("dp", None),
            P("dp"),
            P("dp"),
            P("dp", "seq", None, None),
            P(),
            P(),
            P(),
            P(),
            P(),
            P(),
            P(),
            P(),
            P(),
            P(),
            P(),
            P(),
            P(),
            P(),
            P(),
            P(),
        ),
        out_specs=(
            P("dp", "seq", None, None),
            P("dp", "seq", None, None),
            P("dp", None),
            P(None, ("dp", "seq")),
            P(("dp", "seq"), None),
            P(("dp", "seq")),
            P(None, ("dp", "seq")),
            P(("dp", "seq")),
            P(("dp", "seq"), None),
            P(("dp", "seq")),
            P(("dp", "seq")),
            P(("dp", "seq"), None),
            P(("dp", "seq")),
            P(("dp", "seq"), None),
            P(("dp", "seq")),
            P(None, ("dp", "seq")),
            P(("dp", "seq")),
            P(("dp", "seq"), None),
            P(("dp", "seq")),
        ),
        check_vma=False,
    )
```

```python
import functools

import jax
import jax.numpy as jnp
import numpy as np
from jax import lax
from jax.experimental import pallas as pl
from jax.experimental.pallas import tpu as pltpu
from jax.sharding import PartitionSpec as P

F32 = jnp.float32
BF16 = jnp.bfloat16
D = 768
FF = 3072
FC = 768
NFC = FF // FC
EPS = 1e-6


def mm(a, b):
    return lax.dot_general(a, b, (((1,), (0,)), ((), ())), preferred_element_type=F32)


def mm_nt(a, b):
    return lax.dot_general(a, b, (((1,), (1,)), ((), ())), preferred_element_type=F32)


def mm_tn(a, b):
    return lax.dot_general(a, b, (((0,), (0,)), ((), ())), preferred_element_type=F32)


def fold8(v):
    total = v[0:8]
    for at in range(8, v.shape[0], 8):
        total = total + v[at : at + 8]
    return total


def norm_parts(v):
    center = v - jnp.mean(v, axis=-1, keepdims=True)
    rs = lax.rsqrt(jnp.mean(center * center, axis=-1, keepdims=True) + EPS)
    return center * rs, rs


def by_core(taps, at, core):
    return jnp.where(core == 1, taps[3 * (2 - at // 3) + at % 3], taps[at])


def gelu_pair(v):
    z = jnp.abs(v) * 0.7071067811865476
    t = 1.0 / (1.0 + 0.3275911 * z)
    e = jnp.exp(-0.5 * (v * v))
    poly = t * (
        0.127414796
        + t * (-0.142248368 + t * (0.7107068705 + t * (-0.7265760135 + t * 0.5307027145)))
    )
    tail = poly * e
    cdf = jnp.where(v >= 0, 1.0 - tail, tail)
    return v * cdf, cdf + v * (e * 0.3989422804014327)


def side_masks():
    place = lax.broadcasted_iota(jnp.int32, (16, 128), 0)
    return place == 0, place == 15


def with_sides(even, odd, masks):
    left = jnp.where(masks[0], 0.0, pltpu.roll(odd, 1, 0))
    right = jnp.where(masks[1], 0.0, pltpu.roll(even, 15, 0))
    return even, odd, left, right


def conv_row(rows, taps):
    even = odd = None
    for a in range(3):
        if rows[a] is None:
            continue
        ev, od, left, right = rows[a]
        for tap, ce, co in ((3 * a, left, ev), (3 * a + 1, ev, od), (3 * a + 2, od, right)):
            even = taps[tap] * ce if even is None else even + taps[tap] * ce
            odd = taps[tap] * co if odd is None else odd + taps[tap] * co
    return even, odd


def tap_products(sums, rows, d_even, d_odd):
    for a in range(3):
        if rows[a] is None:
            continue
        ev, od, left, right = rows[a]
        for tap, ce, co in ((3 * a, left, ev), (3 * a + 1, ev, od), (3 * a + 2, od, right)):
            term = fold8(d_even * ce + d_odd * co)
            sums[tap] = term if sums[tap] is None else sums[tap] + term


MESH = pl.DeviceIdType.MESH


def spot():
    dp = lax.axis_index("dp")
    seq = lax.axis_index("seq")
    return dict(dp=dp, seq=seq, x=dp // 8, zl=(dp // 4) % 2, y=dp % 4, zh=seq // 2, core=seq % 2)


def seq_peer(me, zh, core):
    return (me["dp"], zh * 2 + core)


def axis_peer(me, axis, offset):
    x, y, z = me["x"], me["y"], me["zh"] * 2 + me["zl"]
    if axis == "x":
        x = (x + offset) % 4
    elif axis == "y":
        y = (y + offset) % 4
    else:
        z = (z + offset) % 4
    return ((x * 2 + z % 2) * 4 + y, (z // 2) * 2 + me["core"])


def remote(src, dst, send, recv, device):
    return pltpu.make_async_remote_copy(
        src_ref=src, dst_ref=dst, send_sem=send, recv_sem=recv, device_id=device,
        device_id_type=MESH,
    )


def arrived(ref, sem):
    pltpu.make_async_copy(ref, ref, sem).wait()


def greet(peers):
    barrier = pltpu.get_barrier_semaphore()
    for peer in peers:
        pl.semaphore_signal(barrier, inc=1, device_id=peer, device_id_type=MESH)
    pl.semaphore_wait(barrier, len(peers))


ORDERS = (("x", "y", "z"), ("y", "z", "x"), ("z", "x", "y"))
EARLY = (
    (("x", "y", "z"), ("x", "y", "z"), ("y", "z", "x")),
    (("y", "x", "z"), ("z", "x", "y"), ("z", "x", "y")),
)


def axis_spot(me, axis):
    return me["zh"] * 2 + me["zl"] if axis == "z" else me[axis]


def early_peer(me, stage, part, offset):
    first, second = (EARLY[which][part][stage] for which in range(2))
    pick = lambda a, b: jnp.where(me["core"] == 0, a, b)
    peers = (axis_peer(me, first, offset), axis_peer(me, second, offset))
    here = pick(axis_spot(me, first), axis_spot(me, second))
    return here, tuple(pick(a, b) for a, b in zip(*peers))


def ffn_kernel(
    x_ref, at_ref, ct_ref, mod_ref, alive_ref, perm_ref, ow_ref, ob_ref, f1_ref, f1b_ref,
    tap_ref, cb_ref, f2_ref, f2b_ref,
    out_ref, s1_ref, go_ref, da_ref, dx_ref, s2_ref, sm_ref,
    x1_s, br_s, h2_s, h2t_s, dffn_s, u_s, duc_s, act_s, du_s, dact_s, ffn_s, dh2_s, acc_s,
    ch_s, pre_s, r1_s, pair_sem, st_send, st_recv,
):
    step = pl.program_id(0)
    me = spot()
    core = me["core"]
    other = seq_peer(me, me["zh"], 1 - core)
    alive = alive_ref[0]

    @pl.when(step == 0)
    def _():
        greet([axis_peer(me, axis, o) for axis in "xyz" for o in (1, 2, 3)] + [other])

    def pair_copy(at):
        slot = at % 2
        return remote(
            ch_s.at[slot, 1 - core], pre_s.at[slot], pair_sem.at[slot, 0], pair_sem.at[slot, 1],
            other,
        )

    def first_copies(at):
        slot = at % 2
        out = []
        for p in range(3):
            for o in (1, 2, 3):
                here, peer = early_peer(me, 0, p, o)
                out.append(
                    remote(
                        ch_s.at[slot, core, p, (here + o) % 4], r1_s.at[slot, o - 1, p],
                        st_send.at[slot, p, o - 1], st_recv.at[slot, p, o - 1], peer,
                    )
                )
        return out

    def first_send(at):
        slot = at % 2
        pair_copy(at).wait()
        for p in range(3):

            def add(a, _):
                ch_s[slot, core, p, a] = ch_s[slot, core, p, a] + pre_s[slot, p, a]
                return 0

            lax.fori_loop(0, 4, add, 0)
        for copy in first_copies(at):
            copy.start()

    def first_take(at):
        slot = at % 2
        for copy in first_copies(at):
            copy.wait()
        for p in range(3):
            here, _peer = early_peer(me, 0, p, 1)
            total = ch_s[slot, core, p, here].astype(F32)
            for o in range(3):
                total = total + r1_s[slot, o, p].astype(F32)
            total = total.astype(BF16)

            @pl.when(core == 0)
            def _():
                s1_ref[p, at] = total

            @pl.when(core == 1)
            def _():
                for c in range(4):
                    s1_ref[p, c, pl.ds(pl.multiple_of(at * 48, 16), 48)] = total[
                        48 * c : 48 * c + 48
                    ]

    @pl.when(step == 0)
    def _():
        br_s[...] = mm(at_ref[...], ow_ref[...]) + ob_ref[...].astype(F32)
        shift2, scale2, gate1, gate2 = (mod_ref[i : i + 1, :] for i in (3, 4, 2, 5))

        def rows_a(r, _):
            at = pl.ds(pl.multiple_of(r * 32, 32), 32)
            x1 = x_ref[at, :].astype(F32) + gate1 * br_s[at, :]
            x1_s[at, :] = x1
            n2, _unused = norm_parts(x1)
            h2_s[at, :] = (n2 * (1.0 + scale2) + shift2).astype(BF16)
            return 0

        lax.fori_loop(0, 18, rows_a, 0)

        def rows_b(r, _):
            at = pl.ds(pl.multiple_of(r * 32, 32), 32)
            dffn_s[at, :] = (ct_ref[at, :].astype(F32) * alive * gate2).astype(BF16)
            return 0

        lax.fori_loop(0, 17, rows_b, 0)
        for p in range(2):
            h2t_s[p] = mm_nt(perm_ref[p], h2_s[0:512, :]).astype(BF16)
        ffn_s[...] = jnp.zeros_like(ffn_s)
        dh2_s[...] = jnp.zeros_like(dh2_s)

    for j in range(3):
        cols = slice(256 * j, 256 * j + 256)
        u_s[:, cols] = (mm(h2_s[...], f1_ref[:, cols]) + f1b_ref[:, cols].astype(F32)).astype(BF16)
        dact_s[:, cols] = mm_nt(dffn_s[...], f2_ref[cols, :])

    @pl.when(step > 0)
    def _():
        first_send(step - 1)

    masks = side_masks()

    def lanes(j, _):
        cols = pl.ds(pl.multiple_of(j * 128, 128), 128)
        taps = [tap_ref[t : t + 1, cols] for t in range(9)]
        taps = [by_core(taps, t, core) for t in range(9)]
        offset = cb_ref[:, cols].astype(F32)

        def sided(ref, l):
            return with_sides(
                ref[32 * l : 32 * l + 16, cols].astype(F32),
                ref[32 * l + 16 : 32 * l + 32, cols].astype(F32),
                masks,
            )

        rows = [None, sided(u_s, 0), sided(u_s, 1)]
        sums = [None] * 9
        bias_sum = None
        for l in range(17):
            ce, co = conv_row(rows, taps)
            ae, ge = gelu_pair(ce + offset)
            ao, go = gelu_pair(co + offset)
            de = (ge * dact_s[32 * l : 32 * l + 16, cols]).astype(BF16)
            do = (go * dact_s[32 * l + 16 : 32 * l + 32, cols]).astype(BF16)
            duc_s[32 * l : 32 * l + 16, cols] = de
            duc_s[32 * l + 16 : 32 * l + 32, cols] = do
            if l < 16:
                act_s[32 * l : 32 * l + 16, cols] = ae.astype(BF16)
                act_s[32 * l + 16 : 32 * l + 32, cols] = ao.astype(BF16)
                de, do = de.astype(F32), do.astype(F32)
                tap_products(sums, rows, de, do)
                term = fold8(de + do)
                bias_sum = term if bias_sum is None else bias_sum + term
                rows = [rows[1], rows[2], sided(u_s, l + 2) if l + 2 < 18 else None]
        for t in range(9):
            s2_ref[t : t + 1, cols] = jnp.sum(by_core(sums, t, core), axis=0, keepdims=True)
        s2_ref[9:10, cols] = jnp.sum(bias_sum, axis=0, keepdims=True)
        back = [taps[8 - t] for t in range(9)]
        rows = [None, sided(duc_s, 0), sided(duc_s, 1)]
        bias_sum = None
        for l in range(16):
            ue, uo = conv_row(rows, back)
            ue, uo = ue.astype(BF16), uo.astype(BF16)
            du_s[32 * l : 32 * l + 16, cols] = ue
            du_s[32 * l + 16 : 32 * l + 32, cols] = uo
            term = fold8(ue.astype(F32) + uo.astype(F32))
            bias_sum = term if bias_sum is None else bias_sum + term
            rows = [rows[1], rows[2], sided(duc_s, l + 2) if l + 2 < 17 else None]
        s2_ref[10:11, cols] = jnp.sum(bias_sum, axis=0, keepdims=True)
        return 0

    lax.fori_loop(0, FC // 128, lanes, 0)

    ffn_s[...] += mm(act_s[...], f2_ref[...])
    dh2_s[...] += mm_nt(du_s[...], f1_ref[...])
    slot = step % 2
    for j in range(3):
        cols = slice(256 * j, 256 * j + 256)
        got = mm(h2t_s[j // 2], du_s[:, cols]).astype(BF16)
        ch_s[slot, 0, j] = got.reshape(4, 192, 256)
    for part in range(3):
        grad = mm_tn(act_s[...], dffn_s[0:512, 256 * part : 256 * part + 256]).astype(BF16)
        for zl in range(2):
            for y in range(4):
                for zh in range(2):
                    at = ((zl * 4 + y) * 2 + zh) * 48
                    z = zh * 2 + zl
                    a, c = (y, z) if part == 0 else (z, y)
                    ch_s[slot, 1, part, a, 48 * c : 48 * c + 48] = grad[at : at + 48, :]
    pair_copy(step).start()

    @pl.when(step > 0)
    def _():
        first_take(step - 1)

    @pl.when(step == NFC - 1)
    def _():
        shift2, scale2, gate1, gate2 = (mod_ref[i : i + 1, :] for i in (3, 4, 2, 5))
        acc_s[...] = jnp.zeros_like(acc_s)
        f2b = f2b_ref[...].astype(F32)

        def rows_c(r, _):
            at = pl.ds(pl.multiple_of(r * 32, 32), 32)
            x1 = x1_s[at, :]
            ffn = ffn_s[at, :] + f2b
            dy = ct_ref[at, :].astype(F32) * alive
            out_ref[at, :] = (alive * (x1 + gate2 * ffn)).astype(BF16)
            n2, rs = norm_parts(x1)
            dh2 = dh2_s[at, :]
            g2 = dh2 * (1.0 + scale2)
            dx1 = dy + rs * (
                g2
                - jnp.mean(g2, axis=-1, keepdims=True)
                - n2 * jnp.mean(g2 * n2, axis=-1, keepdims=True)
            )
            dx_ref[at, :] = dx1
            dbr = (dx1 * gate1).astype(BF16)
            da_ref[at, :] = dbr
            acc_s[0] += fold8(dx1 * br_s[at, :])
            acc_s[1] += fold8(dh2)
            acc_s[2] += fold8(dh2 * n2)
            acc_s[3] += fold8(dy * ffn)
            acc_s[4] += fold8(dbr.astype(F32))
            acc_s[5] += fold8(dffn_s[at, :].astype(F32))
            return 0

        lax.fori_loop(0, 16, rows_c, 0)
        for i in range(6):
            sm_ref[i : i + 1, :] = jnp.sum(acc_s[i], axis=0, keepdims=True)
        first_send(step)
        for p in range(3):
            h2t_s[p] = mm_nt(perm_ref[p], at_ref[0:512, :]).astype(BF16)
            go_ref[p] = mm(h2t_s[p], da_ref[:, 256 * p : 256 * p + 256]).astype(BF16)
        da_ref[...] = mm_nt(da_ref[...], ow_ref[...]).astype(BF16)
        first_take(step)


def ffn_call(x, at, ct, mod, alive, perm, ow, ob, f1, f1b, taps, cb, f2, f2b):
    whole = lambda s: pl.BlockSpec(s, lambda i: (0,) * len(s))
    return pl.pallas_call(
        ffn_kernel,
        grid=(NFC,),
        in_specs=[
            whole((576, D)), whole((576, D)), whole((576, D)), whole((8, D)),
            pl.BlockSpec(memory_space=pltpu.SMEM),
            whole((3, D, D)), whole((D, D)), whole((1, D)),
            pl.BlockSpec((D, FC), lambda i: (0, i)),
            pl.BlockSpec((1, FC), lambda i: (0, i)),
            pl.BlockSpec((16, FC), lambda i: (0, i)),
            pl.BlockSpec((1, FC), lambda i: (0, i)),
            pl.BlockSpec((FC, D), lambda i: (i, 0)),
            whole((1, D)),
        ],
        out_specs=[
            whole((512, D)),
            whole((3, 4, 192, 256)),
            whole((3, D, 256)),
            whole((512, D)), whole((512, D)),
            pl.BlockSpec((16, FC), lambda i: (0, i)),
            whole((8, D)),
        ],
        out_shape=[
            jax.ShapeDtypeStruct((512, D), BF16),
            jax.ShapeDtypeStruct((3, 4, 192, 256), BF16),
            jax.ShapeDtypeStruct((3, D, 256), BF16),
            jax.ShapeDtypeStruct((512, D), BF16),
            jax.ShapeDtypeStruct((512, D), F32),
            jax.ShapeDtypeStruct((16, FF), F32),
            jax.ShapeDtypeStruct((8, D), F32),
        ],
        scratch_shapes=[
            pltpu.VMEM((576, D), F32), pltpu.VMEM((576, D), F32), pltpu.VMEM((576, D), BF16),
            pltpu.VMEM((3, D, 512), BF16), pltpu.VMEM((544, D), BF16),
            pltpu.VMEM((576, FC), BF16), pltpu.VMEM((544, FC), BF16), pltpu.VMEM((512, FC), BF16),
            pltpu.VMEM((512, FC), BF16), pltpu.VMEM((544, FC), F32),
            pltpu.VMEM((512, D), F32), pltpu.VMEM((512, D), F32), pltpu.VMEM((6, 8, D), F32),
            pltpu.VMEM((2, 2, 3, 4, 192, 256), BF16), pltpu.VMEM((2, 3, 4, 192, 256), BF16),
            pltpu.VMEM((2, 3, 3, 192, 256), BF16), pltpu.SemaphoreType.DMA((2, 2)),
            pltpu.SemaphoreType.DMA((2, 3, 3)), pltpu.SemaphoreType.DMA((2, 3, 3)),
        ],
        compiler_params=pltpu.CompilerParams(
            dimension_semantics=("arbitrary",), vmem_limit_bytes=60 * 2**20,
            collective_id=3, has_side_effects=True,
        ),
        name="ffn",
    )(x, at, ct, mod, alive, perm, ow, ob, f1, f1b, taps, cb, f2, f2b)


def place_matrix(count, flip, inverse):
    rows = count // 32
    out = lax.broadcasted_iota(jnp.int32, (count, count), 0)
    at = lax.broadcasted_iota(jnp.int32, (count, count), 1)
    row = out // 32
    row = jnp.where(flip, rows - 1 - row, row)
    low = out % 32
    if inverse:
        low = (low % 2) * 16 + low // 2
    else:
        low = (low % 16) * 2 + low // 16
    return jnp.where(at == row * 32 + low, 1.0, 0.0).astype(BF16)


def head_lanes(values, half):
    lane = lax.broadcasted_iota(jnp.int32, values.shape, 1)
    return jnp.where((lane // 64) == half, values, jnp.zeros_like(values))


def attn_kernel(
    lat_ref, ct_ref, cond_ref, time_ref, table_ref, mw_ref, mb_ref, w_ref, qb_ref, tap_ref, cb_ref,
    x_out, ct_out, h_out, hcg_out, qkv_out, p_out, at_out, mod_out,
    xr_s, xh_s, x_s, c_s, h_s, hcg_s, sb_s, w_s, qkv_s, p_s, ag_s, at_s, mod_s, table_s, mw_s,
    send0, recv0, sem_pair, sem_loc,
):
    me = spot()
    zh, core, seq = me["zh"], me["core"], me["seq"]
    other = seq_peer(me, zh, 1 - core)
    w_load = pltpu.make_async_copy(w_ref, w_s, sem_loc.at[0])
    table_load = pltpu.make_async_copy(table_ref, table_s, sem_loc.at[10])
    mw_load = pltpu.make_async_copy(mw_ref, mw_s, sem_loc.at[11])
    for copy in (table_load, mw_load, w_load):
        copy.start()

    greet(
        [
            seq_peer(me, (zh + dz) % 2, (core + dc) % 2)
            for dz, dc in ((0, 1), (1, 0), (1, 1))
        ]
    )
    slot = jnp.where(zh == 0, core, 1 - core)
    inner = jnp.logical_or(seq == 1, seq == 2)
    halo_core = jnp.where(seq == 1, 1, 0)
    halo_at = pl.multiple_of(jnp.where(seq == 1, 192, 0), 64)

    def sends(arrays, act):
        for a in arrays:
            ref = (lat_ref, ct_ref)[a]
            for j in range(2):
                own = jnp.logical_and(zh == j, core == zh)
                main = (ref.at[j], xr_s.at[a, slot])
                halo = (ref.at[j, pl.ds(halo_at, 64)], xh_s.at[a])

                @pl.when(own)
                def _():
                    act(lambda: pltpu.make_async_copy(*main, recv0.at[a, slot]), True)

                @pl.when(jnp.logical_not(own))
                def _():
                    act(
                        lambda: remote(*main, send0.at[a, j, 0], recv0.at[a, slot], seq_peer(me, j, zh)),
                        False,
                    )

                @pl.when(jnp.logical_and(inner, zh == j))
                def _():
                    act(lambda: pltpu.make_async_copy(*halo, recv0.at[a, 2]), True)

                @pl.when(jnp.logical_and(inner, zh != j))
                def _():
                    act(
                        lambda: remote(
                            *halo, send0.at[a, j, 1], recv0.at[a, 2], seq_peer(me, j, halo_core)
                        ),
                        False,
                    )

    sends((0,), lambda make, local: make().start())

    flip = core == 1
    big = place_matrix(256, flip, False)
    small = place_matrix(64, flip, False)

    table_load.wait()
    here = lax.broadcasted_iota(jnp.int32, (8, table_s.shape[0]), 1)
    one_hot = jnp.where(here == time_ref[zh], 1.0, 0.0).astype(BF16)
    cond = jnp.where(zh == 0, cond_ref[0:1, :], cond_ref[1:2, :]) + mm(one_hot, table_s[...])
    silu = (cond / (1.0 + jnp.exp(-cond))).astype(BF16)
    mw_load.wait()
    for i in range(6):
        cols = slice(D * i, D * i + D)
        mod_s[i : i + 1, :] = (mm(silu, mw_s[:, cols]) + mb_ref[:, cols])[0:1]
    mod_s[6:7, :] = cond[0:1]
    mod_s[7:8, :] = silu[0:1].astype(F32)
    shift1, scale1 = mod_s[0:1, :], mod_s[1:2, :]

    def placed(a, into):
        for b in range(2):
            arrived(xr_s.at[a, b], recv0.at[a, b])
            into[256 * b : 256 * b + 256, :] = mm(big, xr_s[a, b]).astype(BF16)
        arrived(xh_s.at[a], recv0.at[a, 2])
        into[512:576, :] = mm(small, xh_s[a]).astype(BF16)

    placed(0, x_s)
    sends((1,), lambda make, local: make().start())

    def rows_a(r, _):
        at = pl.ds(pl.multiple_of(r * 32, 32), 32)
        n1, _unused = norm_parts(x_s[at, :].astype(F32))
        h_s[at, :] = (n1 * (1.0 + scale1) + shift1).astype(BF16)
        return 0

    lax.fori_loop(0, 18, rows_a, 0)
    outs = [
        pltpu.make_async_copy(x_s, x_out, sem_loc.at[1]),
        pltpu.make_async_copy(h_s, h_out, sem_loc.at[2]),
        pltpu.make_async_copy(mod_s, mod_out, sem_loc.at[12]),
    ]
    for copy in outs:
        copy.start()
    masks = side_masks()

    def lanes(j, _):
        cols = pl.ds(pl.multiple_of(j * 128, 128), 128)
        taps = [tap_ref[t : t + 1, cols] for t in range(9)]
        taps = [by_core(taps, t, core) for t in range(9)]
        offset = cb_ref[:, cols].astype(F32)

        def sided(l):
            return with_sides(
                h_s[32 * l : 32 * l + 16, cols].astype(F32),
                h_s[32 * l + 16 : 32 * l + 32, cols].astype(F32),
                masks,
            )

        rows = [None, sided(0), sided(1)]
        for l in range(16):
            ce, co = conv_row(rows, taps)
            ce, co = (ce + offset).astype(BF16), (co + offset).astype(BF16)
            if l % 2 == 0:
                hcg_s[0, l // 2, 0, :, cols] = ce
                hcg_s[0, l // 2, 1, :, cols] = co
            else:
                sb_s[l // 2, 0, :, cols] = ce
                sb_s[l // 2, 1, :, cols] = co
            rows = [rows[1], rows[2], sided(l + 2) if l < 15 else None]
        return 0

    lax.fori_loop(0, D // 128, lanes, 0)
    hc_copy = remote(sb_s, hcg_s.at[1], sem_pair.at[0], sem_pair.at[1], other)
    hc_copy.start()
    w_load.wait()

    def project(half):
        got = mm(hcg_s[half].reshape(256, D), w_s[...]) + qb_ref[...]
        qkv_s[half] = got.astype(BF16).reshape(8, 2, 16, 3 * D)

    project(0)
    hc_copy.wait()
    outs.append(pltpu.make_async_copy(hcg_s, hcg_out, sem_loc.at[3]))
    outs[-1].start()
    project(1)
    outs.append(pltpu.make_async_copy(qkv_s, qkv_out, sem_loc.at[4]))
    outs[-1].start()

    def attend(i, _):
        pc, pair = i // 6, i % 6

        def part(which):
            cols = pl.ds(pl.multiple_of(which * D + pair * 128, 128), 128)
            return jnp.concatenate(
                [qkv_s[half, :, pc, :, cols].reshape(128, 128) for half in range(2)], axis=0
            )

        q, k, v = part(0), part(1), part(2)
        v_t = v.T
        got = []
        for half in range(2):
            scores = mm_nt(k, head_lanes(q, half)) * 0.125
            e = jnp.exp(scores - jnp.max(scores, axis=0, keepdims=True))
            low = (e * (1.0 / jnp.sum(e, axis=0, keepdims=True))).astype(BF16)
            p_s[2 * i + half] = low
            got.append(mm(v_t[64 * half : 64 * half + 64], low))
        o = jnp.concatenate(got, axis=0).T.astype(BF16)
        cols = pl.ds(pl.multiple_of(pair * 128, 128), 128)
        for half in range(2):
            ag_s[half, :, pc, :, cols] = o[128 * half : 128 * half + 128].reshape(8, 16, 128)
        return 0

    lax.fori_loop(0, 12, attend, 0)
    back = [
        remote(ag_s.at[1], at_s.at[pl.ds(0, 8), 1], sem_pair.at[2], sem_pair.at[3], other),
        remote(ag_s.at[0, 7], at_s.at[8, 1], sem_pair.at[4], sem_pair.at[5], other),
        pltpu.make_async_copy(ag_s.at[0], at_s.at[pl.ds(0, 8), 0], sem_loc.at[5]),
        pltpu.make_async_copy(ag_s.at[1, 7], at_s.at[8, 0], sem_loc.at[6]),
    ]
    for copy in back:
        copy.start()
    outs.append(pltpu.make_async_copy(p_s, p_out, sem_loc.at[7]))
    outs[-1].start()
    placed(1, c_s)
    outs.append(pltpu.make_async_copy(c_s, ct_out, sem_loc.at[8]))
    outs[-1].start()
    for copy in back:
        copy.wait()
    outs.append(pltpu.make_async_copy(at_s, at_out, sem_loc.at[9]))
    outs[-1].start()
    for copy in outs:
        copy.wait()

    def finish(make, local):
        if not local:
            make().wait_send()

    sends((0, 1), finish)


VMEM_SPEC = pl.BlockSpec(memory_space=pltpu.VMEM)
ANY_SPEC = pl.BlockSpec(memory_space=pl.ANY)
SMEM_SPEC = pl.BlockSpec(memory_space=pltpu.SMEM)


def attn_call(lat, ct, cond, times, table, mw, mb, w, qb, taps, cb):
    G = (2, 8, 2, 16)
    shape = jax.ShapeDtypeStruct
    return pl.pallas_call(
        attn_kernel,
        in_specs=[
            ANY_SPEC, ANY_SPEC, VMEM_SPEC, SMEM_SPEC, ANY_SPEC, ANY_SPEC, VMEM_SPEC, ANY_SPEC,
            VMEM_SPEC, VMEM_SPEC, VMEM_SPEC,
        ],
        out_specs=[ANY_SPEC] * 8,
        out_shape=[
            shape((576, D), BF16), shape((576, D), BF16), shape((576, D), BF16),
            shape(G + (D,), BF16), shape(G + (3 * D,), BF16), shape((24, 256, 256), BF16),
            shape((9, 2, 2, 16, D), BF16), shape((8, D), F32),
        ],
        scratch_shapes=[
            pltpu.VMEM((2, 2, 256, D), BF16), pltpu.VMEM((2, 64, D), BF16),
            pltpu.VMEM((576, D), BF16), pltpu.VMEM((576, D), BF16), pltpu.VMEM((576, D), BF16),
            pltpu.VMEM(G + (D,), BF16), pltpu.VMEM((8, 2, 16, D), BF16),
            pltpu.VMEM((D, 3 * D), BF16), pltpu.VMEM(G + (3 * D,), BF16),
            pltpu.VMEM((24, 256, 256), BF16), pltpu.VMEM(G + (D,), BF16),
            pltpu.VMEM((9, 2, 2, 16, D), BF16),
            pltpu.VMEM((8, D), F32), pltpu.VMEM(table.shape, BF16), pltpu.VMEM(mw.shape, BF16),
            pltpu.SemaphoreType.DMA((2, 2, 2)), pltpu.SemaphoreType.DMA((2, 3)),
            pltpu.SemaphoreType.DMA((6,)), pltpu.SemaphoreType.DMA((13,)),
        ],
        compiler_params=pltpu.CompilerParams(
            collective_id=1, has_side_effects=True, vmem_limit_bytes=56 * 2**20
        ),
        name="attend",
    )(lat, ct, cond, times, table, mw, mb, w, qb, taps, cb)


def back_kernel(
    da_ref, qkv_ref, p_ref, hcg_ref, h_ref, x_ref, dx_ref, mod_ref, time_ref, w_ref, mw_ref,
    tap_ref, perm_ref, o_ref, s1_ref, go_ref, s2_ref, sb_ref,
    oret_out, iret_out, fe_out, fl_out, se_out, sl_out, de_out, dl_out,
    qkv_s, p_s, w_s, mw_s, perm_s, dag_s, dqkv_s, hct_s, dhc_s, dh_s, gh_s, ig_s, os_s, is_s,
    lg_s, prl_s, r1l, s1l, r2e, r2l, t3e, t3l, r3e, r3l, fe_s, fl_s,
    acc_s, sv_s, se_p, se_r, se_s, se_f, sl_p, sl_r, sl_s, sl_f, mp_s, mr_s, mpl_s, mrl_s,
    item_s, de_s, dl_s,
    loc, pair_sem, ret_send, ret_recv, st_send, st_recv, sm_send, sm_recv, dm_send, dm_recv,
):
    me = spot()
    zh, core = me["zh"], me["core"]
    other = seq_peer(me, zh, 1 - core)
    loads = [
        pltpu.make_async_copy(qkv_ref, qkv_s, loc.at[0]),
        pltpu.make_async_copy(p_ref, p_s, loc.at[1]),
        pltpu.make_async_copy(w_ref, w_s, loc.at[2]),
        pltpu.make_async_copy(perm_ref, perm_s, loc.at[3]),
        pltpu.make_async_copy(da_ref.at[:, 0], dag_s.at[0], loc.at[4]),
        pltpu.make_async_copy(mw_ref, mw_s, loc.at[5]),
        pltpu.make_async_copy(go_ref, lg_s.at[1, :, 0], loc.at[6]),
    ]
    for at in (4, 0, 1, 3, 2, 6, 5):
        loads[at].start()
    peers = [axis_peer(me, axis, o) for axis in "xyz" for o in (1, 2, 3)]
    greet(peers + [other, seq_peer(me, 1 - zh, 1 - core)])

    da_copy = remote(da_ref.at[:, 1], dag_s.at[1], pair_sem.at[0, 0], pair_sem.at[0, 1], other)
    da_copy.start()

    def stage_sends(stage, bufs, late):
        out = []
        for p in range(3):
            for o in (1, 2, 3):
                if late:
                    axis = ORDERS[p][stage]
                    here, peer = axis_spot(me, axis), axis_peer(me, axis, o)
                else:
                    here, peer = early_peer(me, stage, p, o)
                src, dst = bufs(p, o, (here + o) % 4)
                copy = remote(
                    src, dst, st_send.at[late, stage, p, o - 1], st_recv.at[late, stage, p, o - 1],
                    peer,
                )
                copy.start()
                out.append(copy)
        return out

    def chunk(there, rows):
        return pl.ds(pl.multiple_of(there * rows, 16), rows)

    st2e = stage_sends(1, lambda p, o, b: (s1_ref.at[p, :, chunk(b, 48)], r2e.at[o - 1, p]), 0)
    mp_s[...] = sb_ref[...]
    mp_copy = remote(mp_s, mr_s, pair_sem.at[1, 0], pair_sem.at[1, 1], other)
    mp_copy.start()
    for half in range(2):
        for q in range(2):
            at = D * (2 * half + q)
            se_p[half, 16 * q : 16 * q + 16, :] = s2_ref[:, at : at + D].astype(BF16)
    se_copy = remote(se_p.at[1 - core], se_r, pair_sem.at[2, 0], pair_sem.at[2, 1], other)
    se_copy.start()

    home = place_matrix(256, core == 1, True)

    def give_back(which, act):
        ref, out = ((os_s, oret_out), (is_s, iret_out))[which]
        for b in range(2):
            to_core = jnp.where(core == 0, b, 1 - b)
            own = jnp.logical_and(zh == core, b == 0)

            @pl.when(own)
            def _():
                act(lambda: pltpu.make_async_copy(ref.at[b], out.at[zh], ret_recv.at[which, zh]), True)

            @pl.when(jnp.logical_not(own))
            def _():
                act(
                    lambda: remote(
                        ref.at[b], out.at[zh], ret_send.at[which, b], ret_recv.at[which, zh],
                        seq_peer(me, core, to_core),
                    ),
                    False,
                )

    for b in range(2):
        os_s[b] = mm(home, o_ref[256 * b : 256 * b + 256, :]).astype(BF16)
    give_back(0, lambda make, local: make().start())

    loads[3].wait()
    for p in range(3):
        hct_s[p] = mm_nt(perm_s[p], hcg_ref[...]).astype(BF16)
    loads[4].wait()
    loads[0].wait()
    loads[1].wait()
    da_copy.wait()

    def attend_back(i, _):
        pc, pair = i // 6, i % 6
        lanes_at = [
            pl.ds(pl.multiple_of(which * D + pair * 128, 128), 128) for which in range(3)
        ]

        def part(ref, cols):
            return jnp.concatenate(
                [ref[half, :, pc, :, cols].reshape(128, 128) for half in range(2)], axis=0
            )

        q, k, v = (part(qkv_s, cols) for cols in lanes_at)
        do = part(dag_s, lanes_at[0])
        k_t = k.T
        dq_t, dk, dv = [], None, None
        for half in range(2):
            dom, qm = head_lanes(do, half), head_lanes(q, half)
            low = p_s[2 * i + half]
            probs = low.astype(F32)
            dp = mm_nt(v, dom)
            ds = (probs * (dp - jnp.sum(probs * dp, axis=0, keepdims=True))).astype(BF16)
            dq_t.append(mm(k_t[64 * half : 64 * half + 64], ds))
            dk_h, dv_h = mm(ds, qm), mm(low, dom)
            dk = dk_h if dk is None else dk + dk_h
            dv = dv_h if dv is None else dv + dv_h
        dq = jnp.concatenate(dq_t, axis=0).T
        for cols, got in zip(lanes_at, (0.125 * dq, 0.125 * dk, dv)):
            got = got.astype(BF16)
            for half in range(2):
                dqkv_s[half, :, pc, :, cols] = got[128 * half : 128 * half + 128].reshape(8, 16, 128)
        return 0

    z_me = axis_spot(me, "z")

    def small_stage(stage, sums, items, kind):
        axis = "xyz"[stage]
        spots = ((z_me, me["y"], me["x"]), (z_me, me["y"]), (z_me,))[stage]
        if stage == 0:
            ref = items.at[core, z_me, me["y"], me["x"]]
        elif stage == 1:
            ref = items.at[core, z_me, me["y"]]
        else:
            ref = items.at[core, z_me]
        out = []
        for o in (1, 2, 3):
            peer = axis_peer(me, axis, o)
            at = (kind, stage, o - 1)
            out.append(
                remote(sums.at[4 * stage], sums.at[4 * stage + o], sm_send.at[at], sm_recv.at[at], peer)
            )
            out.append(remote(ref, ref, dm_send.at[at], dm_recv.at[at], peer))
        for copy in out:
            copy.start()
        return out

    def small_take(stage, sums, items, kind, copies, last):
        axis = "xyz"[stage]
        for copy in copies:
            copy.wait_send()
        for o in (1, 2, 3):
            at = (kind, stage, o - 1)
            arrived(sums.at[4 * stage + o], sm_recv.at[at])
            there = (axis_spot(me, axis) + 4 - o) % 4
            if stage == 0:
                ref = items.at[core, z_me, me["y"], there]
            elif stage == 1:
                ref = items.at[core, z_me, there]
            else:
                ref = items.at[core, there]
            arrived(ref, dm_recv.at[at])
        total = sums[4 * stage].astype(F32)
        for o in (1, 2, 3):
            total = total + sums[4 * stage + o].astype(F32)
        if stage < 2:
            sums[4 * stage + 4] = total.astype(BF16)
        else:
            last[...] = total

    def lane_rows(values, count):
        return [
            values[i : i + 1, 128 * l : 128 * l + 128] for i in range(count) for l in range(6)
        ]

    ends = []

    def spread(done, out, at):
        for copy in (
            pltpu.make_async_copy(done, out.at[core], loc.at[at]),
            remote(done, out.at[core], pair_sem.at[at, 0], pair_sem.at[at, 1], other),
        ):
            copy.start()
            ends.append(copy)

    def second(own, recv, panels, p, here):
        out = []
        for k in range(panels):
            total = own[p, k, chunk(here, 48), :].astype(F32)
            for o in range(3):
                total = total + recv[o, p, k].astype(F32)
            out.append(total)
        return out

    lax.fori_loop(0, 6, attend_back, 0)
    mp_copy.wait()
    item_s[2:6, :] = (mp_s[0:4, :] + mr_s[0:4, :]).astype(BF16).astype(F32)
    time_id = time_ref[zh]
    stamp = jnp.ones((1, 128), F32)
    rows = lane_rows(item_s[2:6, :], 4) + lane_rows(mod_ref[7:8, :], 1)
    rows += [stamp * (time_id // 32).astype(F32), stamp * (time_id % 32).astype(F32)]
    both = jnp.concatenate(rows, axis=0).astype(BF16)
    de_s[core, z_me, me["y"], me["x"]] = jnp.where(core == 0, both[0:16], both[16:32])
    se_copy.wait()
    se_s[0] = (se_p[core].astype(F32) + se_r[...].astype(F32)).astype(BF16)
    small = small_stage(0, se_s, de_s, 0)
    for copy in st2e:
        copy.wait()
    for p in range(3):
        got = second(s1_ref, r2e, 4, p, early_peer(me, 1, p, 1)[0])

        @pl.when(core == 0)
        def _():
            for c in range(4):
                t3e[p, c] = jnp.concatenate(
                    [got[k][12 * c : 12 * c + 12] for k in range(4)], axis=0
                ).astype(BF16)

        @pl.when(core == 1)
        def _():
            for c in range(4):
                t3e[p, c] = got[c].astype(BF16)

    st3e = stage_sends(2, lambda p, o, c: (t3e.at[p, c], r3e.at[o - 1, p]), 0)
    lax.fori_loop(6, 12, attend_back, 0)
    small_take(0, se_s, de_s, 0, small, se_f)
    small = small_stage(1, se_s, de_s, 0)

    loads[2].wait()
    for half in (1, 0):
        got = mm_nt(dqkv_s[half].reshape(256, 3 * D), w_s[...]).astype(BF16)
        dhc_s[half] = got.reshape(8, 2, 16, D)
        if half == 1:
            dhc_copy = remote(
                dhc_s.at[1], dh_s.at[pl.ds(0, 8), 1], pair_sem.at[3, 0], pair_sem.at[3, 1], other
            )
            dhc_copy.start()
    near = [
        pltpu.make_async_copy(dhc_s.at[0], dh_s.at[pl.ds(0, 8), 0], loc.at[7]),
        pltpu.make_async_copy(dhc_s.at[1, 7], dh_s.at[8, 0], loc.at[8]),
    ]
    for copy in near:
        copy.start()
    loads[6].wait()
    for p in range(3):
        for at, to in (
            (512 * p, (0, p, 0)), (512 * p + 256, (0, p, 1)), (1536 + 256 * p, (1, p, 1))
        ):
            lg_s[to] = mm(
                hct_s[p], dqkv_s[:, :, :, :, at : at + 256].reshape(512, 256)
            ).astype(BF16)
    late = [
        remote(lg_s.at[1 - core, p], prl_s.at[p], pair_sem.at[4 + p, 0], pair_sem.at[4 + p, 1], other)
        for p in range(3)
    ]
    for copy in late:
        copy.start()
    ones = jnp.ones((8, 512), BF16)
    for row, at in ((10, 0), (11, 2 * D)):
        sums = mm(ones, dqkv_s[:, :, :, :, at : at + D].reshape(512, D))
        sv_s[row : row + 1, :] = sums[0:1]
    sv_s[12:14, :] = sb_ref[4:6, :]
    sv_s[14:16, :] = jnp.zeros((2, D), F32)

    dhc_copy.wait()
    for copy in near:
        copy.wait()
    masks = side_masks()

    def lanes(j, _):
        cols = pl.ds(pl.multiple_of(j * 128, 128), 128)
        taps = [tap_ref[t : t + 1, cols] for t in range(9)]
        back = [by_core(taps, 8 - t, core) for t in range(9)]

        def sided_d(l):
            return with_sides(
                dh_s[l // 2, l % 2, 0, :, cols].astype(F32),
                dh_s[l // 2, l % 2, 1, :, cols].astype(F32),
                masks,
            )

        def sided_h(l):
            return with_sides(
                h_ref[32 * l : 32 * l + 16, cols].astype(F32),
                h_ref[32 * l + 16 : 32 * l + 32, cols].astype(F32),
                masks,
            )

        rows = [None, sided_d(0), sided_d(1)]
        rows_h = [None, sided_h(0), sided_h(1)]
        sums = [None] * 9
        bias_sum = None
        for l in range(16):
            ge, go = conv_row(rows, back)
            gh_s[32 * l : 32 * l + 16, cols] = ge
            gh_s[32 * l + 16 : 32 * l + 32, cols] = go
            de, do = rows[1][0], rows[1][1]
            tap_products(sums, rows_h, de, do)
            term = fold8(de + do)
            bias_sum = term if bias_sum is None else bias_sum + term
            if l < 15:
                rows = [rows[1], rows[2], sided_d(l + 2)]
                rows_h = [rows_h[1], rows_h[2], sided_h(l + 2)]
        for t in range(9):
            total = jnp.sum(by_core(sums, t, core), axis=0, keepdims=True)
            sv_s[t : t + 1, cols] = total
        sv_s[9:10, cols] = jnp.sum(bias_sum, axis=0, keepdims=True)
        return 0

    lax.fori_loop(0, D // 128, lanes, 0)
    scale1 = mod_ref[1:2, :]
    acc_s[...] = jnp.zeros_like(acc_s)

    def rows_n(r, _):
        at = pl.ds(pl.multiple_of(r * 32, 32), 32)
        n1, rs = norm_parts(x_ref[at, :].astype(F32))
        dh = gh_s[at, :]
        g1 = dh * (1.0 + scale1)
        got = dx_ref[at, :] + rs * (
            g1
            - jnp.mean(g1, axis=-1, keepdims=True)
            - n1 * jnp.mean(g1 * n1, axis=-1, keepdims=True)
        )
        ig_s[at, :] = got.astype(BF16)
        acc_s[0] += fold8(dh)
        acc_s[1] += fold8(dh * n1)
        return 0

    lax.fori_loop(0, 16, rows_n, 0)
    mpl_s[...] = jnp.zeros_like(mpl_s)
    for i in range(2):
        mpl_s[i : i + 1, :] = jnp.sum(acc_s[i], axis=0, keepdims=True)
    mpl_copy = remote(mpl_s, mrl_s, pair_sem.at[7, 0], pair_sem.at[7, 1], other)
    mpl_copy.start()
    for half in range(2):
        sl_p[half] = sv_s[:, 384 * half : 384 * half + 384].astype(BF16)
    sl_copy = remote(sl_p.at[1 - core], sl_r, pair_sem.at[8, 0], pair_sem.at[8, 1], other)
    sl_copy.start()
    for copy in late:
        copy.wait()
    for p in range(3):
        for k in range(2):
            lg_s[core, p, k] = lg_s[core, p, k] + prl_s[p, k]
    st1l = stage_sends(
        0, lambda p, o, a: (lg_s.at[core, p, :, chunk(a, 192)], r1l.at[o - 1, p]), 1
    )
    for b in range(2):
        is_s[b] = mm(home, ig_s[256 * b : 256 * b + 256, :]).astype(BF16)
    give_back(1, lambda make, local: make().start())
    small_take(1, se_s, de_s, 0, small, se_f)
    small = small_stage(2, se_s, de_s, 0)

    mpl_copy.wait()
    item_s[0:2, :] = (mpl_s[0:2, :] + mrl_s[0:2, :]).astype(BF16).astype(F32)
    loads[5].wait()
    cond = mod_ref[6:7, :]
    d_silu = jnp.zeros((8, D), F32)
    for i in range(6):
        row = jnp.concatenate([item_s[i : i + 1, :]] * 8, axis=0).astype(BF16)
        d_silu = d_silu + mm_nt(row, mw_s[:, D * i : D * i + D])
    slope = 1.0 / (1.0 + jnp.exp(-cond))
    d_cond = (slope * (1.0 + cond * (1.0 - slope))) * d_silu[0:1]
    zeros = [jnp.zeros((1, 128), F32)]
    rows_0 = jnp.concatenate(lane_rows(item_s[0:2, :], 2) + zeros * 4, axis=0)
    rows_1 = jnp.concatenate(lane_rows(d_cond, 1) + zeros * 10, axis=0)
    dl_s[core, z_me, me["y"], me["x"]] = jnp.where(core == 0, rows_0, rows_1).astype(BF16)
    sl_copy.wait()
    sl_s[0] = (sl_p[core].astype(F32) + sl_r[...].astype(F32)).astype(BF16)
    small_l = small_stage(0, sl_s, dl_s, 1)

    def finish(copies, own, recv, done, out, at, spots):
        for copy in copies:
            copy.wait()
        for p in range(3):
            total = own[p, spots[p]].astype(F32)
            for o in range(3):
                total = total + recv[o, p].astype(F32)
            done[p] = total
        spread(done, out, at)

    finish(st3e, t3e, r3e, fe_s, fe_out, 9, [early_peer(me, 2, p, 1)[0] for p in range(3)])
    spots = [[axis_spot(me, ORDERS[p][stage]) for p in range(3)] for stage in range(3)]
    for copy in st1l:
        copy.wait()
    for p in range(3):
        for k in range(2):
            total = lg_s[core, p, k, chunk(spots[0][p], 192), :].astype(F32)
            for o in range(3):
                total = total + r1l[o, p, k].astype(F32)
            s1l[p, k] = total.astype(BF16)
    st2l = stage_sends(1, lambda p, o, b: (s1l.at[p, :, chunk(b, 48)], r2l.at[o - 1, p]), 1)
    small_take(0, sl_s, dl_s, 1, small_l, sl_f)
    small_l = small_stage(1, sl_s, dl_s, 1)
    small_take(2, se_s, de_s, 0, small, se_f)
    spread(se_f, se_out, 10)
    ends.append(
        remote(de_s.at[core], de_s.at[core], pair_sem.at[11, 0], pair_sem.at[11, 1], other)
    )
    ends[-1].start()
    for copy in st2l:
        copy.wait()
    for p in range(3):
        got = second(s1l, r2l, 2, p, spots[1][p])
        for c in range(4):
            t3l[p, c] = jnp.concatenate(
                [got[0][12 * c : 12 * c + 12], got[1][12 * c : 12 * c + 12], jnp.zeros((8, 256), F32)],
                axis=0,
            ).astype(BF16)
    st3l = stage_sends(2, lambda p, o, c: (t3l.at[p, c], r3l.at[o - 1, p]), 1)
    small_take(1, sl_s, dl_s, 1, small_l, sl_f)
    small_l = small_stage(2, sl_s, dl_s, 1)
    finish(st3l, t3l, r3l, fl_s, fl_out, 12, spots[2])
    small_take(2, sl_s, dl_s, 1, small_l, sl_f)
    spread(sl_f, sl_out, 13)
    ends.append(
        remote(dl_s.at[core], dl_s.at[core], pair_sem.at[14, 0], pair_sem.at[14, 1], other)
    )
    ends[-1].start()
    for which in range(2):
        give_back(which, lambda make, local: None if local else make().wait_send())
        for item_slot in range(2):
            out = (oret_out, iret_out)[which]
            arrived(out.at[item_slot], ret_recv.at[which, item_slot])
    for copy in ends:
        copy.wait()
    last = [
        pltpu.make_async_copy(de_s, de_out, loc.at[11]),
        pltpu.make_async_copy(dl_s, dl_out, loc.at[14]),
    ]
    for copy in last:
        copy.start()
    for copy in last:
        copy.wait()


def back_call(
    da, qkv, p, hcg, h, x, dx, mod, times, w, mw, taps, perm, o, s1, go, s2, sb
):
    G = (2, 8, 2, 16)
    shape = jax.ShapeDtypeStruct
    V = pltpu.VMEM
    items = (2, 4, 4, 4, 16, 128)
    DMA = pltpu.SemaphoreType.DMA
    return pl.pallas_call(
        back_kernel,
        in_specs=[
            ANY_SPEC, ANY_SPEC, ANY_SPEC, VMEM_SPEC, VMEM_SPEC, VMEM_SPEC, VMEM_SPEC, VMEM_SPEC,
            SMEM_SPEC, ANY_SPEC, ANY_SPEC, VMEM_SPEC, ANY_SPEC, VMEM_SPEC, VMEM_SPEC, ANY_SPEC,
            VMEM_SPEC, VMEM_SPEC,
        ],
        out_specs=[ANY_SPEC] * 8,
        out_shape=[
            shape((2, 256, D), BF16), shape((2, 256, D), BF16),
            shape((2, 3, 48, 256), F32), shape((2, 3, 32, 256), F32),
            shape((2, 32, D), F32), shape((2, 16, 384), F32),
            shape(items, BF16), shape(items, BF16),
        ],
        scratch_shapes=[
            V(G + (3 * D,), BF16), V((24, 256, 256), BF16), V((D, 3 * D), BF16),
            V(mw.shape, BF16), V((3, D, D), BF16), V(G + (D,), BF16), V(G + (3 * D,), BF16),
            V((3, D, 512), BF16), V(G + (D,), BF16), V((9, 2, 2, 16, D), BF16), V((512, D), F32),
            V((512, D), BF16), V((2, 256, D), BF16), V((2, 256, D), BF16),
            V((2, 3, 2, D, 256), BF16), V((3, 2, D, 256), BF16), V((3, 3, 2, 192, 256), BF16),
            V((3, 2, 192, 256), BF16), V((3, 3, 4, 48, 256), BF16), V((3, 3, 2, 48, 256), BF16),
            V((3, 4, 48, 256), BF16), V((3, 4, 32, 256), BF16), V((3, 3, 48, 256), BF16),
            V((3, 3, 32, 256), BF16), V((3, 48, 256), F32), V((3, 32, 256), F32),
            V((2, 8, D), F32), V((16, D), F32),
            V((2, 32, D), BF16), V((32, D), BF16), V((12, 32, D), BF16), V((32, D), F32),
            V((2, 16, 384), BF16), V((16, 384), BF16), V((12, 16, 384), BF16), V((16, 384), F32),
            V((8, D), F32), V((8, D), F32), V((8, D), F32), V((8, D), F32), V((8, D), F32),
            V(items, BF16), V(items, BF16),
            DMA((15,)), DMA((15, 2)), DMA((2, 2)), DMA((2, 2)), DMA((2, 3, 3, 3)),
            DMA((2, 3, 3, 3)), DMA((2, 3, 3)), DMA((2, 3, 3)), DMA((2, 3, 3)), DMA((2, 3, 3)),
        ],
        compiler_params=pltpu.CompilerParams(
            collective_id=2, has_side_effects=True, vmem_limit_bytes=60 * 2**20
        ),
        name="back",
    )(da, qkv, p, hcg, h, x, dx, mod, times, w, mw, taps, perm, o, s1, go, s2, sb)


def perm_matrices():
    at = np.arange(D)
    rows = []
    for order in ORDERS:
        spots = dict(zip(order, (at // 192, at // 48 % 4, at // 12 % 4)))
        x, y, z = spots["x"], spots["y"], spots["z"]
        rows.append((((x * 2 + z % 2) * 4 + y) * 2 + z // 2) * 12 + at % 12)
    return np.stack(rows).astype(np.int32)


def local(
    latents, conditioning, timesteps, item_counts, cotangent, time_table, mod_weight, mod_bias,
    conv_attn_weight, conv_attn_bias, qkv_weight, query_bias, value_bias, out_weight, out_bias,
    fc1_weight, fc1_bias, conv_ffn_weight, conv_ffn_bias, fc2_weight, fc2_bias,
):
    core = lax.axis_index("seq") % 2
    shard = lax.axis_index("dp") * 4 + lax.axis_index("seq")
    alive = (lax.axis_index("seq") // 2 < item_counts).astype(F32)
    perm = (perm_matrices()[:, :, None] == np.arange(D)[None, None, :]).astype(BF16)
    taps_attn = jnp.pad(conv_attn_weight.astype(F32), ((0, 7), (0, 0)))
    taps_ffn = jnp.pad(conv_ffn_weight.astype(F32), ((0, 7), (0, 0)))
    qkv_bias = jnp.concatenate(
        (query_bias.astype(F32), jnp.zeros((D,), F32), value_bias.astype(F32))
    )[None]
    x, ct, h, hcg, qkv, p, at, mod = attn_call(
        latents.reshape(2, 256, D), cotangent.reshape(2, 256, D), conditioning, timesteps,
        time_table, mod_weight, mod_bias[None], qkv_weight, qkv_bias, taps_attn,
        conv_attn_bias[None],
    )
    out, s1, go, da, dx, s2, sb = ffn_call(
        x, at.reshape(576, D), ct, mod, alive, perm, out_weight, out_bias[None], fc1_weight,
        fc1_bias[None], taps_ffn, conv_ffn_bias[None], fc2_weight, fc2_bias[None],
    )
    out, ig, fe, fl, se, sl, de, dl = back_call(
        da.reshape(8, 2, 2, 16, D), qkv, p, hcg.reshape(512, D), h, x, dx, mod, timesteps,
        qkv_weight, mod_weight, taps_attn, perm, out, s1, go, s2, sb,
    )
    output = out.reshape(2, 8, 32, D)
    input_grad = ig.reshape(2, 8, 32, D).astype(F32)

    def items(v):
        v = v.reshape(2, 2, 2, 4, 4, 16, 128).transpose(4, 2, 3, 1, 0, 5, 6)
        return v.reshape(64, 32, 128)

    early, late_rows = items(de), items(dl)
    d_mod = jnp.concatenate((late_rows[:, :12], early[:, :24]), axis=1).reshape(64, 6 * D)
    all_silu = early[:, 24:30].reshape(64, D)
    all_times = (32.0 * early[:, 30, 0].astype(F32) + early[:, 31, 0].astype(F32)).astype(jnp.int32)
    all_cond_grad = late_rows[:, 16:22].reshape(64, D)
    cond_grad = lax.dynamic_slice_in_dim(
        all_cond_grad, lax.axis_index("dp") * 2, 2, axis=0
    ).astype(F32)
    my_silu = lax.dynamic_slice_in_dim(all_silu, shard * 6, 6, axis=1)
    mod_grad = lax.dot_general(
        my_silu, d_mod, (((0,), (0,)), ((), ())), preferred_element_type=F32
    )
    mod_bias_grad = jnp.sum(
        lax.dynamic_slice_in_dim(d_mod, shard * 36, 36, axis=1).astype(F32), axis=0
    )
    my_cond_grad = lax.dynamic_slice_in_dim(all_cond_grad, shard * 6, 6, axis=1)
    table_grad = jnp.dot(
        (jnp.arange(1000)[:, None] == all_times[None, :]).astype(BF16), my_cond_grad,
        preferred_element_type=F32,
    )
    six = lambda v: lax.dynamic_slice_in_dim(v, core * 6, 6, axis=-2)
    fc1_grad = six(fe[0].reshape(3, 4, 12, 256)).transpose(2, 1, 0, 3).reshape(6, FF)
    fc2_grad = lax.dynamic_slice_in_dim(fe[1], core * 24, 24, axis=1).transpose(1, 0, 2)
    late = six(fl[:, :, :24].reshape(2, 3, 2, 12, 256))
    qkv_grad = jnp.concatenate(
        (
            late[0].transpose(2, 0, 1, 3).reshape(6, 1536),
            late[1, :, 1].transpose(1, 0, 2).reshape(6, D),
        ),
        axis=1,
    )
    out_grad = late[1, :, 0].transpose(1, 0, 2).reshape(6, D)
    wide = se.reshape(4, 16, D).transpose(1, 0, 2).reshape(16, FF)
    wide = lax.dynamic_slice_in_dim(wide, shard * 24, 24, axis=1)
    slim = lax.dynamic_slice_in_dim(
        sl.transpose(1, 0, 2).reshape(16, D), shard * 6, 6, axis=1
    )
    return (
        output, input_grad, cond_grad, table_grad, mod_grad, mod_bias_grad, slim[:9], slim[9],
        qkv_grad, slim[10], slim[11], out_grad, slim[12], fc1_grad, wide[10], wide[:9], wide[9],
        fc2_grad.reshape(24, D), slim[13],
    )


def solution(mesh):
    return jax.shard_map(
        local,
        mesh=mesh,
        in_specs=(
            P("dp", "seq", None, None),
            P("dp", None),
            P("dp"),
            P("dp"),
            P("dp", "seq", None, None),
            P(),
            P(),
            P(),
            P(),
            P(),
            P(),
            P(),
            P(),
            P(),
            P(),
            P(),
            P(),
            P(),
            P(),
            P(),
            P(),
        ),
        out_specs=(
            P("dp", "seq", None, None),
            P("dp", "seq", None, None),
            P("dp", None),
            P(None, ("dp", "seq")),
            P(("dp", "seq"), None),
            P(("dp", "seq")),
            P(None, ("dp", "seq")),
            P(("dp", "seq")),
            P(("dp", "seq"), None),
            P(("dp", "seq")),
            P(("dp", "seq")),
            P(("dp", "seq"), None),
            P(("dp", "seq")),
            P(("dp", "seq"), None),
            P(("dp", "seq")),
            P(None, ("dp", "seq")),
            P(("dp", "seq")),
            P(("dp", "seq"), None),
            P(("dp", "seq")),
        ),
        check_vma=False,
    )
```

```python
import functools

import jax
import jax.numpy as jnp
import numpy as np
from jax import lax
from jax.experimental import pallas as pl
from jax.experimental.pallas import tpu as pltpu
from jax.sharding import PartitionSpec as P

F32 = jnp.float32
BF16 = jnp.bfloat16
D = 768
FF = 3072
FC = 768
NFC = FF // FC
EPS = 1e-6


def mm(a, b):
    return lax.dot_general(a, b, (((1,), (0,)), ((), ())), preferred_element_type=F32)


def mm_nt(a, b):
    return lax.dot_general(a, b, (((1,), (1,)), ((), ())), preferred_element_type=F32)


def mm_tn(a, b):
    return lax.dot_general(a, b, (((0,), (0,)), ((), ())), preferred_element_type=F32)


def row(v):
    return v.astype(F32).reshape(1, v.shape[0])


def fold8(v):
    total = v[0:8]
    for at in range(8, v.shape[0], 8):
        total = total + v[at : at + 8]
    return total


def norm_parts(v):
    center = v - jnp.mean(v, axis=-1, keepdims=True)
    rs = lax.rsqrt(jnp.mean(center * center, axis=-1, keepdims=True) + EPS)
    return center * rs, rs


def by_core(taps, at, core):
    return jnp.where(core == 1, taps[3 * (2 - at // 3) + at % 3], taps[at])


def gelu_pair(v):
    z = jnp.abs(v) * 0.7071067811865476
    t = 1.0 / (1.0 + 0.3275911 * z)
    e = jnp.exp(-0.5 * (v * v))
    poly = t * (
        0.127414796
        + t * (-0.142248368 + t * (0.7107068705 + t * (-0.7265760135 + t * 0.5307027145)))
    )
    tail = poly * e
    cdf = jnp.where(v >= 0, 1.0 - tail, tail)
    return v * cdf, cdf + v * (e * 0.3989422804014327)


def side_masks():
    place = lax.broadcasted_iota(jnp.int32, (16, 128), 0)
    return place == 0, place == 15


def with_sides(even, odd, masks):
    left = jnp.where(masks[0], 0.0, pltpu.roll(odd, 1, 0))
    right = jnp.where(masks[1], 0.0, pltpu.roll(even, 15, 0))
    return even, odd, left, right


def conv_row(rows, taps):
    even = odd = None
    for a in range(3):
        if rows[a] is None:
            continue
        ev, od, left, right = rows[a]
        for tap, ce, co in ((3 * a, left, ev), (3 * a + 1, ev, od), (3 * a + 2, od, right)):
            even = taps[tap] * ce if even is None else even + taps[tap] * ce
            odd = taps[tap] * co if odd is None else odd + taps[tap] * co
    return even, odd


def tap_products(sums, rows, d_even, d_odd):
    for a in range(3):
        if rows[a] is None:
            continue
        ev, od, left, right = rows[a]
        for tap, ce, co in ((3 * a, left, ev), (3 * a + 1, ev, od), (3 * a + 2, od, right)):
            term = fold8(d_even * ce + d_odd * co)
            sums[tap] = term if sums[tap] is None else sums[tap] + term


MESH = pl.DeviceIdType.MESH


def spot():
    dp = lax.axis_index("dp")
    seq = lax.axis_index("seq")
    return dict(dp=dp, seq=seq, x=dp // 8, zl=(dp // 4) % 2, y=dp % 4, zh=seq // 2, core=seq % 2)


def seq_peer(me, zh, core):
    return (me["dp"], zh * 2 + core)


def axis_peer(me, axis, offset):
    x, y, z = me["x"], me["y"], me["zh"] * 2 + me["zl"]
    if axis == "x":
        x = (x + offset) % 4
    elif axis == "y":
        y = (y + offset) % 4
    else:
        z = (z + offset) % 4
    return ((x * 2 + z % 2) * 4 + y, (z // 2) * 2 + me["core"])


def remote(src, dst, send, recv, device):
    return pltpu.make_async_remote_copy(
        src_ref=src, dst_ref=dst, send_sem=send, recv_sem=recv, device_id=device,
        device_id_type=MESH,
    )


def arrived(ref, sem):
    pltpu.make_async_copy(ref, ref, sem).wait()


def hail(peers):
    barrier = pltpu.get_barrier_semaphore()
    for peer in peers:
        pl.semaphore_signal(barrier, inc=1, device_id=peer, device_id_type=MESH)


def heard(count):
    pl.semaphore_wait(pltpu.get_barrier_semaphore(), count)


def greet(peers):
    hail(peers)
    heard(len(peers))


ORDERS = (("x", "y", "z"), ("y", "z", "x"), ("z", "x", "y"))
EARLY = (
    (("x", "y", "z"), ("x", "y", "z"), ("y", "z", "x")),
    (("y", "x", "z"), ("z", "x", "y"), ("z", "x", "y")),
)


def axis_spot(me, axis):
    return me["zh"] * 2 + me["zl"] if axis == "z" else me[axis]


def early_peer(me, stage, part, offset):
    first, second = (EARLY[which][part][stage] for which in range(2))
    pick = lambda a, b: jnp.where(me["core"] == 0, a, b)
    peers = (axis_peer(me, first, offset), axis_peer(me, second, offset))
    here = pick(axis_spot(me, first), axis_spot(me, second))
    return here, tuple(pick(a, b) for a, b in zip(*peers))


def ffn_kernel(
    x_ref, at_ref, ct_ref, mod_ref, alive_ref, perm_ref, ow_ref, ob_ref, f1_ref, f1b_ref,
    tap_ref, cb_ref, f2_ref, f2b_ref,
    out_ref, s1_ref, last_ref, dbr_ref, da_ref, dx_ref, s2_ref, sm_ref,
    x1_s, br_s, h2_s, h2t_s, dffn_s, u_s, duc_s, act_s, du_s, dact_s, ffn_s, dh2_s, acc_s,
    ch_s, pre_s, r1_s, bias_s, das_s, dar_s, pair_sem, st_send, st_recv,
):
    step = pl.program_id(0)
    me = spot()
    core = me["core"]
    other = seq_peer(me, me["zh"], 1 - core)
    alive = alive_ref[0]

    @pl.when(step == 0)
    def _():
        bias_s[0:1, :] = row(f1b_ref[...])
        bias_s[1:2, :] = row(cb_ref[...])
        hail([axis_peer(me, axis, o) for axis in "xyz" for o in (1, 2, 3)] + [other])

    def pair_copy(at):
        slot = at % 2
        return remote(
            ch_s.at[slot, 1 - core], pre_s.at[slot], pair_sem.at[slot, 0], pair_sem.at[slot, 1],
            other,
        )

    def first_copies(at):
        slot = at % 2
        out = []
        for p in range(3):
            for o in (1, 2, 3):
                here, peer = early_peer(me, 0, p, o)
                out.append(
                    remote(
                        ch_s.at[slot, core, p, (here + o) % 4], r1_s.at[slot, o - 1, p],
                        st_send.at[slot, p, o - 1], st_recv.at[slot, p, o - 1], peer,
                    )
                )
        return out

    def pair_add(at):
        slot = at % 2
        pair_copy(at).wait()
        for p in range(3):

            def add(a, _):
                ch_s[slot, core, p, a] = ch_s[slot, core, p, a] + pre_s[slot, p, a]
                return 0

            lax.fori_loop(0, 4, add, 0)

    def first_send(at):
        pair_add(at)
        for copy in first_copies(at):
            copy.start()

    def first_take(at):
        slot = at % 2
        for copy in first_copies(at):
            copy.wait()
        for p in range(3):
            here, _peer = early_peer(me, 0, p, 1)
            total = ch_s[slot, core, p, here].astype(F32)
            for o in range(3):
                total = total + r1_s[slot, o, p].astype(F32)
            total = total.astype(BF16)

            @pl.when(core == 0)
            def _():
                s1_ref[p, at] = total

            @pl.when(core == 1)
            def _():
                for c in range(4):
                    s1_ref[p, c, pl.ds(pl.multiple_of(at * 48, 16), 48)] = total[
                        48 * c : 48 * c + 48
                    ]

    @pl.when(step == 0)
    def _():
        br_s[...] = mm(at_ref[...], ow_ref[...]) + row(ob_ref[...])
        shift2, scale2, gate1, gate2 = (mod_ref[i : i + 1, :] for i in (3, 4, 2, 5))

        def rows_a(r, _):
            at = pl.ds(pl.multiple_of(r * 96, 96), 96)
            x1 = x_ref[at, :].astype(F32) + gate1 * br_s[at, :]
            x1_s[at, :] = x1
            n2, _unused = norm_parts(x1)
            h2_s[at, :] = (n2 * (1.0 + scale2) + shift2).astype(BF16)
            return 0

        lax.fori_loop(0, 6, rows_a, 0)

        def rows_b(r, _):
            at = pl.ds(pl.multiple_of(r * 272, 16), 272)
            dffn_s[at, :] = (ct_ref[at, :].astype(F32) * alive * gate2).astype(BF16)
            return 0

        lax.fori_loop(0, 2, rows_b, 0)
        for p in range(2):
            h2t_s[p] = mm_nt(perm_ref[p], h2_s[0:512, :]).astype(BF16)
        ffn_s[...] = jnp.zeros_like(ffn_s)
        dh2_s[...] = jnp.zeros_like(dh2_s)

    for j in range(3):
        cols = slice(256 * j, 256 * j + 256)
        u_s[:, cols] = (mm(h2_s[...], f1_ref[:, cols]) + bias_s[0:1, pl.ds(pl.multiple_of(step * FC + 256 * j, 256), 256)]).astype(BF16)
        dact_s[:, cols] = mm_nt(dffn_s[...], f2_ref[cols, :])

    @pl.when(step == 0)
    def _():
        heard(10)

    @pl.when(step > 0)
    def _():
        first_send(step - 1)

    masks = side_masks()

    def lanes(j, _):
        cols = pl.ds(pl.multiple_of(j * 128, 128), 128)
        taps = tap_ref[:, cols].astype(F32)
        taps = [taps[t : t + 1] for t in range(9)]
        taps = [by_core(taps, t, core) for t in range(9)]
        offset = bias_s[1:2, pl.ds(pl.multiple_of(step * FC + j * 128, 128), 128)]

        def sided(ref, l):
            return with_sides(
                ref[32 * l : 32 * l + 16, cols].astype(F32),
                ref[32 * l + 16 : 32 * l + 32, cols].astype(F32),
                masks,
            )

        rows = [None, sided(u_s, 0), sided(u_s, 1)]
        sums = [None] * 9
        bias_sum = None
        for l in range(17):
            ce, co = conv_row(rows, taps)
            ae, ge = gelu_pair(ce + offset)
            ao, go = gelu_pair(co + offset)
            de = (ge * dact_s[32 * l : 32 * l + 16, cols]).astype(BF16)
            do = (go * dact_s[32 * l + 16 : 32 * l + 32, cols]).astype(BF16)
            duc_s[32 * l : 32 * l + 16, cols] = de
            duc_s[32 * l + 16 : 32 * l + 32, cols] = do
            if l < 16:
                act_s[32 * l : 32 * l + 16, cols] = ae.astype(BF16)
                act_s[32 * l + 16 : 32 * l + 32, cols] = ao.astype(BF16)
                de, do = de.astype(F32), do.astype(F32)
                tap_products(sums, rows, de, do)
                term = fold8(de + do)
                bias_sum = term if bias_sum is None else bias_sum + term
                rows = [rows[1], rows[2], sided(u_s, l + 2) if l + 2 < 18 else None]
        for t in range(9):
            s2_ref[t : t + 1, cols] = jnp.sum(by_core(sums, t, core), axis=0, keepdims=True)
        s2_ref[9:10, cols] = jnp.sum(bias_sum, axis=0, keepdims=True)
        back = [taps[8 - t] for t in range(9)]
        rows = [None, sided(duc_s, 0), sided(duc_s, 1)]
        bias_sum = None
        for l in range(16):
            ue, uo = conv_row(rows, back)
            ue, uo = ue.astype(BF16), uo.astype(BF16)
            du_s[32 * l : 32 * l + 16, cols] = ue
            du_s[32 * l + 16 : 32 * l + 32, cols] = uo
            term = fold8(ue.astype(F32) + uo.astype(F32))
            bias_sum = term if bias_sum is None else bias_sum + term
            rows = [rows[1], rows[2], sided(duc_s, l + 2) if l + 2 < 17 else None]
        s2_ref[10:11, cols] = jnp.sum(bias_sum, axis=0, keepdims=True)
        return 0

    lax.fori_loop(0, FC // 128, lanes, 0)

    slot = step % 2
    for j in range(3):
        cols = slice(256 * j, 256 * j + 256)
        got = mm(h2t_s[j // 2], du_s[:, cols]).astype(BF16)
        ch_s[slot, 0, j] = got.reshape(4, 192, 256)
    for part in range(3):
        grad = mm_tn(act_s[...], dffn_s[0:512, 256 * part : 256 * part + 256]).astype(BF16)
        for zl in range(2):
            for y in range(4):
                for zh in range(2):
                    at = ((zl * 4 + y) * 2 + zh) * 48
                    z = zh * 2 + zl
                    a, c = (y, z) if part == 0 else (z, y)
                    ch_s[slot, 1, part, a, 48 * c : 48 * c + 48] = grad[at : at + 48, :]
    pair_copy(step).start()
    ffn_s[...] += mm(act_s[...], f2_ref[...])
    dh2_s[...] += mm_nt(du_s[...], f1_ref[...])

    @pl.when(step > 0)
    def _():
        first_take(step - 1)

    @pl.when(step == NFC - 1)
    def _():
        shift2, scale2, gate1, gate2 = (mod_ref[i : i + 1, :] for i in (3, 4, 2, 5))
        acc_s[...] = jnp.zeros_like(acc_s)
        f2b = row(f2b_ref[...])

        def rows_c(r, _):
            at = pl.ds(pl.multiple_of(r * 128, 128), 128)
            x1 = x1_s[at, :]
            ffn = ffn_s[at, :] + f2b
            dy = ct_ref[at, :].astype(F32) * alive
            out_ref[at, :] = (alive * (x1 + gate2 * ffn)).astype(BF16)
            n2, rs = norm_parts(x1)
            dh2 = dh2_s[at, :]
            g2 = dh2 * (1.0 + scale2)
            dx1 = dy + rs * (
                g2
                - jnp.mean(g2, axis=-1, keepdims=True)
                - n2 * jnp.mean(g2 * n2, axis=-1, keepdims=True)
            )
            dx_ref[at, :] = dx1
            dbr = (dx1 * gate1).astype(BF16)
            dbr_ref[pl.ds(2 * r, 2)] = dbr.reshape(2, 2, 2, 16, D)
            acc_s[0] += fold8(dx1 * br_s[at, :])
            acc_s[1] += fold8(dh2)
            acc_s[2] += fold8(dh2 * n2)
            acc_s[3] += fold8(dy * ffn)
            acc_s[4] += fold8(dbr.astype(F32))
            acc_s[5] += fold8(dffn_s[at, :].astype(F32))
            return 0

        lax.fori_loop(0, 4, rows_c, 0)
        for i in range(6):
            sm_ref[i : i + 1, :] = jnp.sum(acc_s[i], axis=0, keepdims=True)
        halves = [dbr_ref[:, parity].reshape(256, D) for parity in range(2)]
        odd = mm_nt(halves[1], ow_ref[...]).astype(BF16)
        das_s[...] = odd.reshape(8, 2, 16, D)
        da_copy = remote(das_s, dar_s, pair_sem.at[2, 0], pair_sem.at[2, 1], other)
        da_copy.start()
        da_ref[0] = mm_nt(halves[0], ow_ref[...]).astype(BF16).reshape(8, 2, 16, D)
        pair_add(step)
        last_ref[...] = ch_s[step % 2, core]
        da_copy.wait()
        da_ref[1] = dar_s[...]


def ffn_call(x, at, ct, mod, alive, perm, ow, ob, f1, f1b, taps, cb, f2, f2b):
    whole = lambda s: pl.BlockSpec(s, lambda i: (0,) * len(s))
    return pl.pallas_call(
        ffn_kernel,
        grid=(NFC,),
        in_specs=[
            whole((576, D)), whole((576, D)), whole((576, D)), whole((8, D)),
            pl.BlockSpec(memory_space=pltpu.SMEM),
            whole((2, D, D)), whole((D, D)), whole((D,)),
            pl.BlockSpec((D, FC), lambda i: (0, i)),
            whole((FF,)),
            pl.BlockSpec((9, FC), lambda i: (0, i)),
            whole((FF,)),
            pl.BlockSpec((FC, D), lambda i: (i, 0)),
            whole((D,)),
        ],
        out_specs=[
            whole((512, D)),
            whole((3, 4, 192, 256)), whole((3, 4, 192, 256)),
            whole((8, 2, 2, 16, D)), whole((2, 8, 2, 16, D)), whole((512, D)),
            pl.BlockSpec((16, FC), lambda i: (0, i)),
            whole((8, D)),
        ],
        out_shape=[
            jax.ShapeDtypeStruct((512, D), BF16),
            jax.ShapeDtypeStruct((3, 4, 192, 256), BF16),
            jax.ShapeDtypeStruct((3, 4, 192, 256), BF16),
            jax.ShapeDtypeStruct((8, 2, 2, 16, D), BF16),
            jax.ShapeDtypeStruct((2, 8, 2, 16, D), BF16),
            jax.ShapeDtypeStruct((512, D), F32),
            jax.ShapeDtypeStruct((16, FF), F32),
            jax.ShapeDtypeStruct((8, D), F32),
        ],
        scratch_shapes=[
            pltpu.VMEM((576, D), F32), pltpu.VMEM((576, D), F32), pltpu.VMEM((576, D), BF16),
            pltpu.VMEM((2, D, 512), BF16), pltpu.VMEM((544, D), BF16),
            pltpu.VMEM((576, FC), BF16), pltpu.VMEM((544, FC), BF16), pltpu.VMEM((512, FC), BF16),
            pltpu.VMEM((512, FC), BF16), pltpu.VMEM((544, FC), F32),
            pltpu.VMEM((512, D), F32), pltpu.VMEM((512, D), F32), pltpu.VMEM((6, 8, D), F32),
            pltpu.VMEM((2, 2, 3, 4, 192, 256), BF16), pltpu.VMEM((2, 3, 4, 192, 256), BF16),
            pltpu.VMEM((2, 3, 3, 192, 256), BF16), pltpu.VMEM((8, FF), F32),
            pltpu.VMEM((8, 2, 16, D), BF16), pltpu.VMEM((8, 2, 16, D), BF16),
            pltpu.SemaphoreType.DMA((3, 2)),
            pltpu.SemaphoreType.DMA((2, 3, 3)), pltpu.SemaphoreType.DMA((2, 3, 3)),
        ],
        compiler_params=pltpu.CompilerParams(
            dimension_semantics=("arbitrary",), vmem_limit_bytes=60 * 2**20,
            collective_id=3, has_side_effects=True,
        ),
        name="ffn",
    )(x, at, ct, mod, alive, perm, ow, ob, f1, f1b, taps, cb, f2, f2b)


def place_matrix(count, flip, inverse):
    rows = count // 32
    out = lax.broadcasted_iota(jnp.int32, (count, count), 0)
    at = lax.broadcasted_iota(jnp.int32, (count, count), 1)
    row = out // 32
    row = jnp.where(flip, rows - 1 - row, row)
    low = out % 32
    if inverse:
        low = (low % 2) * 16 + low // 2
    else:
        low = (low % 16) * 2 + low // 16
    return jnp.where(at == row * 32 + low, 1.0, 0.0).astype(BF16)


def head_lanes(values, half):
    lane = lax.broadcasted_iota(jnp.int32, values.shape, 1)
    return jnp.where((lane // 64) == half, values, jnp.zeros_like(values))


def attn_kernel(
    lat_ref, ct_ref, cond_ref, time_ref, table_ref, mw_ref, mb_ref, w_ref, qb_ref, vb_ref,
    tap_ref, cb_ref,
    x_out, ct_out, h_out, hcg_out, qkv_out, p_out, at_out, mod_out,
    xr_s, xh_s, x_s, c_s, h_s, hcg_s, sb_s, w_s, qkv_s, p_s, ag_s, at_s, mod_s, table_s, mw_s, cb_s,
    send0, recv0, sem_pair, sem_loc,
):
    me = spot()
    zh, core, seq = me["zh"], me["core"], me["seq"]
    other = seq_peer(me, zh, 1 - core)
    w_load = pltpu.make_async_copy(w_ref, w_s, sem_loc.at[0])
    table_load = pltpu.make_async_copy(table_ref, table_s, sem_loc.at[10])
    mw_load = pltpu.make_async_copy(mw_ref, mw_s, sem_loc.at[11])
    for copy in (table_load, mw_load, w_load):
        copy.start()

    greet(
        [
            seq_peer(me, (zh + dz) % 2, (core + dc) % 2)
            for dz, dc in ((0, 1), (1, 0), (1, 1))
        ]
    )
    slot = jnp.where(zh == 0, core, 1 - core)
    inner = jnp.logical_or(seq == 1, seq == 2)
    halo_core = jnp.where(seq == 1, 1, 0)
    halo_at = pl.multiple_of(jnp.where(seq == 1, 192, 0), 64)

    def sends(arrays, act):
        for a in arrays:
            ref = (lat_ref, ct_ref)[a]
            for j in range(2):
                own = jnp.logical_and(zh == j, core == zh)
                main = (ref.at[j], xr_s.at[a, slot])
                halo = (ref.at[j, pl.ds(halo_at, 64)], xh_s.at[a])

                @pl.when(own)
                def _():
                    act(lambda: pltpu.make_async_copy(*main, recv0.at[a, slot]), True)

                @pl.when(jnp.logical_not(own))
                def _():
                    act(
                        lambda: remote(*main, send0.at[a, j, 0], recv0.at[a, slot], seq_peer(me, j, zh)),
                        False,
                    )

                @pl.when(jnp.logical_and(inner, zh == j))
                def _():
                    act(lambda: pltpu.make_async_copy(*halo, recv0.at[a, 2]), True)

                @pl.when(jnp.logical_and(inner, zh != j))
                def _():
                    act(
                        lambda: remote(
                            *halo, send0.at[a, j, 1], recv0.at[a, 2], seq_peer(me, j, halo_core)
                        ),
                        False,
                    )

    sends((0,), lambda make, local: make().start())

    flip = core == 1
    big = place_matrix(256, flip, False)
    small = place_matrix(64, flip, False)

    table_load.wait()
    here = lax.broadcasted_iota(jnp.int32, (8, table_s.shape[0]), 1)
    one_hot = jnp.where(here == time_ref[zh], 1.0, 0.0).astype(BF16)
    cond = jnp.where(zh == 0, cond_ref[0:1, :], cond_ref[1:2, :]) + mm(one_hot, table_s[...])
    silu = (cond / (1.0 + jnp.exp(-cond))).astype(BF16)
    mw_load.wait()
    for i in range(6):
        cols = slice(D * i, D * i + D)
        mod_s[i : i + 1, :] = (mm(silu, mw_s[:, cols]) + row(mb_ref[cols]))[0:1]
    mod_s[6:7, :] = cond[0:1]
    mod_s[7:8, :] = silu[0:1].astype(F32)
    shift1, scale1 = mod_s[0:1, :], mod_s[1:2, :]

    def placed(a, into):
        for b in range(2):
            arrived(xr_s.at[a, b], recv0.at[a, b])
            into[256 * b : 256 * b + 256, :] = mm(big, xr_s[a, b]).astype(BF16)
        arrived(xh_s.at[a], recv0.at[a, 2])
        into[512:576, :] = mm(small, xh_s[a]).astype(BF16)

    placed(0, x_s)
    sends((1,), lambda make, local: make().start())

    def rows_a(r, _):
        at = pl.ds(pl.multiple_of(r * 96, 96), 96)
        n1, _unused = norm_parts(x_s[at, :].astype(F32))
        h_s[at, :] = (n1 * (1.0 + scale1) + shift1).astype(BF16)
        return 0

    lax.fori_loop(0, 6, rows_a, 0)
    outs = [
        pltpu.make_async_copy(x_s, x_out, sem_loc.at[1]),
        pltpu.make_async_copy(h_s, h_out, sem_loc.at[2]),
        pltpu.make_async_copy(mod_s, mod_out, sem_loc.at[12]),
    ]
    for copy in outs:
        copy.start()
    masks = side_masks()

    def lanes(j, _):
        cols = pl.ds(pl.multiple_of(j * 128, 128), 128)
        taps = tap_ref[:, cols].astype(F32)
        taps = [taps[t : t + 1] for t in range(9)]
        taps = [by_core(taps, t, core) for t in range(9)]
        offset = cb_s[0:1, cols]

        def sided(l):
            return with_sides(
                h_s[32 * l : 32 * l + 16, cols].astype(F32),
                h_s[32 * l + 16 : 32 * l + 32, cols].astype(F32),
                masks,
            )

        rows = [None, sided(0), sided(1)]
        for l in range(16):
            ce, co = conv_row(rows, taps)
            ce, co = (ce + offset).astype(BF16), (co + offset).astype(BF16)
            if l % 2 == 0:
                hcg_s[0, l // 2, 0, :, cols] = ce
                hcg_s[0, l // 2, 1, :, cols] = co
            else:
                sb_s[l // 2, 0, :, cols] = ce
                sb_s[l // 2, 1, :, cols] = co
            rows = [rows[1], rows[2], sided(l + 2) if l < 15 else None]
        return 0

    cb_s[0:1, :] = row(cb_ref[...])
    lax.fori_loop(0, D // 128, lanes, 0)
    hc_copy = remote(sb_s, hcg_s.at[1], sem_pair.at[0], sem_pair.at[1], other)
    hc_copy.start()
    w_load.wait()

    def project(half):
        for i, bias in enumerate((qb_ref, None, vb_ref)):
            cols = slice(D * i, D * i + D)
            got = mm(hcg_s[half].reshape(256, D), w_s[:, cols])
            if bias is not None:
                got = got + row(bias[...])
            qkv_s[half, :, :, :, cols] = got.astype(BF16).reshape(8, 2, 16, D)

    project(0)
    hc_copy.wait()
    outs.append(pltpu.make_async_copy(hcg_s, hcg_out, sem_loc.at[3]))
    outs[-1].start()
    project(1)
    outs.append(pltpu.make_async_copy(qkv_s, qkv_out, sem_loc.at[4]))
    outs[-1].start()

    def attend(i, _):
        pc, pair = i // 6, i % 6

        def part(which):
            cols = pl.ds(pl.multiple_of(which * D + pair * 128, 128), 128)
            return jnp.concatenate(
                [qkv_s[half, :, pc, :, cols].reshape(128, 128) for half in range(2)], axis=0
            )

        q, k, v = part(0), part(1), part(2)
        v_t = v.T
        got = []
        for half in range(2):
            scores = mm_nt(k, head_lanes(q, half)) * 0.125
            e = jnp.exp(scores - jnp.max(scores, axis=0, keepdims=True))
            low = (e * (1.0 / jnp.sum(e, axis=0, keepdims=True))).astype(BF16)
            p_s[2 * i + half] = low
            got.append(mm(v_t[64 * half : 64 * half + 64], low))
        o = jnp.concatenate(got, axis=0).T.astype(BF16)
        cols = pl.ds(pl.multiple_of(pair * 128, 128), 128)
        for half in range(2):
            ag_s[half, :, pc, :, cols] = o[128 * half : 128 * half + 128].reshape(8, 16, 128)
        return 0

    lax.fori_loop(0, 12, attend, 0, unroll=2)
    back = [
        remote(ag_s.at[1], at_s.at[pl.ds(0, 8), 1], sem_pair.at[2], sem_pair.at[3], other),
        remote(ag_s.at[0, 7], at_s.at[8, 1], sem_pair.at[4], sem_pair.at[5], other),
        pltpu.make_async_copy(ag_s.at[0], at_s.at[pl.ds(0, 8), 0], sem_loc.at[5]),
        pltpu.make_async_copy(ag_s.at[1, 7], at_s.at[8, 0], sem_loc.at[6]),
    ]
    for copy in back:
        copy.start()
    outs.append(pltpu.make_async_copy(p_s, p_out, sem_loc.at[7]))
    outs[-1].start()
    placed(1, c_s)
    outs.append(pltpu.make_async_copy(c_s, ct_out, sem_loc.at[8]))
    outs[-1].start()
    for copy in back:
        copy.wait()
    outs.append(pltpu.make_async_copy(at_s, at_out, sem_loc.at[9]))
    outs[-1].start()
    for copy in outs:
        copy.wait()

    def finish(make, local):
        if not local:
            make().wait_send()

    sends((0, 1), finish)


VMEM_SPEC = pl.BlockSpec(memory_space=pltpu.VMEM)
ANY_SPEC = pl.BlockSpec(memory_space=pl.ANY)
SMEM_SPEC = pl.BlockSpec(memory_space=pltpu.SMEM)


def attn_call(lat, ct, cond, times, table, mw, mb, w, qb, vb, taps, cb):
    G = (2, 8, 2, 16)
    shape = jax.ShapeDtypeStruct
    return pl.pallas_call(
        attn_kernel,
        in_specs=[
            ANY_SPEC, ANY_SPEC, VMEM_SPEC, SMEM_SPEC, ANY_SPEC, ANY_SPEC, VMEM_SPEC, ANY_SPEC,
            VMEM_SPEC, VMEM_SPEC, VMEM_SPEC, VMEM_SPEC,
        ],
        out_specs=[ANY_SPEC] * 8,
        out_shape=[
            shape((576, D), BF16), shape((576, D), BF16), shape((576, D), BF16),
            shape(G + (D,), BF16), shape(G + (3 * D,), BF16), shape((24, 256, 256), BF16),
            shape((9, 2, 2, 16, D), BF16), shape((8, D), F32),
        ],
        scratch_shapes=[
            pltpu.VMEM((2, 2, 256, D), BF16), pltpu.VMEM((2, 64, D), BF16),
            pltpu.VMEM((576, D), BF16), pltpu.VMEM((576, D), BF16), pltpu.VMEM((576, D), BF16),
            pltpu.VMEM(G + (D,), BF16), pltpu.VMEM((8, 2, 16, D), BF16),
            pltpu.VMEM((D, 3 * D), BF16), pltpu.VMEM(G + (3 * D,), BF16),
            pltpu.VMEM((24, 256, 256), BF16), pltpu.VMEM(G + (D,), BF16),
            pltpu.VMEM((9, 2, 2, 16, D), BF16),
            pltpu.VMEM((8, D), F32), pltpu.VMEM(table.shape, BF16), pltpu.VMEM(mw.shape, BF16),
            pltpu.VMEM((8, D), F32),
            pltpu.SemaphoreType.DMA((2, 2, 2)), pltpu.SemaphoreType.DMA((2, 3)),
            pltpu.SemaphoreType.DMA((6,)), pltpu.SemaphoreType.DMA((13,)),
        ],
        compiler_params=pltpu.CompilerParams(
            collective_id=1, has_side_effects=True, vmem_limit_bytes=56 * 2**20
        ),
        name="attend",
    )(lat, ct, cond, times, table, mw, mb, w, qb, vb, taps, cb)


def back_kernel(
    da_ref, qkv_ref, p_ref, hcg_hbm, h_hbm, x_hbm, dx_hbm, mod_ref, time_ref, w_ref, mw_ref,
    tap_ref, perm_ref, o_hbm, s1_ref, last_hbm, dbr_hbm, at_hbm, s2_ref, sb_ref,
    oret_out, iret_out, fe_out, fl_out, se_out, sl_out, de_out, dl_out,
    qkv_s, p_s, w_s, mw_s, perm_s, dag_s, dqkv_s, hct_s, dhc_s, dh_s, gh_s, ig_s, os_s, is_s,
    lg_s, prl_s, s1_s, r1x, r1l, s1l, r2e, r2l, t3e, t3l, r3e, r3l, fe_s, fl_s,
    acc_s, sv_s, se_p, se_r, se_s, se_f, sl_p, sl_r, sl_s, sl_f, mp_s, mr_s, mpl_s, mrl_s,
    item_s, de_s, dl_s, hcg_ref, h_ref, x_ref, dx_ref, o_ref, last_ref, dbr_ref, at_ref,
    loc, pair_sem, ret_send, ret_recv, st_send, st_recv, sm_send, sm_recv, dm_send, dm_recv,
):
    me = spot()
    zh, core = me["zh"], me["core"]
    other = seq_peer(me, zh, 1 - core)
    loads = [
        pltpu.make_async_copy(*pair, loc.at[15 + at])
        for at, pair in enumerate((
            (perm_ref, perm_s), (at_hbm, at_ref), (dbr_hbm, dbr_ref), (hcg_hbm, hcg_ref),
            (last_hbm, last_ref), (o_hbm, o_ref), (da_ref, dag_s), (qkv_ref, qkv_s),
            (p_ref, p_s), (w_ref, w_s), (s1_ref, s1_s), (h_hbm, h_ref), (x_hbm, x_ref),
            (dx_hbm, dx_ref), (mw_ref, mw_s),
        ))
    ]
    for load in loads:
        load.start()
    peers = [axis_peer(me, axis, o) for axis in "xyz" for o in (1, 2, 3)]
    peers += [other, seq_peer(me, 1 - zh, 1 - core)]
    hail(peers)

    def stage_sends(stage, bufs, late, parts=(0, 1, 2)):
        out = []
        for p in parts:
            for o in (1, 2, 3):
                if late:
                    axis = ORDERS[p][stage]
                    here, peer = axis_spot(me, axis), axis_peer(me, axis, o)
                else:
                    here, peer = early_peer(me, stage, p, o)
                src, dst = bufs(p, o, (here + o) % 4)
                copy = remote(
                    src, dst, st_send.at[late, stage, p, o - 1], st_recv.at[late, stage, p, o - 1],
                    peer,
                )
                copy.start()
                out.append(copy)
        return out

    def chunk(there, rows):
        return pl.ds(pl.multiple_of(there * rows, 16), rows)

    home = place_matrix(256, core == 1, True)

    def give_back(which, act):
        ref, out = ((os_s, oret_out), (is_s, iret_out))[which]
        for b in range(2):
            to_core = jnp.where(core == 0, b, 1 - b)
            own = jnp.logical_and(zh == core, b == 0)

            @pl.when(own)
            def _():
                act(lambda: pltpu.make_async_copy(ref.at[b], out.at[zh], ret_recv.at[which, zh]), True)

            @pl.when(jnp.logical_not(own))
            def _():
                act(
                    lambda: remote(
                        ref.at[b], out.at[zh], ret_send.at[which, b], ret_recv.at[which, zh],
                        seq_peer(me, core, to_core),
                    ),
                    False,
                )

    for load in loads[:4]:
        load.wait()
    for p in range(3):
        at_t = mm_nt(perm_s[p], at_ref[0:512, :]).astype(BF16)
        lg_s[1, p, 0] = mm(at_t, dbr_ref[:, 256 * p : 256 * p + 256]).astype(BF16)
        hct_s[p] = mm_nt(perm_s[p], hcg_ref[...]).astype(BF16)
    heard(len(peers))
    loads[4].wait()
    st1x = stage_sends(0, lambda p, o, a: (last_ref.at[p, a], r1x.at[o - 1, p]), 0)
    mp_s[...] = sb_ref[...]
    mp_copy = remote(mp_s, mr_s, pair_sem.at[1, 0], pair_sem.at[1, 1], other)
    mp_copy.start()
    for half in range(2):
        for q in range(2):
            at = D * (2 * half + q)
            se_p[half, 16 * q : 16 * q + 16, :] = s2_ref[:, at : at + D].astype(BF16)
    se_copy = remote(se_p.at[1 - core], se_r, pair_sem.at[2, 0], pair_sem.at[2, 1], other)
    se_copy.start()

    loads[5].wait()
    for b in range(2):
        os_s[b] = mm(home, o_ref[256 * b : 256 * b + 256, :]).astype(BF16)
    give_back(0, lambda make, local: make().start())
    for load in loads[6:9]:
        load.wait()

    def attend_back(i, _):
        pc, pair = i // 6, i % 6
        lanes_at = [
            pl.ds(pl.multiple_of(which * D + pair * 128, 128), 128) for which in range(3)
        ]

        def part(ref, cols):
            return jnp.concatenate(
                [ref[half, :, pc, :, cols].reshape(128, 128) for half in range(2)], axis=0
            )

        q, k, v = (part(qkv_s, cols) for cols in lanes_at)
        do = part(dag_s, lanes_at[0])
        k_t = k.T
        dq_t, dk, dv = [], None, None
        for half in range(2):
            dom, qm = head_lanes(do, half), head_lanes(q, half)
            low = p_s[2 * i + half]
            probs = low.astype(F32)
            dp = mm_nt(v, dom)
            ds = (probs * (dp - jnp.sum(probs * dp, axis=0, keepdims=True))).astype(BF16)
            dq_t.append(mm(k_t[64 * half : 64 * half + 64], ds))
            dk_h, dv_h = mm(ds, qm), mm(low, dom)
            dk = dk_h if dk is None else dk + dk_h
            dv = dv_h if dv is None else dv + dv_h
        dq = jnp.concatenate(dq_t, axis=0).T
        for cols, got in zip(lanes_at, (0.125 * dq, 0.125 * dk, dv)):
            got = got.astype(BF16)
            for half in range(2):
                dqkv_s[half, :, pc, :, cols] = got[128 * half : 128 * half + 128].reshape(8, 16, 128)
        return 0

    z_me = axis_spot(me, "z")

    def small_stage(stage, sums, items, kind):
        axis = "xyz"[stage]
        spots = ((z_me, me["y"], me["x"]), (z_me, me["y"]), (z_me,))[stage]
        if stage == 0:
            ref = items.at[core, z_me, me["y"], me["x"]]
        elif stage == 1:
            ref = items.at[core, z_me, me["y"]]
        else:
            ref = items.at[core, z_me]
        out = []
        for o in (1, 2, 3):
            peer = axis_peer(me, axis, o)
            at = (kind, stage, o - 1)
            out.append(
                remote(sums.at[4 * stage], sums.at[4 * stage + o], sm_send.at[at], sm_recv.at[at], peer)
            )
            out.append(remote(ref, ref, dm_send.at[at], dm_recv.at[at], peer))
        for copy in out:
            copy.start()
        return out

    def small_take(stage, sums, items, kind, copies, last):
        axis = "xyz"[stage]
        for copy in copies:
            copy.wait_send()
        for o in (1, 2, 3):
            at = (kind, stage, o - 1)
            arrived(sums.at[4 * stage + o], sm_recv.at[at])
            there = (axis_spot(me, axis) + 4 - o) % 4
            if stage == 0:
                ref = items.at[core, z_me, me["y"], there]
            elif stage == 1:
                ref = items.at[core, z_me, there]
            else:
                ref = items.at[core, there]
            arrived(ref, dm_recv.at[at])
        total = sums[4 * stage].astype(F32)
        for o in (1, 2, 3):
            total = total + sums[4 * stage + o].astype(F32)
        if stage < 2:
            sums[4 * stage + 4] = total.astype(BF16)
        else:
            last[...] = total

    def lane_rows(values, count):
        return [
            values[i : i + 1, 128 * l : 128 * l + 128] for i in range(count) for l in range(6)
        ]

    ends = []

    def spread(done, out, at):
        for copy in (
            pltpu.make_async_copy(done, out.at[core], loc.at[at]),
            remote(done, out.at[core], pair_sem.at[at, 0], pair_sem.at[at, 1], other),
        ):
            copy.start()
            ends.append(copy)

    def second(own, recv, panels, p, here):
        out = []
        for k in range(panels):
            total = own[p, k, chunk(here, 48), :].astype(F32)
            for o in range(3):
                total = total + recv[o, p, k].astype(F32)
            out.append(total)
        return out

    def finish(copies, own, recv, done, out, at, spots):
        for copy in copies:
            copy.wait()
        for p in range(3):
            total = own[p, spots[p]].astype(F32)
            for o in range(3):
                total = total + recv[o, p].astype(F32)
            done[p] = total
        spread(done, out, at)

    lax.fori_loop(0, 6, attend_back, 0, unroll=2)
    mp_copy.wait()
    item_s[2:6, :] = (mp_s[0:4, :] + mr_s[0:4, :]).astype(BF16).astype(F32)
    time_id = time_ref[zh]
    stamp = jnp.ones((1, 128), F32)
    rows = lane_rows(item_s[2:6, :], 4) + lane_rows(mod_ref[7:8, :], 1)
    rows += [stamp * (time_id // 32).astype(F32), stamp * (time_id % 32).astype(F32)]
    both = jnp.concatenate(rows, axis=0).astype(BF16)
    de_s[core, z_me, me["y"], me["x"]] = jnp.where(core == 0, both[0:16], both[16:32])
    se_copy.wait()
    se_s[0] = (se_p[core].astype(F32) + se_r[...].astype(F32)).astype(BF16)
    small = small_stage(0, se_s, de_s, 0)
    lax.fori_loop(6, 12, attend_back, 0, unroll=2)
    late = []
    for p in range(3):
        for at, to in (
            (512 * p, (0, p, 0)), (512 * p + 256, (0, p, 1)), (1536 + 256 * p, (1, p, 1))
        ):
            lg_s[to] = mm(
                hct_s[p], dqkv_s[:, :, :, :, at : at + 256].reshape(512, 256)
            ).astype(BF16)
        late.append(
            remote(
                lg_s.at[1 - core, p], prl_s.at[p], pair_sem.at[4 + p, 0], pair_sem.at[4 + p, 1],
                other,
            )
        )
        late[-1].start()
    loads[9].wait()
    for half in (1, 0):
        got = mm_nt(dqkv_s[half].reshape(256, 3 * D), w_s[...]).astype(BF16)
        dhc_s[half] = got.reshape(8, 2, 16, D)
        if half == 1:
            dhc_copy = remote(
                dhc_s.at[1], dh_s.at[pl.ds(0, 8), 1], pair_sem.at[3, 0], pair_sem.at[3, 1], other
            )
            dhc_copy.start()
    near = [
        pltpu.make_async_copy(dhc_s.at[0], dh_s.at[pl.ds(0, 8), 0], loc.at[7]),
        pltpu.make_async_copy(dhc_s.at[1, 7], dh_s.at[8, 0], loc.at[8]),
    ]
    for copy in near:
        copy.start()
    loads[10].wait()
    for copy in st1x:
        copy.wait()
    for p in range(3):
        here, _peer = early_peer(me, 0, p, 1)
        total = last_ref[p, here].astype(F32)
        for o in range(3):
            total = total + r1x[o, p].astype(F32)
        total = total.astype(BF16)

        @pl.when(core == 0)
        def _():
            s1_s[p, 3] = total

        @pl.when(core == 1)
        def _():
            for c in range(4):
                s1_s[p, c, 144:192] = total[48 * c : 48 * c + 48]

    st2e = stage_sends(1, lambda p, o, b: (s1_s.at[p, :, chunk(b, 48)], r2e.at[o - 1, p]), 0)
    small_take(0, se_s, de_s, 0, small, se_f)
    small = small_stage(1, se_s, de_s, 0)
    ones = jnp.ones((8, 512), BF16)
    for row, at in ((10, 0), (11, 2 * D)):
        sums = mm(ones, dqkv_s[:, :, :, :, at : at + D].reshape(512, D))
        sv_s[row : row + 1, :] = sums[0:1]
    sv_s[12:14, :] = sb_ref[4:6, :]
    sv_s[14:16, :] = jnp.zeros((2, D), F32)

    dhc_copy.wait()
    for copy in near:
        copy.wait()
    loads[11].wait()
    masks = side_masks()

    def lanes(j, _):
        cols = pl.ds(pl.multiple_of(j * 128, 128), 128)
        taps = tap_ref[:, cols].astype(F32)
        taps = [taps[t : t + 1] for t in range(9)]
        back = [by_core(taps, 8 - t, core) for t in range(9)]

        def sided_d(l):
            return with_sides(
                dh_s[l // 2, l % 2, 0, :, cols].astype(F32),
                dh_s[l // 2, l % 2, 1, :, cols].astype(F32),
                masks,
            )

        def sided_h(l):
            return with_sides(
                h_ref[32 * l : 32 * l + 16, cols].astype(F32),
                h_ref[32 * l + 16 : 32 * l + 32, cols].astype(F32),
                masks,
            )

        rows = [None, sided_d(0), sided_d(1)]
        rows_h = [None, sided_h(0), sided_h(1)]
        sums = [None] * 9
        bias_sum = None
        for l in range(16):
            ge, go = conv_row(rows, back)
            gh_s[32 * l : 32 * l + 16, cols] = ge
            gh_s[32 * l + 16 : 32 * l + 32, cols] = go
            de, do = rows[1][0], rows[1][1]
            tap_products(sums, rows_h, de, do)
            term = fold8(de + do)
            bias_sum = term if bias_sum is None else bias_sum + term
            if l < 15:
                rows = [rows[1], rows[2], sided_d(l + 2)]
                rows_h = [rows_h[1], rows_h[2], sided_h(l + 2)]
        for t in range(9):
            total = jnp.sum(by_core(sums, t, core), axis=0, keepdims=True)
            sv_s[t : t + 1, cols] = total
        sv_s[9:10, cols] = jnp.sum(bias_sum, axis=0, keepdims=True)
        return 0

    lax.fori_loop(0, D // 128, lanes, 0)
    st1l = []
    for p in range(3):
        late[p].wait()
        for k in range(2):
            lg_s[core, p, k] = lg_s[core, p, k] + prl_s[p, k]
        st1l += stage_sends(
            0, lambda p, o, a: (lg_s.at[core, p, :, chunk(a, 192)], r1l.at[o - 1, p]), 1, (p,)
        )
    for load in loads[12:14]:
        load.wait()
    scale1 = mod_ref[1:2, :]
    acc_s[...] = jnp.zeros_like(acc_s)

    def rows_n(r, _):
        at = pl.ds(pl.multiple_of(r * 128, 128), 128)
        n1, rs = norm_parts(x_ref[at, :].astype(F32))
        dh = gh_s[at, :]
        g1 = dh * (1.0 + scale1)
        got = dx_ref[at, :] + rs * (
            g1
            - jnp.mean(g1, axis=-1, keepdims=True)
            - n1 * jnp.mean(g1 * n1, axis=-1, keepdims=True)
        )
        ig_s[at, :] = got.astype(BF16)
        acc_s[0] += fold8(dh)
        acc_s[1] += fold8(dh * n1)
        return 0

    lax.fori_loop(0, 4, rows_n, 0)
    mpl_s[...] = jnp.zeros_like(mpl_s)
    for i in range(2):
        mpl_s[i : i + 1, :] = jnp.sum(acc_s[i], axis=0, keepdims=True)
    mpl_copy = remote(mpl_s, mrl_s, pair_sem.at[7, 0], pair_sem.at[7, 1], other)
    mpl_copy.start()
    for half in range(2):
        sl_p[half] = sv_s[:, 384 * half : 384 * half + 384].astype(BF16)
    sl_copy = remote(sl_p.at[1 - core], sl_r, pair_sem.at[8, 0], pair_sem.at[8, 1], other)
    sl_copy.start()
    for b in range(2):
        is_s[b] = mm(home, ig_s[256 * b : 256 * b + 256, :]).astype(BF16)
    mpl_copy.wait()
    item_s[0:2, :] = (mpl_s[0:2, :] + mrl_s[0:2, :]).astype(BF16).astype(F32)
    loads[14].wait()
    cond = mod_ref[6:7, :]
    d_silu = jnp.zeros((8, D), F32)
    for i in range(6):
        row = jnp.concatenate([item_s[i : i + 1, :]] * 8, axis=0).astype(BF16)
        d_silu = d_silu + mm_nt(row, mw_s[:, D * i : D * i + D])
    slope = 1.0 / (1.0 + jnp.exp(-cond))
    d_cond = (slope * (1.0 + cond * (1.0 - slope))) * d_silu[0:1]
    zeros = [jnp.zeros((1, 128), F32)]
    rows_0 = jnp.concatenate(lane_rows(item_s[0:2, :], 2) + zeros * 4, axis=0)
    rows_1 = jnp.concatenate(lane_rows(d_cond, 1) + zeros * 10, axis=0)
    dl_s[core, z_me, me["y"], me["x"]] = jnp.where(core == 0, rows_0, rows_1).astype(BF16)
    sl_copy.wait()
    sl_s[0] = (sl_p[core].astype(F32) + sl_r[...].astype(F32)).astype(BF16)
    small_l = small_stage(0, sl_s, dl_s, 1)

    small_take(1, se_s, de_s, 0, small, se_f)
    small = small_stage(2, se_s, de_s, 0)
    for copy in st2e:
        copy.wait()
    for p in range(3):
        got = second(s1_s, r2e, 4, p, early_peer(me, 1, p, 1)[0])

        @pl.when(core == 0)
        def _():
            for c in range(4):
                t3e[p, c] = jnp.concatenate(
                    [got[k][12 * c : 12 * c + 12] for k in range(4)], axis=0
                ).astype(BF16)

        @pl.when(core == 1)
        def _():
            for c in range(4):
                t3e[p, c] = got[c].astype(BF16)

    st3e = stage_sends(2, lambda p, o, c: (t3e.at[p, c], r3e.at[o - 1, p]), 0)

    small_take(0, sl_s, dl_s, 1, small_l, sl_f)
    small_l = small_stage(1, sl_s, dl_s, 1)
    spots = [[axis_spot(me, ORDERS[p][stage]) for p in range(3)] for stage in range(3)]
    st2l, st3l = [], []
    for p in range(3):
        for copy in st1l[3 * p : 3 * p + 3]:
            copy.wait()
        for k in range(2):
            total = lg_s[core, p, k, chunk(spots[0][p], 192), :].astype(F32)
            for o in range(3):
                total = total + r1l[o, p, k].astype(F32)
            s1l[p, k] = total.astype(BF16)
        st2l += stage_sends(
            1, lambda p, o, b: (s1l.at[p, :, chunk(b, 48)], r2l.at[o - 1, p]), 1, (p,)
        )
    give_back(1, lambda make, local: make().start())
    small_take(1, sl_s, dl_s, 1, small_l, sl_f)
    small_l = small_stage(2, sl_s, dl_s, 1)
    for p in range(3):
        for copy in st2l[3 * p : 3 * p + 3]:
            copy.wait()
        got = second(s1l, r2l, 2, p, spots[1][p])
        for c in range(4):
            t3l[p, c] = jnp.concatenate(
                [got[0][12 * c : 12 * c + 12], got[1][12 * c : 12 * c + 12], jnp.zeros((8, 256), F32)],
                axis=0,
            ).astype(BF16)
        st3l += stage_sends(2, lambda p, o, c: (t3l.at[p, c], r3l.at[o - 1, p]), 1, (p,))
    small_take(2, se_s, de_s, 0, small, se_f)
    spread(se_f, se_out, 10)
    ends.append(
        remote(de_s.at[core], de_s.at[core], pair_sem.at[11, 0], pair_sem.at[11, 1], other)
    )
    ends[-1].start()
    finish(st3e, t3e, r3e, fe_s, fe_out, 9, [early_peer(me, 2, p, 1)[0] for p in range(3)])
    small_take(2, sl_s, dl_s, 1, small_l, sl_f)
    spread(sl_f, sl_out, 13)
    ends.append(
        remote(dl_s.at[core], dl_s.at[core], pair_sem.at[14, 0], pair_sem.at[14, 1], other)
    )
    ends[-1].start()
    finish(st3l, t3l, r3l, fl_s, fl_out, 12, spots[2])
    for which in range(2):
        give_back(which, lambda make, local: None if local else make().wait_send())
        for item_slot in range(2):
            out = (oret_out, iret_out)[which]
            arrived(out.at[item_slot], ret_recv.at[which, item_slot])
    for copy in ends:
        copy.wait()
    last = [
        pltpu.make_async_copy(de_s, de_out, loc.at[11]),
        pltpu.make_async_copy(dl_s, dl_out, loc.at[14]),
    ]
    for copy in last:
        copy.start()
    for copy in last:
        copy.wait()


def back_call(
    da, qkv, p, hcg, h, x, dx, mod, times, w, mw, taps, perm, o, s1, last, dbr, at, s2, sb
):
    G = (2, 8, 2, 16)
    shape = jax.ShapeDtypeStruct
    V = pltpu.VMEM
    items = (2, 4, 4, 4, 16, 128)
    DMA = pltpu.SemaphoreType.DMA
    return pl.pallas_call(
        back_kernel,
        in_specs=[
            ANY_SPEC, ANY_SPEC, ANY_SPEC, ANY_SPEC, ANY_SPEC, ANY_SPEC, ANY_SPEC, VMEM_SPEC,
            SMEM_SPEC, ANY_SPEC, ANY_SPEC, VMEM_SPEC, ANY_SPEC, ANY_SPEC, ANY_SPEC, ANY_SPEC,
            ANY_SPEC, ANY_SPEC, VMEM_SPEC, VMEM_SPEC,
        ],
        out_specs=[ANY_SPEC] * 8,
        out_shape=[
            shape((2, 256, D), BF16), shape((2, 256, D), BF16),
            shape((2, 3, 48, 256), F32), shape((2, 3, 32, 256), F32),
            shape((2, 32, D), F32), shape((2, 16, 384), F32),
            shape(items, BF16), shape(items, BF16),
        ],
        scratch_shapes=[
            V(G + (3 * D,), BF16), V((24, 256, 256), BF16), V((D, 3 * D), BF16),
            V(mw.shape, BF16), V((3, D, D), BF16), V(G + (D,), BF16), V(G + (3 * D,), BF16),
            V((3, D, 512), BF16), V(G + (D,), BF16), V((9, 2, 2, 16, D), BF16), V((512, D), F32),
            V((512, D), BF16), V((2, 256, D), BF16), V((2, 256, D), BF16),
            V((2, 3, 2, D, 256), BF16), V((3, 2, D, 256), BF16), V((3, 4, 192, 256), BF16), V((3, 3, 192, 256), BF16),
            V((3, 3, 2, 192, 256), BF16),
            V((3, 2, 192, 256), BF16), V((3, 3, 4, 48, 256), BF16), V((3, 3, 2, 48, 256), BF16),
            V((3, 4, 48, 256), BF16), V((3, 4, 32, 256), BF16), V((3, 3, 48, 256), BF16),
            V((3, 3, 32, 256), BF16), V((3, 48, 256), F32), V((3, 32, 256), F32),
            V((2, 8, D), F32), V((16, D), F32),
            V((2, 32, D), BF16), V((32, D), BF16), V((12, 32, D), BF16), V((32, D), F32),
            V((2, 16, 384), BF16), V((16, 384), BF16), V((12, 16, 384), BF16), V((16, 384), F32),
            V((8, D), F32), V((8, D), F32), V((8, D), F32), V((8, D), F32), V((8, D), F32),
            V(items, BF16), V(items, BF16),
            V((512, D), BF16), V((576, D), BF16), V((576, D), BF16), V((512, D), F32),
            V((512, D), BF16), V((3, 4, 192, 256), BF16), V((512, D), BF16), V((576, D), BF16),
            DMA((30,)), DMA((15, 2)), DMA((2, 2)), DMA((2, 2)), DMA((2, 3, 3, 3)),
            DMA((2, 3, 3, 3)), DMA((2, 3, 3)), DMA((2, 3, 3)), DMA((2, 3, 3)), DMA((2, 3, 3)),
        ],
        compiler_params=pltpu.CompilerParams(
            collective_id=2, has_side_effects=True, vmem_limit_bytes=60 * 2**20
        ),
        name="back",
    )(da, qkv, p, hcg, h, x, dx, mod, times, w, mw, taps, perm, o, s1, last, dbr, at, s2, sb)


def share_kernel(
    out_ref, ig_ref, fe_hbm, fl_hbm, se_hbm, sl_hbm, de_hbm, dl_hbm,
    o_out, ig_out, cond_out, table_out, mw_out, mb_out, aw_out, ab_out, qkv_out, qb_out, vb_out,
    ow_out, ob_out, f1_out, f1b_out, fw_out, fb_out, f2_out, f2b_out,
    ig_s, o_s, igf_s, e_s, l_s, fe_ref, fl_ref, se_ref, sl_ref, de_ref, dl_ref, sem,
):
    me = spot()
    core = me["core"]
    shard = me["dp"] * 4 + me["seq"]
    ig_load = pltpu.make_async_copy(ig_ref, ig_s, sem.at[0])
    o_load = pltpu.make_async_copy(out_ref, o_s, sem.at[9])
    o_move = pltpu.make_async_copy(o_s, o_out, sem.at[1])
    loads = [
        pltpu.make_async_copy(*pair, sem.at[3 + at])
        for at, pair in enumerate((
            (fe_hbm, fe_ref), (fl_hbm, fl_ref), (se_hbm, se_ref), (sl_hbm, sl_ref),
            (de_hbm, de_ref), (dl_hbm, dl_ref),
        ))
    ]
    for load in loads:
        load.start()
    ig_load.start()
    o_load.start()
    o_load.wait()
    o_move.start()
    ig_load.wait()
    igf_s[...] = ig_s[...].astype(F32)
    ig_move = pltpu.make_async_copy(igf_s, ig_out, sem.at[2])
    ig_move.start()
    for load in loads:
        load.wait()
    e_s[...] = de_ref[...].reshape(2048, 128).astype(F32)
    l_s[...] = dl_ref[...].reshape(2048, 128).astype(F32)

    def six(v, at):
        return jnp.where(core == 0, v[at : at + 6], v[at + 6 : at + 12])

    for p in range(3):
        early0, early1 = fe_ref[0, p], fe_ref[1, p]
        for i in range(4):
            at = D * i + 256 * p
            f1_out[:, at : at + 256] = six(early0, 12 * i)
        f2_out[:, 256 * p : 256 * p + 256] = jnp.where(core == 0, early1[0:24], early1[24:48])
        late0, late1 = fl_ref[0, p], fl_ref[1, p]
        for k in range(2):
            at = 512 * p + 256 * k
            qkv_out[:, at : at + 256] = six(late0, 12 * k)
        at = 1536 + 256 * p
        qkv_out[:, at : at + 256] = six(late1, 12)
        ow_out[:, 256 * p : 256 * p + 256] = six(late1, 0)

    def columns(start, count=D):
        at = lax.broadcasted_iota(jnp.int32, (count, 128), 0)
        to = lax.broadcasted_iota(jnp.int32, (count, 128), 1)
        return at == start + to

    def exact(a, b):
        return lax.dot_general(
            a, b.astype(F32), (((1,), (0,)), ((), ())), preferred_element_type=F32,
            precision=lax.Precision.HIGHEST,
        )

    mine = columns(shard * 6)
    slim = exact(jnp.concatenate((sl_ref[0], sl_ref[1]), axis=1), mine)
    aw_out[...] = slim.T[0:6, 0:9]
    for ref, at in ((ab_out, 9), (qb_out, 10), (vb_out, 11), (ob_out, 12), (f2b_out, 13)):
        ref[...] = slim[at : at + 1, 0:6].reshape(6)
    quarter = shard // 32
    wide = se_ref[quarter // 2, pl.ds(pl.multiple_of(quarter % 2 * 16, 16), 16), :]
    wide = exact(wide, columns(shard % 32 * 24))
    fw_out[...] = wide[0:9, 0:24]
    fb_out[...] = wide[9:10, 0:24].reshape(24)
    f1b_out[...] = wide[10:11, 0:24].reshape(24)

    def item_rows(ref, at):
        return ref[pl.ds(at // 16 * 1024 + at % 16, 64, stride=16), :]

    silu = jnp.concatenate([item_rows(e_s, 24 + l) for l in range(6)], axis=1)
    silu = mm(silu.astype(BF16), mine.astype(BF16)).astype(BF16)
    sums = []
    for at in range(36):
        d_mod = item_rows(l_s, at) if at < 12 else item_rows(e_s, at - 12)
        mw_out[:, 128 * at : 128 * at + 128] = mm_tn(silu, d_mod.astype(BF16))[0:6]
        sums.append(jnp.sum(d_mod, axis=0, keepdims=True))
    total = jnp.concatenate(sums, axis=1)
    total = exact(jnp.concatenate([total] * 8, axis=0), columns(shard * 36, 6 * D))
    mb_out[...] = total[0:1, 0:36].reshape(36)

    cond = jnp.concatenate([item_rows(l_s, 16 + l) for l in range(6)], axis=1).astype(BF16)
    here = lax.broadcasted_iota(jnp.int32, (8, 64), 1)
    slot = lax.broadcasted_iota(jnp.int32, (8, 64), 0)
    own = here == ((slot * 2 + me["zl"]) * 4 + me["y"]) * 4 + me["x"]
    own = jnp.logical_and(own, slot < 2)
    cond_out[...] = mm(own.astype(BF16), cond)[0:2]
    times = 32.0 * item_rows(e_s, 30) + item_rows(e_s, 31)
    bucket = lax.broadcasted_iota(jnp.int32, (64, 1024), 1).astype(F32)
    hot = (bucket == jnp.concatenate([times] * 8, axis=1)).astype(BF16)
    my_cond = mm(cond, mine.astype(BF16)).astype(BF16)
    table_out[...] = mm_tn(my_cond, hot)[0:6, 0 : table_out.shape[1]]

    ig_move.wait()
    o_move.wait()


def share_call(buckets, *args):
    shapes = [
        ((2, 256, D), BF16), ((2, 256, D), F32), ((2, D), F32), ((6, buckets), F32),
        ((6, 6 * D), F32), ((36,), F32), ((6, 9), F32), ((6,), F32), ((6, 3 * D), F32),
        ((6,), F32), ((6,), F32), ((6, D), F32), ((6,), F32), ((6, FF), F32), ((24,), F32),
        ((9, 24), F32), ((24,), F32), ((24, D), F32), ((6,), F32),
    ]
    return pl.pallas_call(
        share_kernel,
        in_specs=[ANY_SPEC] * 8,
        out_specs=[ANY_SPEC] * 2 + [VMEM_SPEC] * 17,
        out_shape=[jax.ShapeDtypeStruct(*s) for s in shapes],
        scratch_shapes=[
            pltpu.VMEM((2, 256, D), BF16), pltpu.VMEM((2, 256, D), BF16),
            pltpu.VMEM((2, 256, D), F32), pltpu.VMEM((2048, 128), F32), pltpu.VMEM((2048, 128), F32),
            *[pltpu.VMEM(v.shape, v.dtype) for v in args[2:]],
            pltpu.SemaphoreType.DMA((10,)),
        ],
        compiler_params=pltpu.CompilerParams(vmem_limit_bytes=60 * 2**20),
        name="share",
    )(*args)


def perm_matrices():
    at = np.arange(D)
    rows = []
    for order in ORDERS:
        spots = dict(zip(order, (at // 192, at // 48 % 4, at // 12 % 4)))
        x, y, z = spots["x"], spots["y"], spots["z"]
        rows.append((((x * 2 + z % 2) * 4 + y) * 2 + z // 2) * 12 + at % 12)
    return np.stack(rows).astype(np.int32)


def local(
    latents, conditioning, timesteps, item_counts, cotangent, time_table, mod_weight, mod_bias,
    conv_attn_weight, conv_attn_bias, qkv_weight, query_bias, value_bias, out_weight, out_bias,
    fc1_weight, fc1_bias, conv_ffn_weight, conv_ffn_bias, fc2_weight, fc2_bias,
):
    alive = (lax.axis_index("seq") // 2 < item_counts).astype(F32)
    perm = (perm_matrices()[:, :, None] == np.arange(D)[None, None, :]).astype(BF16)
    x, ct, h, hcg, qkv, p, at, mod = attn_call(
        latents.reshape(2, 256, D), cotangent.reshape(2, 256, D), conditioning, timesteps,
        time_table, mod_weight, mod_bias, qkv_weight, query_bias, value_bias, conv_attn_weight,
        conv_attn_bias,
    )
    at = at.reshape(576, D)
    out, s1, last, dbr, da, dx, s2, sb = ffn_call(
        x, at, ct, mod, alive, perm, out_weight, out_bias, fc1_weight, fc1_bias, conv_ffn_weight,
        conv_ffn_bias, fc2_weight, fc2_bias,
    )
    got = back_call(
        da, qkv, p, hcg.reshape(512, D), h, x, dx, mod, timesteps,
        qkv_weight, mod_weight, conv_attn_weight, perm, out, s1, last,
        dbr.reshape(512, D), at, s2, sb,
    )
    outs = list(share_call(time_table.shape[0], *got))
    outs[0], outs[1] = outs[0].reshape(latents.shape), outs[1].reshape(latents.shape)
    outs[3], outs[6] = outs[3].T, outs[6].T
    return tuple(outs)


def solution(mesh):
    return jax.shard_map(
        local,
        mesh=mesh,
        in_specs=(
            P("dp", "seq", None, None),
            P("dp", None),
            P("dp"),
            P("dp"),
            P("dp", "seq", None, None),
            P(),
            P(),
            P(),
            P(),
            P(),
            P(),
            P(),
            P(),
            P(),
            P(),
            P(),
            P(),
            P(),
            P(),
            P(),
            P(),
        ),
        out_specs=(
            P("dp", "seq", None, None),
            P("dp", "seq", None, None),
            P("dp", None),
            P(None, ("dp", "seq")),
            P(("dp", "seq"), None),
            P(("dp", "seq")),
            P(None, ("dp", "seq")),
            P(("dp", "seq")),
            P(("dp", "seq"), None),
            P(("dp", "seq")),
            P(("dp", "seq")),
            P(("dp", "seq"), None),
            P(("dp", "seq")),
            P(("dp", "seq"), None),
            P(("dp", "seq")),
            P(None, ("dp", "seq")),
            P(("dp", "seq")),
            P(("dp", "seq"), None),
            P(("dp", "seq")),
        ),
        check_vma=False,
    )
```

```python
import functools

import jax
import jax.numpy as jnp
import numpy as np
from jax import lax
from jax.experimental import pallas as pl
from jax.experimental.pallas import tpu as pltpu
from jax.sharding import PartitionSpec as P

F32 = jnp.float32
BF16 = jnp.bfloat16
D = 768
FF = 3072
FC = 768
NFC = FF // FC
EPS = 1e-6


def mm(a, b):
    return lax.dot_general(a, b, (((1,), (0,)), ((), ())), preferred_element_type=F32)


def mm_nt(a, b):
    return lax.dot_general(a, b, (((1,), (1,)), ((), ())), preferred_element_type=F32)


def mm_tn(a, b):
    return lax.dot_general(a, b, (((0,), (0,)), ((), ())), preferred_element_type=F32)


def row(v):
    return v.astype(F32).reshape(1, v.shape[0])


def fold8(v):
    total = v[0:8]
    for at in range(8, v.shape[0], 8):
        total = total + v[at : at + 8]
    return total


def norm_parts(v):
    center = v - jnp.mean(v, axis=-1, keepdims=True)
    rs = lax.rsqrt(jnp.mean(center * center, axis=-1, keepdims=True) + EPS)
    return center * rs, rs


def by_core(taps, at, core):
    return jnp.where(core == 1, taps[3 * (2 - at // 3) + at % 3], taps[at])


def gelu_pair(v):
    z = jnp.abs(v) * 0.7071067811865476
    t = 1.0 / (1.0 + 0.3275911 * z)
    e = jnp.exp(-0.5 * (v * v))
    poly = t * (
        0.127414796
        + t * (-0.142248368 + t * (0.7107068705 + t * (-0.7265760135 + t * 0.5307027145)))
    )
    tail = poly * e
    cdf = jnp.where(v >= 0, 1.0 - tail, tail)
    return v * cdf, cdf + v * (e * 0.3989422804014327)


def side_masks():
    place = lax.broadcasted_iota(jnp.int32, (16, 128), 0)
    return place == 0, place == 15


def with_sides(even, odd, masks):
    left = jnp.where(masks[0], 0.0, pltpu.roll(odd, 1, 0))
    right = jnp.where(masks[1], 0.0, pltpu.roll(even, 15, 0))
    return even, odd, left, right


def conv_row(rows, taps):
    even = odd = None
    for a in range(3):
        if rows[a] is None:
            continue
        ev, od, left, right = rows[a]
        for tap, ce, co in ((3 * a, left, ev), (3 * a + 1, ev, od), (3 * a + 2, od, right)):
            even = taps[tap] * ce if even is None else even + taps[tap] * ce
            odd = taps[tap] * co if odd is None else odd + taps[tap] * co
    return even, odd


def tap_products(sums, rows, d_even, d_odd):
    for a in range(3):
        if rows[a] is None:
            continue
        ev, od, left, right = rows[a]
        for tap, ce, co in ((3 * a, left, ev), (3 * a + 1, ev, od), (3 * a + 2, od, right)):
            term = fold8(d_even * ce + d_odd * co)
            sums[tap] = term if sums[tap] is None else sums[tap] + term


MESH = pl.DeviceIdType.MESH


def spot():
    dp = lax.axis_index("dp")
    seq = lax.axis_index("seq")
    x, zl, y, zh, core = dp >> 3, (dp >> 2) & 1, dp & 3, seq >> 1, seq & 1
    z = zh * 2 + zl
    me = dict(dp=dp, seq=seq, x=x, zl=zl, y=y, zh=zh, z=z, core=core)
    for o in (1, 2, 3):
        me["x", o] = ((((x + o) & 3) << 3) + (dp & 7), seq)
        me["y", o] = ((dp & 28) + ((y + o) & 3), seq)
        to = (z + o) & 3
        me["z", o] = ((dp & 27) + ((to & 1) << 2), (to & 2) + core)
    return me


def seq_peer(me, zh, core):
    return (me["dp"], zh * 2 + core)


def axis_peer(me, axis, offset):
    return me[axis, offset]


def remote(src, dst, send, recv, device):
    return pltpu.make_async_remote_copy(
        src_ref=src, dst_ref=dst, send_sem=send, recv_sem=recv, device_id=device,
        device_id_type=MESH,
    )


def arrived(ref, sem):
    pltpu.make_async_copy(ref, ref, sem).wait()


def hail(peers):
    barrier = pltpu.get_barrier_semaphore()
    for peer in peers:
        pl.semaphore_signal(barrier, inc=1, device_id=peer, device_id_type=MESH)


def heard(count):
    pl.semaphore_wait(pltpu.get_barrier_semaphore(), count)


def greet(peers):
    hail(peers)
    heard(len(peers))


ORDERS = (("x", "y", "z"), ("y", "x", "z"), ("z", "x", "y"))
EARLY = (
    (("x", "y", "z"), ("x", "y", "z"), ("y", "x", "z")),
    (("y", "x", "z"), ("z", "x", "y"), ("z", "x", "y")),
)


LATE = (
    (((0, 1, 2), (3, 6, 7), (8, 9, "g0")), ((4,), (5,), (10,))),
    (((12, 13, 14), (15, "g1", "g2"), ("g3", "g4", "g5")), ((11,), (16,), (17,))),
)


def axis_spot(me, axis):
    return me[axis]


def early_peer(me, stage, part, offset):
    key = (stage, part, offset)
    if key not in me:
        first, second = (EARLY[which][part][stage] for which in range(2))
        if first == second:
            me[key] = me[first], me[first, offset]
        else:
            pick = lambda a, b: jnp.where(me["core"] == 0, a, b)
            peer = tuple(pick(a, b) for a, b in zip(me[first, offset], me[second, offset]))
            me[key] = pick(me[first], me[second]), peer
    return me[key]


def ffn_kernel(
    x_ref, at_ref, ct_ref, mod_ref, alive_ref, perm_ref, ow_ref, ob_ref, f1_ref, f1b_ref,
    tap_ref, cb_ref, f2_ref, f2b_ref,
    out_ref, s1_ref, last_ref, dbr_ref, da_ref, dx_ref, s2_ref, sm_ref,
    x1_s, br_s, h2_s, h2t_s, dffn_s, u_s, duc_s, act_s, du_s, dact_s, ffn_s, dh2_s, acc_s,
    ch_s, pre_s, r1_s, bias_s, das_s, dar_s, pair_sem, st_send, st_recv,
):
    step = pl.program_id(0)
    me = spot()
    core = me["core"]
    other = seq_peer(me, me["zh"], 1 - core)
    for p in range(3):
        for o in (1, 2, 3):
            early_peer(me, 0, p, o)
    alive = alive_ref[0]

    @pl.when(step == 0)
    def _():
        bias_s[0:1, :] = row(f1b_ref[...])
        bias_s[1:2, :] = row(cb_ref[...])
        hail([axis_peer(me, axis, o) for axis in "xyz" for o in (1, 2, 3)] + [other])

    def pair_copy(at):
        slot = at % 2
        return remote(
            ch_s.at[slot, 1 - core], pre_s.at[slot], pair_sem.at[slot, 0], pair_sem.at[slot, 1],
            other,
        )

    def first_copies(at):
        slot = at % 2
        out = []
        for p in range(3):
            for o in (1, 2, 3):
                here, peer = early_peer(me, 0, p, o)
                out.append(
                    remote(
                        ch_s.at[slot, core, p, (here + o) & 3], r1_s.at[at, o - 1, p],
                        st_send.at[at, p, o - 1], st_recv.at[at, p, o - 1], peer,
                    )
                )
        return out

    def pair_add(at):
        slot = at % 2
        pair_copy(at).wait()
        for p in range(3):

            def add(a, _):
                ch_s[slot, core, p, a] = ch_s[slot, core, p, a] + pre_s[slot, p, a]
                return 0

            lax.fori_loop(0, 4, add, 0)

    def first_send(at):
        pair_add(at)
        for copy in first_copies(at):
            copy.start()

    def first_take(at):
        slot = at % 2
        for copy in first_copies(at):
            copy.wait()
        for p in range(3):
            here, _peer = early_peer(me, 0, p, 1)
            total = ch_s[slot, core, p, here].astype(F32)
            for o in range(3):
                total = total + r1_s[at, o, p].astype(F32)
            total = total.astype(BF16)

            @pl.when(core == 0)
            def _():
                s1_ref[p, at] = total

            @pl.when(core == 1)
            def _():
                for c in range(4):
                    s1_ref[p, c, pl.ds(pl.multiple_of(at * 48, 16), 48)] = total[
                        48 * c : 48 * c + 48
                    ]

    @pl.when(step == 0)
    def _():
        br_s[...] = mm(at_ref[...], ow_ref[...]) + row(ob_ref[...])
        shift2, scale2, gate1, gate2 = (mod_ref[i : i + 1, :] for i in (3, 4, 2, 5))

        def rows_a(r, _):
            at = pl.ds(pl.multiple_of(r * 96, 96), 96)
            x1 = x_ref[at, :].astype(F32) + gate1 * br_s[at, :]
            x1_s[at, :] = x1
            n2, _unused = norm_parts(x1)
            h2_s[at, :] = (n2 * (1.0 + scale2) + shift2).astype(BF16)
            return 0

        lax.fori_loop(0, 6, rows_a, 0)

        def rows_b(r, _):
            at = pl.ds(pl.multiple_of(r * 272, 16), 272)
            dffn_s[at, :] = (ct_ref[at, :].astype(F32) * alive * gate2).astype(BF16)
            return 0

        lax.fori_loop(0, 2, rows_b, 0)
        for p in range(2):
            h2t_s[p] = mm_nt(perm_ref[p], h2_s[0:512, :]).astype(BF16)
        ffn_s[...] = jnp.zeros_like(ffn_s)
        dh2_s[...] = jnp.zeros_like(dh2_s)

    @pl.when(step == 0)
    def _():
        heard(10)

    masks = side_masks()

    def lanes(j):
        cols = slice(128 * j, 128 * j + 128)
        taps = tap_ref[:, cols].astype(F32)
        taps = [taps[t : t + 1] for t in range(9)]
        taps = [by_core(taps, t, core) for t in range(9)]
        offset = bias_s[1:2, pl.ds(pl.multiple_of(step * FC + j * 128, 128), 128)]

        def sided(ref, l):
            return with_sides(
                ref[32 * l : 32 * l + 16, cols].astype(F32),
                ref[32 * l + 16 : 32 * l + 32, cols].astype(F32),
                masks,
            )

        rows = [None, sided(u_s, 0), sided(u_s, 1)]
        sums = [None] * 9
        bias_sum = None
        for l in range(17):
            ce, co = conv_row(rows, taps)
            ae, ge = gelu_pair(ce + offset)
            ao, go = gelu_pair(co + offset)
            de = (ge * dact_s[32 * l : 32 * l + 16, cols]).astype(BF16)
            do = (go * dact_s[32 * l + 16 : 32 * l + 32, cols]).astype(BF16)
            duc_s[32 * l : 32 * l + 16, cols] = de
            duc_s[32 * l + 16 : 32 * l + 32, cols] = do
            if l < 16:
                act_s[32 * l : 32 * l + 16, cols] = ae.astype(BF16)
                act_s[32 * l + 16 : 32 * l + 32, cols] = ao.astype(BF16)
                de, do = de.astype(F32), do.astype(F32)
                tap_products(sums, rows, de, do)
                term = fold8(de + do)
                bias_sum = term if bias_sum is None else bias_sum + term
                rows = [rows[1], rows[2], sided(u_s, l + 2) if l + 2 < 18 else None]
        for t in range(9):
            s2_ref[t : t + 1, cols] = jnp.sum(by_core(sums, t, core), axis=0, keepdims=True)
        s2_ref[9:10, cols] = jnp.sum(bias_sum, axis=0, keepdims=True)
        back = [taps[8 - t] for t in range(9)]
        rows = [None, sided(duc_s, 0), sided(duc_s, 1)]
        bias_sum = None
        for l in range(16):
            ue, uo = conv_row(rows, back)
            ue, uo = ue.astype(BF16), uo.astype(BF16)
            du_s[32 * l : 32 * l + 16, cols] = ue
            du_s[32 * l + 16 : 32 * l + 32, cols] = uo
            term = fold8(ue.astype(F32) + uo.astype(F32))
            bias_sum = term if bias_sum is None else bias_sum + term
            rows = [rows[1], rows[2], sided(duc_s, l + 2) if l + 2 < 17 else None]
        s2_ref[10:11, cols] = jnp.sum(bias_sum, axis=0, keepdims=True)

    slot = step % 2

    def into(j):
        cols = slice(256 * j, 256 * j + 256)
        offset = bias_s[0:1, pl.ds(pl.multiple_of(step * FC + 256 * j, 256), 256)]
        u_s[:, cols] = (mm(h2_s[...], f1_ref[:, cols]) + offset).astype(BF16)
        dact_s[:, cols] = mm_nt(dffn_s[...], f2_ref[cols, :])

    def out_of(j):
        cols = slice(256 * j, 256 * j + 256)
        got = mm(h2t_s[j // 2], du_s[:, cols]).astype(BF16)
        ch_s[slot, 0, j] = got.reshape(4, 192, 256)
        grad = mm_tn(act_s[:, cols], dffn_s[0:512, :]).astype(BF16)
        for at in range(0, 256, 16):
            chip, inner = (256 * j + at) // 48, (256 * j + at) % 48
            zl, y, zh = chip // 8, chip // 2 % 4, chip % 2
            z = zh * 2 + zl
            for part in range(3):
                a, c = (y, z) if part == 0 else (z, y)
                ch_s[slot, 1, part, a, 48 * c + inner : 48 * c + inner + 16] = grad[
                    at : at + 16, 256 * part : 256 * part + 256
                ]
        ffn_s[...] += mm(act_s[:, cols], f2_ref[cols, :])
        dh2_s[...] += mm_nt(du_s[:, cols], f1_ref[:, cols])

    into(0)
    into(1)
    lanes(0)
    lanes(1)
    into(2)

    @pl.when(step > 1)
    def _():
        first_take(step - 2)

    out_of(0)

    @pl.when(step > 0)
    def _():
        first_send(step - 1)

    lanes(2)
    lanes(3)
    out_of(1)
    lanes(4)
    lanes(5)
    out_of(2)
    pair_copy(step).start()

    @pl.when(step == NFC - 1)
    def _():
        shift2, scale2, gate1, gate2 = (mod_ref[i : i + 1, :] for i in (3, 4, 2, 5))
        acc_s[...] = jnp.zeros_like(acc_s)
        f2b = row(f2b_ref[...])

        def rows_c(r, _):
            at = pl.ds(pl.multiple_of(r * 128, 128), 128)
            x1 = x1_s[at, :]
            ffn = ffn_s[at, :] + f2b
            dy = ct_ref[at, :].astype(F32) * alive
            out_ref[at, :] = (alive * (x1 + gate2 * ffn)).astype(BF16)
            n2, rs = norm_parts(x1)
            dh2 = dh2_s[at, :]
            g2 = dh2 * (1.0 + scale2)
            dx1 = dy + rs * (
                g2
                - jnp.mean(g2, axis=-1, keepdims=True)
                - n2 * jnp.mean(g2 * n2, axis=-1, keepdims=True)
            )
            dx_ref[at, :] = dx1
            dbr = (dx1 * gate1).astype(BF16)
            dbr_ref[pl.ds(2 * r, 2)] = dbr.reshape(2, 2, 2, 16, D)
            acc_s[0] += fold8(dx1 * br_s[at, :])
            acc_s[1] += fold8(dh2)
            acc_s[2] += fold8(dh2 * n2)
            acc_s[3] += fold8(dy * ffn)
            acc_s[4] += fold8(dbr.astype(F32))
            acc_s[5] += fold8(dffn_s[at, :].astype(F32))
            return 0

        lax.fori_loop(0, 4, rows_c, 0)
        for i in range(6):
            sm_ref[i : i + 1, :] = jnp.sum(acc_s[i], axis=0, keepdims=True)
        halves = [dbr_ref[:, parity].reshape(256, D) for parity in range(2)]
        odd = mm_nt(halves[1], ow_ref[...]).astype(BF16)
        das_s[...] = odd.reshape(8, 2, 16, D)
        da_copy = remote(das_s, dar_s, pair_sem.at[2, 0], pair_sem.at[2, 1], other)
        da_copy.start()
        da_ref[0] = mm_nt(halves[0], ow_ref[...]).astype(BF16).reshape(8, 2, 16, D)
        pair_add(step)
        last_ref[...] = ch_s[step % 2, core]
        first_take(step - 1)
        da_copy.wait()
        da_ref[1] = dar_s[...]


def ffn_call(x, at, ct, mod, alive, perm, ow, ob, f1, f1b, taps, cb, f2, f2b):
    whole = lambda s: pl.BlockSpec(s, lambda i: (0,) * len(s))
    return pl.pallas_call(
        ffn_kernel,
        grid=(NFC,),
        in_specs=[
            whole((576, D)), whole((576, D)), whole((576, D)), whole((8, D)),
            pl.BlockSpec(memory_space=pltpu.SMEM),
            whole((2, D, D)), whole((D, D)), whole((D,)),
            pl.BlockSpec((D, FC), lambda i: (0, i)),
            whole((FF,)),
            pl.BlockSpec((9, FC), lambda i: (0, i)),
            whole((FF,)),
            pl.BlockSpec((FC, D), lambda i: (i, 0)),
            whole((D,)),
        ],
        out_specs=[
            whole((512, D)),
            whole((3, 4, 192, 256)), whole((3, 4, 192, 256)),
            whole((8, 2, 2, 16, D)), whole((2, 8, 2, 16, D)), whole((512, D)),
            pl.BlockSpec((16, FC), lambda i: (0, i)),
            whole((8, D)),
        ],
        out_shape=[
            jax.ShapeDtypeStruct((512, D), BF16),
            jax.ShapeDtypeStruct((3, 4, 192, 256), BF16),
            jax.ShapeDtypeStruct((3, 4, 192, 256), BF16),
            jax.ShapeDtypeStruct((8, 2, 2, 16, D), BF16),
            jax.ShapeDtypeStruct((2, 8, 2, 16, D), BF16),
            jax.ShapeDtypeStruct((512, D), F32),
            jax.ShapeDtypeStruct((16, FF), F32),
            jax.ShapeDtypeStruct((8, D), F32),
        ],
        scratch_shapes=[
            pltpu.VMEM((576, D), F32), pltpu.VMEM((576, D), F32), pltpu.VMEM((576, D), BF16),
            pltpu.VMEM((2, D, 512), BF16), pltpu.VMEM((544, D), BF16),
            pltpu.VMEM((576, FC), BF16), pltpu.VMEM((544, FC), BF16), pltpu.VMEM((512, FC), BF16),
            pltpu.VMEM((512, FC), BF16), pltpu.VMEM((544, FC), F32),
            pltpu.VMEM((512, D), F32), pltpu.VMEM((512, D), F32), pltpu.VMEM((6, 8, D), F32),
            pltpu.VMEM((2, 2, 3, 4, 192, 256), BF16), pltpu.VMEM((2, 3, 4, 192, 256), BF16),
            pltpu.VMEM((3, 3, 3, 192, 256), BF16), pltpu.VMEM((8, FF), F32),
            pltpu.VMEM((8, 2, 16, D), BF16), pltpu.VMEM((8, 2, 16, D), BF16),
            pltpu.SemaphoreType.DMA((3, 2)),
            pltpu.SemaphoreType.DMA((3, 3, 3)), pltpu.SemaphoreType.DMA((3, 3, 3)),
        ],
        compiler_params=pltpu.CompilerParams(
            dimension_semantics=("arbitrary",), vmem_limit_bytes=60 * 2**20,
            collective_id=3, has_side_effects=True,
        ),
        name="ffn",
    )(x, at, ct, mod, alive, perm, ow, ob, f1, f1b, taps, cb, f2, f2b)


def place_matrix(count, flip, inverse):
    rows = count // 32
    out = lax.broadcasted_iota(jnp.int32, (count, count), 0)
    at = lax.broadcasted_iota(jnp.int32, (count, count), 1)
    row = out // 32
    row = jnp.where(flip, rows - 1 - row, row)
    low = out % 32
    if inverse:
        low = (low % 2) * 16 + low // 2
    else:
        low = (low % 16) * 2 + low // 16
    return jnp.where(at == row * 32 + low, 1.0, 0.0).astype(BF16)


def head_lanes(values, half):
    lane = lax.broadcasted_iota(jnp.int32, values.shape, 1)
    return jnp.where((lane // 64) == half, values, jnp.zeros_like(values))


def attn_kernel(
    lat_ref, ct_ref, cond_ref, time_ref, table_ref, mw_ref, mb_ref, w_ref, qb_ref, vb_ref,
    tap_ref, cb_ref,
    x_out, ct_out, h_out, hcg_out, qkv_out, p_out, at_out, mod_out,
    xr_s, xh_s, x_s, c_s, h_s, hcg_s, sb_s, w_s, qkv_s, p_s, ag_s, at_s, mod_s, table_s, mw_s, cb_s,
    send0, recv0, sem_pair, sem_loc,
):
    me = spot()
    zh, core, seq = me["zh"], me["core"], me["seq"]
    other = seq_peer(me, zh, 1 - core)
    w_load = pltpu.make_async_copy(w_ref, w_s, sem_loc.at[0])
    table_load = pltpu.make_async_copy(table_ref, table_s, sem_loc.at[10])
    mw_load = pltpu.make_async_copy(mw_ref, mw_s, sem_loc.at[11])
    for copy in (table_load, mw_load, w_load):
        copy.start()

    greet(
        [
            seq_peer(me, (zh + dz) % 2, (core + dc) % 2)
            for dz, dc in ((0, 1), (1, 0), (1, 1))
        ]
    )
    slot = jnp.where(zh == 0, core, 1 - core)
    inner = jnp.logical_or(seq == 1, seq == 2)
    halo_core = jnp.where(seq == 1, 1, 0)
    halo_at = pl.multiple_of(jnp.where(seq == 1, 192, 0), 64)

    def sends(arrays, act):
        for a in arrays:
            ref = (lat_ref, ct_ref)[a]
            for j in range(2):
                own = jnp.logical_and(zh == j, core == zh)
                main = (ref.at[j], xr_s.at[a, slot])
                halo = (ref.at[j, pl.ds(halo_at, 64)], xh_s.at[a])

                @pl.when(own)
                def _():
                    act(lambda: pltpu.make_async_copy(*main, recv0.at[a, slot]), True)

                @pl.when(jnp.logical_not(own))
                def _():
                    act(
                        lambda: remote(*main, send0.at[a, j, 0], recv0.at[a, slot], seq_peer(me, j, zh)),
                        False,
                    )

                @pl.when(jnp.logical_and(inner, zh == j))
                def _():
                    act(lambda: pltpu.make_async_copy(*halo, recv0.at[a, 2]), True)

                @pl.when(jnp.logical_and(inner, zh != j))
                def _():
                    act(
                        lambda: remote(
                            *halo, send0.at[a, j, 1], recv0.at[a, 2], seq_peer(me, j, halo_core)
                        ),
                        False,
                    )

    sends((0,), lambda make, local: make().start())

    flip = core == 1
    big = place_matrix(256, flip, False)
    small = place_matrix(64, flip, False)

    table_load.wait()
    here = lax.broadcasted_iota(jnp.int32, (8, table_s.shape[0]), 1)
    one_hot = jnp.where(here == time_ref[zh], 1.0, 0.0).astype(BF16)
    cond = jnp.where(zh == 0, cond_ref[0:1, :], cond_ref[1:2, :]) + mm(one_hot, table_s[...])
    silu = (cond / (1.0 + jnp.exp(-cond))).astype(BF16)
    mw_load.wait()
    for i in range(6):
        cols = slice(D * i, D * i + D)
        mod_s[i : i + 1, :] = (mm(silu, mw_s[:, cols]) + row(mb_ref[cols]))[0:1]
    mod_s[6:7, :] = cond[0:1]
    mod_s[7:8, :] = silu[0:1].astype(F32)
    shift1, scale1 = mod_s[0:1, :], mod_s[1:2, :]

    def placed(a, into):
        for b in range(2):
            arrived(xr_s.at[a, b], recv0.at[a, b])
            into[256 * b : 256 * b + 256, :] = mm(big, xr_s[a, b]).astype(BF16)
        arrived(xh_s.at[a], recv0.at[a, 2])
        into[512:576, :] = mm(small, xh_s[a]).astype(BF16)

    placed(0, x_s)
    sends((1,), lambda make, local: make().start())

    def rows_a(r, _):
        at = pl.ds(pl.multiple_of(r * 96, 96), 96)
        n1, _unused = norm_parts(x_s[at, :].astype(F32))
        h_s[at, :] = (n1 * (1.0 + scale1) + shift1).astype(BF16)
        return 0

    lax.fori_loop(0, 6, rows_a, 0)
    outs = [
        pltpu.make_async_copy(x_s, x_out, sem_loc.at[1]),
        pltpu.make_async_copy(h_s, h_out, sem_loc.at[2]),
        pltpu.make_async_copy(mod_s, mod_out, sem_loc.at[12]),
    ]
    for copy in outs:
        copy.start()
    masks = side_masks()

    def lanes(j, _):
        cols = pl.ds(pl.multiple_of(j * 128, 128), 128)
        taps = tap_ref[:, cols].astype(F32)
        taps = [taps[t : t + 1] for t in range(9)]
        taps = [by_core(taps, t, core) for t in range(9)]
        offset = cb_s[0:1, cols]

        def sided(l):
            return with_sides(
                h_s[32 * l : 32 * l + 16, cols].astype(F32),
                h_s[32 * l + 16 : 32 * l + 32, cols].astype(F32),
                masks,
            )

        rows = [None, sided(0), sided(1)]
        for l in range(16):
            ce, co = conv_row(rows, taps)
            ce, co = (ce + offset).astype(BF16), (co + offset).astype(BF16)
            if l % 2 == 0:
                hcg_s[0, l // 2, 0, :, cols] = ce
                hcg_s[0, l // 2, 1, :, cols] = co
            else:
                sb_s[l // 2, 0, :, cols] = ce
                sb_s[l // 2, 1, :, cols] = co
            rows = [rows[1], rows[2], sided(l + 2) if l < 15 else None]
        return 0

    cb_s[0:1, :] = row(cb_ref[...])
    lax.fori_loop(0, D // 128, lanes, 0)
    hc_copy = remote(sb_s, hcg_s.at[1], sem_pair.at[0], sem_pair.at[1], other)
    hc_copy.start()
    w_load.wait()

    def project(half):
        for i, bias in enumerate((qb_ref, None, vb_ref)):
            cols = slice(D * i, D * i + D)
            got = mm(hcg_s[half].reshape(256, D), w_s[:, cols])
            if bias is not None:
                got = got + row(bias[...])
            qkv_s[half, :, :, :, cols] = got.astype(BF16).reshape(8, 2, 16, D)

    project(0)
    hc_copy.wait()
    outs.append(pltpu.make_async_copy(hcg_s, hcg_out, sem_loc.at[3]))
    outs[-1].start()
    project(1)
    outs.append(pltpu.make_async_copy(qkv_s, qkv_out, sem_loc.at[4]))
    outs[-1].start()

    def attend(pair, _):
        heads = [(pc, half) for pc in range(2) for half in range(2)]

        def part(which, pc):
            cols = pl.ds(pl.multiple_of(which * D + pair * 128, 128), 128)
            return jnp.concatenate(
                [qkv_s[half, :, pc, :, cols].reshape(128, 128) for half in range(2)], axis=0
            )

        q, k, v = ([part(which, pc) for pc in range(2)] for which in range(3))
        scores = [mm_nt(k[pc], head_lanes(q[pc], half)) * 0.125 for pc, half in heads]
        v_t = [v[pc].T for pc in range(2)]
        top = [jnp.max(n, axis=0, keepdims=True) for n in scores]
        e = [jnp.exp(n - m) for n, m in zip(scores, top)]
        scale = [1.0 / jnp.sum(n, axis=0, keepdims=True) for n in e]
        low = [(n * m).astype(BF16) for n, m in zip(e, scale)]
        for (pc, half), n in zip(heads, low):
            p_s[2 * (6 * pc + pair) + half] = n
        got = [mm(v_t[pc][64 * half : 64 * half + 64], n) for (pc, half), n in zip(heads, low)]
        cols = pl.ds(pl.multiple_of(pair * 128, 128), 128)
        for pc in range(2):
            o = jnp.concatenate(got[2 * pc : 2 * pc + 2], axis=0).T.astype(BF16)
            for half in range(2):
                ag_s[half, :, pc, :, cols] = o[128 * half : 128 * half + 128].reshape(8, 16, 128)
        return 0

    lax.fori_loop(0, 6, attend, 0)
    back = [
        remote(ag_s.at[1], at_s.at[pl.ds(0, 8), 1], sem_pair.at[2], sem_pair.at[3], other),
        remote(ag_s.at[0, 7], at_s.at[8, 1], sem_pair.at[4], sem_pair.at[5], other),
        pltpu.make_async_copy(ag_s.at[0], at_s.at[pl.ds(0, 8), 0], sem_loc.at[5]),
        pltpu.make_async_copy(ag_s.at[1, 7], at_s.at[8, 0], sem_loc.at[6]),
    ]
    for copy in back:
        copy.start()
    outs.append(pltpu.make_async_copy(p_s, p_out, sem_loc.at[7]))
    outs[-1].start()
    placed(1, c_s)
    outs.append(pltpu.make_async_copy(c_s, ct_out, sem_loc.at[8]))
    outs[-1].start()
    for copy in back:
        copy.wait()
    outs.append(pltpu.make_async_copy(at_s, at_out, sem_loc.at[9]))
    outs[-1].start()
    for copy in outs:
        copy.wait()

    def finish(make, local):
        if not local:
            make().wait_send()

    sends((0, 1), finish)


VMEM_SPEC = pl.BlockSpec(memory_space=pltpu.VMEM)
ANY_SPEC = pl.BlockSpec(memory_space=pl.ANY)
SMEM_SPEC = pl.BlockSpec(memory_space=pltpu.SMEM)


def attn_call(lat, ct, cond, times, table, mw, mb, w, qb, vb, taps, cb):
    G = (2, 8, 2, 16)
    shape = jax.ShapeDtypeStruct
    return pl.pallas_call(
        attn_kernel,
        in_specs=[
            ANY_SPEC, ANY_SPEC, VMEM_SPEC, SMEM_SPEC, ANY_SPEC, ANY_SPEC, VMEM_SPEC, ANY_SPEC,
            VMEM_SPEC, VMEM_SPEC, VMEM_SPEC, VMEM_SPEC,
        ],
        out_specs=[ANY_SPEC] * 8,
        out_shape=[
            shape((576, D), BF16), shape((576, D), BF16), shape((576, D), BF16),
            shape(G + (D,), BF16), shape(G + (3 * D,), BF16), shape((24, 256, 256), BF16),
            shape((9, 2, 2, 16, D), BF16), shape((8, D), F32),
        ],
        scratch_shapes=[
            pltpu.VMEM((2, 2, 256, D), BF16), pltpu.VMEM((2, 64, D), BF16),
            pltpu.VMEM((576, D), BF16), pltpu.VMEM((576, D), BF16), pltpu.VMEM((576, D), BF16),
            pltpu.VMEM(G + (D,), BF16), pltpu.VMEM((8, 2, 16, D), BF16),
            pltpu.VMEM((D, 3 * D), BF16), pltpu.VMEM(G + (3 * D,), BF16),
            pltpu.VMEM((24, 256, 256), BF16), pltpu.VMEM(G + (D,), BF16),
            pltpu.VMEM((9, 2, 2, 16, D), BF16),
            pltpu.VMEM((8, D), F32), pltpu.VMEM(table.shape, BF16), pltpu.VMEM(mw.shape, BF16),
            pltpu.VMEM((8, D), F32),
            pltpu.SemaphoreType.DMA((2, 2, 2)), pltpu.SemaphoreType.DMA((2, 3)),
            pltpu.SemaphoreType.DMA((6,)), pltpu.SemaphoreType.DMA((13,)),
        ],
        compiler_params=pltpu.CompilerParams(
            collective_id=1, has_side_effects=True, vmem_limit_bytes=56 * 2**20
        ),
        name="attend",
    )(lat, ct, cond, times, table, mw, mb, w, qb, vb, taps, cb)


def back_kernel(
    da_ref, qkv_ref, p_ref, hcg_hbm, h_hbm, x_hbm, dx_hbm, mod_ref, time_ref, w_ref, mw_ref,
    tap_ref, perm_ref, o_hbm, s1_ref, last_hbm, dbr_hbm, at_hbm, s2_ref, sb_ref,
    oret_out, iret_out, fe_out, fl_out, se_out, sl_out, de_out, dl_out,
    qkv_s, p_s, w_s, mw_s, perm_s, dag_s, dqkv_s, hct_s, dhc_s, dh_s, gh_s, ig_s, os_s, is_s,
    lg_s, prl_s, s1_s, r1x, r1l, s1l, r2e, r2l, t3e, t3a, t3b, r3e, r3a, r3b, fe_s, fl_s,
    acc_s, sv_s, se_p, se_r, se_s, se_f, sl_p, sl_r, sl_s, sl_f, mp_s, mr_s, mpl_s, mrl_s,
    item_s, de_s, dl_s, hcg_ref, h_ref, x_ref, dx_ref, o_ref, last_ref, dbr_ref, at_ref,
    loc, pair_sem, ret_send, ret_recv, st_send, st_recv, sm_send, sm_recv, dm_send, dm_recv,
):
    me = spot()
    zh, core = me["zh"], me["core"]
    other = seq_peer(me, zh, 1 - core)
    loads = [
        pltpu.make_async_copy(*pair, loc.at[20 + at])
        for at, pair in enumerate((
            (da_ref, dag_s), (qkv_ref, qkv_s), (perm_ref, perm_s), (hcg_hbm, hcg_ref),
            (at_hbm, at_ref), (dbr_hbm, dbr_ref), (p_ref, p_s), (last_hbm, last_ref),
            (o_hbm, o_ref), (w_ref, w_s), (s1_ref, s1_s), (h_hbm, h_ref), (x_hbm, x_ref),
            (dx_hbm, dx_ref), (mw_ref, mw_s),
        ))
    ]
    for load in loads:
        load.start()
    peers = [axis_peer(me, axis, o) for axis in "xyz" for o in (1, 2, 3)]
    peers += [other, seq_peer(me, 1 - zh, 1 - core)]
    hail(peers)

    def stage_sends(stage, bufs, kind, parts=(0, 1, 2)):
        out = []
        for p in parts:
            for o in (1, 2, 3):
                if kind:
                    axis = ORDERS[p][stage]
                    here, peer = axis_spot(me, axis), axis_peer(me, axis, o)
                else:
                    here, peer = early_peer(me, stage, p, o)
                src, dst = bufs(p, o, (here + o) & 3)
                copy = remote(
                    src, dst, st_send.at[kind, stage, p, o - 1], st_recv.at[kind, stage, p, o - 1],
                    peer,
                )
                copy.start()
                out.append(copy)
        return out

    def chunk(there, rows):
        return pl.ds(pl.multiple_of(there * rows, 16), rows)

    home = place_matrix(256, core == 1, True)

    def give_back(which, act):
        ref, out = ((os_s, oret_out), (is_s, iret_out))[which]
        for b in range(2):
            to_core = jnp.where(core == 0, b, 1 - b)
            own = jnp.logical_and(zh == core, b == 0)

            @pl.when(own)
            def _():
                act(lambda: pltpu.make_async_copy(ref.at[b], out.at[zh], ret_recv.at[which, zh]), True)

            @pl.when(jnp.logical_not(own))
            def _():
                act(
                    lambda: remote(
                        ref.at[b], out.at[zh], ret_send.at[which, b], ret_recv.at[which, zh],
                        seq_peer(me, core, to_core),
                    ),
                    False,
                )

    def pairs(pair, _):
        heads = [(pc, half) for pc in range(2) for half in range(2)]
        lanes_at = [
            pl.ds(pl.multiple_of(which * D + pair * 128, 128), 128) for which in range(3)
        ]

        def part(ref, cols, pc):
            return jnp.concatenate(
                [ref[half, :, pc, :, cols].reshape(128, 128) for half in range(2)], axis=0
            )

        q, k, v = ([part(qkv_s, cols, pc) for pc in range(2)] for cols in lanes_at)
        do = [part(dag_s, lanes_at[0], pc) for pc in range(2)]
        dom = [head_lanes(do[pc], half) for pc, half in heads]
        dp = [mm_nt(v[pc], n) for (pc, _), n in zip(heads, dom)]
        low = [p_s[2 * (6 * pc + pair) + half] for pc, half in heads]
        dv = [mm(n, m) for n, m in zip(low, dom)]
        k_t = [k[pc].T for pc in range(2)]
        qm = [head_lanes(q[pc], half) for pc, half in heads]
        probs = [n.astype(F32) for n in low]
        sums = [jnp.sum(n * m, axis=0, keepdims=True) for n, m in zip(probs, dp)]
        ds = [(n * (m - t)).astype(BF16) for n, m, t in zip(probs, dp, sums)]
        dk = [mm(n, m) for n, m in zip(ds, qm)]
        dq = [mm(k_t[pc][64 * half : 64 * half + 64], n) for (pc, half), n in zip(heads, ds)]
        for pc in range(2):
            at = 2 * pc
            turned = jnp.concatenate(dq[at : at + 2], axis=0).T
            grads = (0.125 * turned, 0.125 * (dk[at] + dk[at + 1]), dv[at] + dv[at + 1])
            for cols, got in zip(lanes_at, grads):
                got = got.astype(BF16)
                for half in range(2):
                    dqkv_s[half, :, pc, :, cols] = got[128 * half : 128 * half + 128].reshape(
                        8, 16, 128
                    )
        return 0

    def out_grads():
        for p, places in (
            (1, ((1, 1, 1), (1, 2, 2))), (2, ((0, 2, 0), (1, 0, 3), (1, 1, 4), (1, 2, 5)))
        ):
            at_t = mm_nt(perm_s[p], at_ref[0:512, :]).astype(BF16)
            cols = jnp.concatenate(
                [dbr_ref[:, 128 * g : 128 * g + 128] for _, _, g in places], axis=1
            )
            got = mm(at_t, cols).astype(BF16)
            for n, (which, u, _) in enumerate(places):
                lg_s[which, p, u] = got[:, 128 * n : 128 * n + 128]

    def late_grads(group):
        copies = []
        for p in range(3):
            for which in range(2):
                blocks = LATE[which][group][p]
                made = [n for n in blocks if not isinstance(n, str)]
                if not made:
                    continue
                cols = jnp.concatenate(
                    [
                        dqkv_s[:, :, :, :, 128 * n : 128 * n + 128].reshape(512, 128)
                        for n in made
                    ],
                    axis=1,
                )
                got = mm(hct_s[p], cols).astype(BF16)
                for n, block in enumerate(made):
                    u = 3 if group else blocks.index(block)
                    lg_s[which, p, u] = got[:, 128 * n : 128 * n + 128]
            part = late_part(group)
            sem = 4 + p if group == 0 else (9, 12, 15)[p]
            copies.append(
                remote(
                    lg_s.at[(1 - core, p) + part], prl_s.at[(p,) + part], pair_sem.at[sem, 0],
                    pair_sem.at[sem, 1], other,
                )
            )
            copies[-1].start()
        return copies

    def late_part(group):
        return (3,) if group else (pl.ds(0, 3),)

    def late_first(group, copies):
        out = []
        part = late_part(group)
        for p in range(3):
            copies[p].wait()
            for u in (3,) if group else (0, 1, 2):
                lg_s[core, p, u] = lg_s[core, p, u] + prl_s[p, u]
            out += stage_sends(
                0,
                lambda p, o, a: (
                    lg_s.at[(core, p) + part + (chunk(a, 192),)], r1l.at[(o - 1, p) + part]
                ),
                1 + group, (p,),
            )
        return out

    def late_second(group, copies):
        out = []
        part = late_part(group)
        for p in range(3):
            for copy in copies[3 * p : 3 * p + 3]:
                copy.wait()
            for u in (3,) if group else (0, 1, 2):
                total = lg_s[core, p, u, chunk(spots[0][p], 192), :].astype(F32)
                for o in range(3):
                    total = total + r1l[o, p, u].astype(F32)
                s1l[p, u] = total.astype(BF16)
            out += stage_sends(
                1,
                lambda p, o, b: (
                    s1l.at[(p,) + part + (chunk(b, 48),)], r2l.at[(o - 1, p) + part]
                ),
                1 + group, (p,),
            )
        return out

    def late_third(group, copies):
        out = []
        t3l, r3l = (t3b, r3b) if group else (t3a, r3a)
        for p in range(3):
            for copy in copies[3 * p : 3 * p + 3]:
                copy.wait()
            got = second(s1l, r2l, (3,) if group else (0, 1, 2), p, spots[1][p])
            pad = jnp.zeros((4 if group else 12, 128), F32)
            for c in range(4):
                t3l[p, c] = jnp.concatenate(
                    [v[12 * c : 12 * c + 12] for v in got] + [pad], axis=0
                ).astype(BF16)
            out += stage_sends(
                2, lambda p, o, c: (t3l.at[p, c], r3l.at[o - 1, p]), 1 + group, (p,)
            )
        return out

    def late_total(group, copies):
        t3l, r3l = (t3b, r3b) if group else (t3a, r3a)
        rows = slice(48, 64) if group else slice(0, 48)
        for copy in copies:
            copy.wait()
        for p in range(3):
            total = t3l[p, spots[2][p]].astype(F32)
            for o in range(3):
                total = total + r3l[o, p].astype(F32)
            fl_s[p, rows, :] = total

    spots = [[axis_spot(me, ORDERS[p][stage]) for p in range(3)] for stage in range(3)]
    z_me = axis_spot(me, "z")

    def small_stage(stage, sums, items, kind):
        axis = "zxy"[stage]
        if stage == 0:
            ref = items.at[core, me["y"], me["x"], z_me]
        elif stage == 1:
            ref = items.at[core, me["y"], me["x"]]
        else:
            ref = items.at[core, me["y"]]
        out = []
        for o in (1, 2, 3):
            peer = axis_peer(me, axis, o)
            at = (kind, stage, o - 1)
            out.append(
                remote(sums.at[4 * stage], sums.at[4 * stage + o], sm_send.at[at], sm_recv.at[at], peer)
            )
            out.append(remote(ref, ref, dm_send.at[at], dm_recv.at[at], peer))
        for copy in out:
            copy.start()
        return out

    def small_take(stage, sums, items, kind, copies, last):
        axis = "zxy"[stage]
        for copy in copies:
            copy.wait_send()
        for o in (1, 2, 3):
            at = (kind, stage, o - 1)
            arrived(sums.at[4 * stage + o], sm_recv.at[at])
            there = (axis_spot(me, axis) + 4 - o) & 3
            if stage == 0:
                ref = items.at[core, me["y"], me["x"], there]
            elif stage == 1:
                ref = items.at[core, me["y"], there]
            else:
                ref = items.at[core, there]
            arrived(ref, dm_recv.at[at])
        total = sums[4 * stage].astype(F32)
        for o in (1, 2, 3):
            total = total + sums[4 * stage + o].astype(F32)
        if stage < 2:
            sums[4 * stage + 4] = total.astype(BF16)
        else:
            last[...] = total

    def lane_rows(values, count):
        return [
            values[i : i + 1, 128 * l : 128 * l + 128] for i in range(count) for l in range(6)
        ]

    ends = []

    def spread(done, out, at):
        for copy in (
            pltpu.make_async_copy(done, out.at[core], loc.at[at]),
            remote(done, out.at[core], pair_sem.at[at, 0], pair_sem.at[at, 1], other),
        ):
            copy.start()
            ends.append(copy)

    def second(own, recv, panels, p, here):
        out = []
        for k in panels:
            total = own[p, k, chunk(here, 48), :].astype(F32)
            for o in range(3):
                total = total + recv[o, p, k].astype(F32)
            out.append(total)
        return out

    def finish(copies, own, recv, done, out, at, places):
        for copy in copies:
            copy.wait()
        for p in range(3):
            total = own[p, places[p]].astype(F32)
            for o in range(3):
                total = total + recv[o, p].astype(F32)
            done[p] = total
        spread(done, out, at)

    def pairs_turn(i, _):
        hct_s[i] = mm_nt(perm_s[i], hcg_ref[...]).astype(BF16)
        return pairs(i, 0)

    for load in loads[:7]:
        load.wait()
    lax.fori_loop(0, 1, pairs_turn, 0)
    heard(len(peers))
    loads[7].wait()
    st1x = stage_sends(0, lambda p, o, a: (last_ref.at[p, a], r1x.at[o - 1, p]), 0)
    mp_s[...] = sb_ref[...]
    mp_copy = remote(mp_s, mr_s, pair_sem.at[1, 0], pair_sem.at[1, 1], other)
    mp_copy.start()
    for half in range(2):
        for q in range(2):
            at = D * (2 * half + q)
            se_p[half, 16 * q : 16 * q + 16, :] = s2_ref[:, at : at + D].astype(BF16)
    se_copy = remote(se_p.at[1 - core], se_r, pair_sem.at[2, 0], pair_sem.at[2, 1], other)
    se_copy.start()

    loads[8].wait()
    for b in range(2):
        os_s[b] = mm(home, o_ref[256 * b : 256 * b + 256, :]).astype(BF16)
    give_back(0, lambda make, local: make().start())
    lax.fori_loop(1, 3, pairs_turn, 0)
    out_grads()
    pairs(3, 0)
    late_a = late_grads(0)
    mp_copy.wait()
    item_s[2:6, :] = (mp_s[0:4, :] + mr_s[0:4, :]).astype(BF16).astype(F32)
    time_id = time_ref[zh]
    stamp = jnp.ones((1, 128), F32)
    rows = lane_rows(item_s[2:6, :], 4) + lane_rows(mod_ref[7:8, :], 1)
    rows += [stamp * (time_id // 32).astype(F32), stamp * (time_id % 32).astype(F32)]
    both = jnp.concatenate(rows, axis=0).astype(BF16)
    de_s[core, me["y"], me["x"], z_me] = jnp.where(core == 0, both[0:16], both[16:32])
    se_copy.wait()
    se_s[0] = (se_p[core].astype(F32) + se_r[...].astype(F32)).astype(BF16)
    small = small_stage(0, se_s, de_s, 0)
    lax.fori_loop(4, 6, pairs, 0)
    late_b = late_grads(1)
    loads[9].wait()
    for half in (1, 0):
        got = mm_nt(dqkv_s[half].reshape(256, 3 * D), w_s[...]).astype(BF16)
        dhc_s[half] = got.reshape(8, 2, 16, D)
        if half == 1:
            dhc_copy = remote(
                dhc_s.at[1], dh_s.at[pl.ds(0, 8), 1], pair_sem.at[3, 0], pair_sem.at[3, 1], other
            )
            dhc_copy.start()
    near = [
        pltpu.make_async_copy(dhc_s.at[0], dh_s.at[pl.ds(0, 8), 0], loc.at[7]),
        pltpu.make_async_copy(dhc_s.at[1, 7], dh_s.at[8, 0], loc.at[8]),
    ]
    for copy in near:
        copy.start()
    st1a = late_first(0, late_a)
    st1b = late_first(1, late_b)
    loads[14].wait()
    d_silu = jnp.zeros((8, D), F32)

    def silu_part(i):
        row = jnp.concatenate([item_s[i : i + 1, :]] * 8, axis=0).astype(BF16)
        return mm_nt(row, mw_s[:, D * i : D * i + D])

    for i in range(2, 6):
        d_silu = d_silu + silu_part(i)
    ones = jnp.ones((8, 512), BF16)
    for row, at in ((10, 0), (11, 2 * D)):
        sums = mm(ones, dqkv_s[:, :, :, :, at : at + D].reshape(512, D))
        sv_s[row : row + 1, :] = sums[0:1]
    sv_s[12:14, :] = sb_ref[4:6, :]
    sv_s[14:16, :] = jnp.zeros((2, D), F32)

    dhc_copy.wait()
    for copy in near:
        copy.wait()
    loads[11].wait()
    masks = side_masks()

    def lanes(j, _):
        cols = pl.ds(pl.multiple_of(j * 128, 128), 128)
        taps = tap_ref[:, cols].astype(F32)
        taps = [taps[t : t + 1] for t in range(9)]
        back = [by_core(taps, 8 - t, core) for t in range(9)]

        def sided_d(l):
            return with_sides(
                dh_s[l // 2, l % 2, 0, :, cols].astype(F32),
                dh_s[l // 2, l % 2, 1, :, cols].astype(F32),
                masks,
            )

        def sided_h(l):
            return with_sides(
                h_ref[32 * l : 32 * l + 16, cols].astype(F32),
                h_ref[32 * l + 16 : 32 * l + 32, cols].astype(F32),
                masks,
            )

        rows = [None, sided_d(0), sided_d(1)]
        rows_h = [None, sided_h(0), sided_h(1)]
        sums = [None] * 9
        bias_sum = None
        for l in range(16):
            ge, go = conv_row(rows, back)
            gh_s[32 * l : 32 * l + 16, cols] = ge
            gh_s[32 * l + 16 : 32 * l + 32, cols] = go
            de, do = rows[1][0], rows[1][1]
            tap_products(sums, rows_h, de, do)
            term = fold8(de + do)
            bias_sum = term if bias_sum is None else bias_sum + term
            if l < 15:
                rows = [rows[1], rows[2], sided_d(l + 2)]
                rows_h = [rows_h[1], rows_h[2], sided_h(l + 2)]
        for t in range(9):
            total = jnp.sum(by_core(sums, t, core), axis=0, keepdims=True)
            sv_s[t : t + 1, cols] = total
        sv_s[9:10, cols] = jnp.sum(bias_sum, axis=0, keepdims=True)
        return 0

    lax.fori_loop(0, D // 128, lanes, 0)
    small_take(0, se_s, de_s, 0, small, se_f)
    small = small_stage(1, se_s, de_s, 0)
    for load in loads[12:14]:
        load.wait()
    scale1 = mod_ref[1:2, :]
    acc_s[...] = jnp.zeros_like(acc_s)

    def rows_n(r, _):
        at = pl.ds(pl.multiple_of(r * 128, 128), 128)
        n1, rs = norm_parts(x_ref[at, :].astype(F32))
        dh = gh_s[at, :]
        g1 = dh * (1.0 + scale1)
        got = dx_ref[at, :] + rs * (
            g1
            - jnp.mean(g1, axis=-1, keepdims=True)
            - n1 * jnp.mean(g1 * n1, axis=-1, keepdims=True)
        )
        ig_s[at, :] = got.astype(BF16)
        acc_s[0] += fold8(dh)
        acc_s[1] += fold8(dh * n1)
        return 0

    lax.fori_loop(0, 4, rows_n, 0)
    mpl_s[...] = jnp.zeros_like(mpl_s)
    for i in range(2):
        mpl_s[i : i + 1, :] = jnp.sum(acc_s[i], axis=0, keepdims=True)
    mpl_copy = remote(mpl_s, mrl_s, pair_sem.at[7, 0], pair_sem.at[7, 1], other)
    mpl_copy.start()
    for half in range(2):
        sl_p[half] = sv_s[:, 384 * half : 384 * half + 384].astype(BF16)
    sl_copy = remote(sl_p.at[1 - core], sl_r, pair_sem.at[8, 0], pair_sem.at[8, 1], other)
    sl_copy.start()
    for b in range(2):
        is_s[b] = mm(home, ig_s[256 * b : 256 * b + 256, :]).astype(BF16)
    mpl_copy.wait()
    item_s[0:2, :] = (mpl_s[0:2, :] + mrl_s[0:2, :]).astype(BF16).astype(F32)
    cond = mod_ref[6:7, :]
    for i in range(2):
        d_silu = d_silu + silu_part(i)
    slope = 1.0 / (1.0 + jnp.exp(-cond))
    d_cond = (slope * (1.0 + cond * (1.0 - slope))) * d_silu[0:1]
    zeros = [jnp.zeros((1, 128), F32)]
    rows_0 = jnp.concatenate(lane_rows(item_s[0:2, :], 2) + zeros * 4, axis=0)
    rows_1 = jnp.concatenate(lane_rows(d_cond, 1) + zeros * 10, axis=0)
    dl_s[core, me["y"], me["x"], z_me] = jnp.where(core == 0, rows_0, rows_1).astype(BF16)
    sl_copy.wait()
    sl_s[0] = (sl_p[core].astype(F32) + sl_r[...].astype(F32)).astype(BF16)
    small_l = small_stage(0, sl_s, dl_s, 1)
    give_back(1, lambda make, local: make().start())
    loads[10].wait()
    for copy in st1x:
        copy.wait()
    for p in range(3):
        here, _peer = early_peer(me, 0, p, 1)
        total = last_ref[p, here].astype(F32)
        for o in range(3):
            total = total + r1x[o, p].astype(F32)
        total = total.astype(BF16)

        @pl.when(core == 0)
        def _():
            s1_s[p, 3] = total

        @pl.when(core == 1)
        def _():
            for c in range(4):
                s1_s[p, c, 144:192] = total[48 * c : 48 * c + 48]

    st2e = stage_sends(1, lambda p, o, b: (s1_s.at[p, :, chunk(b, 48)], r2e.at[o - 1, p]), 0)
    small_take(1, se_s, de_s, 0, small, se_f)
    small = small_stage(2, se_s, de_s, 0)
    st2a = late_second(0, st1a)
    small_take(0, sl_s, dl_s, 1, small_l, sl_f)
    small_l = small_stage(1, sl_s, dl_s, 1)
    st2b = late_second(1, st1b)
    for copy in st2e:
        copy.wait()
    for p in range(3):
        got = second(s1_s, r2e, range(4), p, early_peer(me, 1, p, 1)[0])

        @pl.when(core == 0)
        def _():
            for c in range(4):
                t3e[p, c] = jnp.concatenate(
                    [got[k][12 * c : 12 * c + 12] for k in range(4)], axis=0
                ).astype(BF16)

        @pl.when(core == 1)
        def _():
            for c in range(4):
                t3e[p, c] = got[c].astype(BF16)

    st3e = stage_sends(2, lambda p, o, c: (t3e.at[p, c], r3e.at[o - 1, p]), 0)
    small_take(2, se_s, de_s, 0, small, se_f)
    spread(se_f, se_out, 10)
    ends.append(
        remote(de_s.at[core], de_s.at[core], pair_sem.at[16, 0], pair_sem.at[16, 1], other)
    )
    ends[-1].start()
    small_take(1, sl_s, dl_s, 1, small_l, sl_f)
    small_l = small_stage(2, sl_s, dl_s, 1)
    st3a = late_third(0, st2a)
    st3b = late_third(1, st2b)
    finish(st3e, t3e, r3e, fe_s, fe_out, 17, [early_peer(me, 2, p, 1)[0] for p in range(3)])
    late_total(0, st3a)
    late_total(1, st3b)
    spread(fl_s, fl_out, 18)
    small_take(2, sl_s, dl_s, 1, small_l, sl_f)
    spread(sl_f, sl_out, 13)
    ends.append(
        remote(dl_s.at[core], dl_s.at[core], pair_sem.at[14, 0], pair_sem.at[14, 1], other)
    )
    ends[-1].start()
    for which in range(2):
        give_back(which, lambda make, local: None if local else make().wait_send())
        for item_slot in range(2):
            out = (oret_out, iret_out)[which]
            arrived(out.at[item_slot], ret_recv.at[which, item_slot])
    for copy in ends:
        copy.wait()
    last = [
        pltpu.make_async_copy(de_s, de_out, loc.at[11]),
        pltpu.make_async_copy(dl_s, dl_out, loc.at[14]),
    ]
    for copy in last:
        copy.start()
    for copy in last:
        copy.wait()


def back_call(
    da, qkv, p, hcg, h, x, dx, mod, times, w, mw, taps, perm, o, s1, last, dbr, at, s2, sb
):
    G = (2, 8, 2, 16)
    shape = jax.ShapeDtypeStruct
    V = pltpu.VMEM
    items = (2, 4, 4, 4, 16, 128)
    DMA = pltpu.SemaphoreType.DMA
    return pl.pallas_call(
        back_kernel,
        in_specs=[
            ANY_SPEC, ANY_SPEC, ANY_SPEC, ANY_SPEC, ANY_SPEC, ANY_SPEC, ANY_SPEC, VMEM_SPEC,
            SMEM_SPEC, ANY_SPEC, ANY_SPEC, VMEM_SPEC, ANY_SPEC, ANY_SPEC, ANY_SPEC, ANY_SPEC,
            ANY_SPEC, ANY_SPEC, VMEM_SPEC, VMEM_SPEC,
        ],
        out_specs=[ANY_SPEC] * 8,
        out_shape=[
            shape((2, 256, D), BF16), shape((2, 256, D), BF16),
            shape((2, 3, 48, 256), F32), shape((2, 3, 64, 128), F32),
            shape((2, 32, D), F32), shape((2, 16, 384), F32),
            shape(items, BF16), shape(items, BF16),
        ],
        scratch_shapes=[
            V(G + (3 * D,), BF16), V((24, 256, 256), BF16), V((D, 3 * D), BF16),
            V(mw.shape, BF16), V((3, D, D), BF16), V(G + (D,), BF16), V(G + (3 * D,), BF16),
            V((3, D, 512), BF16), V(G + (D,), BF16), V((9, 2, 2, 16, D), BF16), V((512, D), F32),
            V((512, D), BF16), V((2, 256, D), BF16), V((2, 256, D), BF16),
            V((2, 3, 4, D, 128), BF16), V((3, 4, D, 128), BF16), V((3, 4, 192, 256), BF16),
            V((3, 3, 192, 256), BF16), V((3, 3, 4, 192, 128), BF16), V((3, 4, 192, 128), BF16),
            V((3, 3, 4, 48, 256), BF16), V((3, 3, 4, 48, 128), BF16), V((3, 4, 48, 256), BF16),
            V((3, 4, 48, 128), BF16), V((3, 4, 16, 128), BF16), V((3, 3, 48, 256), BF16),
            V((3, 3, 48, 128), BF16), V((3, 3, 16, 128), BF16), V((3, 48, 256), F32),
            V((3, 64, 128), F32),
            V((2, 8, D), F32), V((16, D), F32),
            V((2, 32, D), BF16), V((32, D), BF16), V((12, 32, D), BF16), V((32, D), F32),
            V((2, 16, 384), BF16), V((16, 384), BF16), V((12, 16, 384), BF16), V((16, 384), F32),
            V((8, D), F32), V((8, D), F32), V((8, D), F32), V((8, D), F32), V((8, D), F32),
            V(items, BF16), V(items, BF16),
            V((512, D), BF16), V((576, D), BF16), V((576, D), BF16), V((512, D), F32),
            V((512, D), BF16), V((3, 4, 192, 256), BF16), V((512, D), BF16), V((576, D), BF16),
            DMA((35,)), DMA((19, 2)), DMA((2, 2)), DMA((2, 2)), DMA((3, 3, 3, 3)),
            DMA((3, 3, 3, 3)), DMA((2, 3, 3)), DMA((2, 3, 3)), DMA((2, 3, 3)), DMA((2, 3, 3)),
        ],
        compiler_params=pltpu.CompilerParams(
            collective_id=2, has_side_effects=True, vmem_limit_bytes=60 * 2**20
        ),
        name="back",
    )(da, qkv, p, hcg, h, x, dx, mod, times, w, mw, taps, perm, o, s1, last, dbr, at, s2, sb)


def share_kernel(
    out_ref, ig_ref, fe_hbm, fl_hbm, se_hbm, sl_hbm, de_hbm, dl_hbm,
    o_out, ig_out, cond_out, table_out, mw_out, mb_out, aw_out, ab_out, qkv_out, qb_out, vb_out,
    ow_out, ob_out, f1_out, f1b_out, fw_out, fb_out, f2_out, f2b_out,
    ig_s, o_s, igf_s, e_s, l_s, fe_ref, fl_ref, se_ref, sl_ref, de_ref, dl_ref, sem,
):
    me = spot()
    core = me["core"]
    shard = me["dp"] * 4 + me["seq"]
    ig_load = pltpu.make_async_copy(ig_ref, ig_s, sem.at[0])
    o_load = pltpu.make_async_copy(out_ref, o_s, sem.at[9])
    o_move = pltpu.make_async_copy(o_s, o_out, sem.at[1])
    loads = [
        pltpu.make_async_copy(*pair, sem.at[3 + at])
        for at, pair in enumerate((
            (fe_hbm, fe_ref), (fl_hbm, fl_ref), (se_hbm, se_ref), (sl_hbm, sl_ref),
            (de_hbm, de_ref), (dl_hbm, dl_ref),
        ))
    ]
    for load in loads:
        load.start()
    ig_load.start()
    o_load.start()
    o_load.wait()
    o_move.start()
    ig_load.wait()
    igf_s[...] = ig_s[...].astype(F32)
    ig_move = pltpu.make_async_copy(igf_s, ig_out, sem.at[2])
    ig_move.start()
    for load in loads:
        load.wait()
    e_s[...] = de_ref[...].reshape(2048, 128).astype(F32)
    l_s[...] = dl_ref[...].reshape(2048, 128).astype(F32)

    def six(v, at):
        return jnp.where(core == 0, v[at : at + 6], v[at + 6 : at + 12])

    for p in range(3):
        early0, early1 = fe_ref[0, p], fe_ref[1, p]
        for i in range(4):
            at = D * i + 256 * p
            f1_out[:, at : at + 256] = six(early0, 12 * i)
        f2_out[:, 256 * p : 256 * p + 256] = jnp.where(core == 0, early1[0:24], early1[24:48])
        for which in range(2):
            late = fl_ref[which, p]
            for group in range(2):
                for u, block in enumerate(LATE[which][group][p]):
                    got = six(late, 48 if group else 12 * u)
                    if isinstance(block, str):
                        at = 128 * int(block[1])
                        ow_out[:, at : at + 128] = got
                    else:
                        qkv_out[:, 128 * block : 128 * block + 128] = got

    def columns(start, count=D):
        at = lax.broadcasted_iota(jnp.int32, (count, 128), 0)
        to = lax.broadcasted_iota(jnp.int32, (count, 128), 1)
        return at == start + to

    def exact(a, b):
        return lax.dot_general(
            a, b.astype(F32), (((1,), (0,)), ((), ())), preferred_element_type=F32,
            precision=lax.Precision.HIGHEST,
        )

    mine = columns(shard * 6)
    slim = exact(jnp.concatenate((sl_ref[0], sl_ref[1]), axis=1), mine)
    aw_out[...] = slim.T[0:6, 0:9]
    for ref, at in ((ab_out, 9), (qb_out, 10), (vb_out, 11), (ob_out, 12), (f2b_out, 13)):
        ref[...] = slim[at : at + 1, 0:6].reshape(6)
    quarter = shard // 32
    wide = se_ref[quarter // 2, pl.ds(pl.multiple_of(quarter % 2 * 16, 16), 16), :]
    wide = exact(wide, columns(shard % 32 * 24))
    fw_out[...] = wide[0:9, 0:24]
    fb_out[...] = wide[9:10, 0:24].reshape(24)
    f1b_out[...] = wide[10:11, 0:24].reshape(24)

    def item_rows(ref, at):
        return ref[pl.ds(at // 16 * 1024 + at % 16, 64, stride=16), :]

    silu = jnp.concatenate([item_rows(e_s, 24 + l) for l in range(6)], axis=1)
    silu = mm(silu.astype(BF16), mine.astype(BF16)).astype(BF16)
    sums = []
    for at in range(36):
        d_mod = item_rows(l_s, at) if at < 12 else item_rows(e_s, at - 12)
        mw_out[:, 128 * at : 128 * at + 128] = mm_tn(silu, d_mod.astype(BF16))[0:6]
        sums.append(jnp.sum(d_mod, axis=0, keepdims=True))
    total = jnp.concatenate(sums, axis=1)
    total = exact(jnp.concatenate([total] * 8, axis=0), columns(shard * 36, 6 * D))
    mb_out[...] = total[0:1, 0:36].reshape(36)

    cond = jnp.concatenate([item_rows(l_s, 16 + l) for l in range(6)], axis=1).astype(BF16)
    here = lax.broadcasted_iota(jnp.int32, (8, 64), 1)
    slot = lax.broadcasted_iota(jnp.int32, (8, 64), 0)
    own = here == (me["y"] * 4 + me["x"]) * 4 + slot * 2 + me["zl"]
    own = jnp.logical_and(own, slot < 2)
    cond_out[...] = mm(own.astype(BF16), cond)[0:2]
    times = 32.0 * item_rows(e_s, 30) + item_rows(e_s, 31)
    bucket = lax.broadcasted_iota(jnp.int32, (64, 1024), 1).astype(F32)
    hot = (bucket == jnp.concatenate([times] * 8, axis=1)).astype(BF16)
    my_cond = mm(cond, mine.astype(BF16)).astype(BF16)
    table_out[...] = mm_tn(my_cond, hot)[0:6, 0 : table_out.shape[1]]

    ig_move.wait()
    o_move.wait()


def share_call(buckets, *args):
    shapes = [
        ((2, 256, D), BF16), ((2, 256, D), F32), ((2, D), F32), ((6, buckets), F32),
        ((6, 6 * D), F32), ((36,), F32), ((6, 9), F32), ((6,), F32), ((6, 3 * D), F32),
        ((6,), F32), ((6,), F32), ((6, D), F32), ((6,), F32), ((6, FF), F32), ((24,), F32),
        ((9, 24), F32), ((24,), F32), ((24, D), F32), ((6,), F32),
    ]
    return pl.pallas_call(
        share_kernel,
        in_specs=[ANY_SPEC] * 8,
        out_specs=[ANY_SPEC] * 2 + [VMEM_SPEC] * 17,
        out_shape=[jax.ShapeDtypeStruct(*s) for s in shapes],
        scratch_shapes=[
            pltpu.VMEM((2, 256, D), BF16), pltpu.VMEM((2, 256, D), BF16),
            pltpu.VMEM((2, 256, D), F32), pltpu.VMEM((2048, 128), F32), pltpu.VMEM((2048, 128), F32),
            *[pltpu.VMEM(v.shape, v.dtype) for v in args[2:]],
            pltpu.SemaphoreType.DMA((10,)),
        ],
        compiler_params=pltpu.CompilerParams(vmem_limit_bytes=60 * 2**20),
        name="share",
    )(*args)


def perm_matrices():
    at = np.arange(D)
    rows = []
    for order in ORDERS:
        spots = dict(zip(order, (at // 192, at // 48 % 4, at // 12 % 4)))
        x, y, z = spots["x"], spots["y"], spots["z"]
        rows.append((((x * 2 + z % 2) * 4 + y) * 2 + z // 2) * 12 + at % 12)
    return np.stack(rows).astype(np.int32)


def local(
    latents, conditioning, timesteps, item_counts, cotangent, time_table, mod_weight, mod_bias,
    conv_attn_weight, conv_attn_bias, qkv_weight, query_bias, value_bias, out_weight, out_bias,
    fc1_weight, fc1_bias, conv_ffn_weight, conv_ffn_bias, fc2_weight, fc2_bias,
):
    alive = (lax.axis_index("seq") // 2 < item_counts).astype(F32)
    perm = (perm_matrices()[:, :, None] == np.arange(D)[None, None, :]).astype(BF16)
    x, ct, h, hcg, qkv, p, at, mod = attn_call(
        latents.reshape(2, 256, D), cotangent.reshape(2, 256, D), conditioning, timesteps,
        time_table, mod_weight, mod_bias, qkv_weight, query_bias, value_bias, conv_attn_weight,
        conv_attn_bias,
    )
    at = at.reshape(576, D)
    out, s1, last, dbr, da, dx, s2, sb = ffn_call(
        x, at, ct, mod, alive, perm, out_weight, out_bias, fc1_weight, fc1_bias, conv_ffn_weight,
        conv_ffn_bias, fc2_weight, fc2_bias,
    )
    got = back_call(
        da, qkv, p, hcg.reshape(512, D), h, x, dx, mod, timesteps,
        qkv_weight, mod_weight, conv_attn_weight, perm, out, s1, last,
        dbr.reshape(512, D), at, s2, sb,
    )
    outs = list(share_call(time_table.shape[0], *got))
    outs[0], outs[1] = outs[0].reshape(latents.shape), outs[1].reshape(latents.shape)
    outs[3], outs[6] = outs[3].T, outs[6].T
    return tuple(outs)


def solution(mesh):
    return jax.shard_map(
        local,
        mesh=mesh,
        in_specs=(
            P("dp", "seq", None, None),
            P("dp", None),
            P("dp"),
            P("dp"),
            P("dp", "seq", None, None),
            P(),
            P(),
            P(),
            P(),
            P(),
            P(),
            P(),
            P(),
            P(),
            P(),
            P(),
            P(),
            P(),
            P(),
            P(),
            P(),
        ),
        out_specs=(
            P("dp", "seq", None, None),
            P("dp", "seq", None, None),
            P("dp", None),
            P(None, ("dp", "seq")),
            P(("dp", "seq"), None),
            P(("dp", "seq")),
            P(None, ("dp", "seq")),
            P(("dp", "seq")),
            P(("dp", "seq"), None),
            P(("dp", "seq")),
            P(("dp", "seq")),
            P(("dp", "seq"), None),
            P(("dp", "seq")),
            P(("dp", "seq"), None),
            P(("dp", "seq")),
            P(None, ("dp", "seq")),
            P(("dp", "seq")),
            P(("dp", "seq"), None),
            P(("dp", "seq")),
        ),
        check_vma=False,
    )
```

```python
import functools

import jax
import jax.numpy as jnp
import numpy as np
from jax import lax
from jax.experimental import pallas as pl
from jax.experimental.pallas import tpu as pltpu
from jax.sharding import PartitionSpec as P

F32 = jnp.float32
BF16 = jnp.bfloat16
D = 768
FF = 3072
FC = 768
NFC = FF // FC
EPS = 1e-6
VMEM_SPEC = pl.BlockSpec(memory_space=pltpu.VMEM)
ANY_SPEC = pl.BlockSpec(memory_space=pl.ANY)
SMEM_SPEC = pl.BlockSpec(memory_space=pltpu.SMEM)


def mm(a, b):
    return lax.dot_general(a, b, (((1,), (0,)), ((), ())), preferred_element_type=F32)


def mm_nt(a, b):
    return lax.dot_general(a, b, (((1,), (1,)), ((), ())), preferred_element_type=F32)


def mm_tn(a, b):
    return lax.dot_general(a, b, (((0,), (0,)), ((), ())), preferred_element_type=F32)


def row(v):
    return v.astype(F32).reshape(1, v.shape[0])


def fold8(v):
    total = v[0:8]
    for at in range(8, v.shape[0], 8):
        total = total + v[at : at + 8]
    return total


def norm_parts(v):
    center = v - jnp.mean(v, axis=-1, keepdims=True)
    rs = lax.rsqrt(jnp.mean(center * center, axis=-1, keepdims=True) + EPS)
    return center * rs, rs


def by_core(taps, at, core):
    return jnp.where(core == 1, taps[3 * (2 - at // 3) + at % 3], taps[at])


def gelu_pair(v):
    d = 1.0 + 0.23164189 * jnp.abs(v)
    t = pl.reciprocal(d, approx=True)
    t = t * (2.0 - d * t)
    e = jnp.exp2(-0.7213475204444817 * (v * v))
    poly = t * (
        0.127414796
        + t * (-0.142248368 + t * (0.7107068705 + t * (-0.7265760135 + t * 0.5307027145)))
    )
    tail = poly * e
    cdf = jnp.where(v >= 0, 1.0 - tail, tail)
    return v * cdf, cdf + v * (e * 0.3989422804014327)


def side_masks():
    place = lax.broadcasted_iota(jnp.int32, (16, 128), 0)
    return place == 0, place == 15


def with_sides(even, odd, masks):
    left = jnp.where(masks[0], 0.0, pltpu.roll(odd, 1, 0))
    right = jnp.where(masks[1], 0.0, pltpu.roll(even, 15, 0))
    return even, odd, left, right


def conv_row(rows, taps):
    even = odd = None
    for a in range(3):
        if rows[a] is None:
            continue
        ev, od, left, right = rows[a]
        for tap, ce, co in ((3 * a, left, ev), (3 * a + 1, ev, od), (3 * a + 2, od, right)):
            even = taps[tap] * ce if even is None else even + taps[tap] * ce
            odd = taps[tap] * co if odd is None else odd + taps[tap] * co
    return even, odd


def with_sides_low(even, odd, masks):
    left = jnp.where(masks[0], 0.0, pltpu.roll(odd.astype(F32), 1, 0)).astype(BF16)
    right = jnp.where(masks[1], 0.0, pltpu.roll(even.astype(F32), 15, 0)).astype(BF16)
    return even, odd, left, right


def tap_pairs(held, rows, d_even, d_odd):
    out = []
    for a in range(3):
        if rows[a] is None:
            out += [None] * 3
            continue
        ev, od, left, right = rows[a]
        for ce, co in ((left, ev), (ev, od), (od, right)):
            out.append(d_even * ce + d_odd * co)
    if held is None:
        return out
    return [b if a is None else a if b is None else a + b for a, b in zip(held, out)]


def tap_products(sums, rows, d_even, d_odd):
    for a in range(3):
        if rows[a] is None:
            continue
        ev, od, left, right = rows[a]
        for tap, ce, co in ((3 * a, left, ev), (3 * a + 1, ev, od), (3 * a + 2, od, right)):
            term = fold8(d_even * ce + d_odd * co)
            sums[tap] = term if sums[tap] is None else sums[tap] + term


MESH = pl.DeviceIdType.MESH


def spot():
    dp = lax.axis_index("dp")
    seq = lax.axis_index("seq")
    x, zl, y, zh, core = dp >> 3, (dp >> 2) & 1, dp & 3, seq >> 1, seq & 1
    z = zh * 2 + zl
    me = dict(dp=dp, seq=seq, x=x, zl=zl, y=y, zh=zh, z=z, core=core)
    for o in (1, 2, 3):
        me["x", o] = ((((x + o) & 3) << 3) + (dp & 7), seq)
        me["y", o] = ((dp & 28) + ((y + o) & 3), seq)
        to = (z + o) & 3
        me["z", o] = ((dp & 27) + ((to & 1) << 2), (to & 2) + core)
    return me


def seq_peer(me, zh, core):
    return (me["dp"], zh * 2 + core)


def axis_peer(me, axis, offset):
    return me[axis, offset]


def remote(src, dst, send, recv, device):
    return pltpu.make_async_remote_copy(
        src_ref=src, dst_ref=dst, send_sem=send, recv_sem=recv, device_id=device,
        device_id_type=MESH,
    )


def arrived(ref, sem):
    pltpu.make_async_copy(ref, ref, sem).wait()


def hail(peers):
    barrier = pltpu.get_barrier_semaphore()
    for peer in peers:
        pl.semaphore_signal(barrier, inc=1, device_id=peer, device_id_type=MESH)


def heard(count):
    pl.semaphore_wait(pltpu.get_barrier_semaphore(), count)


def greet(peers):
    hail(peers)
    heard(len(peers))


ORDERS = (("x", "y", "z"), ("y", "x", "z"), ("z", "x", "y"))
EARLY = (
    (("x", "y", "z"), ("x", "y", "z"), ("y", "x", "z")),
    (("y", "x", "z"), ("z", "x", "y"), ("z", "x", "y")),
)


LATE = (
    (((0, 1, 2), (3, 6, 7), (8, 9, "g0")), ((4,), (5,), (10,))),
    (((12, 13, 14), (15, "g1", "g2"), ("g3", "g4", "g5")), ((11,), (16,), (17,))),
)


def axis_spot(me, axis):
    return me[axis]


def early_peer(me, stage, part, offset):
    key = (stage, part, offset)
    if key not in me:
        first, second = (EARLY[which][part][stage] for which in range(2))
        if first == second:
            me[key] = me[first], me[first, offset]
        else:
            pick = lambda a, b: jnp.where(me["core"] == 0, a, b)
            peer = tuple(pick(a, b) for a, b in zip(me[first, offset], me[second, offset]))
            me[key] = pick(me[first], me[second]), peer
    return me[key]


def ffn_kernel(
    x_ref, at_ref, ct_hbm, mod_ref, alive_ref, perm_hbm, ow_ref, ob_ref, f1_ref, f1b_ref,
    tap_ref, cb_ref, f2_ref, f2b_ref,
    out_hbm, s1_ref, last_ref, dbr_hbm, da_ref, dx_hbm, s2_ref, sm_ref,
    x1_s, br_s, h2_s, h2t_s, dffn_s, u_s, duc_s, act_s, du_s, dact_s, ffn_s, dh2_s, acc_s,
    ch_s, pre_s, r1_s, bias_s, das_s, dar_s, ct_ref, perm_ref, out_ref, dbr_ref, dx_ref, pair_sem, st_send, st_recv, loc,
):
    step = pl.program_id(0)
    me = spot()
    core = me["core"]
    other = seq_peer(me, me["zh"], 1 - core)
    for p in range(3):
        for o in (1, 2, 3):
            early_peer(me, 0, p, o)
    alive = alive_ref[0]

    ct_load = pltpu.make_async_copy(ct_hbm, ct_ref, loc.at[0])
    perm_load = pltpu.make_async_copy(perm_hbm.at[pl.ds(0, 2)], perm_ref, loc.at[1])

    @pl.when(step == 0)
    def _():
        ct_load.start()
        perm_load.start()
        bias_s[0:1, :] = row(f1b_ref[...])
        bias_s[1:2, :] = row(cb_ref[...])
        hail([axis_peer(me, axis, o) for axis in "xyz" for o in (1, 2, 3)] + [other])

    def pair_copy(at):
        slot = at % 2
        return remote(
            ch_s.at[slot, 1 - core], pre_s.at[slot], pair_sem.at[slot, 0], pair_sem.at[slot, 1],
            other,
        )

    def first_copies(at):
        slot = at % 2
        out = []
        for p in range(3):
            for o in (1, 2, 3):
                here, peer = early_peer(me, 0, p, o)
                out.append(
                    remote(
                        ch_s.at[slot, core, p, (here + o) & 3], r1_s.at[at, o - 1, p],
                        st_send.at[at, p, o - 1], st_recv.at[at, p, o - 1], peer,
                    )
                )
        return out

    def pair_add(at):
        slot = at % 2
        pair_copy(at).wait()
        for p in range(3):

            def add(a, _):
                ch_s[slot, core, p, a] = ch_s[slot, core, p, a] + pre_s[slot, p, a]
                return 0

            lax.fori_loop(0, 4, add, 0)

    def first_send(at):
        pair_add(at)
        for copy in first_copies(at):
            copy.start()

    def first_take(at):
        slot = at % 2
        for copy in first_copies(at):
            copy.wait()
        for p in range(3):
            here, _peer = early_peer(me, 0, p, 1)
            total = ch_s[slot, core, p, here].astype(F32)
            for o in range(3):
                total = total + r1_s[at, o, p].astype(F32)
            total = total.astype(BF16)

            @pl.when(core == 0)
            def _():
                s1_ref[p, at] = total

            @pl.when(core == 1)
            def _():
                for c in range(4):
                    s1_ref[p, c, pl.ds(pl.multiple_of(at * 48, 16), 48)] = total[
                        48 * c : 48 * c + 48
                    ]

    @pl.when(step == 0)
    def _():
        br_s[...] = mm(at_ref[...], ow_ref[...]) + row(ob_ref[...])
        shift2, scale2, gate1, gate2 = (mod_ref[i : i + 1, :] for i in (3, 4, 2, 5))

        def rows_a(r, _):
            at = pl.ds(pl.multiple_of(r * 96, 96), 96)
            x1 = x_ref[at, :].astype(F32) + gate1 * br_s[at, :]
            x1_s[at, :] = x1
            n2, _unused = norm_parts(x1)
            h2_s[at, :] = (n2 * (1.0 + scale2) + shift2).astype(BF16)
            return 0

        lax.fori_loop(0, 6, rows_a, 0)

        ct_load.wait()

        def rows_b(r, _):
            at = pl.ds(pl.multiple_of(r * 272, 16), 272)
            dffn_s[at, :] = (ct_ref[at, :].astype(F32) * alive * gate2).astype(BF16)
            return 0

        lax.fori_loop(0, 2, rows_b, 0)
        perm_load.wait()
        for p in range(2):
            h2t_s[p] = mm_nt(perm_ref[p], h2_s[0:512, :]).astype(BF16)
        ffn_s[...] = jnp.zeros_like(ffn_s)
        dh2_s[...] = jnp.zeros_like(dh2_s)

    @pl.when(step == 0)
    def _():
        heard(10)

    masks = side_masks()

    def lanes(j):
        cols = slice(128 * j, 128 * j + 128)
        taps = tap_ref[:, cols].astype(F32)
        taps = [taps[t : t + 1] for t in range(9)]
        taps = [by_core(taps, t, core) for t in range(9)]
        taps = [jnp.broadcast_to(v, (16, 128)).astype(BF16) for v in taps]
        offset = bias_s[1:2, pl.ds(pl.multiple_of(step * FC + j * 128, 128), 128)]

        def sided(ref, l):
            return with_sides_low(
                ref[32 * l : 32 * l + 16, cols], ref[32 * l + 16 : 32 * l + 32, cols], masks
            )

        rows = [None, sided(u_s, 0), sided(u_s, 1)]
        sums = [None] * 9
        held = bias_sum = None
        for l in range(17):
            ce, co = conv_row(rows, taps)
            ae, ge = gelu_pair(ce.astype(F32) + offset)
            ao, go = gelu_pair(co.astype(F32) + offset)
            de = (ge * dact_s[32 * l : 32 * l + 16, cols]).astype(BF16)
            do = (go * dact_s[32 * l + 16 : 32 * l + 32, cols]).astype(BF16)
            duc_s[32 * l : 32 * l + 16, cols] = de
            duc_s[32 * l + 16 : 32 * l + 32, cols] = do
            if l < 16:
                act_s[32 * l : 32 * l + 16, cols] = ae.astype(BF16)
                act_s[32 * l + 16 : 32 * l + 32, cols] = ao.astype(BF16)
                held = tap_pairs(held if l % 2 else None, rows, de, do)
                if l % 2:
                    for t in range(9):
                        term = fold8(held[t].astype(F32))
                        sums[t] = term if sums[t] is None else sums[t] + term
                term = fold8(de.astype(F32) + do.astype(F32))
                bias_sum = term if bias_sum is None else bias_sum + term
                rows = [rows[1], rows[2], sided(u_s, l + 2) if l + 2 < 18 else None]
        for t in range(9):
            s2_ref[t : t + 1, cols] = jnp.sum(by_core(sums, t, core), axis=0, keepdims=True)
        s2_ref[9:10, cols] = jnp.sum(bias_sum, axis=0, keepdims=True)
        back = [taps[8 - t] for t in range(9)]
        rows = [None, sided(duc_s, 0), sided(duc_s, 1)]
        bias_sum = None
        for l in range(16):
            ue, uo = conv_row(rows, back)
            du_s[32 * l : 32 * l + 16, cols] = ue
            du_s[32 * l + 16 : 32 * l + 32, cols] = uo
            term = fold8(ue.astype(F32) + uo.astype(F32))
            bias_sum = term if bias_sum is None else bias_sum + term
            rows = [rows[1], rows[2], sided(duc_s, l + 2) if l + 2 < 17 else None]
        s2_ref[10:11, cols] = jnp.sum(bias_sum, axis=0, keepdims=True)

    slot = step % 2

    def into(j):
        cols = slice(256 * j, 256 * j + 256)
        offset = bias_s[0:1, pl.ds(pl.multiple_of(step * FC + 256 * j, 256), 256)]
        u_s[:, cols] = (mm(h2_s[...], f1_ref[:, cols]) + offset).astype(BF16)
        dact_s[:, cols] = mm_nt(dffn_s[...], f2_ref[cols, :])

    def out_of(j):
        cols = slice(256 * j, 256 * j + 256)
        got = mm(h2t_s[j // 2], du_s[:, cols]).astype(BF16)
        ch_s[slot, 0, j] = got.reshape(4, 192, 256)
        grad = mm_tn(act_s[:, cols], dffn_s[0:512, :]).astype(BF16)
        for at in range(0, 256, 16):
            chip, inner = (256 * j + at) // 48, (256 * j + at) % 48
            zl, y, zh = chip // 8, chip // 2 % 4, chip % 2
            z = zh * 2 + zl
            for part in range(3):
                a, c = (y, z) if part == 0 else (z, y)
                ch_s[slot, 1, part, a, 48 * c + inner : 48 * c + inner + 16] = grad[
                    at : at + 16, 256 * part : 256 * part + 256
                ]
        ffn_s[...] += mm(act_s[:, cols], f2_ref[cols, :])
        dh2_s[...] += mm_nt(du_s[:, cols], f1_ref[:, cols])

    into(0)
    into(1)
    lanes(0)
    lanes(1)
    into(2)

    @pl.when(step > 1)
    def _():
        first_take(step - 2)

    out_of(0)

    @pl.when(step > 0)
    def _():
        first_send(step - 1)

    lanes(2)
    lanes(3)
    out_of(1)
    lanes(4)
    lanes(5)
    out_of(2)
    pair_copy(step).start()

    @pl.when(step == NFC - 1)
    def _():
        shift2, scale2, gate1, gate2 = (mod_ref[i : i + 1, :] for i in (3, 4, 2, 5))
        acc_s[...] = jnp.zeros_like(acc_s)
        f2b = row(f2b_ref[...])

        def rows_c(r, _):
            at = pl.ds(pl.multiple_of(r * 128, 128), 128)
            x1 = x1_s[at, :]
            ffn = ffn_s[at, :] + f2b
            dy = ct_ref[at, :].astype(F32) * alive
            out_ref[at, :] = (alive * (x1 + gate2 * ffn)).astype(BF16)
            n2, rs = norm_parts(x1)
            dh2 = dh2_s[at, :]
            g2 = dh2 * (1.0 + scale2)
            dx1 = dy + rs * (
                g2
                - jnp.mean(g2, axis=-1, keepdims=True)
                - n2 * jnp.mean(g2 * n2, axis=-1, keepdims=True)
            )
            dx_ref[at, :] = dx1
            dbr = (dx1 * gate1).astype(BF16)
            dbr_ref[pl.ds(2 * r, 2)] = dbr.reshape(2, 2, 2, 16, D)
            acc_s[0] += fold8(dx1 * br_s[at, :])
            acc_s[1] += fold8(dh2)
            acc_s[2] += fold8(dh2 * n2)
            acc_s[3] += fold8(dy * ffn)
            acc_s[4] += fold8(dbr.astype(F32))
            acc_s[5] += fold8(dffn_s[at, :].astype(F32))
            return 0

        lax.fori_loop(0, 4, rows_c, 0)
        for i in range(6):
            sm_ref[i : i + 1, :] = jnp.sum(acc_s[i], axis=0, keepdims=True)
        moves = [
            pltpu.make_async_copy(out_ref, out_hbm, loc.at[2]),
            pltpu.make_async_copy(dbr_ref, dbr_hbm, loc.at[3]),
            pltpu.make_async_copy(dx_ref, dx_hbm, loc.at[4]),
        ]
        for copy in moves:
            copy.start()
        halves = [dbr_ref[:, parity].reshape(256, D) for parity in range(2)]
        odd = mm_nt(halves[1], ow_ref[...]).astype(BF16)
        das_s[...] = odd.reshape(8, 2, 16, D)
        da_copy = remote(das_s, dar_s, pair_sem.at[2, 0], pair_sem.at[2, 1], other)
        da_copy.start()
        da_ref[0] = mm_nt(halves[0], ow_ref[...]).astype(BF16).reshape(8, 2, 16, D)
        pair_add(step)
        last_ref[...] = ch_s[step % 2, core]
        first_take(step - 1)
        da_copy.wait()
        da_ref[1] = dar_s[...]
        for copy in moves:
            copy.wait()


def ffn_call(x, at, ct, mod, alive, perm, ow, ob, f1, f1b, taps, cb, f2, f2b):
    whole = lambda s: pl.BlockSpec(s, lambda i: (0,) * len(s))
    return pl.pallas_call(
        ffn_kernel,
        grid=(NFC,),
        in_specs=[
            whole((576, D)), whole((576, D)), ANY_SPEC, whole((8, D)),
            pl.BlockSpec(memory_space=pltpu.SMEM),
            ANY_SPEC, whole((D, D)), whole((D,)),
            pl.BlockSpec((D, FC), lambda i: (0, i)),
            whole((FF,)),
            pl.BlockSpec((9, FC), lambda i: (0, i)),
            whole((FF,)),
            pl.BlockSpec((FC, D), lambda i: (i, 0)),
            whole((D,)),
        ],
        out_specs=[
            ANY_SPEC,
            whole((3, 4, 192, 256)), whole((3, 4, 192, 256)),
            ANY_SPEC, whole((2, 8, 2, 16, D)), ANY_SPEC,
            pl.BlockSpec((16, FC), lambda i: (0, i)),
            whole((8, D)),
        ],
        out_shape=[
            jax.ShapeDtypeStruct((512, D), BF16),
            jax.ShapeDtypeStruct((3, 4, 192, 256), BF16),
            jax.ShapeDtypeStruct((3, 4, 192, 256), BF16),
            jax.ShapeDtypeStruct((8, 2, 2, 16, D), BF16),
            jax.ShapeDtypeStruct((2, 8, 2, 16, D), BF16),
            jax.ShapeDtypeStruct((512, D), F32),
            jax.ShapeDtypeStruct((16, FF), F32),
            jax.ShapeDtypeStruct((8, D), F32),
        ],
        scratch_shapes=[
            pltpu.VMEM((576, D), F32), pltpu.VMEM((576, D), F32), pltpu.VMEM((576, D), BF16),
            pltpu.VMEM((2, D, 512), BF16), pltpu.VMEM((544, D), BF16),
            pltpu.VMEM((576, FC), BF16), pltpu.VMEM((544, FC), BF16), pltpu.VMEM((512, FC), BF16),
            pltpu.VMEM((512, FC), BF16), pltpu.VMEM((544, FC), F32),
            pltpu.VMEM((512, D), F32), pltpu.VMEM((512, D), F32), pltpu.VMEM((6, 8, D), F32),
            pltpu.VMEM((2, 2, 3, 4, 192, 256), BF16), pltpu.VMEM((2, 3, 4, 192, 256), BF16),
            pltpu.VMEM((3, 3, 3, 192, 256), BF16), pltpu.VMEM((8, FF), F32),
            pltpu.VMEM((8, 2, 16, D), BF16), pltpu.VMEM((8, 2, 16, D), BF16),
            pltpu.VMEM((576, D), BF16), pltpu.VMEM((2, D, D), BF16), pltpu.VMEM((512, D), BF16),
            pltpu.VMEM((8, 2, 2, 16, D), BF16), pltpu.VMEM((512, D), F32),
            pltpu.SemaphoreType.DMA((3, 2)),
            pltpu.SemaphoreType.DMA((3, 3, 3)), pltpu.SemaphoreType.DMA((3, 3, 3)),
            pltpu.SemaphoreType.DMA((5,)),
        ],
        compiler_params=pltpu.CompilerParams(
            dimension_semantics=("arbitrary",), vmem_limit_bytes=60 * 2**20,
            collective_id=3, has_side_effects=True,
        ),
        name="ffn",
    )(x, at, ct, mod, alive, perm, ow, ob, f1, f1b, taps, cb, f2, f2b)


def place_matrix(count, flip, inverse):
    rows = count // 32
    out = lax.broadcasted_iota(jnp.int32, (count, count), 0)
    at = lax.broadcasted_iota(jnp.int32, (count, count), 1)
    row = out // 32
    row = jnp.where(flip, rows - 1 - row, row)
    low = out % 32
    if inverse:
        low = (low % 2) * 16 + low // 2
    else:
        low = (low % 16) * 2 + low // 16
    return jnp.where(at == row * 32 + low, 1.0, 0.0).astype(BF16)


def head_lanes(values, half):
    lane = lax.broadcasted_iota(jnp.int32, values.shape, 1)
    return jnp.where((lane // 64) == half, values, jnp.zeros_like(values))


def attn_kernel(
    lat_ref, ct_ref, cond_ref, time_ref, table_ref, mw_ref, mb_ref, w_ref, qb_ref, vb_ref,
    tap_ref, cb_ref,
    x_out, ct_out, h_out, hcg_out, qkv_out, p_out, at_out, mod_out,
    xr_s, xh_s, x_s, c_s, h_s, hcg_s, sb_s, w_s, qkv_s, p_s, ag_s, at_s, mod_s, table_s, mw_s, cb_s,
    send0, recv0, sem_pair, sem_loc,
):
    me = spot()
    zh, core, seq = me["zh"], me["core"], me["seq"]
    other = seq_peer(me, zh, 1 - core)
    w_load = pltpu.make_async_copy(w_ref, w_s, sem_loc.at[0])
    table_load = pltpu.make_async_copy(table_ref, table_s, sem_loc.at[10])
    mw_load = pltpu.make_async_copy(mw_ref, mw_s, sem_loc.at[11])
    for copy in (table_load, mw_load, w_load):
        copy.start()

    greet(
        [
            seq_peer(me, (zh + dz) % 2, (core + dc) % 2)
            for dz, dc in ((0, 1), (1, 0), (1, 1))
        ]
    )
    slot = jnp.where(zh == 0, core, 1 - core)
    inner = jnp.logical_or(seq == 1, seq == 2)
    halo_core = jnp.where(seq == 1, 1, 0)
    halo_at = pl.multiple_of(jnp.where(seq == 1, 192, 0), 64)

    def sends(arrays, act):
        for a in arrays:
            ref = (lat_ref, ct_ref)[a]
            for j in range(2):
                own = jnp.logical_and(zh == j, core == zh)
                main = (ref.at[j], xr_s.at[a, slot])
                halo = (ref.at[j, pl.ds(halo_at, 64)], xh_s.at[a])

                @pl.when(own)
                def _():
                    act(lambda: pltpu.make_async_copy(*main, recv0.at[a, slot]), True)

                @pl.when(jnp.logical_not(own))
                def _():
                    act(
                        lambda: remote(*main, send0.at[a, j, 0], recv0.at[a, slot], seq_peer(me, j, zh)),
                        False,
                    )

                @pl.when(jnp.logical_and(inner, zh == j))
                def _():
                    act(lambda: pltpu.make_async_copy(*halo, recv0.at[a, 2]), True)

                @pl.when(jnp.logical_and(inner, zh != j))
                def _():
                    act(
                        lambda: remote(
                            *halo, send0.at[a, j, 1], recv0.at[a, 2], seq_peer(me, j, halo_core)
                        ),
                        False,
                    )

    sends((0,), lambda make, local: make().start())

    flip = core == 1
    big = place_matrix(256, flip, False)
    small = place_matrix(64, flip, False)

    table_load.wait()
    here = lax.broadcasted_iota(jnp.int32, (8, table_s.shape[0]), 1)
    one_hot = jnp.where(here == time_ref[zh], 1.0, 0.0).astype(BF16)
    cond = jnp.where(zh == 0, cond_ref[0:1, :], cond_ref[1:2, :]) + mm(one_hot, table_s[...])
    silu = (cond / (1.0 + jnp.exp(-cond))).astype(BF16)
    mw_load.wait()
    for i in range(6):
        cols = slice(D * i, D * i + D)
        mod_s[i : i + 1, :] = (mm(silu, mw_s[:, cols]) + row(mb_ref[cols]))[0:1]
    mod_s[6:7, :] = cond[0:1]
    mod_s[7:8, :] = silu[0:1].astype(F32)
    shift1, scale1 = mod_s[0:1, :], mod_s[1:2, :]

    def placed(a, into):
        for b in range(2):
            arrived(xr_s.at[a, b], recv0.at[a, b])
            into[256 * b : 256 * b + 256, :] = mm(big, xr_s[a, b]).astype(BF16)
        arrived(xh_s.at[a], recv0.at[a, 2])
        into[512:576, :] = mm(small, xh_s[a]).astype(BF16)

    placed(0, x_s)
    sends((1,), lambda make, local: make().start())

    def rows_a(r, _):
        at = pl.ds(pl.multiple_of(r * 96, 96), 96)
        n1, _unused = norm_parts(x_s[at, :].astype(F32))
        h_s[at, :] = (n1 * (1.0 + scale1) + shift1).astype(BF16)
        return 0

    lax.fori_loop(0, 6, rows_a, 0)
    outs = [
        pltpu.make_async_copy(x_s, x_out, sem_loc.at[1]),
        pltpu.make_async_copy(h_s, h_out, sem_loc.at[2]),
        pltpu.make_async_copy(mod_s, mod_out, sem_loc.at[12]),
    ]
    for copy in outs:
        copy.start()
    masks = side_masks()

    def lanes(j, _):
        cols = pl.ds(pl.multiple_of(j * 128, 128), 128)
        taps = tap_ref[:, cols].astype(F32)
        taps = [taps[t : t + 1] for t in range(9)]
        taps = [by_core(taps, t, core) for t in range(9)]
        offset = cb_s[0:1, cols]

        def sided(l):
            return with_sides(
                h_s[32 * l : 32 * l + 16, cols].astype(F32),
                h_s[32 * l + 16 : 32 * l + 32, cols].astype(F32),
                masks,
            )

        rows = [None, sided(0), sided(1)]
        for l in range(16):
            ce, co = conv_row(rows, taps)
            ce, co = (ce + offset).astype(BF16), (co + offset).astype(BF16)
            if l % 2 == 0:
                hcg_s[0, l // 2, 0, :, cols] = ce
                hcg_s[0, l // 2, 1, :, cols] = co
            else:
                sb_s[l // 2, 0, :, cols] = ce
                sb_s[l // 2, 1, :, cols] = co
            rows = [rows[1], rows[2], sided(l + 2) if l < 15 else None]
        return 0

    cb_s[0:1, :] = row(cb_ref[...])
    lax.fori_loop(0, D // 128, lanes, 0)
    hc_copy = remote(sb_s, hcg_s.at[1], sem_pair.at[0], sem_pair.at[1], other)
    hc_copy.start()
    w_load.wait()

    def project(half):
        for i, bias in enumerate((qb_ref, None, vb_ref)):
            cols = slice(D * i, D * i + D)
            got = mm(hcg_s[half].reshape(256, D), w_s[:, cols])
            if bias is not None:
                got = got + row(bias[...])
            qkv_s[half, :, :, :, cols] = got.astype(BF16).reshape(8, 2, 16, D)

    project(0)
    hc_copy.wait()
    outs.append(pltpu.make_async_copy(hcg_s, hcg_out, sem_loc.at[3]))
    outs[-1].start()
    project(1)
    outs.append(pltpu.make_async_copy(qkv_s, qkv_out, sem_loc.at[4]))
    outs[-1].start()

    def attend(pair, _):
        heads = [(pc, half) for pc in range(2) for half in range(2)]

        def part(which, pc):
            cols = pl.ds(pl.multiple_of(which * D + pair * 128, 128), 128)
            return jnp.concatenate(
                [qkv_s[half, :, pc, :, cols].reshape(128, 128) for half in range(2)], axis=0
            )

        q, k, v = ([part(which, pc) for pc in range(2)] for which in range(3))
        scores = [mm_nt(k[pc], head_lanes(q[pc], half)) * 0.125 for pc, half in heads]
        v_t = [v[pc].T for pc in range(2)]
        top = [jnp.max(n, axis=0, keepdims=True) for n in scores]
        e = [jnp.exp(n - m) for n, m in zip(scores, top)]
        scale = [1.0 / jnp.sum(n, axis=0, keepdims=True) for n in e]
        low = [(n * m).astype(BF16) for n, m in zip(e, scale)]
        for (pc, half), n in zip(heads, low):
            p_s[2 * (6 * pc + pair) + half] = n
        got = [mm(v_t[pc][64 * half : 64 * half + 64], n) for (pc, half), n in zip(heads, low)]
        cols = pl.ds(pl.multiple_of(pair * 128, 128), 128)
        for pc in range(2):
            o = jnp.concatenate(got[2 * pc : 2 * pc + 2], axis=0).T.astype(BF16)
            for half in range(2):
                ag_s[half, :, pc, :, cols] = o[128 * half : 128 * half + 128].reshape(8, 16, 128)
        return 0

    lax.fori_loop(0, 6, attend, 0)
    back = [
        remote(ag_s.at[1], at_s.at[pl.ds(0, 8), 1], sem_pair.at[2], sem_pair.at[3], other),
        remote(ag_s.at[0, 7], at_s.at[8, 1], sem_pair.at[4], sem_pair.at[5], other),
        pltpu.make_async_copy(ag_s.at[0], at_s.at[pl.ds(0, 8), 0], sem_loc.at[5]),
        pltpu.make_async_copy(ag_s.at[1, 7], at_s.at[8, 0], sem_loc.at[6]),
    ]
    for copy in back:
        copy.start()
    outs.append(pltpu.make_async_copy(p_s, p_out, sem_loc.at[7]))
    outs[-1].start()
    placed(1, c_s)
    outs.append(pltpu.make_async_copy(c_s, ct_out, sem_loc.at[8]))
    outs[-1].start()
    for copy in back:
        copy.wait()
    outs.append(pltpu.make_async_copy(at_s, at_out, sem_loc.at[9]))
    outs[-1].start()
    for copy in outs:
        copy.wait()

    def finish(make, local):
        if not local:
            make().wait_send()

    sends((0, 1), finish)


def attn_call(lat, ct, cond, times, table, mw, mb, w, qb, vb, taps, cb):
    G = (2, 8, 2, 16)
    shape = jax.ShapeDtypeStruct
    return pl.pallas_call(
        attn_kernel,
        in_specs=[
            ANY_SPEC, ANY_SPEC, VMEM_SPEC, SMEM_SPEC, ANY_SPEC, ANY_SPEC, VMEM_SPEC, ANY_SPEC,
            VMEM_SPEC, VMEM_SPEC, VMEM_SPEC, VMEM_SPEC,
        ],
        out_specs=[ANY_SPEC] * 8,
        out_shape=[
            shape((576, D), BF16), shape((576, D), BF16), shape((576, D), BF16),
            shape(G + (D,), BF16), shape(G + (3 * D,), BF16), shape((24, 256, 256), BF16),
            shape((9, 2, 2, 16, D), BF16), shape((8, D), F32),
        ],
        scratch_shapes=[
            pltpu.VMEM((2, 2, 256, D), BF16), pltpu.VMEM((2, 64, D), BF16),
            pltpu.VMEM((576, D), BF16), pltpu.VMEM((576, D), BF16), pltpu.VMEM((576, D), BF16),
            pltpu.VMEM(G + (D,), BF16), pltpu.VMEM((8, 2, 16, D), BF16),
            pltpu.VMEM((D, 3 * D), BF16), pltpu.VMEM(G + (3 * D,), BF16),
            pltpu.VMEM((24, 256, 256), BF16), pltpu.VMEM(G + (D,), BF16),
            pltpu.VMEM((9, 2, 2, 16, D), BF16),
            pltpu.VMEM((8, D), F32), pltpu.VMEM(table.shape, BF16), pltpu.VMEM(mw.shape, BF16),
            pltpu.VMEM((8, D), F32),
            pltpu.SemaphoreType.DMA((2, 2, 2)), pltpu.SemaphoreType.DMA((2, 3)),
            pltpu.SemaphoreType.DMA((6,)), pltpu.SemaphoreType.DMA((13,)),
        ],
        compiler_params=pltpu.CompilerParams(
            collective_id=1, has_side_effects=True, vmem_limit_bytes=56 * 2**20
        ),
        name="attend",
    )(lat, ct, cond, times, table, mw, mb, w, qb, vb, taps, cb)


def back_kernel(
    da_ref, qkv_ref, p_ref, hcg_hbm, h_hbm, x_hbm, dx_hbm, mod_ref, time_ref, w_ref, mw_ref,
    tap_ref, perm_ref, o_hbm, s1_ref, last_hbm, dbr_hbm, at_hbm, s2_ref, sb_ref,
    oret_out, iret_out, fe_out, fl_out, se_out, sl_out, de_out, dl_out,
    qkv_s, p_s, w_s, mw_s, perm_s, dag_s, dqkv_s, hct_s, dhc_s, dh_s, gh_s, ig_s, os_s, is_s,
    lg_s, prl_s, s1_s, r1x, r1l, s1l, r2e, r2l, t3e, t3a, t3b, r3e, r3a, r3b, fe_s, fl_s,
    acc_s, sv_s, se_p, se_r, se_s, se_f, sl_p, sl_r, sl_s, sl_f, mp_s, mr_s, mpl_s, mrl_s,
    item_s, de_s, dl_s, hcg_ref, h_ref, x_ref, dx_ref, o_ref, last_ref, dbr_ref, at_ref,
    loc, pair_sem, ret_send, ret_recv, st_send, st_recv, sm_send, sm_recv, dm_send, dm_recv,
):
    me = spot()
    zh, core = me["zh"], me["core"]
    other = seq_peer(me, zh, 1 - core)
    loads = [
        pltpu.make_async_copy(*pair, loc.at[20 + at])
        for at, pair in enumerate((
            (da_ref, dag_s), (qkv_ref, qkv_s), (perm_ref, perm_s), (hcg_hbm, hcg_ref),
            (at_hbm, at_ref), (dbr_hbm, dbr_ref), (p_ref, p_s), (last_hbm, last_ref),
            (o_hbm, o_ref), (w_ref, w_s), (s1_ref, s1_s), (h_hbm, h_ref), (x_hbm, x_ref),
            (dx_hbm, dx_ref), (mw_ref, mw_s),
        ))
    ]
    for load in loads:
        load.start()
    peers = [axis_peer(me, axis, o) for axis in "xyz" for o in (1, 2, 3)]
    peers += [other, seq_peer(me, 1 - zh, 1 - core)]
    hail(peers)

    def stage_sends(stage, bufs, kind, parts=(0, 1, 2)):
        out = []
        for p in parts:
            for o in (1, 2, 3):
                if kind:
                    axis = ORDERS[p][stage]
                    here, peer = axis_spot(me, axis), axis_peer(me, axis, o)
                else:
                    here, peer = early_peer(me, stage, p, o)
                src, dst = bufs(p, o, (here + o) & 3)
                copy = remote(
                    src, dst, st_send.at[kind, stage, p, o - 1], st_recv.at[kind, stage, p, o - 1],
                    peer,
                )
                copy.start()
                out.append(copy)
        return out

    def chunk(there, rows):
        return pl.ds(pl.multiple_of(there * rows, 16), rows)

    home = place_matrix(256, core == 1, True)

    def give_back(which, act):
        ref, out = ((os_s, oret_out), (is_s, iret_out))[which]
        for b in range(2):
            to_core = jnp.where(core == 0, b, 1 - b)
            own = jnp.logical_and(zh == core, b == 0)

            @pl.when(own)
            def _():
                act(lambda: pltpu.make_async_copy(ref.at[b], out.at[zh], ret_recv.at[which, zh]), True)

            @pl.when(jnp.logical_not(own))
            def _():
                act(
                    lambda: remote(
                        ref.at[b], out.at[zh], ret_send.at[which, b], ret_recv.at[which, zh],
                        seq_peer(me, core, to_core),
                    ),
                    False,
                )

    def pairs(pair, _):
        heads = [(pc, half) for pc in range(2) for half in range(2)]
        lanes_at = [
            pl.ds(pl.multiple_of(which * D + pair * 128, 128), 128) for which in range(3)
        ]

        def part(ref, cols, pc):
            return jnp.concatenate(
                [ref[half, :, pc, :, cols].reshape(128, 128) for half in range(2)], axis=0
            )

        q, k, v = ([part(qkv_s, cols, pc) for pc in range(2)] for cols in lanes_at)
        do = [part(dag_s, lanes_at[0], pc) for pc in range(2)]
        dom = [head_lanes(do[pc], half) for pc, half in heads]
        dp = [mm_nt(v[pc], n) for (pc, _), n in zip(heads, dom)]
        low = [p_s[2 * (6 * pc + pair) + half] for pc, half in heads]
        dv = [mm(n, m) for n, m in zip(low, dom)]
        k_t = [k[pc].T for pc in range(2)]
        qm = [head_lanes(q[pc], half) for pc, half in heads]
        probs = [n.astype(F32) for n in low]
        sums = [jnp.sum(n * m, axis=0, keepdims=True) for n, m in zip(probs, dp)]
        ds = [(n * (m - t)).astype(BF16) for n, m, t in zip(probs, dp, sums)]
        dk = [mm(n, m) for n, m in zip(ds, qm)]
        dq = [mm(k_t[pc][64 * half : 64 * half + 64], n) for (pc, half), n in zip(heads, ds)]
        for pc in range(2):
            at = 2 * pc
            turned = jnp.concatenate(dq[at : at + 2], axis=0).T
            grads = (0.125 * turned, 0.125 * (dk[at] + dk[at + 1]), dv[at] + dv[at + 1])
            for cols, got in zip(lanes_at, grads):
                got = got.astype(BF16)
                for half in range(2):
                    dqkv_s[half, :, pc, :, cols] = got[128 * half : 128 * half + 128].reshape(
                        8, 16, 128
                    )
        return 0

    def out_grads():
        for p, places in (
            (1, ((1, 1, 1), (1, 2, 2))), (2, ((0, 2, 0), (1, 0, 3), (1, 1, 4), (1, 2, 5)))
        ):
            at_t = mm_nt(perm_s[p], at_ref[0:512, :]).astype(BF16)
            cols = jnp.concatenate(
                [dbr_ref[:, 128 * g : 128 * g + 128] for _, _, g in places], axis=1
            )
            got = mm(at_t, cols).astype(BF16)
            for n, (which, u, _) in enumerate(places):
                lg_s[which, p, u] = got[:, 128 * n : 128 * n + 128]

    def late_grads(group):
        copies = []
        for p in range(3):
            for which in range(2):
                blocks = LATE[which][group][p]
                made = [n for n in blocks if not isinstance(n, str)]
                if not made:
                    continue
                cols = jnp.concatenate(
                    [
                        dqkv_s[:, :, :, :, 128 * n : 128 * n + 128].reshape(512, 128)
                        for n in made
                    ],
                    axis=1,
                )
                got = mm(hct_s[p], cols).astype(BF16)
                for n, block in enumerate(made):
                    u = 3 if group else blocks.index(block)
                    lg_s[which, p, u] = got[:, 128 * n : 128 * n + 128]
            part = late_part(group)
            sem = 4 + p if group == 0 else (9, 12, 15)[p]
            copies.append(
                remote(
                    lg_s.at[(1 - core, p) + part], prl_s.at[(p,) + part], pair_sem.at[sem, 0],
                    pair_sem.at[sem, 1], other,
                )
            )
            copies[-1].start()
        return copies

    def late_part(group):
        return (3,) if group else (pl.ds(0, 3),)

    def late_first(group, copies):
        out = []
        part = late_part(group)
        for p in range(3):
            copies[p].wait()
            for u in (3,) if group else (0, 1, 2):
                lg_s[core, p, u] = lg_s[core, p, u] + prl_s[p, u]
            out += stage_sends(
                0,
                lambda p, o, a: (
                    lg_s.at[(core, p) + part + (chunk(a, 192),)], r1l.at[(o - 1, p) + part]
                ),
                1 + group, (p,),
            )
        return out

    def late_second(group, copies):
        out = []
        part = late_part(group)
        for p in range(3):
            for copy in copies[3 * p : 3 * p + 3]:
                copy.wait()
            for u in (3,) if group else (0, 1, 2):
                total = lg_s[core, p, u, chunk(spots[0][p], 192), :].astype(F32)
                for o in range(3):
                    total = total + r1l[o, p, u].astype(F32)
                s1l[p, u] = total.astype(BF16)
            out += stage_sends(
                1,
                lambda p, o, b: (
                    s1l.at[(p,) + part + (chunk(b, 48),)], r2l.at[(o - 1, p) + part]
                ),
                1 + group, (p,),
            )
        return out

    def late_third(group, copies):
        out = []
        t3l, r3l = (t3b, r3b) if group else (t3a, r3a)
        for p in range(3):
            for copy in copies[3 * p : 3 * p + 3]:
                copy.wait()
            got = second(s1l, r2l, (3,) if group else (0, 1, 2), p, spots[1][p])
            pad = jnp.zeros((4 if group else 12, 128), F32)
            for c in range(4):
                t3l[p, c] = jnp.concatenate(
                    [v[12 * c : 12 * c + 12] for v in got] + [pad], axis=0
                ).astype(BF16)
            out += stage_sends(
                2, lambda p, o, c: (t3l.at[p, c], r3l.at[o - 1, p]), 1 + group, (p,)
            )
        return out

    def late_total(group, copies):
        t3l, r3l = (t3b, r3b) if group else (t3a, r3a)
        rows = slice(48, 64) if group else slice(0, 48)
        for copy in copies:
            copy.wait()
        for p in range(3):
            total = t3l[p, spots[2][p]].astype(F32)
            for o in range(3):
                total = total + r3l[o, p].astype(F32)
            fl_s[p, rows, :] = total

    spots = [[axis_spot(me, ORDERS[p][stage]) for p in range(3)] for stage in range(3)]
    z_me = axis_spot(me, "z")

    def small_stage(stage, sums, items, kind):
        axis = "zxy"[stage]
        if stage == 0:
            ref = items.at[core, me["y"], me["x"], z_me]
        elif stage == 1:
            ref = items.at[core, me["y"], me["x"]]
        else:
            ref = items.at[core, me["y"]]
        out = []
        for o in (1, 2, 3):
            peer = axis_peer(me, axis, o)
            at = (kind, stage, o - 1)
            out.append(
                remote(sums.at[4 * stage], sums.at[4 * stage + o], sm_send.at[at], sm_recv.at[at], peer)
            )
            out.append(remote(ref, ref, dm_send.at[at], dm_recv.at[at], peer))
        for copy in out:
            copy.start()
        return out

    def small_take(stage, sums, items, kind, copies, last):
        axis = "zxy"[stage]
        for copy in copies:
            copy.wait_send()
        for o in (1, 2, 3):
            at = (kind, stage, o - 1)
            arrived(sums.at[4 * stage + o], sm_recv.at[at])
            there = (axis_spot(me, axis) + 4 - o) & 3
            if stage == 0:
                ref = items.at[core, me["y"], me["x"], there]
            elif stage == 1:
                ref = items.at[core, me["y"], there]
            else:
                ref = items.at[core, there]
            arrived(ref, dm_recv.at[at])
        total = sums[4 * stage].astype(F32)
        for o in (1, 2, 3):
            total = total + sums[4 * stage + o].astype(F32)
        if stage < 2:
            sums[4 * stage + 4] = total.astype(BF16)
        else:
            last[...] = total

    def lane_rows(values, count):
        return [
            values[i : i + 1, 128 * l : 128 * l + 128] for i in range(count) for l in range(6)
        ]

    ends = []

    def spread(done, out, at):
        for copy in (
            pltpu.make_async_copy(done, out.at[core], loc.at[at]),
            remote(done, out.at[core], pair_sem.at[at, 0], pair_sem.at[at, 1], other),
        ):
            copy.start()
            ends.append(copy)

    def second(own, recv, panels, p, here):
        out = []
        for k in panels:
            total = own[p, k, chunk(here, 48), :].astype(F32)
            for o in range(3):
                total = total + recv[o, p, k].astype(F32)
            out.append(total)
        return out

    def finish(copies, own, recv, done, out, at, places):
        for copy in copies:
            copy.wait()
        for p in range(3):
            total = own[p, places[p]].astype(F32)
            for o in range(3):
                total = total + recv[o, p].astype(F32)
            done[p] = total
        spread(done, out, at)

    def pairs_turn(i, _):
        hct_s[i] = mm_nt(perm_s[i], hcg_ref[...]).astype(BF16)
        return pairs(i, 0)

    for load in loads[:7]:
        load.wait()
    lax.fori_loop(0, 1, pairs_turn, 0)
    heard(len(peers))
    loads[7].wait()
    st1x = stage_sends(0, lambda p, o, a: (last_ref.at[p, a], r1x.at[o - 1, p]), 0)
    mp_s[...] = sb_ref[...]
    mp_copy = remote(mp_s, mr_s, pair_sem.at[1, 0], pair_sem.at[1, 1], other)
    mp_copy.start()
    for half in range(2):
        for q in range(2):
            at = D * (2 * half + q)
            se_p[half, 16 * q : 16 * q + 16, :] = s2_ref[:, at : at + D].astype(BF16)
    se_copy = remote(se_p.at[1 - core], se_r, pair_sem.at[2, 0], pair_sem.at[2, 1], other)
    se_copy.start()

    loads[8].wait()
    for b in range(2):
        os_s[b] = mm(home, o_ref[256 * b : 256 * b + 256, :]).astype(BF16)
    give_back(0, lambda make, local: make().start())
    lax.fori_loop(1, 3, pairs_turn, 0)
    out_grads()
    pairs(3, 0)
    late_a = late_grads(0)
    mp_copy.wait()
    item_s[2:6, :] = (mp_s[0:4, :] + mr_s[0:4, :]).astype(BF16).astype(F32)
    time_id = time_ref[zh]
    stamp = jnp.ones((1, 128), F32)
    rows = lane_rows(item_s[2:6, :], 4) + lane_rows(mod_ref[7:8, :], 1)
    rows += [stamp * (time_id // 32).astype(F32), stamp * (time_id % 32).astype(F32)]
    both = jnp.concatenate(rows, axis=0).astype(BF16)
    de_s[core, me["y"], me["x"], z_me] = jnp.where(core == 0, both[0:16], both[16:32])
    se_copy.wait()
    se_s[0] = (se_p[core].astype(F32) + se_r[...].astype(F32)).astype(BF16)
    small = small_stage(0, se_s, de_s, 0)
    lax.fori_loop(4, 6, pairs, 0)
    late_b = late_grads(1)
    loads[9].wait()
    for half in (1, 0):
        got = mm_nt(dqkv_s[half].reshape(256, 3 * D), w_s[...]).astype(BF16)
        dhc_s[half] = got.reshape(8, 2, 16, D)
        if half == 1:
            dhc_copy = remote(
                dhc_s.at[1], dh_s.at[pl.ds(0, 8), 1], pair_sem.at[3, 0], pair_sem.at[3, 1], other
            )
            dhc_copy.start()
    near = [
        pltpu.make_async_copy(dhc_s.at[0], dh_s.at[pl.ds(0, 8), 0], loc.at[7]),
        pltpu.make_async_copy(dhc_s.at[1, 7], dh_s.at[8, 0], loc.at[8]),
    ]
    for copy in near:
        copy.start()
    st1a = late_first(0, late_a)
    st1b = late_first(1, late_b)
    loads[14].wait()
    d_silu = jnp.zeros((8, D), F32)

    def silu_part(i):
        row = jnp.concatenate([item_s[i : i + 1, :]] * 8, axis=0).astype(BF16)
        return mm_nt(row, mw_s[:, D * i : D * i + D])

    for i in range(2, 6):
        d_silu = d_silu + silu_part(i)
    ones = jnp.ones((8, 512), BF16)
    for row, at in ((10, 0), (11, 2 * D)):
        sums = mm(ones, dqkv_s[:, :, :, :, at : at + D].reshape(512, D))
        sv_s[row : row + 1, :] = sums[0:1]
    sv_s[12:14, :] = sb_ref[4:6, :]
    sv_s[14:16, :] = jnp.zeros((2, D), F32)

    dhc_copy.wait()
    for copy in near:
        copy.wait()
    loads[11].wait()
    masks = side_masks()

    def lanes(j, _):
        cols = pl.ds(pl.multiple_of(j * 128, 128), 128)
        taps = tap_ref[:, cols].astype(F32)
        taps = [taps[t : t + 1] for t in range(9)]
        back = [by_core(taps, 8 - t, core) for t in range(9)]

        def sided_d(l):
            return with_sides(
                dh_s[l // 2, l % 2, 0, :, cols].astype(F32),
                dh_s[l // 2, l % 2, 1, :, cols].astype(F32),
                masks,
            )

        def sided_h(l):
            return with_sides(
                h_ref[32 * l : 32 * l + 16, cols].astype(F32),
                h_ref[32 * l + 16 : 32 * l + 32, cols].astype(F32),
                masks,
            )

        rows = [None, sided_d(0), sided_d(1)]
        rows_h = [None, sided_h(0), sided_h(1)]
        sums = [None] * 9
        bias_sum = None
        for l in range(16):
            ge, go = conv_row(rows, back)
            gh_s[32 * l : 32 * l + 16, cols] = ge
            gh_s[32 * l + 16 : 32 * l + 32, cols] = go
            de, do = rows[1][0], rows[1][1]
            tap_products(sums, rows_h, de, do)
            term = fold8(de + do)
            bias_sum = term if bias_sum is None else bias_sum + term
            if l < 15:
                rows = [rows[1], rows[2], sided_d(l + 2)]
                rows_h = [rows_h[1], rows_h[2], sided_h(l + 2)]
        for t in range(9):
            total = jnp.sum(by_core(sums, t, core), axis=0, keepdims=True)
            sv_s[t : t + 1, cols] = total
        sv_s[9:10, cols] = jnp.sum(bias_sum, axis=0, keepdims=True)
        return 0

    lax.fori_loop(0, D // 128, lanes, 0)
    small_take(0, se_s, de_s, 0, small, se_f)
    small = small_stage(1, se_s, de_s, 0)
    for load in loads[12:14]:
        load.wait()
    scale1 = mod_ref[1:2, :]
    acc_s[...] = jnp.zeros_like(acc_s)

    def rows_n(r, _):
        at = pl.ds(pl.multiple_of(r * 128, 128), 128)
        n1, rs = norm_parts(x_ref[at, :].astype(F32))
        dh = gh_s[at, :]
        g1 = dh * (1.0 + scale1)
        got = dx_ref[at, :] + rs * (
            g1
            - jnp.mean(g1, axis=-1, keepdims=True)
            - n1 * jnp.mean(g1 * n1, axis=-1, keepdims=True)
        )
        ig_s[at, :] = got.astype(BF16)
        acc_s[0] += fold8(dh)
        acc_s[1] += fold8(dh * n1)
        return 0

    lax.fori_loop(0, 4, rows_n, 0)
    mpl_s[...] = jnp.zeros_like(mpl_s)
    for i in range(2):
        mpl_s[i : i + 1, :] = jnp.sum(acc_s[i], axis=0, keepdims=True)
    mpl_copy = remote(mpl_s, mrl_s, pair_sem.at[7, 0], pair_sem.at[7, 1], other)
    mpl_copy.start()
    for half in range(2):
        sl_p[half] = sv_s[:, 384 * half : 384 * half + 384].astype(BF16)
    sl_copy = remote(sl_p.at[1 - core], sl_r, pair_sem.at[8, 0], pair_sem.at[8, 1], other)
    sl_copy.start()
    for b in range(2):
        is_s[b] = mm(home, ig_s[256 * b : 256 * b + 256, :]).astype(BF16)
    mpl_copy.wait()
    item_s[0:2, :] = (mpl_s[0:2, :] + mrl_s[0:2, :]).astype(BF16).astype(F32)
    cond = mod_ref[6:7, :]
    for i in range(2):
        d_silu = d_silu + silu_part(i)
    slope = 1.0 / (1.0 + jnp.exp(-cond))
    d_cond = (slope * (1.0 + cond * (1.0 - slope))) * d_silu[0:1]
    zeros = [jnp.zeros((1, 128), F32)]
    rows_0 = jnp.concatenate(lane_rows(item_s[0:2, :], 2) + zeros * 4, axis=0)
    rows_1 = jnp.concatenate(lane_rows(d_cond, 1) + zeros * 10, axis=0)
    dl_s[core, me["y"], me["x"], z_me] = jnp.where(core == 0, rows_0, rows_1).astype(BF16)
    sl_copy.wait()
    sl_s[0] = (sl_p[core].astype(F32) + sl_r[...].astype(F32)).astype(BF16)
    small_l = small_stage(0, sl_s, dl_s, 1)
    give_back(1, lambda make, local: make().start())
    loads[10].wait()
    for copy in st1x:
        copy.wait()
    for p in range(3):
        here, _peer = early_peer(me, 0, p, 1)
        total = last_ref[p, here].astype(F32)
        for o in range(3):
            total = total + r1x[o, p].astype(F32)
        total = total.astype(BF16)

        @pl.when(core == 0)
        def _():
            s1_s[p, 3] = total

        @pl.when(core == 1)
        def _():
            for c in range(4):
                s1_s[p, c, 144:192] = total[48 * c : 48 * c + 48]

    st2e = stage_sends(1, lambda p, o, b: (s1_s.at[p, :, chunk(b, 48)], r2e.at[o - 1, p]), 0)
    small_take(1, se_s, de_s, 0, small, se_f)
    small = small_stage(2, se_s, de_s, 0)
    st2a = late_second(0, st1a)
    small_take(0, sl_s, dl_s, 1, small_l, sl_f)
    small_l = small_stage(1, sl_s, dl_s, 1)
    st2b = late_second(1, st1b)
    for copy in st2e:
        copy.wait()
    for p in range(3):
        got = second(s1_s, r2e, range(4), p, early_peer(me, 1, p, 1)[0])

        @pl.when(core == 0)
        def _():
            for c in range(4):
                t3e[p, c] = jnp.concatenate(
                    [got[k][12 * c : 12 * c + 12] for k in range(4)], axis=0
                ).astype(BF16)

        @pl.when(core == 1)
        def _():
            for c in range(4):
                t3e[p, c] = got[c].astype(BF16)

    st3e = stage_sends(2, lambda p, o, c: (t3e.at[p, c], r3e.at[o - 1, p]), 0)
    small_take(2, se_s, de_s, 0, small, se_f)
    spread(se_f, se_out, 10)
    ends.append(
        remote(de_s.at[core], de_s.at[core], pair_sem.at[16, 0], pair_sem.at[16, 1], other)
    )
    ends[-1].start()
    small_take(1, sl_s, dl_s, 1, small_l, sl_f)
    small_l = small_stage(2, sl_s, dl_s, 1)
    st3a = late_third(0, st2a)
    st3b = late_third(1, st2b)
    finish(st3e, t3e, r3e, fe_s, fe_out, 17, [early_peer(me, 2, p, 1)[0] for p in range(3)])
    late_total(0, st3a)
    late_total(1, st3b)
    spread(fl_s, fl_out, 18)
    small_take(2, sl_s, dl_s, 1, small_l, sl_f)
    spread(sl_f, sl_out, 13)
    ends.append(
        remote(dl_s.at[core], dl_s.at[core], pair_sem.at[14, 0], pair_sem.at[14, 1], other)
    )
    ends[-1].start()
    for which in range(2):
        give_back(which, lambda make, local: None if local else make().wait_send())
        for item_slot in range(2):
            out = (oret_out, iret_out)[which]
            arrived(out.at[item_slot], ret_recv.at[which, item_slot])
    for copy in ends:
        copy.wait()
    last = [
        pltpu.make_async_copy(de_s, de_out, loc.at[11]),
        pltpu.make_async_copy(dl_s, dl_out, loc.at[14]),
    ]
    for copy in last:
        copy.start()
    for copy in last:
        copy.wait()


def back_call(
    da, qkv, p, hcg, h, x, dx, mod, times, w, mw, taps, perm, o, s1, last, dbr, at, s2, sb
):
    G = (2, 8, 2, 16)
    shape = jax.ShapeDtypeStruct
    V = pltpu.VMEM
    items = (2, 4, 4, 4, 16, 128)
    DMA = pltpu.SemaphoreType.DMA
    return pl.pallas_call(
        back_kernel,
        in_specs=[
            ANY_SPEC, ANY_SPEC, ANY_SPEC, ANY_SPEC, ANY_SPEC, ANY_SPEC, ANY_SPEC, VMEM_SPEC,
            SMEM_SPEC, ANY_SPEC, ANY_SPEC, VMEM_SPEC, ANY_SPEC, ANY_SPEC, ANY_SPEC, ANY_SPEC,
            ANY_SPEC, ANY_SPEC, VMEM_SPEC, VMEM_SPEC,
        ],
        out_specs=[ANY_SPEC] * 8,
        out_shape=[
            shape((2, 256, D), BF16), shape((2, 256, D), BF16),
            shape((2, 3, 48, 256), F32), shape((2, 3, 64, 128), F32),
            shape((2, 32, D), F32), shape((2, 16, 384), F32),
            shape(items, BF16), shape(items, BF16),
        ],
        scratch_shapes=[
            V(G + (3 * D,), BF16), V((24, 256, 256), BF16), V((D, 3 * D), BF16),
            V(mw.shape, BF16), V((3, D, D), BF16), V(G + (D,), BF16), V(G + (3 * D,), BF16),
            V((3, D, 512), BF16), V(G + (D,), BF16), V((9, 2, 2, 16, D), BF16), V((512, D), F32),
            V((512, D), BF16), V((2, 256, D), BF16), V((2, 256, D), BF16),
            V((2, 3, 4, D, 128), BF16), V((3, 4, D, 128), BF16), V((3, 4, 192, 256), BF16),
            V((3, 3, 192, 256), BF16), V((3, 3, 4, 192, 128), BF16), V((3, 4, 192, 128), BF16),
            V((3, 3, 4, 48, 256), BF16), V((3, 3, 4, 48, 128), BF16), V((3, 4, 48, 256), BF16),
            V((3, 4, 48, 128), BF16), V((3, 4, 16, 128), BF16), V((3, 3, 48, 256), BF16),
            V((3, 3, 48, 128), BF16), V((3, 3, 16, 128), BF16), V((3, 48, 256), F32),
            V((3, 64, 128), F32),
            V((2, 8, D), F32), V((16, D), F32),
            V((2, 32, D), BF16), V((32, D), BF16), V((12, 32, D), BF16), V((32, D), F32),
            V((2, 16, 384), BF16), V((16, 384), BF16), V((12, 16, 384), BF16), V((16, 384), F32),
            V((8, D), F32), V((8, D), F32), V((8, D), F32), V((8, D), F32), V((8, D), F32),
            V(items, BF16), V(items, BF16),
            V((512, D), BF16), V((576, D), BF16), V((576, D), BF16), V((512, D), F32),
            V((512, D), BF16), V((3, 4, 192, 256), BF16), V((512, D), BF16), V((576, D), BF16),
            DMA((35,)), DMA((19, 2)), DMA((2, 2)), DMA((2, 2)), DMA((3, 3, 3, 3)),
            DMA((3, 3, 3, 3)), DMA((2, 3, 3)), DMA((2, 3, 3)), DMA((2, 3, 3)), DMA((2, 3, 3)),
        ],
        compiler_params=pltpu.CompilerParams(
            collective_id=2, has_side_effects=True, vmem_limit_bytes=60 * 2**20
        ),
        name="back",
    )(da, qkv, p, hcg, h, x, dx, mod, times, w, mw, taps, perm, o, s1, last, dbr, at, s2, sb)


def share_kernel(
    out_ref, ig_ref, fe_hbm, fl_hbm, se_hbm, sl_hbm, de_hbm, dl_hbm,
    o_out, ig_out, cond_out, table_out, mw_out, mb_out, aw_out, ab_out, qkv_out, qb_out, vb_out,
    ow_out, ob_out, f1_out, f1b_out, fw_out, fb_out, f2_out, f2b_out,
    ig_s, o_s, igf_s, e_s, l_s, fe_ref, fl_ref, se_ref, sl_ref, de_ref, dl_ref, sem,
):
    me = spot()
    core = me["core"]
    shard = me["dp"] * 4 + me["seq"]
    ig_load = pltpu.make_async_copy(ig_ref, ig_s, sem.at[0])
    o_load = pltpu.make_async_copy(out_ref, o_s, sem.at[9])
    o_move = pltpu.make_async_copy(o_s, o_out, sem.at[1])
    loads = [
        pltpu.make_async_copy(*pair, sem.at[3 + at])
        for at, pair in enumerate((
            (fe_hbm, fe_ref), (fl_hbm, fl_ref), (se_hbm, se_ref), (sl_hbm, sl_ref),
            (de_hbm, de_ref), (dl_hbm, dl_ref),
        ))
    ]
    for load in loads:
        load.start()
    ig_load.start()
    o_load.start()
    o_load.wait()
    o_move.start()
    ig_load.wait()
    igf_s[...] = ig_s[...].astype(F32)
    ig_move = pltpu.make_async_copy(igf_s, ig_out, sem.at[2])
    ig_move.start()
    for load in loads:
        load.wait()
    e_s[...] = de_ref[...].reshape(2048, 128).astype(F32)
    l_s[...] = dl_ref[...].reshape(2048, 128).astype(F32)

    def six(v, at):
        return jnp.where(core == 0, v[at : at + 6], v[at + 6 : at + 12])

    for p in range(3):
        early0, early1 = fe_ref[0, p], fe_ref[1, p]
        for i in range(4):
            at = D * i + 256 * p
            f1_out[:, at : at + 256] = six(early0, 12 * i)
        f2_out[:, 256 * p : 256 * p + 256] = jnp.where(core == 0, early1[0:24], early1[24:48])
        for which in range(2):
            late = fl_ref[which, p]
            for group in range(2):
                for u, block in enumerate(LATE[which][group][p]):
                    got = six(late, 48 if group else 12 * u)
                    if isinstance(block, str):
                        at = 128 * int(block[1])
                        ow_out[:, at : at + 128] = got
                    else:
                        qkv_out[:, 128 * block : 128 * block + 128] = got

    def columns(start, count=D):
        at = lax.broadcasted_iota(jnp.int32, (count, 128), 0)
        to = lax.broadcasted_iota(jnp.int32, (count, 128), 1)
        return at == start + to

    def exact(a, b):
        return lax.dot_general(
            a, b.astype(F32), (((1,), (0,)), ((), ())), preferred_element_type=F32,
            precision=lax.Precision.HIGHEST,
        )

    mine = columns(shard * 6)
    slim = exact(jnp.concatenate((sl_ref[0], sl_ref[1]), axis=1), mine)
    aw_out[...] = slim.T[0:6, 0:9]
    for ref, at in ((ab_out, 9), (qb_out, 10), (vb_out, 11), (ob_out, 12), (f2b_out, 13)):
        ref[...] = slim[at : at + 1, 0:6].reshape(6)
    quarter = shard // 32
    wide = se_ref[quarter // 2, pl.ds(pl.multiple_of(quarter % 2 * 16, 16), 16), :]
    wide = exact(wide, columns(shard % 32 * 24))
    fw_out[...] = wide[0:9, 0:24]
    fb_out[...] = wide[9:10, 0:24].reshape(24)
    f1b_out[...] = wide[10:11, 0:24].reshape(24)

    def item_rows(ref, at):
        return ref[pl.ds(at // 16 * 1024 + at % 16, 64, stride=16), :]

    silu = jnp.concatenate([item_rows(e_s, 24 + l) for l in range(6)], axis=1)
    silu = mm(silu.astype(BF16), mine.astype(BF16)).astype(BF16)
    sums = []
    for at in range(36):
        d_mod = item_rows(l_s, at) if at < 12 else item_rows(e_s, at - 12)
        mw_out[:, 128 * at : 128 * at + 128] = mm_tn(silu, d_mod.astype(BF16))[0:6]
        sums.append(jnp.sum(d_mod, axis=0, keepdims=True))
    total = jnp.concatenate(sums, axis=1)
    total = exact(jnp.concatenate([total] * 8, axis=0), columns(shard * 36, 6 * D))
    mb_out[...] = total[0:1, 0:36].reshape(36)

    cond = jnp.concatenate([item_rows(l_s, 16 + l) for l in range(6)], axis=1).astype(BF16)
    here = lax.broadcasted_iota(jnp.int32, (8, 64), 1)
    slot = lax.broadcasted_iota(jnp.int32, (8, 64), 0)
    own = here == (me["y"] * 4 + me["x"]) * 4 + slot * 2 + me["zl"]
    own = jnp.logical_and(own, slot < 2)
    cond_out[...] = mm(own.astype(BF16), cond)[0:2]
    times = 32.0 * item_rows(e_s, 30) + item_rows(e_s, 31)
    bucket = lax.broadcasted_iota(jnp.int32, (64, 1024), 1).astype(F32)
    hot = (bucket == jnp.concatenate([times] * 8, axis=1)).astype(BF16)
    my_cond = mm(cond, mine.astype(BF16)).astype(BF16)
    table_out[...] = mm_tn(my_cond, hot)[0:6, 0 : table_out.shape[1]]

    ig_move.wait()
    o_move.wait()


def share_call(buckets, *args):
    shapes = [
        ((2, 256, D), BF16), ((2, 256, D), F32), ((2, D), F32), ((6, buckets), F32),
        ((6, 6 * D), F32), ((36,), F32), ((6, 9), F32), ((6,), F32), ((6, 3 * D), F32),
        ((6,), F32), ((6,), F32), ((6, D), F32), ((6,), F32), ((6, FF), F32), ((24,), F32),
        ((9, 24), F32), ((24,), F32), ((24, D), F32), ((6,), F32),
    ]
    return pl.pallas_call(
        share_kernel,
        in_specs=[ANY_SPEC] * 8,
        out_specs=[ANY_SPEC] * 2 + [VMEM_SPEC] * 17,
        out_shape=[jax.ShapeDtypeStruct(*s) for s in shapes],
        scratch_shapes=[
            pltpu.VMEM((2, 256, D), BF16), pltpu.VMEM((2, 256, D), BF16),
            pltpu.VMEM((2, 256, D), F32), pltpu.VMEM((2048, 128), F32), pltpu.VMEM((2048, 128), F32),
            *[pltpu.VMEM(v.shape, v.dtype) for v in args[2:]],
            pltpu.SemaphoreType.DMA((10,)),
        ],
        compiler_params=pltpu.CompilerParams(vmem_limit_bytes=60 * 2**20),
        name="share",
    )(*args)


def perm_matrices():
    at = np.arange(D)
    rows = []
    for order in ORDERS:
        spots = dict(zip(order, (at // 192, at // 48 % 4, at // 12 % 4)))
        x, y, z = spots["x"], spots["y"], spots["z"]
        rows.append((((x * 2 + z % 2) * 4 + y) * 2 + z // 2) * 12 + at % 12)
    return np.stack(rows).astype(np.int32)


def local(
    latents, conditioning, timesteps, item_counts, cotangent, time_table, mod_weight, mod_bias,
    conv_attn_weight, conv_attn_bias, qkv_weight, query_bias, value_bias, out_weight, out_bias,
    fc1_weight, fc1_bias, conv_ffn_weight, conv_ffn_bias, fc2_weight, fc2_bias,
):
    alive = (lax.axis_index("seq") // 2 < item_counts).astype(F32)
    perm = (perm_matrices()[:, :, None] == np.arange(D)[None, None, :]).astype(BF16)
    x, ct, h, hcg, qkv, p, at, mod = attn_call(
        latents.reshape(2, 256, D), cotangent.reshape(2, 256, D), conditioning, timesteps,
        time_table, mod_weight, mod_bias, qkv_weight, query_bias, value_bias, conv_attn_weight,
        conv_attn_bias,
    )
    at = at.reshape(576, D)
    out, s1, last, dbr, da, dx, s2, sb = ffn_call(
        x, at, ct, mod, alive, perm, out_weight, out_bias, fc1_weight, fc1_bias, conv_ffn_weight,
        conv_ffn_bias, fc2_weight, fc2_bias,
    )
    got = back_call(
        da, qkv, p, hcg.reshape(512, D), h, x, dx, mod, timesteps,
        qkv_weight, mod_weight, conv_attn_weight, perm, out, s1, last,
        dbr.reshape(512, D), at, s2, sb,
    )
    outs = list(share_call(time_table.shape[0], *got))
    outs[0], outs[1] = outs[0].reshape(latents.shape), outs[1].reshape(latents.shape)
    outs[3], outs[6] = outs[3].T, outs[6].T
    return tuple(outs)


def solution(mesh):
    return jax.shard_map(
        local,
        mesh=mesh,
        in_specs=(
            P("dp", "seq", None, None),
            P("dp", None),
            P("dp"),
            P("dp"),
            P("dp", "seq", None, None),
            P(),
            P(),
            P(),
            P(),
            P(),
            P(),
            P(),
            P(),
            P(),
            P(),
            P(),
            P(),
            P(),
            P(),
            P(),
            P(),
        ),
        out_specs=(
            P("dp", "seq", None, None),
            P("dp", "seq", None, None),
            P("dp", None),
            P(None, ("dp", "seq")),
            P(("dp", "seq"), None),
            P(("dp", "seq")),
            P(None, ("dp", "seq")),
            P(("dp", "seq")),
            P(("dp", "seq"), None),
            P(("dp", "seq")),
            P(("dp", "seq")),
            P(("dp", "seq"), None),
            P(("dp", "seq")),
            P(("dp", "seq"), None),
            P(("dp", "seq")),
            P(None, ("dp", "seq")),
            P(("dp", "seq")),
            P(("dp", "seq"), None),
            P(("dp", "seq")),
        ),
        check_vma=False,
    )
```

```python
import functools

import jax
import jax.numpy as jnp
import numpy as np
from jax import lax
from jax.experimental import pallas as pl
from jax.experimental.pallas import tpu as pltpu
from jax.sharding import PartitionSpec as P

F32 = jnp.float32
BF16 = jnp.bfloat16
D = 768
FF = 3072
FC = 768
NFC = FF // FC
EPS = 1e-6
VMEM_SPEC = pl.BlockSpec(memory_space=pltpu.VMEM)
ANY_SPEC = pl.BlockSpec(memory_space=pl.ANY)
SMEM_SPEC = pl.BlockSpec(memory_space=pltpu.SMEM)


def mm(a, b):
    return lax.dot_general(a, b, (((1,), (0,)), ((), ())), preferred_element_type=F32)


def mm_nt(a, b):
    return lax.dot_general(a, b, (((1,), (1,)), ((), ())), preferred_element_type=F32)


def mm_tn(a, b):
    return lax.dot_general(a, b, (((0,), (0,)), ((), ())), preferred_element_type=F32)


def row(v):
    return v.astype(F32).reshape(1, v.shape[0])


def fold8(v):
    total = v[0:8]
    for at in range(8, v.shape[0], 8):
        total = total + v[at : at + 8]
    return total


def norm_parts(v):
    center = v - jnp.mean(v, axis=-1, keepdims=True)
    rs = lax.rsqrt(jnp.mean(center * center, axis=-1, keepdims=True) + EPS)
    return center * rs, rs


def by_core(taps, at, core):
    return jnp.where(core == 1, taps[3 * (2 - at // 3) + at % 3], taps[at])


def gelu_pair(v):
    d = 1.0 + 0.23164189 * jnp.abs(v)
    t = pl.reciprocal(d, approx=True)
    t = t * (2.0 - d * t)
    e = jnp.exp2(-0.7213475204444817 * (v * v))
    poly = t * (
        0.127414796
        + t * (-0.142248368 + t * (0.7107068705 + t * (-0.7265760135 + t * 0.5307027145)))
    )
    tail = poly * e
    cdf = jnp.where(v >= 0, 1.0 - tail, tail)
    return v * cdf, cdf + v * (e * 0.3989422804014327)


def side_masks():
    place = lax.broadcasted_iota(jnp.int32, (16, 128), 0)
    return place == 0, place == 15


def with_sides(even, odd, masks):
    left = jnp.where(masks[0], 0.0, pltpu.roll(odd, 1, 0))
    right = jnp.where(masks[1], 0.0, pltpu.roll(even, 15, 0))
    return even, odd, left, right


def conv_row(rows, taps):
    even = odd = None
    for a in range(3):
        if rows[a] is None:
            continue
        ev, od, left, right = rows[a]
        for tap, ce, co in ((3 * a, left, ev), (3 * a + 1, ev, od), (3 * a + 2, od, right)):
            even = taps[tap] * ce if even is None else even + taps[tap] * ce
            odd = taps[tap] * co if odd is None else odd + taps[tap] * co
    return even, odd


def with_sides_low(even, odd, masks):
    left = jnp.where(masks[0], 0.0, pltpu.roll(odd.astype(F32), 1, 0)).astype(BF16)
    right = jnp.where(masks[1], 0.0, pltpu.roll(even.astype(F32), 15, 0)).astype(BF16)
    return even, odd, left, right


def tap_pairs(held, rows, d_even, d_odd):
    out = []
    for a in range(3):
        if rows[a] is None:
            out += [None] * 3
            continue
        ev, od, left, right = rows[a]
        for ce, co in ((left, ev), (ev, od), (od, right)):
            out.append(d_even * ce + d_odd * co)
    if held is None:
        return out
    return [b if a is None else a if b is None else a + b for a, b in zip(held, out)]


def tap_products(sums, rows, d_even, d_odd):
    for a in range(3):
        if rows[a] is None:
            continue
        ev, od, left, right = rows[a]
        for tap, ce, co in ((3 * a, left, ev), (3 * a + 1, ev, od), (3 * a + 2, od, right)):
            term = fold8(d_even * ce + d_odd * co)
            sums[tap] = term if sums[tap] is None else sums[tap] + term


MESH = pl.DeviceIdType.MESH


def spot():
    dp = lax.axis_index("dp")
    seq = lax.axis_index("seq")
    x, zl, y, zh, core = dp >> 3, (dp >> 2) & 1, dp & 3, seq >> 1, seq & 1
    z = zh * 2 + zl
    me = dict(dp=dp, seq=seq, x=x, zl=zl, y=y, zh=zh, z=z, core=core)
    for o in (1, 2, 3):
        me["x", o] = ((((x + o) & 3) << 3) + (dp & 7), seq)
        me["y", o] = ((dp & 28) + ((y + o) & 3), seq)
        to = (z + o) & 3
        me["z", o] = ((dp & 27) + ((to & 1) << 2), (to & 2) + core)
    return me


def seq_peer(me, zh, core):
    return (me["dp"], zh * 2 + core)


def axis_peer(me, axis, offset):
    return me[axis, offset]


def remote(src, dst, send, recv, device):
    return pltpu.make_async_remote_copy(
        src_ref=src, dst_ref=dst, send_sem=send, recv_sem=recv, device_id=device,
        device_id_type=MESH,
    )


def arrived(ref, sem):
    pltpu.make_async_copy(ref, ref, sem).wait()


def hail(peers):
    barrier = pltpu.get_barrier_semaphore()
    for peer in peers:
        pl.semaphore_signal(barrier, inc=1, device_id=peer, device_id_type=MESH)


def heard(count):
    pl.semaphore_wait(pltpu.get_barrier_semaphore(), count)


def greet(peers):
    hail(peers)
    heard(len(peers))


ORDERS = (("x", "y", "z"), ("y", "x", "z"), ("z", "x", "y"))
EARLY = (
    (("x", "y", "z"), ("x", "y", "z"), ("y", "x", "z")),
    (("y", "x", "z"), ("z", "x", "y"), ("z", "x", "y")),
)


LATE = (
    (((0, 1, 2), (3, 6, 7), (8, 9, "g0")), ((4,), (5,), (10,))),
    (((12, 13, 14), (15, "g1", "g2"), ("g3", "g4", "g5")), ((11,), (16,), (17,))),
)


def axis_spot(me, axis):
    return me[axis]


def early_peer(me, stage, part, offset):
    key = (stage, part, offset)
    if key not in me:
        first, second = (EARLY[which][part][stage] for which in range(2))
        if first == second:
            me[key] = me[first], me[first, offset]
        else:
            pick = lambda a, b: jnp.where(me["core"] == 0, a, b)
            peer = tuple(pick(a, b) for a, b in zip(me[first, offset], me[second, offset]))
            me[key] = pick(me[first], me[second]), peer
    return me[key]


def ffn_kernel(
    x_ref, at_ref, ct_hbm, mod_ref, alive_ref, perm_hbm, ow_ref, ob_ref, f1_ref, f1b_ref,
    tap_ref, cb_ref, f2_ref, f2b_ref,
    out_hbm, s1_ref, last_ref, dbr_hbm, da_ref, dx_hbm, s2_ref, sm_ref,
    x1_s, br_s, h2_s, h2t_s, dffn_s, u_s, duc_s, act_s, du_s, dact_s, ffn_s, dh2_s, acc_s,
    ch_s, pre_s, r1_s, bias_s, das_s, dar_s, ct_ref, perm_ref, out_ref, dbr_ref, dx_ref, pair_sem, st_send, st_recv, loc,
):
    step = pl.program_id(0)
    me = spot()
    core = me["core"]
    other = seq_peer(me, me["zh"], 1 - core)
    for p in range(3):
        for o in (1, 2, 3):
            early_peer(me, 0, p, o)
    alive = alive_ref[0]

    ct_load = pltpu.make_async_copy(ct_hbm, ct_ref, loc.at[0])
    perm_load = pltpu.make_async_copy(perm_hbm.at[pl.ds(0, 2)], perm_ref, loc.at[1])

    @pl.when(step == 0)
    def _():
        ct_load.start()
        perm_load.start()
        bias_s[0:1, :] = row(f1b_ref[...])
        bias_s[1:2, :] = row(cb_ref[...])
        hail([axis_peer(me, axis, o) for axis in "xyz" for o in (1, 2, 3)] + [other])

    def pair_copy(at):
        slot = at % 2
        return remote(
            ch_s.at[slot, 1 - core], pre_s.at[slot], pair_sem.at[slot, 0], pair_sem.at[slot, 1],
            other,
        )

    def first_copies(at):
        slot = at % 2
        out = []
        for p in range(3):
            for o in (1, 2, 3):
                here, peer = early_peer(me, 0, p, o)
                out.append(
                    remote(
                        ch_s.at[slot, core, p, (here + o) & 3], r1_s.at[at, o - 1, p],
                        st_send.at[at, p, o - 1], st_recv.at[at, p, o - 1], peer,
                    )
                )
        return out

    def pair_add(at):
        slot = at % 2
        pair_copy(at).wait()
        for p in range(3):

            def add(a, _):
                ch_s[slot, core, p, a] = ch_s[slot, core, p, a] + pre_s[slot, p, a]
                return 0

            lax.fori_loop(0, 4, add, 0)

    def first_send(at):
        pair_add(at)
        for copy in first_copies(at):
            copy.start()

    def first_take(at):
        slot = at % 2
        for copy in first_copies(at):
            copy.wait()
        for p in range(3):
            here, _peer = early_peer(me, 0, p, 1)
            total = ch_s[slot, core, p, here].astype(F32)
            for o in range(3):
                total = total + r1_s[at, o, p].astype(F32)
            total = total.astype(BF16)

            @pl.when(core == 0)
            def _():
                s1_ref[p, at] = total

            @pl.when(core == 1)
            def _():
                for c in range(4):
                    s1_ref[p, c, pl.ds(pl.multiple_of(at * 48, 16), 48)] = total[
                        48 * c : 48 * c + 48
                    ]

    @pl.when(step == 0)
    def _():
        br_s[...] = mm(at_ref[...], ow_ref[...]) + row(ob_ref[...])
        shift2, scale2, gate1, gate2 = (mod_ref[i : i + 1, :] for i in (3, 4, 2, 5))

        def rows_a(r, _):
            at = pl.ds(pl.multiple_of(r * 96, 96), 96)
            x1 = x_ref[at, :].astype(F32) + gate1 * br_s[at, :]
            x1_s[at, :] = x1
            n2, _unused = norm_parts(x1)
            h2_s[at, :] = (n2 * (1.0 + scale2) + shift2).astype(BF16)
            return 0

        lax.fori_loop(0, 6, rows_a, 0)

        ct_load.wait()

        def rows_b(r, _):
            at = pl.ds(pl.multiple_of(r * 272, 16), 272)
            dffn_s[at, :] = (ct_ref[at, :].astype(F32) * alive * gate2).astype(BF16)
            return 0

        lax.fori_loop(0, 2, rows_b, 0)
        perm_load.wait()
        for p in range(2):
            h2t_s[p] = mm_nt(perm_ref[p], h2_s[0:512, :]).astype(BF16)
        ffn_s[...] = jnp.zeros_like(ffn_s)
        dh2_s[...] = jnp.zeros_like(dh2_s)

    @pl.when(step == 0)
    def _():
        heard(10)

    masks = side_masks()

    def lanes(j):
        cols = slice(128 * j, 128 * j + 128)
        taps = tap_ref[:, cols].astype(F32)
        taps = [taps[t : t + 1] for t in range(9)]
        taps = [by_core(taps, t, core) for t in range(9)]
        taps = [jnp.broadcast_to(v, (16, 128)).astype(BF16) for v in taps]
        offset = bias_s[1:2, pl.ds(pl.multiple_of(step * FC + j * 128, 128), 128)]

        def sided(ref, l):
            return with_sides_low(
                ref[32 * l : 32 * l + 16, cols], ref[32 * l + 16 : 32 * l + 32, cols], masks
            )

        rows = [None, sided(u_s, 0), sided(u_s, 1)]
        sums = [None] * 9
        held = bias_sum = None
        for l in range(17):
            ce, co = conv_row(rows, taps)
            ae, ge = gelu_pair(ce.astype(F32) + offset)
            ao, go = gelu_pair(co.astype(F32) + offset)
            de = (ge * dact_s[32 * l : 32 * l + 16, cols]).astype(BF16)
            do = (go * dact_s[32 * l + 16 : 32 * l + 32, cols]).astype(BF16)
            duc_s[32 * l : 32 * l + 16, cols] = de
            duc_s[32 * l + 16 : 32 * l + 32, cols] = do
            if l < 16:
                act_s[32 * l : 32 * l + 16, cols] = ae.astype(BF16)
                act_s[32 * l + 16 : 32 * l + 32, cols] = ao.astype(BF16)
                held = tap_pairs(held if l % 2 else None, rows, de, do)
                if l % 2:
                    for t in range(9):
                        term = fold8(held[t].astype(F32))
                        sums[t] = term if sums[t] is None else sums[t] + term
                term = fold8(de.astype(F32) + do.astype(F32))
                bias_sum = term if bias_sum is None else bias_sum + term
                rows = [rows[1], rows[2], sided(u_s, l + 2) if l + 2 < 18 else None]
        for t in range(9):
            s2_ref[t : t + 1, cols] = jnp.sum(by_core(sums, t, core), axis=0, keepdims=True)
        s2_ref[9:10, cols] = jnp.sum(bias_sum, axis=0, keepdims=True)
        back = [taps[8 - t] for t in range(9)]
        rows = [None, sided(duc_s, 0), sided(duc_s, 1)]
        bias_sum = None
        for l in range(16):
            ue, uo = conv_row(rows, back)
            du_s[32 * l : 32 * l + 16, cols] = ue
            du_s[32 * l + 16 : 32 * l + 32, cols] = uo
            term = fold8(ue.astype(F32) + uo.astype(F32))
            bias_sum = term if bias_sum is None else bias_sum + term
            rows = [rows[1], rows[2], sided(duc_s, l + 2) if l + 2 < 17 else None]
        s2_ref[10:11, cols] = jnp.sum(bias_sum, axis=0, keepdims=True)

    slot = step % 2

    def into(j):
        cols = slice(256 * j, 256 * j + 256)
        offset = bias_s[0:1, pl.ds(pl.multiple_of(step * FC + 256 * j, 256), 256)]
        u_s[:, cols] = (mm(h2_s[...], f1_ref[:, cols]) + offset).astype(BF16)
        dact_s[:, cols] = mm_nt(dffn_s[...], f2_ref[cols, :])

    def out_of(j):
        cols = slice(256 * j, 256 * j + 256)
        got = mm(h2t_s[j // 2], du_s[:, cols]).astype(BF16)
        ch_s[slot, 0, j] = got.reshape(4, 192, 256)
        grad = mm_tn(act_s[:, cols], dffn_s[0:512, :]).astype(BF16)
        for at in range(0, 256, 16):
            chip, inner = (256 * j + at) // 48, (256 * j + at) % 48
            zl, y, zh = chip // 8, chip // 2 % 4, chip % 2
            z = zh * 2 + zl
            for part in range(3):
                a, c = (y, z) if part == 0 else (z, y)
                ch_s[slot, 1, part, a, 48 * c + inner : 48 * c + inner + 16] = grad[
                    at : at + 16, 256 * part : 256 * part + 256
                ]
        ffn_s[...] += mm(act_s[:, cols], f2_ref[cols, :])
        dh2_s[...] += mm_nt(du_s[:, cols], f1_ref[:, cols])

    into(0)
    into(1)
    lanes(0)
    lanes(1)
    into(2)

    @pl.when(step > 1)
    def _():
        first_take(step - 2)

    out_of(0)

    @pl.when(step > 0)
    def _():
        first_send(step - 1)

    lanes(2)
    lanes(3)
    out_of(1)
    lanes(4)
    lanes(5)
    out_of(2)
    pair_copy(step).start()

    @pl.when(step == NFC - 1)
    def _():
        shift2, scale2, gate1, gate2 = (mod_ref[i : i + 1, :] for i in (3, 4, 2, 5))
        acc_s[...] = jnp.zeros_like(acc_s)
        f2b = row(f2b_ref[...])

        def rows_c(r, _):
            at = pl.ds(pl.multiple_of(r * 128, 128), 128)
            x1 = x1_s[at, :]
            ffn = ffn_s[at, :] + f2b
            dy = ct_ref[at, :].astype(F32) * alive
            out_ref[at, :] = (alive * (x1 + gate2 * ffn)).astype(BF16)
            n2, rs = norm_parts(x1)
            dh2 = dh2_s[at, :]
            g2 = dh2 * (1.0 + scale2)
            dx1 = dy + rs * (
                g2
                - jnp.mean(g2, axis=-1, keepdims=True)
                - n2 * jnp.mean(g2 * n2, axis=-1, keepdims=True)
            )
            dx_ref[at, :] = dx1
            dbr = (dx1 * gate1).astype(BF16)
            dbr_ref[pl.ds(2 * r, 2)] = dbr.reshape(2, 2, 2, 16, D)
            acc_s[0] += fold8(dx1 * br_s[at, :])
            acc_s[1] += fold8(dh2)
            acc_s[2] += fold8(dh2 * n2)
            acc_s[3] += fold8(dy * ffn)
            acc_s[4] += fold8(dbr.astype(F32))
            acc_s[5] += fold8(dffn_s[at, :].astype(F32))
            return 0

        lax.fori_loop(0, 4, rows_c, 0)
        for i in range(6):
            sm_ref[i : i + 1, :] = jnp.sum(acc_s[i], axis=0, keepdims=True)
        moves = [
            pltpu.make_async_copy(out_ref, out_hbm, loc.at[2]),
            pltpu.make_async_copy(dbr_ref, dbr_hbm, loc.at[3]),
            pltpu.make_async_copy(dx_ref, dx_hbm, loc.at[4]),
        ]
        for copy in moves:
            copy.start()
        halves = [dbr_ref[:, parity].reshape(256, D) for parity in range(2)]
        odd = mm_nt(halves[1], ow_ref[...]).astype(BF16)
        das_s[...] = odd.reshape(8, 2, 16, D)
        da_copy = remote(das_s, dar_s, pair_sem.at[2, 0], pair_sem.at[2, 1], other)
        da_copy.start()
        da_ref[0] = mm_nt(halves[0], ow_ref[...]).astype(BF16).reshape(8, 2, 16, D)
        pair_add(step)
        last_ref[...] = ch_s[step % 2, core]
        first_take(step - 1)
        da_copy.wait()
        da_ref[1] = dar_s[...]
        for copy in moves:
            copy.wait()


def ffn_call(x, at, ct, mod, alive, perm, ow, ob, f1, f1b, taps, cb, f2, f2b):
    whole = lambda s: pl.BlockSpec(s, lambda i: (0,) * len(s))
    return pl.pallas_call(
        ffn_kernel,
        grid=(NFC,),
        in_specs=[
            whole((576, D)), whole((576, D)), ANY_SPEC, whole((8, D)),
            pl.BlockSpec(memory_space=pltpu.SMEM),
            ANY_SPEC, whole((D, D)), whole((D,)),
            pl.BlockSpec((D, FC), lambda i: (0, i)),
            whole((FF,)),
            pl.BlockSpec((9, FC), lambda i: (0, i)),
            whole((FF,)),
            pl.BlockSpec((FC, D), lambda i: (i, 0)),
            whole((D,)),
        ],
        out_specs=[
            ANY_SPEC,
            whole((3, 4, 192, 256)), whole((3, 4, 192, 256)),
            ANY_SPEC, whole((2, 8, 2, 16, D)), ANY_SPEC,
            pl.BlockSpec((16, FC), lambda i: (0, i)),
            whole((8, D)),
        ],
        out_shape=[
            jax.ShapeDtypeStruct((512, D), BF16),
            jax.ShapeDtypeStruct((3, 4, 192, 256), BF16),
            jax.ShapeDtypeStruct((3, 4, 192, 256), BF16),
            jax.ShapeDtypeStruct((8, 2, 2, 16, D), BF16),
            jax.ShapeDtypeStruct((2, 8, 2, 16, D), BF16),
            jax.ShapeDtypeStruct((512, D), F32),
            jax.ShapeDtypeStruct((16, FF), F32),
            jax.ShapeDtypeStruct((8, D), F32),
        ],
        scratch_shapes=[
            pltpu.VMEM((576, D), F32), pltpu.VMEM((576, D), F32), pltpu.VMEM((576, D), BF16),
            pltpu.VMEM((2, D, 512), BF16), pltpu.VMEM((544, D), BF16),
            pltpu.VMEM((576, FC), BF16), pltpu.VMEM((544, FC), BF16), pltpu.VMEM((512, FC), BF16),
            pltpu.VMEM((512, FC), BF16), pltpu.VMEM((544, FC), F32),
            pltpu.VMEM((512, D), F32), pltpu.VMEM((512, D), F32), pltpu.VMEM((6, 8, D), F32),
            pltpu.VMEM((2, 2, 3, 4, 192, 256), BF16), pltpu.VMEM((2, 3, 4, 192, 256), BF16),
            pltpu.VMEM((3, 3, 3, 192, 256), BF16), pltpu.VMEM((8, FF), F32),
            pltpu.VMEM((8, 2, 16, D), BF16), pltpu.VMEM((8, 2, 16, D), BF16),
            pltpu.VMEM((576, D), BF16), pltpu.VMEM((2, D, D), BF16), pltpu.VMEM((512, D), BF16),
            pltpu.VMEM((8, 2, 2, 16, D), BF16), pltpu.VMEM((512, D), F32),
            pltpu.SemaphoreType.DMA((3, 2)),
            pltpu.SemaphoreType.DMA((3, 3, 3)), pltpu.SemaphoreType.DMA((3, 3, 3)),
            pltpu.SemaphoreType.DMA((5,)),
        ],
        compiler_params=pltpu.CompilerParams(
            dimension_semantics=("arbitrary",), vmem_limit_bytes=60 * 2**20,
            collective_id=3, has_side_effects=True,
        ),
        name="ffn",
    )(x, at, ct, mod, alive, perm, ow, ob, f1, f1b, taps, cb, f2, f2b)


def place_matrix(count, flip, inverse):
    rows = count // 32
    out = lax.broadcasted_iota(jnp.int32, (count, count), 0)
    at = lax.broadcasted_iota(jnp.int32, (count, count), 1)
    row = out // 32
    row = jnp.where(flip, rows - 1 - row, row)
    low = out % 32
    if inverse:
        low = (low % 2) * 16 + low // 2
    else:
        low = (low % 16) * 2 + low // 16
    return jnp.where(at == row * 32 + low, 1.0, 0.0).astype(BF16)


def head_lanes(values, half):
    lane = lax.broadcasted_iota(jnp.int32, values.shape, 1)
    return jnp.where((lane // 64) == half, values, jnp.zeros_like(values))


def attn_kernel(
    lat_ref, ct_ref, cond_ref, time_ref, table_ref, mw_ref, mb_ref, w_ref, qb_ref, vb_ref,
    tap_ref, cb_ref,
    x_out, ct_out, h_out, hcg_out, qkv_out, p_out, at_out, mod_out,
    xr_s, xh_s, x_s, c_s, h_s, hcg_s, sb_s, w_s, qkv_s, p_s, ag_s, at_s, mod_s, table_s, mw_s, cb_s,
    send0, recv0, sem_pair, sem_loc,
):
    me = spot()
    zh, core, seq = me["zh"], me["core"], me["seq"]
    other = seq_peer(me, zh, 1 - core)
    w_load = pltpu.make_async_copy(w_ref, w_s, sem_loc.at[0])
    table_load = pltpu.make_async_copy(table_ref, table_s, sem_loc.at[10])
    mw_load = pltpu.make_async_copy(mw_ref, mw_s, sem_loc.at[11])
    for copy in (table_load, mw_load, w_load):
        copy.start()

    greet(
        [
            seq_peer(me, (zh + dz) % 2, (core + dc) % 2)
            for dz, dc in ((0, 1), (1, 0), (1, 1))
        ]
    )
    slot = jnp.where(zh == 0, core, 1 - core)
    inner = jnp.logical_or(seq == 1, seq == 2)
    halo_core = jnp.where(seq == 1, 1, 0)
    halo_at = pl.multiple_of(jnp.where(seq == 1, 192, 0), 64)

    def sends(arrays, act):
        for a in arrays:
            ref = (lat_ref, ct_ref)[a]
            for j in range(2):
                own = jnp.logical_and(zh == j, core == zh)
                main = (ref.at[j], xr_s.at[a, slot])
                halo = (ref.at[j, pl.ds(halo_at, 64)], xh_s.at[a])

                @pl.when(own)
                def _():
                    act(lambda: pltpu.make_async_copy(*main, recv0.at[a, slot]), True)

                @pl.when(jnp.logical_not(own))
                def _():
                    act(
                        lambda: remote(*main, send0.at[a, j, 0], recv0.at[a, slot], seq_peer(me, j, zh)),
                        False,
                    )

                @pl.when(jnp.logical_and(inner, zh == j))
                def _():
                    act(lambda: pltpu.make_async_copy(*halo, recv0.at[a, 2]), True)

                @pl.when(jnp.logical_and(inner, zh != j))
                def _():
                    act(
                        lambda: remote(
                            *halo, send0.at[a, j, 1], recv0.at[a, 2], seq_peer(me, j, halo_core)
                        ),
                        False,
                    )

    sends((0,), lambda make, local: make().start())

    flip = core == 1
    big = place_matrix(256, flip, False)
    small = place_matrix(64, flip, False)

    table_load.wait()
    here = lax.broadcasted_iota(jnp.int32, (8, table_s.shape[0]), 1)
    one_hot = jnp.where(here == time_ref[zh], 1.0, 0.0).astype(BF16)
    cond = jnp.where(zh == 0, cond_ref[0:1, :], cond_ref[1:2, :]) + mm(one_hot, table_s[...])
    silu = (cond / (1.0 + jnp.exp(-cond))).astype(BF16)
    mw_load.wait()
    for i in range(6):
        cols = slice(D * i, D * i + D)
        mod_s[i : i + 1, :] = (mm(silu, mw_s[:, cols]) + row(mb_ref[cols]))[0:1]
    mod_s[6:7, :] = cond[0:1]
    mod_s[7:8, :] = silu[0:1].astype(F32)
    shift1, scale1 = mod_s[0:1, :], mod_s[1:2, :]

    def placed(a, into):
        for b in range(2):
            arrived(xr_s.at[a, b], recv0.at[a, b])
            into[256 * b : 256 * b + 256, :] = mm(big, xr_s[a, b]).astype(BF16)
        arrived(xh_s.at[a], recv0.at[a, 2])
        into[512:576, :] = mm(small, xh_s[a]).astype(BF16)

    placed(0, x_s)
    sends((1,), lambda make, local: make().start())

    def rows_a(r, _):
        at = pl.ds(pl.multiple_of(r * 96, 96), 96)
        n1, _unused = norm_parts(x_s[at, :].astype(F32))
        h_s[at, :] = (n1 * (1.0 + scale1) + shift1).astype(BF16)
        return 0

    lax.fori_loop(0, 6, rows_a, 0)
    outs = [
        pltpu.make_async_copy(x_s, x_out, sem_loc.at[1]),
        pltpu.make_async_copy(h_s, h_out, sem_loc.at[2]),
        pltpu.make_async_copy(mod_s, mod_out, sem_loc.at[12]),
    ]
    for copy in outs:
        copy.start()
    masks = side_masks()

    def lanes(j, _):
        cols = pl.ds(pl.multiple_of(j * 128, 128), 128)
        taps = tap_ref[:, cols].astype(F32)
        taps = [taps[t : t + 1] for t in range(9)]
        taps = [by_core(taps, t, core) for t in range(9)]
        offset = cb_s[0:1, cols]

        def sided(l):
            return with_sides(
                h_s[32 * l : 32 * l + 16, cols].astype(F32),
                h_s[32 * l + 16 : 32 * l + 32, cols].astype(F32),
                masks,
            )

        rows = [None, sided(0), sided(1)]
        for l in range(16):
            ce, co = conv_row(rows, taps)
            ce, co = (ce + offset).astype(BF16), (co + offset).astype(BF16)
            if l % 2 == 0:
                hcg_s[0, l // 2, 0, :, cols] = ce
                hcg_s[0, l // 2, 1, :, cols] = co
            else:
                sb_s[l // 2, 0, :, cols] = ce
                sb_s[l // 2, 1, :, cols] = co
            rows = [rows[1], rows[2], sided(l + 2) if l < 15 else None]
        return 0

    cb_s[0:1, :] = row(cb_ref[...])
    lax.fori_loop(0, D // 128, lanes, 0)
    hc_copy = remote(sb_s, hcg_s.at[1], sem_pair.at[0], sem_pair.at[1], other)
    hc_copy.start()
    w_load.wait()

    def project(half):
        for i, bias in enumerate((qb_ref, None, vb_ref)):
            cols = slice(D * i, D * i + D)
            got = mm(hcg_s[half].reshape(256, D), w_s[:, cols])
            if bias is not None:
                got = got + row(bias[...])
            qkv_s[half, :, :, :, cols] = got.astype(BF16).reshape(8, 2, 16, D)

    project(0)
    hc_copy.wait()
    outs.append(pltpu.make_async_copy(hcg_s, hcg_out, sem_loc.at[3]))
    outs[-1].start()
    project(1)
    outs.append(pltpu.make_async_copy(qkv_s, qkv_out, sem_loc.at[4]))
    outs[-1].start()

    def attend(pair, _):
        heads = [(pc, half) for pc in range(2) for half in range(2)]

        def part(which, pc):
            cols = pl.ds(pl.multiple_of(which * D + pair * 128, 128), 128)
            return jnp.concatenate(
                [qkv_s[half, :, pc, :, cols].reshape(128, 128) for half in range(2)], axis=0
            )

        q, k, v = ([part(which, pc) for pc in range(2)] for which in range(3))
        scores = [mm_nt(k[pc], head_lanes(q[pc], half)) * 0.125 for pc, half in heads]
        v_t = [v[pc].T for pc in range(2)]
        top = [jnp.max(n, axis=0, keepdims=True) for n in scores]
        e = [jnp.exp(n - m) for n, m in zip(scores, top)]
        scale = [1.0 / jnp.sum(n, axis=0, keepdims=True) for n in e]
        low = [(n * m).astype(BF16) for n, m in zip(e, scale)]
        for (pc, half), n in zip(heads, low):
            p_s[2 * (6 * pc + pair) + half] = n
        got = [mm(v_t[pc][64 * half : 64 * half + 64], n) for (pc, half), n in zip(heads, low)]
        cols = pl.ds(pl.multiple_of(pair * 128, 128), 128)
        for pc in range(2):
            o = jnp.concatenate(got[2 * pc : 2 * pc + 2], axis=0).T.astype(BF16)
            for half in range(2):
                ag_s[half, :, pc, :, cols] = o[128 * half : 128 * half + 128].reshape(8, 16, 128)
        return 0

    lax.fori_loop(0, 6, attend, 0)
    back = [
        remote(ag_s.at[1], at_s.at[pl.ds(0, 8), 1], sem_pair.at[2], sem_pair.at[3], other),
        remote(ag_s.at[0, 7], at_s.at[8, 1], sem_pair.at[4], sem_pair.at[5], other),
        pltpu.make_async_copy(ag_s.at[0], at_s.at[pl.ds(0, 8), 0], sem_loc.at[5]),
        pltpu.make_async_copy(ag_s.at[1, 7], at_s.at[8, 0], sem_loc.at[6]),
    ]
    for copy in back:
        copy.start()
    outs.append(pltpu.make_async_copy(p_s, p_out, sem_loc.at[7]))
    outs[-1].start()
    placed(1, c_s)
    outs.append(pltpu.make_async_copy(c_s, ct_out, sem_loc.at[8]))
    outs[-1].start()
    for copy in back:
        copy.wait()
    outs.append(pltpu.make_async_copy(at_s, at_out, sem_loc.at[9]))
    outs[-1].start()
    for copy in outs:
        copy.wait()

    def finish(make, local):
        if not local:
            make().wait_send()

    sends((0, 1), finish)


def attn_call(lat, ct, cond, times, table, mw, mb, w, qb, vb, taps, cb):
    G = (2, 8, 2, 16)
    shape = jax.ShapeDtypeStruct
    return pl.pallas_call(
        attn_kernel,
        in_specs=[
            ANY_SPEC, ANY_SPEC, VMEM_SPEC, SMEM_SPEC, ANY_SPEC, ANY_SPEC, VMEM_SPEC, ANY_SPEC,
            VMEM_SPEC, VMEM_SPEC, VMEM_SPEC, VMEM_SPEC,
        ],
        out_specs=[ANY_SPEC] * 8,
        out_shape=[
            shape((576, D), BF16), shape((576, D), BF16), shape((576, D), BF16),
            shape(G + (D,), BF16), shape(G + (3 * D,), BF16), shape((24, 256, 256), BF16),
            shape((9, 2, 2, 16, D), BF16), shape((8, D), F32),
        ],
        scratch_shapes=[
            pltpu.VMEM((2, 2, 256, D), BF16), pltpu.VMEM((2, 64, D), BF16),
            pltpu.VMEM((576, D), BF16), pltpu.VMEM((576, D), BF16), pltpu.VMEM((576, D), BF16),
            pltpu.VMEM(G + (D,), BF16), pltpu.VMEM((8, 2, 16, D), BF16),
            pltpu.VMEM((D, 3 * D), BF16), pltpu.VMEM(G + (3 * D,), BF16),
            pltpu.VMEM((24, 256, 256), BF16), pltpu.VMEM(G + (D,), BF16),
            pltpu.VMEM((9, 2, 2, 16, D), BF16),
            pltpu.VMEM((8, D), F32), pltpu.VMEM(table.shape, BF16), pltpu.VMEM(mw.shape, BF16),
            pltpu.VMEM((8, D), F32),
            pltpu.SemaphoreType.DMA((2, 2, 2)), pltpu.SemaphoreType.DMA((2, 3)),
            pltpu.SemaphoreType.DMA((6,)), pltpu.SemaphoreType.DMA((13,)),
        ],
        compiler_params=pltpu.CompilerParams(
            collective_id=1, has_side_effects=True, vmem_limit_bytes=56 * 2**20
        ),
        name="attend",
    )(lat, ct, cond, times, table, mw, mb, w, qb, vb, taps, cb)


def back_kernel(
    da_ref, qkv_ref, p_ref, hcg_hbm, h_hbm, x_hbm, dx_hbm, mod_ref, time_ref, w_ref, mw_ref,
    tap_ref, perm_ref, o_hbm, s1_ref, last_hbm, dbr_hbm, at_hbm, s2_ref, sb_ref,
    oret_out, iret_out, fe_out, fl_out, se_out, sl_out, de_out, dl_out,
    qkv_s, p_s, w_s, mw_s, perm_s, dag_s, dqkv_s, hct_s, dhc_s, dh_s, gh_s, ig_s, os_s, is_s,
    lg_s, prl_s, s1_s, r1x, r1l, s1l, r2e, r2l, t3e, t3a, t3b, r3e, r3a, r3b, fe_s, fl_s,
    acc_s, sv_s, se_p, se_r, se_s, se_f, sl_p, sl_r, sl_s, sl_f, mp_s, mr_s, mpl_s, mrl_s,
    item_s, de_s, dl_s, hcg_ref, h_ref, x_ref, dx_ref, o_ref, last_ref, dbr_ref, at_ref,
    loc, pair_sem, ret_send, ret_recv, st_send, st_recv, sm_send, sm_recv, dm_send, dm_recv,
):
    me = spot()
    zh, core = me["zh"], me["core"]
    other = seq_peer(me, zh, 1 - core)
    loads = [
        pltpu.make_async_copy(*pair, loc.at[20 + at])
        for at, pair in enumerate((
            (da_ref, dag_s), (qkv_ref, qkv_s), (perm_ref, perm_s), (hcg_hbm, hcg_ref),
            (at_hbm, at_ref), (dbr_hbm, dbr_ref), (p_ref, p_s), (last_hbm, last_ref),
            (o_hbm, o_ref), (w_ref, w_s), (s1_ref, s1_s), (h_hbm, h_ref), (x_hbm, x_ref),
            (dx_hbm, dx_ref), (mw_ref, mw_s),
        ))
    ]
    for load in loads:
        load.start()
    peers = [axis_peer(me, axis, o) for axis in "xyz" for o in (1, 2, 3)]
    peers += [other, seq_peer(me, 1 - zh, 1 - core)]
    hail(peers)

    def stage_sends(stage, bufs, kind, parts=(0, 1, 2)):
        out = []
        for p in parts:
            for o in (1, 2, 3):
                if kind:
                    axis = ORDERS[p][stage]
                    here, peer = axis_spot(me, axis), axis_peer(me, axis, o)
                else:
                    here, peer = early_peer(me, stage, p, o)
                src, dst = bufs(p, o, (here + o) & 3)
                copy = remote(
                    src, dst, st_send.at[kind, stage, p, o - 1], st_recv.at[kind, stage, p, o - 1],
                    peer,
                )
                copy.start()
                out.append(copy)
        return out

    def chunk(there, rows):
        return pl.ds(pl.multiple_of(there * rows, 16), rows)

    home = place_matrix(256, core == 1, True)

    def give_back(which, act):
        ref, out = ((os_s, oret_out), (is_s, iret_out))[which]
        for b in range(2):
            to_core = jnp.where(core == 0, b, 1 - b)
            own = jnp.logical_and(zh == core, b == 0)

            @pl.when(own)
            def _():
                act(lambda: pltpu.make_async_copy(ref.at[b], out.at[zh], ret_recv.at[which, zh]), True)

            @pl.when(jnp.logical_not(own))
            def _():
                act(
                    lambda: remote(
                        ref.at[b], out.at[zh], ret_send.at[which, b], ret_recv.at[which, zh],
                        seq_peer(me, core, to_core),
                    ),
                    False,
                )

    def pairs(pair, _):
        heads = [(pc, half) for pc in range(2) for half in range(2)]
        lanes_at = [
            pl.ds(pl.multiple_of(which * D + pair * 128, 128), 128) for which in range(3)
        ]

        def part(ref, cols, pc):
            return jnp.concatenate(
                [ref[half, :, pc, :, cols].reshape(128, 128) for half in range(2)], axis=0
            )

        q, k, v = ([part(qkv_s, cols, pc) for pc in range(2)] for cols in lanes_at)
        do = [part(dag_s, lanes_at[0], pc) for pc in range(2)]
        dom = [head_lanes(do[pc], half) for pc, half in heads]
        dp = [mm_nt(v[pc], n) for (pc, _), n in zip(heads, dom)]
        low = [p_s[2 * (6 * pc + pair) + half] for pc, half in heads]
        dv = [mm(n, m) for n, m in zip(low, dom)]
        k_t = [k[pc].T for pc in range(2)]
        qm = [head_lanes(q[pc], half) for pc, half in heads]
        probs = [n.astype(F32) for n in low]
        sums = [jnp.sum(n * m, axis=0, keepdims=True) for n, m in zip(probs, dp)]
        ds = [(n * (m - t)).astype(BF16) for n, m, t in zip(probs, dp, sums)]
        dk = [mm(n, m) for n, m in zip(ds, qm)]
        dq = [mm(k_t[pc][64 * half : 64 * half + 64], n) for (pc, half), n in zip(heads, ds)]
        for pc in range(2):
            at = 2 * pc
            turned = jnp.concatenate(dq[at : at + 2], axis=0).T
            grads = (0.125 * turned, 0.125 * (dk[at] + dk[at + 1]), dv[at] + dv[at + 1])
            for cols, got in zip(lanes_at, grads):
                got = got.astype(BF16)
                for half in range(2):
                    dqkv_s[half, :, pc, :, cols] = got[128 * half : 128 * half + 128].reshape(
                        8, 16, 128
                    )
        return 0

    def out_grads():
        for p, places in (
            (1, ((1, 1, 1), (1, 2, 2))), (2, ((0, 2, 0), (1, 0, 3), (1, 1, 4), (1, 2, 5)))
        ):
            at_t = mm_nt(perm_s[p], at_ref[0:512, :]).astype(BF16)
            cols = jnp.concatenate(
                [dbr_ref[:, 128 * g : 128 * g + 128] for _, _, g in places], axis=1
            )
            got = mm(at_t, cols).astype(BF16)
            for n, (which, u, _) in enumerate(places):
                lg_s[which, p, u] = got[:, 128 * n : 128 * n + 128]

    def late_grads(group):
        copies = []
        for p in range(3):
            for which in range(2):
                blocks = LATE[which][group][p]
                made = [n for n in blocks if not isinstance(n, str)]
                if not made:
                    continue
                cols = jnp.concatenate(
                    [
                        dqkv_s[:, :, :, :, 128 * n : 128 * n + 128].reshape(512, 128)
                        for n in made
                    ],
                    axis=1,
                )
                got = mm(hct_s[p], cols).astype(BF16)
                for n, block in enumerate(made):
                    u = 3 if group else blocks.index(block)
                    lg_s[which, p, u] = got[:, 128 * n : 128 * n + 128]
            part = late_part(group)
            sem = 4 + p if group == 0 else (9, 12, 15)[p]
            copies.append(
                remote(
                    lg_s.at[(1 - core, p) + part], prl_s.at[(p,) + part], pair_sem.at[sem, 0],
                    pair_sem.at[sem, 1], other,
                )
            )
            copies[-1].start()
        return copies

    def late_part(group):
        return (3,) if group else (pl.ds(0, 3),)

    def late_first(group, copies):
        out = []
        part = late_part(group)
        for p in range(3):
            copies[p].wait()
            for u in (3,) if group else (0, 1, 2):
                lg_s[core, p, u] = lg_s[core, p, u] + prl_s[p, u]
            out += stage_sends(
                0,
                lambda p, o, a: (
                    lg_s.at[(core, p) + part + (chunk(a, 192),)], r1l.at[(o - 1, p) + part]
                ),
                1 + group, (p,),
            )
        return out

    def late_second(group, copies):
        out = []
        part = late_part(group)
        for p in range(3):
            for copy in copies[3 * p : 3 * p + 3]:
                copy.wait()
            for u in (3,) if group else (0, 1, 2):
                total = lg_s[core, p, u, chunk(spots[0][p], 192), :].astype(F32)
                for o in range(3):
                    total = total + r1l[o, p, u].astype(F32)
                s1l[p, u] = total.astype(BF16)
            out += stage_sends(
                1,
                lambda p, o, b: (
                    s1l.at[(p,) + part + (chunk(b, 48),)], r2l.at[(o - 1, p) + part]
                ),
                1 + group, (p,),
            )
        return out

    def late_third(group, copies):
        out = []
        t3l, r3l = (t3b, r3b) if group else (t3a, r3a)
        for p in range(3):
            for copy in copies[3 * p : 3 * p + 3]:
                copy.wait()
            got = second(s1l, r2l, (3,) if group else (0, 1, 2), p, spots[1][p])
            pad = jnp.zeros((4 if group else 12, 128), F32)
            for c in range(4):
                t3l[p, c] = jnp.concatenate(
                    [v[12 * c : 12 * c + 12] for v in got] + [pad], axis=0
                ).astype(BF16)
            out += stage_sends(
                2, lambda p, o, c: (t3l.at[p, c], r3l.at[o - 1, p]), 1 + group, (p,)
            )
        return out

    def late_total(group, copies):
        t3l, r3l = (t3b, r3b) if group else (t3a, r3a)
        rows = slice(48, 64) if group else slice(0, 48)
        for copy in copies:
            copy.wait()
        for p in range(3):
            total = t3l[p, spots[2][p]].astype(F32)
            for o in range(3):
                total = total + r3l[o, p].astype(F32)
            fl_s[p, rows, :] = total

    spots = [[axis_spot(me, ORDERS[p][stage]) for p in range(3)] for stage in range(3)]
    z_me = axis_spot(me, "z")

    def small_stage(stage, sums, items, kind):
        axis = "zxy"[stage]
        if stage == 0:
            ref = items.at[core, me["y"], me["x"], z_me]
        elif stage == 1:
            ref = items.at[core, me["y"], me["x"]]
        else:
            ref = items.at[core, me["y"]]
        out = []
        for o in (1, 2, 3):
            peer = axis_peer(me, axis, o)
            at = (kind, stage, o - 1)
            out.append(
                remote(sums.at[4 * stage], sums.at[4 * stage + o], sm_send.at[at], sm_recv.at[at], peer)
            )
            out.append(remote(ref, ref, dm_send.at[at], dm_recv.at[at], peer))
        for copy in out:
            copy.start()
        return out

    def small_take(stage, sums, items, kind, copies, last):
        axis = "zxy"[stage]
        for copy in copies:
            copy.wait_send()
        for o in (1, 2, 3):
            at = (kind, stage, o - 1)
            arrived(sums.at[4 * stage + o], sm_recv.at[at])
            there = (axis_spot(me, axis) + 4 - o) & 3
            if stage == 0:
                ref = items.at[core, me["y"], me["x"], there]
            elif stage == 1:
                ref = items.at[core, me["y"], there]
            else:
                ref = items.at[core, there]
            arrived(ref, dm_recv.at[at])
        total = sums[4 * stage].astype(F32)
        for o in (1, 2, 3):
            total = total + sums[4 * stage + o].astype(F32)
        if stage < 2:
            sums[4 * stage + 4] = total.astype(BF16)
        else:
            last[...] = total

    def lane_rows(values, count):
        return [
            values[i : i + 1, 128 * l : 128 * l + 128] for i in range(count) for l in range(6)
        ]

    ends = []

    def spread(done, out, at):
        for copy in (
            pltpu.make_async_copy(done, out.at[core], loc.at[at]),
            remote(done, out.at[core], pair_sem.at[at, 0], pair_sem.at[at, 1], other),
        ):
            copy.start()
            ends.append(copy)

    def second(own, recv, panels, p, here):
        out = []
        for k in panels:
            total = own[p, k, chunk(here, 48), :].astype(F32)
            for o in range(3):
                total = total + recv[o, p, k].astype(F32)
            out.append(total)
        return out

    def finish(copies, own, recv, done, out, at, places):
        for copy in copies:
            copy.wait()
        for p in range(3):
            total = own[p, places[p]].astype(F32)
            for o in range(3):
                total = total + recv[o, p].astype(F32)
            done[p] = total
        spread(done, out, at)

    def pairs_turn(i, _):
        hct_s[i] = mm_nt(perm_s[i], hcg_ref[...]).astype(BF16)
        return pairs(i, 0)

    for load in loads[:7]:
        load.wait()
    lax.fori_loop(0, 1, pairs_turn, 0)
    heard(len(peers))
    loads[7].wait()
    st1x = stage_sends(0, lambda p, o, a: (last_ref.at[p, a], r1x.at[o - 1, p]), 0)
    mp_s[...] = sb_ref[...]
    mp_copy = remote(mp_s, mr_s, pair_sem.at[1, 0], pair_sem.at[1, 1], other)
    mp_copy.start()
    for half in range(2):
        for q in range(2):
            at = D * (2 * half + q)
            se_p[half, 16 * q : 16 * q + 16, :] = s2_ref[:, at : at + D].astype(BF16)
    se_copy = remote(se_p.at[1 - core], se_r, pair_sem.at[2, 0], pair_sem.at[2, 1], other)
    se_copy.start()

    loads[8].wait()
    for b in range(2):
        os_s[b] = mm(home, o_ref[256 * b : 256 * b + 256, :]).astype(BF16)
    give_back(0, lambda make, local: make().start())
    lax.fori_loop(1, 3, pairs_turn, 0)
    out_grads()
    pairs(3, 0)
    late_a = late_grads(0)
    mp_copy.wait()
    item_s[2:6, :] = (mp_s[0:4, :] + mr_s[0:4, :]).astype(BF16).astype(F32)
    time_id = time_ref[zh]
    stamp = jnp.ones((1, 128), F32)
    rows = lane_rows(item_s[2:6, :], 4) + lane_rows(mod_ref[7:8, :], 1)
    rows += [stamp * (time_id // 32).astype(F32), stamp * (time_id % 32).astype(F32)]
    both = jnp.concatenate(rows, axis=0).astype(BF16)
    de_s[core, me["y"], me["x"], z_me] = jnp.where(core == 0, both[0:16], both[16:32])
    se_copy.wait()
    se_s[0] = (se_p[core].astype(F32) + se_r[...].astype(F32)).astype(BF16)
    small = small_stage(0, se_s, de_s, 0)
    lax.fori_loop(4, 6, pairs, 0)
    late_b = late_grads(1)
    loads[9].wait()
    for half in (1, 0):
        got = mm_nt(dqkv_s[half].reshape(256, 3 * D), w_s[...]).astype(BF16)
        dhc_s[half] = got.reshape(8, 2, 16, D)
        if half == 1:
            dhc_copy = remote(
                dhc_s.at[1], dh_s.at[pl.ds(0, 8), 1], pair_sem.at[3, 0], pair_sem.at[3, 1], other
            )
            dhc_copy.start()
    near = [
        pltpu.make_async_copy(dhc_s.at[0], dh_s.at[pl.ds(0, 8), 0], loc.at[7]),
        pltpu.make_async_copy(dhc_s.at[1, 7], dh_s.at[8, 0], loc.at[8]),
    ]
    for copy in near:
        copy.start()
    st1a = late_first(0, late_a)
    st1b = late_first(1, late_b)
    loads[14].wait()
    d_silu = jnp.zeros((8, D), F32)

    def silu_part(i):
        row = jnp.concatenate([item_s[i : i + 1, :]] * 8, axis=0).astype(BF16)
        return mm_nt(row, mw_s[:, D * i : D * i + D])

    for i in range(2, 6):
        d_silu = d_silu + silu_part(i)
    ones = jnp.ones((8, 512), BF16)
    for row, at in ((10, 0), (11, 2 * D)):
        sums = mm(ones, dqkv_s[:, :, :, :, at : at + D].reshape(512, D))
        sv_s[row : row + 1, :] = sums[0:1]
    sv_s[12:14, :] = sb_ref[4:6, :]
    sv_s[14:16, :] = jnp.zeros((2, D), F32)

    dhc_copy.wait()
    for copy in near:
        copy.wait()
    loads[11].wait()
    masks = side_masks()

    def lanes(j, _):
        cols = pl.ds(pl.multiple_of(j * 128, 128), 128)
        taps = tap_ref[:, cols].astype(F32)
        taps = [taps[t : t + 1] for t in range(9)]
        back = [by_core(taps, 8 - t, core) for t in range(9)]
        back = [jnp.broadcast_to(v, (16, 128)).astype(BF16) for v in back]

        def sided_d(l):
            return with_sides_low(
                dh_s[l // 2, l % 2, 0, :, cols], dh_s[l // 2, l % 2, 1, :, cols], masks
            )

        def sided_h(l):
            return with_sides_low(
                h_ref[32 * l : 32 * l + 16, cols], h_ref[32 * l + 16 : 32 * l + 32, cols], masks
            )

        rows = [None, sided_d(0), sided_d(1)]
        rows_h = [None, sided_h(0), sided_h(1)]
        sums = [None] * 9
        held = bias_sum = None
        for l in range(16):
            ge, go = conv_row(rows, back)
            gh_s[32 * l : 32 * l + 16, cols] = ge.astype(F32)
            gh_s[32 * l + 16 : 32 * l + 32, cols] = go.astype(F32)
            de, do = rows[1][0], rows[1][1]
            held = tap_pairs(held if l % 2 else None, rows_h, de, do)
            if l % 2:
                for t in range(9):
                    term = fold8(held[t].astype(F32))
                    sums[t] = term if sums[t] is None else sums[t] + term
            term = fold8(de.astype(F32) + do.astype(F32))
            bias_sum = term if bias_sum is None else bias_sum + term
            if l < 15:
                rows = [rows[1], rows[2], sided_d(l + 2)]
                rows_h = [rows_h[1], rows_h[2], sided_h(l + 2)]
        for t in range(9):
            total = jnp.sum(by_core(sums, t, core), axis=0, keepdims=True)
            sv_s[t : t + 1, cols] = total
        sv_s[9:10, cols] = jnp.sum(bias_sum, axis=0, keepdims=True)
        return 0

    lax.fori_loop(0, D // 128, lanes, 0)
    small_take(0, se_s, de_s, 0, small, se_f)
    small = small_stage(1, se_s, de_s, 0)
    for load in loads[12:14]:
        load.wait()
    scale1 = mod_ref[1:2, :]
    acc_s[...] = jnp.zeros_like(acc_s)

    def rows_n(r, _):
        at = pl.ds(pl.multiple_of(r * 128, 128), 128)
        n1, rs = norm_parts(x_ref[at, :].astype(F32))
        dh = gh_s[at, :]
        g1 = dh * (1.0 + scale1)
        got = dx_ref[at, :] + rs * (
            g1
            - jnp.mean(g1, axis=-1, keepdims=True)
            - n1 * jnp.mean(g1 * n1, axis=-1, keepdims=True)
        )
        ig_s[at, :] = got.astype(BF16)
        acc_s[0] += fold8(dh)
        acc_s[1] += fold8(dh * n1)
        return 0

    lax.fori_loop(0, 4, rows_n, 0)
    mpl_s[...] = jnp.zeros_like(mpl_s)
    for i in range(2):
        mpl_s[i : i + 1, :] = jnp.sum(acc_s[i], axis=0, keepdims=True)
    mpl_copy = remote(mpl_s, mrl_s, pair_sem.at[7, 0], pair_sem.at[7, 1], other)
    mpl_copy.start()
    for half in range(2):
        sl_p[half] = sv_s[:, 384 * half : 384 * half + 384].astype(BF16)
    sl_copy = remote(sl_p.at[1 - core], sl_r, pair_sem.at[8, 0], pair_sem.at[8, 1], other)
    sl_copy.start()
    for b in range(2):
        is_s[b] = mm(home, ig_s[256 * b : 256 * b + 256, :]).astype(BF16)
    mpl_copy.wait()
    item_s[0:2, :] = (mpl_s[0:2, :] + mrl_s[0:2, :]).astype(BF16).astype(F32)
    cond = mod_ref[6:7, :]
    for i in range(2):
        d_silu = d_silu + silu_part(i)
    slope = 1.0 / (1.0 + jnp.exp(-cond))
    d_cond = (slope * (1.0 + cond * (1.0 - slope))) * d_silu[0:1]
    zeros = [jnp.zeros((1, 128), F32)]
    rows_0 = jnp.concatenate(lane_rows(item_s[0:2, :], 2) + zeros * 4, axis=0)
    rows_1 = jnp.concatenate(lane_rows(d_cond, 1) + zeros * 10, axis=0)
    dl_s[core, me["y"], me["x"], z_me] = jnp.where(core == 0, rows_0, rows_1).astype(BF16)
    sl_copy.wait()
    sl_s[0] = (sl_p[core].astype(F32) + sl_r[...].astype(F32)).astype(BF16)
    small_l = small_stage(0, sl_s, dl_s, 1)
    give_back(1, lambda make, local: make().start())
    loads[10].wait()
    for copy in st1x:
        copy.wait()
    for p in range(3):
        here, _peer = early_peer(me, 0, p, 1)
        total = last_ref[p, here].astype(F32)
        for o in range(3):
            total = total + r1x[o, p].astype(F32)
        total = total.astype(BF16)

        @pl.when(core == 0)
        def _():
            s1_s[p, 3] = total

        @pl.when(core == 1)
        def _():
            for c in range(4):
                s1_s[p, c, 144:192] = total[48 * c : 48 * c + 48]

    st2e = stage_sends(1, lambda p, o, b: (s1_s.at[p, :, chunk(b, 48)], r2e.at[o - 1, p]), 0)
    small_take(1, se_s, de_s, 0, small, se_f)
    small = small_stage(2, se_s, de_s, 0)
    st2a = late_second(0, st1a)
    small_take(0, sl_s, dl_s, 1, small_l, sl_f)
    small_l = small_stage(1, sl_s, dl_s, 1)
    st2b = late_second(1, st1b)
    for copy in st2e:
        copy.wait()
    for p in range(3):
        got = second(s1_s, r2e, range(4), p, early_peer(me, 1, p, 1)[0])

        @pl.when(core == 0)
        def _():
            for c in range(4):
                t3e[p, c] = jnp.concatenate(
                    [got[k][12 * c : 12 * c + 12] for k in range(4)], axis=0
                ).astype(BF16)

        @pl.when(core == 1)
        def _():
            for c in range(4):
                t3e[p, c] = got[c].astype(BF16)

    st3e = stage_sends(2, lambda p, o, c: (t3e.at[p, c], r3e.at[o - 1, p]), 0)
    small_take(2, se_s, de_s, 0, small, se_f)
    spread(se_f, se_out, 10)
    spread(de_s.at[core], de_out, 16)
    small_take(1, sl_s, dl_s, 1, small_l, sl_f)
    small_l = small_stage(2, sl_s, dl_s, 1)
    st3a = late_third(0, st2a)
    st3b = late_third(1, st2b)
    finish(st3e, t3e, r3e, fe_s, fe_out, 17, [early_peer(me, 2, p, 1)[0] for p in range(3)])
    late_total(0, st3a)
    late_total(1, st3b)
    spread(fl_s, fl_out, 18)
    small_take(2, sl_s, dl_s, 1, small_l, sl_f)
    spread(sl_f, sl_out, 13)
    spread(dl_s.at[core], dl_out, 14)
    for which in range(2):
        give_back(which, lambda make, local: None if local else make().wait_send())
        for item_slot in range(2):
            out = (oret_out, iret_out)[which]
            arrived(out.at[item_slot], ret_recv.at[which, item_slot])
    for copy in ends:
        copy.wait()


def back_call(
    da, qkv, p, hcg, h, x, dx, mod, times, w, mw, taps, perm, o, s1, last, dbr, at, s2, sb
):
    G = (2, 8, 2, 16)
    shape = jax.ShapeDtypeStruct
    V = pltpu.VMEM
    items = (2, 4, 4, 4, 16, 128)
    DMA = pltpu.SemaphoreType.DMA
    return pl.pallas_call(
        back_kernel,
        in_specs=[
            ANY_SPEC, ANY_SPEC, ANY_SPEC, ANY_SPEC, ANY_SPEC, ANY_SPEC, ANY_SPEC, VMEM_SPEC,
            SMEM_SPEC, ANY_SPEC, ANY_SPEC, VMEM_SPEC, ANY_SPEC, ANY_SPEC, ANY_SPEC, ANY_SPEC,
            ANY_SPEC, ANY_SPEC, VMEM_SPEC, VMEM_SPEC,
        ],
        out_specs=[ANY_SPEC] * 8,
        out_shape=[
            shape((2, 256, D), BF16), shape((2, 256, D), BF16),
            shape((2, 3, 48, 256), F32), shape((2, 3, 64, 128), F32),
            shape((2, 32, D), F32), shape((2, 16, 384), F32),
            shape(items, BF16), shape(items, BF16),
        ],
        scratch_shapes=[
            V(G + (3 * D,), BF16), V((24, 256, 256), BF16), V((D, 3 * D), BF16),
            V(mw.shape, BF16), V((3, D, D), BF16), V(G + (D,), BF16), V(G + (3 * D,), BF16),
            V((3, D, 512), BF16), V(G + (D,), BF16), V((9, 2, 2, 16, D), BF16), V((512, D), F32),
            V((512, D), BF16), V((2, 256, D), BF16), V((2, 256, D), BF16),
            V((2, 3, 4, D, 128), BF16), V((3, 4, D, 128), BF16), V((3, 4, 192, 256), BF16),
            V((3, 3, 192, 256), BF16), V((3, 3, 4, 192, 128), BF16), V((3, 4, 192, 128), BF16),
            V((3, 3, 4, 48, 256), BF16), V((3, 3, 4, 48, 128), BF16), V((3, 4, 48, 256), BF16),
            V((3, 4, 48, 128), BF16), V((3, 4, 16, 128), BF16), V((3, 3, 48, 256), BF16),
            V((3, 3, 48, 128), BF16), V((3, 3, 16, 128), BF16), V((3, 48, 256), F32),
            V((3, 64, 128), F32),
            V((2, 8, D), F32), V((16, D), F32),
            V((2, 32, D), BF16), V((32, D), BF16), V((12, 32, D), BF16), V((32, D), F32),
            V((2, 16, 384), BF16), V((16, 384), BF16), V((12, 16, 384), BF16), V((16, 384), F32),
            V((8, D), F32), V((8, D), F32), V((8, D), F32), V((8, D), F32), V((8, D), F32),
            V(items, BF16), V(items, BF16),
            V((512, D), BF16), V((576, D), BF16), V((576, D), BF16), V((512, D), F32),
            V((512, D), BF16), V((3, 4, 192, 256), BF16), V((512, D), BF16), V((576, D), BF16),
            DMA((35,)), DMA((19, 2)), DMA((2, 2)), DMA((2, 2)), DMA((3, 3, 3, 3)),
            DMA((3, 3, 3, 3)), DMA((2, 3, 3)), DMA((2, 3, 3)), DMA((2, 3, 3)), DMA((2, 3, 3)),
        ],
        compiler_params=pltpu.CompilerParams(
            collective_id=2, has_side_effects=True, vmem_limit_bytes=60 * 2**20
        ),
        name="back",
    )(da, qkv, p, hcg, h, x, dx, mod, times, w, mw, taps, perm, o, s1, last, dbr, at, s2, sb)


def share_kernel(
    out_ref, ig_ref, fe_hbm, fl_hbm, se_hbm, sl_hbm, de_hbm, dl_hbm,
    o_out, ig_out, cond_out, table_out, mw_out, mb_out, aw_out, ab_out, qkv_out, qb_out, vb_out,
    ow_out, ob_out, f1_out, f1b_out, fw_out, fb_out, f2_out, f2b_out,
    ig_s, o_s, igf_s, e_s, l_s, fe_ref, fl_ref, se_ref, sl_ref, de_ref, dl_ref, sem,
):
    me = spot()
    core = me["core"]
    shard = me["dp"] * 4 + me["seq"]
    ig_load = pltpu.make_async_copy(ig_ref, ig_s, sem.at[0])
    o_load = pltpu.make_async_copy(out_ref, o_s, sem.at[9])
    o_move = pltpu.make_async_copy(o_s, o_out, sem.at[1])
    loads = [
        pltpu.make_async_copy(*pair, sem.at[3 + at])
        for at, pair in enumerate((
            (fe_hbm, fe_ref), (fl_hbm, fl_ref), (se_hbm, se_ref), (sl_hbm, sl_ref),
            (de_hbm, de_ref), (dl_hbm, dl_ref),
        ))
    ]
    for load in loads:
        load.start()
    ig_load.start()
    o_load.start()
    o_load.wait()
    o_move.start()
    ig_load.wait()
    igf_s[...] = ig_s[...].astype(F32)
    ig_move = pltpu.make_async_copy(igf_s, ig_out, sem.at[2])
    ig_move.start()
    for load in loads:
        load.wait()
    e_s[...] = de_ref[...].reshape(2048, 128).astype(F32)
    l_s[...] = dl_ref[...].reshape(2048, 128).astype(F32)

    def six(v, at):
        return jnp.where(core == 0, v[at : at + 6], v[at + 6 : at + 12])

    for p in range(3):
        early0, early1 = fe_ref[0, p], fe_ref[1, p]
        for i in range(4):
            at = D * i + 256 * p
            f1_out[:, at : at + 256] = six(early0, 12 * i)
        f2_out[:, 256 * p : 256 * p + 256] = jnp.where(core == 0, early1[0:24], early1[24:48])
        for which in range(2):
            late = fl_ref[which, p]
            for group in range(2):
                for u, block in enumerate(LATE[which][group][p]):
                    got = six(late, 48 if group else 12 * u)
                    if isinstance(block, str):
                        at = 128 * int(block[1])
                        ow_out[:, at : at + 128] = got
                    else:
                        qkv_out[:, 128 * block : 128 * block + 128] = got

    def columns(start, count=D):
        at = lax.broadcasted_iota(jnp.int32, (count, 128), 0)
        to = lax.broadcasted_iota(jnp.int32, (count, 128), 1)
        return at == start + to

    def exact(a, b):
        return lax.dot_general(
            a, b.astype(F32), (((1,), (0,)), ((), ())), preferred_element_type=F32,
            precision=lax.Precision.HIGHEST,
        )

    mine = columns(shard * 6)
    slim = exact(jnp.concatenate((sl_ref[0], sl_ref[1]), axis=1), mine)
    aw_out[...] = slim.T[0:6, 0:9]
    for ref, at in ((ab_out, 9), (qb_out, 10), (vb_out, 11), (ob_out, 12), (f2b_out, 13)):
        ref[...] = slim[at : at + 1, 0:6].reshape(6)
    quarter = shard // 32
    wide = se_ref[quarter // 2, pl.ds(pl.multiple_of(quarter % 2 * 16, 16), 16), :]
    wide = exact(wide, columns(shard % 32 * 24))
    fw_out[...] = wide[0:9, 0:24]
    fb_out[...] = wide[9:10, 0:24].reshape(24)
    f1b_out[...] = wide[10:11, 0:24].reshape(24)

    def item_rows(ref, at):
        return ref[pl.ds(at // 16 * 1024 + at % 16, 64, stride=16), :]

    silu = jnp.concatenate([item_rows(e_s, 24 + l) for l in range(6)], axis=1)
    silu = mm(silu.astype(BF16), mine.astype(BF16)).astype(BF16)
    sums = []
    for at in range(36):
        d_mod = item_rows(l_s, at) if at < 12 else item_rows(e_s, at - 12)
        mw_out[:, 128 * at : 128 * at + 128] = mm_tn(silu, d_mod.astype(BF16))[0:6]
        sums.append(jnp.sum(d_mod, axis=0, keepdims=True))
    total = jnp.concatenate(sums, axis=1)
    total = exact(jnp.concatenate([total] * 8, axis=0), columns(shard * 36, 6 * D))
    mb_out[...] = total[0:1, 0:36].reshape(36)

    cond = jnp.concatenate([item_rows(l_s, 16 + l) for l in range(6)], axis=1).astype(BF16)
    here = lax.broadcasted_iota(jnp.int32, (8, 64), 1)
    slot = lax.broadcasted_iota(jnp.int32, (8, 64), 0)
    own = here == (me["y"] * 4 + me["x"]) * 4 + slot * 2 + me["zl"]
    own = jnp.logical_and(own, slot < 2)
    cond_out[...] = mm(own.astype(BF16), cond)[0:2]
    times = 32.0 * item_rows(e_s, 30) + item_rows(e_s, 31)
    bucket = lax.broadcasted_iota(jnp.int32, (64, 1024), 1).astype(F32)
    hot = (bucket == jnp.concatenate([times] * 8, axis=1)).astype(BF16)
    my_cond = mm(cond, mine.astype(BF16)).astype(BF16)
    table_out[...] = mm_tn(my_cond, hot)[0:6, 0 : table_out.shape[1]]

    ig_move.wait()
    o_move.wait()


def share_call(buckets, *args):
    shapes = [
        ((2, 256, D), BF16), ((2, 256, D), F32), ((2, D), F32), ((6, buckets), F32),
        ((6, 6 * D), F32), ((36,), F32), ((6, 9), F32), ((6,), F32), ((6, 3 * D), F32),
        ((6,), F32), ((6,), F32), ((6, D), F32), ((6,), F32), ((6, FF), F32), ((24,), F32),
        ((9, 24), F32), ((24,), F32), ((24, D), F32), ((6,), F32),
    ]
    return pl.pallas_call(
        share_kernel,
        in_specs=[ANY_SPEC] * 8,
        out_specs=[ANY_SPEC] * 2 + [VMEM_SPEC] * 17,
        out_shape=[jax.ShapeDtypeStruct(*s) for s in shapes],
        scratch_shapes=[
            pltpu.VMEM((2, 256, D), BF16), pltpu.VMEM((2, 256, D), BF16),
            pltpu.VMEM((2, 256, D), F32), pltpu.VMEM((2048, 128), F32), pltpu.VMEM((2048, 128), F32),
            *[pltpu.VMEM(v.shape, v.dtype) for v in args[2:]],
            pltpu.SemaphoreType.DMA((10,)),
        ],
        compiler_params=pltpu.CompilerParams(vmem_limit_bytes=60 * 2**20),
        name="share",
    )(*args)


def perm_matrices():
    at = np.arange(D)
    rows = []
    for order in ORDERS:
        spots = dict(zip(order, (at // 192, at // 48 % 4, at // 12 % 4)))
        x, y, z = spots["x"], spots["y"], spots["z"]
        rows.append((((x * 2 + z % 2) * 4 + y) * 2 + z // 2) * 12 + at % 12)
    return np.stack(rows).astype(np.int32)


def local(
    latents, conditioning, timesteps, item_counts, cotangent, time_table, mod_weight, mod_bias,
    conv_attn_weight, conv_attn_bias, qkv_weight, query_bias, value_bias, out_weight, out_bias,
    fc1_weight, fc1_bias, conv_ffn_weight, conv_ffn_bias, fc2_weight, fc2_bias,
):
    alive = (lax.axis_index("seq") // 2 < item_counts).astype(F32)
    perm = (perm_matrices()[:, :, None] == np.arange(D)[None, None, :]).astype(BF16)
    x, ct, h, hcg, qkv, p, at, mod = attn_call(
        latents.reshape(2, 256, D), cotangent.reshape(2, 256, D), conditioning, timesteps,
        time_table, mod_weight, mod_bias, qkv_weight, query_bias, value_bias, conv_attn_weight,
        conv_attn_bias,
    )
    at = at.reshape(576, D)
    out, s1, last, dbr, da, dx, s2, sb = ffn_call(
        x, at, ct, mod, alive, perm, out_weight, out_bias, fc1_weight, fc1_bias, conv_ffn_weight,
        conv_ffn_bias, fc2_weight, fc2_bias,
    )
    got = back_call(
        da, qkv, p, hcg.reshape(512, D), h, x, dx, mod, timesteps,
        qkv_weight, mod_weight, conv_attn_weight, perm, out, s1, last,
        dbr.reshape(512, D), at, s2, sb,
    )
    outs = list(share_call(time_table.shape[0], *got))
    outs[0], outs[1] = outs[0].reshape(latents.shape), outs[1].reshape(latents.shape)
    outs[3], outs[6] = outs[3].T, outs[6].T
    return tuple(outs)


def solution(mesh):
    return jax.shard_map(
        local,
        mesh=mesh,
        in_specs=(
            P("dp", "seq", None, None),
            P("dp", None),
            P("dp"),
            P("dp"),
            P("dp", "seq", None, None),
            P(),
            P(),
            P(),
            P(),
            P(),
            P(),
            P(),
            P(),
            P(),
            P(),
            P(),
            P(),
            P(),
            P(),
            P(),
            P(),
        ),
        out_specs=(
            P("dp", "seq", None, None),
            P("dp", "seq", None, None),
            P("dp", None),
            P(None, ("dp", "seq")),
            P(("dp", "seq"), None),
            P(("dp", "seq")),
            P(None, ("dp", "seq")),
            P(("dp", "seq")),
            P(("dp", "seq"), None),
            P(("dp", "seq")),
            P(("dp", "seq")),
            P(("dp", "seq"), None),
            P(("dp", "seq")),
            P(("dp", "seq"), None),
            P(("dp", "seq")),
            P(None, ("dp", "seq")),
            P(("dp", "seq")),
            P(("dp", "seq"), None),
            P(("dp", "seq")),
        ),
        check_vma=False,
    )
```

```python
import functools

import jax
import jax.numpy as jnp
import numpy as np
from jax import lax
from jax.experimental import pallas as pl
from jax.experimental.pallas import tpu as pltpu
from jax.sharding import PartitionSpec as P

F32 = jnp.float32
BF16 = jnp.bfloat16
D = 768
FF = 3072
FC = 768
NFC = FF // FC
EPS = 1e-6
VMEM_SPEC = pl.BlockSpec(memory_space=pltpu.VMEM)
ANY_SPEC = pl.BlockSpec(memory_space=pl.ANY)
SMEM_SPEC = pl.BlockSpec(memory_space=pltpu.SMEM)


def mm(a, b):
    return lax.dot_general(a, b, (((1,), (0,)), ((), ())), preferred_element_type=F32)


def mm_nt(a, b):
    return lax.dot_general(a, b, (((1,), (1,)), ((), ())), preferred_element_type=F32)


def mm_tn(a, b):
    return lax.dot_general(a, b, (((0,), (0,)), ((), ())), preferred_element_type=F32)


def row(v):
    return v.astype(F32).reshape(1, v.shape[0])


def fold8(v):
    total = v[0:8]
    for at in range(8, v.shape[0], 8):
        total = total + v[at : at + 8]
    return total


def norm_parts(v):
    center = v - jnp.mean(v, axis=-1, keepdims=True)
    rs = lax.rsqrt(jnp.mean(center * center, axis=-1, keepdims=True) + EPS)
    return center * rs, rs


def by_core(taps, at, core):
    return jnp.where(core == 1, taps[3 * (2 - at // 3) + at % 3], taps[at])


def gelu_pair(v):
    d = 1.0 + 0.23164189 * jnp.abs(v)
    t = pl.reciprocal(d, approx=True)
    t = t * (2.0 - d * t)
    e = jnp.exp2(-0.7213475204444817 * (v * v))
    poly = t * (
        0.127414796
        + t * (-0.142248368 + t * (0.7107068705 + t * (-0.7265760135 + t * 0.5307027145)))
    )
    tail = poly * e
    cdf = jnp.where(v >= 0, 1.0 - tail, tail)
    return v * cdf, cdf + v * (e * 0.3989422804014327)


def side_masks():
    place = lax.broadcasted_iota(jnp.int32, (16, 128), 0)
    return place == 0, place == 15


def with_sides(even, odd, masks):
    left = jnp.where(masks[0], 0.0, pltpu.roll(odd, 1, 0))
    right = jnp.where(masks[1], 0.0, pltpu.roll(even, 15, 0))
    return even, odd, left, right


def conv_row(rows, taps):
    even = odd = None
    for a in range(3):
        if rows[a] is None:
            continue
        ev, od, left, right = rows[a]
        for tap, ce, co in ((3 * a, left, ev), (3 * a + 1, ev, od), (3 * a + 2, od, right)):
            even = taps[tap] * ce if even is None else even + taps[tap] * ce
            odd = taps[tap] * co if odd is None else odd + taps[tap] * co
    return even, odd


def with_sides_low(even, odd, masks):
    left = jnp.where(masks[0], 0.0, pltpu.roll(odd.astype(F32), 1, 0)).astype(BF16)
    right = jnp.where(masks[1], 0.0, pltpu.roll(even.astype(F32), 15, 0)).astype(BF16)
    return even, odd, left, right


def tap_pairs(held, rows, d_even, d_odd):
    out = []
    for a in range(3):
        if rows[a] is None:
            out += [None] * 3
            continue
        ev, od, left, right = rows[a]
        for ce, co in ((left, ev), (ev, od), (od, right)):
            out.append(d_even * ce + d_odd * co)
    if held is None:
        return out
    return [b if a is None else a if b is None else a + b for a, b in zip(held, out)]


def tap_products(sums, rows, d_even, d_odd):
    for a in range(3):
        if rows[a] is None:
            continue
        ev, od, left, right = rows[a]
        for tap, ce, co in ((3 * a, left, ev), (3 * a + 1, ev, od), (3 * a + 2, od, right)):
            term = fold8(d_even * ce + d_odd * co)
            sums[tap] = term if sums[tap] is None else sums[tap] + term


MESH = pl.DeviceIdType.MESH


def spot():
    dp = lax.axis_index("dp")
    seq = lax.axis_index("seq")
    x, zl, y, zh, core = dp >> 3, (dp >> 2) & 1, dp & 3, seq >> 1, seq & 1
    z = zh * 2 + zl
    me = dict(dp=dp, seq=seq, x=x, zl=zl, y=y, zh=zh, z=z, core=core)
    for o in (1, 2, 3):
        me["x", o] = ((((x + o) & 3) << 3) + (dp & 7), seq)
        me["y", o] = ((dp & 28) + ((y + o) & 3), seq)
        to = (z + o) & 3
        me["z", o] = ((dp & 27) + ((to & 1) << 2), (to & 2) + core)
    return me


def seq_peer(me, zh, core):
    return (me["dp"], zh * 2 + core)


def axis_peer(me, axis, offset):
    return me[axis, offset]


def remote(src, dst, send, recv, device):
    return pltpu.make_async_remote_copy(
        src_ref=src, dst_ref=dst, send_sem=send, recv_sem=recv, device_id=device,
        device_id_type=MESH,
    )


def arrived(ref, sem):
    pltpu.make_async_copy(ref, ref, sem).wait()


def hail(peers):
    barrier = pltpu.get_barrier_semaphore()
    for peer in peers:
        pl.semaphore_signal(barrier, inc=1, device_id=peer, device_id_type=MESH)


def heard(count):
    pl.semaphore_wait(pltpu.get_barrier_semaphore(), count)


def greet(peers):
    hail(peers)
    heard(len(peers))


ORDERS = (("x", "y", "z"), ("y", "x", "z"), ("z", "x", "y"))
EARLY = (
    (("x", "y", "z"), ("x", "y", "z"), ("y", "x", "z")),
    (("y", "x", "z"), ("z", "x", "y"), ("z", "x", "y")),
)


LATE = (
    (((0, 1, 2), (3, 6, 7), (8, 9, "g0")), ((4,), (5,), (10,))),
    (((12, 13, 14), (15, "g1", "g2"), ("g3", "g4", "g5")), ((11,), (16,), (17,))),
)


def axis_spot(me, axis):
    return me[axis]


def early_peer(me, stage, part, offset):
    key = (stage, part, offset)
    if key not in me:
        first, second = (EARLY[which][part][stage] for which in range(2))
        if first == second:
            me[key] = me[first], me[first, offset]
        else:
            pick = lambda a, b: jnp.where(me["core"] == 0, a, b)
            peer = tuple(pick(a, b) for a, b in zip(me[first, offset], me[second, offset]))
            me[key] = pick(me[first], me[second]), peer
    return me[key]


def ffn_kernel(
    x_ref, at_ref, ct_hbm, mod_ref, alive_ref, perm_hbm, ow_ref, ob_ref, f1_ref, f1b_ref,
    tap_ref, cb_ref, f2_ref, f2b_ref,
    out_hbm, s1_ref, last_ref, dbr_hbm, da_ref, dx_hbm, s2_ref, sm_ref,
    x1_s, br_s, h2_s, h2t_s, dffn_s, u_s, duc_s, act_s, du_s, dact_s, ffn_s, dh2_s, acc_s,
    ch_s, pre_s, r1_s, bias_s, das_s, dar_s, ct_ref, perm_ref, out_ref, dbr_ref, dx_ref, pair_sem, st_send, st_recv, loc,
):
    step = pl.program_id(0)
    me = spot()
    core = me["core"]
    other = seq_peer(me, me["zh"], 1 - core)
    for p in range(3):
        for o in (1, 2, 3):
            early_peer(me, 0, p, o)
    alive = alive_ref[0]

    ct_load = pltpu.make_async_copy(ct_hbm, ct_ref, loc.at[0])
    perm_load = pltpu.make_async_copy(perm_hbm.at[pl.ds(0, 2)], perm_ref, loc.at[1])

    @pl.when(step == 0)
    def _():
        ct_load.start()
        perm_load.start()
        bias_s[0:1, :] = row(f1b_ref[...])
        bias_s[1:2, :] = row(cb_ref[...])
        hail([axis_peer(me, axis, o) for axis in "xyz" for o in (1, 2, 3)] + [other])

    def pair_copy(at):
        slot = at % 2
        return remote(
            ch_s.at[slot, 1 - core], pre_s.at[slot], pair_sem.at[slot, 0], pair_sem.at[slot, 1],
            other,
        )

    def first_copies(at):
        slot = at % 2
        out = []
        for p in range(3):
            for o in (1, 2, 3):
                here, peer = early_peer(me, 0, p, o)
                out.append(
                    remote(
                        ch_s.at[slot, core, p, (here + o) & 3], r1_s.at[at, o - 1, p],
                        st_send.at[at, p, o - 1], st_recv.at[at, p, o - 1], peer,
                    )
                )
        return out

    def pair_add(at):
        slot = at % 2
        pair_copy(at).wait()
        for p in range(3):

            def add(a, _):
                ch_s[slot, core, p, a] = ch_s[slot, core, p, a] + pre_s[slot, p, a]
                return 0

            lax.fori_loop(0, 4, add, 0)

    def first_send(at):
        pair_add(at)
        for copy in first_copies(at):
            copy.start()

    def first_take(at):
        slot = at % 2
        for copy in first_copies(at):
            copy.wait()
        for p in range(3):
            here, _peer = early_peer(me, 0, p, 1)
            total = ch_s[slot, core, p, here].astype(F32)
            for o in range(3):
                total = total + r1_s[at, o, p].astype(F32)
            total = total.astype(BF16)

            @pl.when(core == 0)
            def _():
                s1_ref[p, at] = total

            @pl.when(core == 1)
            def _():
                for c in range(4):
                    s1_ref[p, c, pl.ds(pl.multiple_of(at * 48, 16), 48)] = total[
                        48 * c : 48 * c + 48
                    ]

    @pl.when(step == 0)
    def _():
        br_s[...] = mm(at_ref[...], ow_ref[...]) + row(ob_ref[...])
        shift2, scale2, gate1, gate2 = (mod_ref[i : i + 1, :] for i in (3, 4, 2, 5))

        def rows_a(r, _):
            at = pl.ds(pl.multiple_of(r * 96, 96), 96)
            x1 = x_ref[at, :].astype(F32) + gate1 * br_s[at, :]
            x1_s[at, :] = x1
            n2, _unused = norm_parts(x1)
            h2_s[at, :] = (n2 * (1.0 + scale2) + shift2).astype(BF16)
            return 0

        lax.fori_loop(0, 6, rows_a, 0)

        ct_load.wait()

        def rows_b(r, _):
            at = pl.ds(pl.multiple_of(r * 272, 16), 272)
            dffn_s[at, :] = (ct_ref[at, :].astype(F32) * alive * gate2).astype(BF16)
            return 0

        lax.fori_loop(0, 2, rows_b, 0)
        perm_load.wait()
        for p in range(2):
            h2t_s[p] = mm_nt(perm_ref[p], h2_s[0:512, :]).astype(BF16)
        ffn_s[...] = jnp.zeros_like(ffn_s)
        dh2_s[...] = jnp.zeros_like(dh2_s)

    @pl.when(step == 0)
    def _():
        heard(10)

    masks = side_masks()

    def lanes(j):
        cols = slice(128 * j, 128 * j + 128)
        taps = tap_ref[:, cols].astype(F32)
        taps = [taps[t : t + 1] for t in range(9)]
        taps = [by_core(taps, t, core) for t in range(9)]
        taps = [jnp.broadcast_to(v, (16, 128)).astype(BF16) for v in taps]
        offset = bias_s[1:2, pl.ds(pl.multiple_of(step * FC + j * 128, 128), 128)]

        def sided(ref, l):
            return with_sides_low(
                ref[32 * l : 32 * l + 16, cols], ref[32 * l + 16 : 32 * l + 32, cols], masks
            )

        rows = [None, sided(u_s, 0), sided(u_s, 1)]
        sums = [None] * 9
        held = bias_sum = None
        for l in range(17):
            ce, co = conv_row(rows, taps)
            ae, ge = gelu_pair(ce.astype(F32) + offset)
            ao, go = gelu_pair(co.astype(F32) + offset)
            de = (ge * dact_s[32 * l : 32 * l + 16, cols]).astype(BF16)
            do = (go * dact_s[32 * l + 16 : 32 * l + 32, cols]).astype(BF16)
            duc_s[32 * l : 32 * l + 16, cols] = de
            duc_s[32 * l + 16 : 32 * l + 32, cols] = do
            if l < 16:
                act_s[32 * l : 32 * l + 16, cols] = ae.astype(BF16)
                act_s[32 * l + 16 : 32 * l + 32, cols] = ao.astype(BF16)
                held = tap_pairs(held if l % 2 else None, rows, de, do)
                if l % 2:
                    for t in range(9):
                        term = fold8(held[t].astype(F32))
                        sums[t] = term if sums[t] is None else sums[t] + term
                term = fold8(de.astype(F32) + do.astype(F32))
                bias_sum = term if bias_sum is None else bias_sum + term
                rows = [rows[1], rows[2], sided(u_s, l + 2) if l + 2 < 18 else None]
        for t in range(9):
            s2_ref[t : t + 1, cols] = jnp.sum(by_core(sums, t, core), axis=0, keepdims=True)
        s2_ref[9:10, cols] = jnp.sum(bias_sum, axis=0, keepdims=True)
        back = [taps[8 - t] for t in range(9)]
        rows = [None, sided(duc_s, 0), sided(duc_s, 1)]
        bias_sum = None
        for l in range(16):
            ue, uo = conv_row(rows, back)
            du_s[32 * l : 32 * l + 16, cols] = ue
            du_s[32 * l + 16 : 32 * l + 32, cols] = uo
            term = fold8(ue.astype(F32) + uo.astype(F32))
            bias_sum = term if bias_sum is None else bias_sum + term
            rows = [rows[1], rows[2], sided(duc_s, l + 2) if l + 2 < 17 else None]
        s2_ref[10:11, cols] = jnp.sum(bias_sum, axis=0, keepdims=True)

    slot = step % 2

    def into(j):
        cols = slice(256 * j, 256 * j + 256)
        offset = bias_s[0:1, pl.ds(pl.multiple_of(step * FC + 256 * j, 256), 256)]
        u_s[:, cols] = (mm(h2_s[...], f1_ref[:, cols]) + offset).astype(BF16)
        dact_s[:, cols] = mm_nt(dffn_s[...], f2_ref[cols, :])

    def out_of(j):
        cols = slice(256 * j, 256 * j + 256)
        got = mm(h2t_s[j // 2], du_s[:, cols]).astype(BF16)
        ch_s[slot, 0, j] = got.reshape(4, 192, 256)
        grad = mm_tn(act_s[:, cols], dffn_s[0:512, :]).astype(BF16)
        for at in range(0, 256, 16):
            chip, inner = (256 * j + at) // 48, (256 * j + at) % 48
            zl, y, zh = chip // 8, chip // 2 % 4, chip % 2
            z = zh * 2 + zl
            for part in range(3):
                a, c = (y, z) if part == 0 else (z, y)
                ch_s[slot, 1, part, a, 48 * c + inner : 48 * c + inner + 16] = grad[
                    at : at + 16, 256 * part : 256 * part + 256
                ]
        ffn_s[...] += mm(act_s[:, cols], f2_ref[cols, :])
        dh2_s[...] += mm_nt(du_s[:, cols], f1_ref[:, cols])

    into(0)
    into(1)
    lanes(0)
    lanes(1)
    into(2)

    @pl.when(step > 1)
    def _():
        first_take(step - 2)

    out_of(0)

    @pl.when(step > 0)
    def _():
        first_send(step - 1)

    lanes(2)
    lanes(3)
    out_of(1)
    lanes(4)
    lanes(5)
    out_of(2)
    pair_copy(step).start()

    @pl.when(step == NFC - 1)
    def _():
        shift2, scale2, gate1, gate2 = (mod_ref[i : i + 1, :] for i in (3, 4, 2, 5))
        acc_s[...] = jnp.zeros_like(acc_s)
        f2b = row(f2b_ref[...])

        def rows_c(r, _):
            at = pl.ds(pl.multiple_of(r * 128, 128), 128)
            x1 = x1_s[at, :]
            ffn = ffn_s[at, :] + f2b
            dy = ct_ref[at, :].astype(F32) * alive
            out_ref[at, :] = (alive * (x1 + gate2 * ffn)).astype(BF16)
            n2, rs = norm_parts(x1)
            dh2 = dh2_s[at, :]
            g2 = dh2 * (1.0 + scale2)
            dx1 = dy + rs * (
                g2
                - jnp.mean(g2, axis=-1, keepdims=True)
                - n2 * jnp.mean(g2 * n2, axis=-1, keepdims=True)
            )
            dx_ref[at, :] = dx1
            dbr = (dx1 * gate1).astype(BF16)
            dbr_ref[pl.ds(2 * r, 2)] = dbr.reshape(2, 2, 2, 16, D)
            acc_s[0] += fold8(dx1 * br_s[at, :])
            acc_s[1] += fold8(dh2)
            acc_s[2] += fold8(dh2 * n2)
            acc_s[3] += fold8(dy * ffn)
            acc_s[4] += fold8(dbr.astype(F32))
            acc_s[5] += fold8(dffn_s[at, :].astype(F32))
            return 0

        lax.fori_loop(0, 4, rows_c, 0)
        for i in range(6):
            sm_ref[i : i + 1, :] = jnp.sum(acc_s[i], axis=0, keepdims=True)
        moves = [
            pltpu.make_async_copy(out_ref, out_hbm, loc.at[2]),
            pltpu.make_async_copy(dbr_ref, dbr_hbm, loc.at[3]),
            pltpu.make_async_copy(dx_ref, dx_hbm, loc.at[4]),
        ]
        for copy in moves:
            copy.start()
        halves = [dbr_ref[:, parity].reshape(256, D) for parity in range(2)]
        odd = mm_nt(halves[1], ow_ref[...]).astype(BF16)
        das_s[...] = odd.reshape(8, 2, 16, D)
        da_copy = remote(das_s, dar_s, pair_sem.at[2, 0], pair_sem.at[2, 1], other)
        da_copy.start()
        da_ref[0] = mm_nt(halves[0], ow_ref[...]).astype(BF16).reshape(8, 2, 16, D)
        pair_add(step)
        last_ref[...] = ch_s[step % 2, core]
        first_take(step - 1)
        da_copy.wait()
        da_ref[1] = dar_s[...]
        for copy in moves:
            copy.wait()


def ffn_call(x, at, ct, mod, alive, perm, ow, ob, f1, f1b, taps, cb, f2, f2b):
    whole = lambda s: pl.BlockSpec(s, lambda i: (0,) * len(s))
    return pl.pallas_call(
        ffn_kernel,
        grid=(NFC,),
        in_specs=[
            whole((576, D)), whole((576, D)), ANY_SPEC, whole((8, D)),
            pl.BlockSpec(memory_space=pltpu.SMEM),
            ANY_SPEC, whole((D, D)), whole((D,)),
            pl.BlockSpec((D, FC), lambda i: (0, i)),
            whole((FF,)),
            pl.BlockSpec((9, FC), lambda i: (0, i)),
            whole((FF,)),
            pl.BlockSpec((FC, D), lambda i: (i, 0)),
            whole((D,)),
        ],
        out_specs=[
            ANY_SPEC,
            whole((3, 4, 192, 256)), whole((3, 4, 192, 256)),
            ANY_SPEC, whole((2, 8, 2, 16, D)), ANY_SPEC,
            pl.BlockSpec((16, FC), lambda i: (0, i)),
            whole((8, D)),
        ],
        out_shape=[
            jax.ShapeDtypeStruct((512, D), BF16),
            jax.ShapeDtypeStruct((3, 4, 192, 256), BF16),
            jax.ShapeDtypeStruct((3, 4, 192, 256), BF16),
            jax.ShapeDtypeStruct((8, 2, 2, 16, D), BF16),
            jax.ShapeDtypeStruct((2, 8, 2, 16, D), BF16),
            jax.ShapeDtypeStruct((512, D), F32),
            jax.ShapeDtypeStruct((16, FF), F32),
            jax.ShapeDtypeStruct((8, D), F32),
        ],
        scratch_shapes=[
            pltpu.VMEM((576, D), F32), pltpu.VMEM((576, D), F32), pltpu.VMEM((576, D), BF16),
            pltpu.VMEM((2, D, 512), BF16), pltpu.VMEM((544, D), BF16),
            pltpu.VMEM((576, FC), BF16), pltpu.VMEM((544, FC), BF16), pltpu.VMEM((512, FC), BF16),
            pltpu.VMEM((512, FC), BF16), pltpu.VMEM((544, FC), F32),
            pltpu.VMEM((512, D), F32), pltpu.VMEM((512, D), F32), pltpu.VMEM((6, 8, D), F32),
            pltpu.VMEM((2, 2, 3, 4, 192, 256), BF16), pltpu.VMEM((2, 3, 4, 192, 256), BF16),
            pltpu.VMEM((3, 3, 3, 192, 256), BF16), pltpu.VMEM((8, FF), F32),
            pltpu.VMEM((8, 2, 16, D), BF16), pltpu.VMEM((8, 2, 16, D), BF16),
            pltpu.VMEM((576, D), BF16), pltpu.VMEM((2, D, D), BF16), pltpu.VMEM((512, D), BF16),
            pltpu.VMEM((8, 2, 2, 16, D), BF16), pltpu.VMEM((512, D), F32),
            pltpu.SemaphoreType.DMA((3, 2)),
            pltpu.SemaphoreType.DMA((3, 3, 3)), pltpu.SemaphoreType.DMA((3, 3, 3)),
            pltpu.SemaphoreType.DMA((5,)),
        ],
        compiler_params=pltpu.CompilerParams(
            dimension_semantics=("arbitrary",), vmem_limit_bytes=60 * 2**20,
            collective_id=3, has_side_effects=True,
        ),
        name="ffn",
    )(x, at, ct, mod, alive, perm, ow, ob, f1, f1b, taps, cb, f2, f2b)


def place_matrix(count, flip, inverse):
    rows = count // 32
    out = lax.broadcasted_iota(jnp.int32, (count, count), 0)
    at = lax.broadcasted_iota(jnp.int32, (count, count), 1)
    row = out // 32
    row = jnp.where(flip, rows - 1 - row, row)
    low = out % 32
    if inverse:
        low = (low % 2) * 16 + low // 2
    else:
        low = (low % 16) * 2 + low // 16
    return jnp.where(at == row * 32 + low, 1.0, 0.0).astype(BF16)


def head_lanes(values, half):
    lane = lax.broadcasted_iota(jnp.int32, values.shape, 1)
    return jnp.where((lane // 64) == half, values, jnp.zeros_like(values))


def attn_kernel(
    lat_ref, ct_ref, cond_ref, time_ref, table_ref, mw_ref, mb_ref, w_ref, qb_ref, vb_ref,
    tap_ref, cb_ref,
    x_out, ct_out, h_out, hcg_out, qkv_out, p_out, at_out, mod_out,
    xr_s, xh_s, x_s, c_s, h_s, hcg_s, sb_s, w_s, qkv_s, p_s, ag_s, at_s, mod_s, table_s, mw_s, cb_s,
    send0, recv0, sem_pair, sem_loc,
):
    me = spot()
    zh, core, seq = me["zh"], me["core"], me["seq"]
    other = seq_peer(me, zh, 1 - core)
    w_load = pltpu.make_async_copy(w_ref, w_s, sem_loc.at[0])
    table_load = pltpu.make_async_copy(table_ref, table_s, sem_loc.at[10])
    mw_load = pltpu.make_async_copy(mw_ref, mw_s, sem_loc.at[11])
    for copy in (table_load, mw_load, w_load):
        copy.start()

    greet(
        [
            seq_peer(me, (zh + dz) % 2, (core + dc) % 2)
            for dz, dc in ((0, 1), (1, 0), (1, 1))
        ]
    )
    slot = jnp.where(zh == 0, core, 1 - core)
    inner = jnp.logical_or(seq == 1, seq == 2)
    halo_core = jnp.where(seq == 1, 1, 0)
    halo_at = pl.multiple_of(jnp.where(seq == 1, 192, 0), 64)

    def sends(arrays, act):
        for a in arrays:
            ref = (lat_ref, ct_ref)[a]
            for j in range(2):
                own = jnp.logical_and(zh == j, core == zh)
                main = (ref.at[j], xr_s.at[a, slot])
                halo = (ref.at[j, pl.ds(halo_at, 64)], xh_s.at[a])

                @pl.when(own)
                def _():
                    act(lambda: pltpu.make_async_copy(*main, recv0.at[a, slot]), True)

                @pl.when(jnp.logical_not(own))
                def _():
                    act(
                        lambda: remote(*main, send0.at[a, j, 0], recv0.at[a, slot], seq_peer(me, j, zh)),
                        False,
                    )

                @pl.when(jnp.logical_and(inner, zh == j))
                def _():
                    act(lambda: pltpu.make_async_copy(*halo, recv0.at[a, 2]), True)

                @pl.when(jnp.logical_and(inner, zh != j))
                def _():
                    act(
                        lambda: remote(
                            *halo, send0.at[a, j, 1], recv0.at[a, 2], seq_peer(me, j, halo_core)
                        ),
                        False,
                    )

    sends((0, 1), lambda make, local: make().start())

    flip = core == 1
    big = place_matrix(256, flip, False)
    small = place_matrix(64, flip, False)

    table_load.wait()
    here = lax.broadcasted_iota(jnp.int32, (8, table_s.shape[0]), 1)
    one_hot = jnp.where(here == time_ref[zh], 1.0, 0.0).astype(BF16)
    cond = jnp.where(zh == 0, cond_ref[0:1, :], cond_ref[1:2, :]) + mm(one_hot, table_s[...])
    silu = (cond / (1.0 + jnp.exp(-cond))).astype(BF16)
    mw_load.wait()
    for i in range(6):
        cols = slice(D * i, D * i + D)
        mod_s[i : i + 1, :] = (mm(silu, mw_s[:, cols]) + row(mb_ref[cols]))[0:1]
    mod_s[6:7, :] = cond[0:1]
    mod_s[7:8, :] = silu[0:1].astype(F32)
    shift1, scale1 = mod_s[0:1, :], mod_s[1:2, :]

    def placed(a, into):
        for b in range(2):
            arrived(xr_s.at[a, b], recv0.at[a, b])
            into[256 * b : 256 * b + 256, :] = mm(big, xr_s[a, b]).astype(BF16)
        arrived(xh_s.at[a], recv0.at[a, 2])
        into[512:576, :] = mm(small, xh_s[a]).astype(BF16)

    placed(0, x_s)

    def rows_a(r, _):
        at = pl.ds(pl.multiple_of(r * 96, 96), 96)
        n1, _unused = norm_parts(x_s[at, :].astype(F32))
        h_s[at, :] = (n1 * (1.0 + scale1) + shift1).astype(BF16)
        return 0

    lax.fori_loop(0, 6, rows_a, 0)
    outs = [
        pltpu.make_async_copy(x_s, x_out, sem_loc.at[1]),
        pltpu.make_async_copy(h_s, h_out, sem_loc.at[2]),
        pltpu.make_async_copy(mod_s, mod_out, sem_loc.at[12]),
    ]
    for copy in outs:
        copy.start()
    masks = side_masks()

    def lanes(j, _):
        cols = pl.ds(pl.multiple_of(j * 128, 128), 128)
        taps = tap_ref[:, cols].astype(F32)
        taps = [taps[t : t + 1] for t in range(9)]
        taps = [by_core(taps, t, core) for t in range(9)]
        offset = cb_s[0:1, cols]

        def sided(l):
            return with_sides(
                h_s[32 * l : 32 * l + 16, cols].astype(F32),
                h_s[32 * l + 16 : 32 * l + 32, cols].astype(F32),
                masks,
            )

        rows = [None, sided(0), sided(1)]
        for l in range(16):
            ce, co = conv_row(rows, taps)
            ce, co = (ce + offset).astype(BF16), (co + offset).astype(BF16)
            if l % 2 == 0:
                hcg_s[0, l // 2, 0, :, cols] = ce
                hcg_s[0, l // 2, 1, :, cols] = co
            else:
                sb_s[l // 2, 0, :, cols] = ce
                sb_s[l // 2, 1, :, cols] = co
            rows = [rows[1], rows[2], sided(l + 2) if l < 15 else None]
        return 0

    cb_s[0:1, :] = row(cb_ref[...])
    lax.fori_loop(0, D // 128, lanes, 0)
    hc_copy = remote(sb_s, hcg_s.at[1], sem_pair.at[0], sem_pair.at[1], other)
    hc_copy.start()
    w_load.wait()

    def project(half):
        for i, bias in enumerate((qb_ref, None, vb_ref)):
            cols = slice(D * i, D * i + D)
            got = mm(hcg_s[half].reshape(256, D), w_s[:, cols])
            if bias is not None:
                got = got + row(bias[...])
            qkv_s[half, :, :, :, cols] = got.astype(BF16).reshape(8, 2, 16, D)

    project(0)
    hc_copy.wait()
    outs.append(pltpu.make_async_copy(hcg_s, hcg_out, sem_loc.at[3]))
    outs[-1].start()
    project(1)
    outs.append(pltpu.make_async_copy(qkv_s, qkv_out, sem_loc.at[4]))
    outs[-1].start()

    def attend(pair, _):
        heads = [(pc, half) for pc in range(2) for half in range(2)]

        def part(which, pc):
            cols = pl.ds(pl.multiple_of(which * D + pair * 128, 128), 128)
            return jnp.concatenate(
                [qkv_s[half, :, pc, :, cols].reshape(128, 128) for half in range(2)], axis=0
            )

        q, k, v = ([part(which, pc) for pc in range(2)] for which in range(3))
        scores = [mm_nt(k[pc], head_lanes(q[pc], half)) * 0.125 for pc, half in heads]
        v_t = [v[pc].T for pc in range(2)]
        top = [jnp.max(n, axis=0, keepdims=True) for n in scores]
        e = [jnp.exp(n - m) for n, m in zip(scores, top)]
        scale = [1.0 / jnp.sum(n, axis=0, keepdims=True) for n in e]
        low = [(n * m).astype(BF16) for n, m in zip(e, scale)]
        for (pc, half), n in zip(heads, low):
            p_s[2 * (6 * pc + pair) + half] = n
        got = [mm(v_t[pc][64 * half : 64 * half + 64], n) for (pc, half), n in zip(heads, low)]
        cols = pl.ds(pl.multiple_of(pair * 128, 128), 128)
        for pc in range(2):
            o = jnp.concatenate(got[2 * pc : 2 * pc + 2], axis=0).T.astype(BF16)
            for half in range(2):
                ag_s[half, :, pc, :, cols] = o[128 * half : 128 * half + 128].reshape(8, 16, 128)
        return 0

    lax.fori_loop(0, 6, attend, 0)
    back = [
        remote(ag_s.at[1], at_s.at[pl.ds(0, 8), 1], sem_pair.at[2], sem_pair.at[3], other),
        remote(ag_s.at[0, 7], at_s.at[8, 1], sem_pair.at[4], sem_pair.at[5], other),
        pltpu.make_async_copy(ag_s.at[0], at_s.at[pl.ds(0, 8), 0], sem_loc.at[5]),
        pltpu.make_async_copy(ag_s.at[1, 7], at_s.at[8, 0], sem_loc.at[6]),
    ]
    for copy in back:
        copy.start()
    outs.append(pltpu.make_async_copy(p_s, p_out, sem_loc.at[7]))
    outs[-1].start()
    placed(1, c_s)
    outs.append(pltpu.make_async_copy(c_s, ct_out, sem_loc.at[8]))
    outs[-1].start()
    for copy in back:
        copy.wait()
    outs.append(pltpu.make_async_copy(at_s, at_out, sem_loc.at[9]))
    outs[-1].start()
    for copy in outs:
        copy.wait()

    def finish(make, local):
        if not local:
            make().wait_send()

    sends((0, 1), finish)


def attn_call(lat, ct, cond, times, table, mw, mb, w, qb, vb, taps, cb):
    G = (2, 8, 2, 16)
    shape = jax.ShapeDtypeStruct
    return pl.pallas_call(
        attn_kernel,
        in_specs=[
            ANY_SPEC, ANY_SPEC, VMEM_SPEC, SMEM_SPEC, ANY_SPEC, ANY_SPEC, VMEM_SPEC, ANY_SPEC,
            VMEM_SPEC, VMEM_SPEC, VMEM_SPEC, VMEM_SPEC,
        ],
        out_specs=[ANY_SPEC] * 8,
        out_shape=[
            shape((576, D), BF16), shape((576, D), BF16), shape((576, D), BF16),
            shape(G + (D,), BF16), shape(G + (3 * D,), BF16), shape((24, 256, 256), BF16),
            shape((9, 2, 2, 16, D), BF16), shape((8, D), F32),
        ],
        scratch_shapes=[
            pltpu.VMEM((2, 2, 256, D), BF16), pltpu.VMEM((2, 64, D), BF16),
            pltpu.VMEM((576, D), BF16), pltpu.VMEM((576, D), BF16), pltpu.VMEM((576, D), BF16),
            pltpu.VMEM(G + (D,), BF16), pltpu.VMEM((8, 2, 16, D), BF16),
            pltpu.VMEM((D, 3 * D), BF16), pltpu.VMEM(G + (3 * D,), BF16),
            pltpu.VMEM((24, 256, 256), BF16), pltpu.VMEM(G + (D,), BF16),
            pltpu.VMEM((9, 2, 2, 16, D), BF16),
            pltpu.VMEM((8, D), F32), pltpu.VMEM(table.shape, BF16), pltpu.VMEM(mw.shape, BF16),
            pltpu.VMEM((8, D), F32),
            pltpu.SemaphoreType.DMA((2, 2, 2)), pltpu.SemaphoreType.DMA((2, 3)),
            pltpu.SemaphoreType.DMA((6,)), pltpu.SemaphoreType.DMA((13,)),
        ],
        compiler_params=pltpu.CompilerParams(
            collective_id=1, has_side_effects=True, vmem_limit_bytes=56 * 2**20
        ),
        name="attend",
    )(lat, ct, cond, times, table, mw, mb, w, qb, vb, taps, cb)


def back_kernel(
    da_ref, qkv_ref, p_ref, hcg_hbm, h_hbm, x_hbm, dx_hbm, mod_ref, time_ref, w_ref, mw_ref,
    tap_ref, perm_ref, o_hbm, s1_ref, last_hbm, dbr_hbm, at_hbm, s2_ref, sb_ref,
    oret_out, iret_out, fe_out, fl_out, se_out, sl_out, de_out, dl_out,
    qkv_s, p_s, w_s, mw_s, perm_s, dag_s, dqkv_s, hct_s, dhc_s, dh_s, gh_s, ig_s, os_s, is_s,
    lg_s, prl_s, s1_s, r1x, r1l, s1l, r2e, r2l, t3e, t3a, t3b, r3e, r3a, r3b, fe_s, fl_s,
    acc_s, sv_s, se_p, se_r, se_s, se_f, sl_p, sl_r, sl_s, sl_f, mp_s, mr_s, mpl_s, mrl_s,
    item_s, de_s, dl_s, hcg_ref, h_ref, x_ref, dx_ref, o_ref, last_ref, dbr_ref, at_ref,
    loc, pair_sem, ret_send, ret_recv, st_send, st_recv, sm_send, sm_recv, dm_send, dm_recv,
):
    me = spot()
    zh, core = me["zh"], me["core"]
    other = seq_peer(me, zh, 1 - core)
    loads = [
        pltpu.make_async_copy(*pair, loc.at[20 + at])
        for at, pair in enumerate((
            (da_ref, dag_s), (qkv_ref, qkv_s), (perm_ref, perm_s), (hcg_hbm, hcg_ref),
            (at_hbm, at_ref), (dbr_hbm, dbr_ref), (p_ref, p_s), (last_hbm, last_ref),
            (o_hbm, o_ref), (w_ref, w_s), (s1_ref, s1_s), (h_hbm, h_ref), (x_hbm, x_ref),
            (dx_hbm, dx_ref), (mw_ref, mw_s),
        ))
    ]
    for load in loads:
        load.start()
    peers = [axis_peer(me, axis, o) for axis in "xyz" for o in (1, 2, 3)]
    peers += [other, seq_peer(me, 1 - zh, 1 - core)]
    hail(peers)

    def stage_sends(stage, bufs, kind, parts=(0, 1, 2)):
        out = []
        for p in parts:
            for o in (1, 2, 3):
                if kind:
                    axis = ORDERS[p][stage]
                    here, peer = axis_spot(me, axis), axis_peer(me, axis, o)
                else:
                    here, peer = early_peer(me, stage, p, o)
                src, dst = bufs(p, o, (here + o) & 3)
                copy = remote(
                    src, dst, st_send.at[kind, stage, p, o - 1], st_recv.at[kind, stage, p, o - 1],
                    peer,
                )
                copy.start()
                out.append(copy)
        return out

    def chunk(there, rows):
        return pl.ds(pl.multiple_of(there * rows, 16), rows)

    home = place_matrix(256, core == 1, True)

    def give_back(which, act):
        ref, out = ((os_s, oret_out), (is_s, iret_out))[which]
        for b in range(2):
            to_core = jnp.where(core == 0, b, 1 - b)
            own = jnp.logical_and(zh == core, b == 0)

            @pl.when(own)
            def _():
                act(lambda: pltpu.make_async_copy(ref.at[b], out.at[zh], ret_recv.at[which, zh]), True)

            @pl.when(jnp.logical_not(own))
            def _():
                act(
                    lambda: remote(
                        ref.at[b], out.at[zh], ret_send.at[which, b], ret_recv.at[which, zh],
                        seq_peer(me, core, to_core),
                    ),
                    False,
                )

    def pairs(pair, _):
        heads = [(pc, half) for pc in range(2) for half in range(2)]
        lanes_at = [
            pl.ds(pl.multiple_of(which * D + pair * 128, 128), 128) for which in range(3)
        ]

        def part(ref, cols, pc):
            return jnp.concatenate(
                [ref[half, :, pc, :, cols].reshape(128, 128) for half in range(2)], axis=0
            )

        q, k, v = ([part(qkv_s, cols, pc) for pc in range(2)] for cols in lanes_at)
        do = [part(dag_s, lanes_at[0], pc) for pc in range(2)]
        dom = [head_lanes(do[pc], half) for pc, half in heads]
        dp = [mm_nt(v[pc], n) for (pc, _), n in zip(heads, dom)]
        low = [p_s[2 * (6 * pc + pair) + half] for pc, half in heads]
        dv = [mm(n, m) for n, m in zip(low, dom)]
        k_t = [k[pc].T for pc in range(2)]
        qm = [head_lanes(q[pc], half) for pc, half in heads]
        probs = [n.astype(F32) for n in low]
        sums = [jnp.sum(n * m, axis=0, keepdims=True) for n, m in zip(probs, dp)]
        ds = [(n * (m - t)).astype(BF16) for n, m, t in zip(probs, dp, sums)]
        dk = [mm(n, m) for n, m in zip(ds, qm)]
        dq = [mm(k_t[pc][64 * half : 64 * half + 64], n) for (pc, half), n in zip(heads, ds)]
        for pc in range(2):
            at = 2 * pc
            turned = jnp.concatenate(dq[at : at + 2], axis=0).T
            grads = (0.125 * turned, 0.125 * (dk[at] + dk[at + 1]), dv[at] + dv[at + 1])
            for cols, got in zip(lanes_at, grads):
                got = got.astype(BF16)
                for half in range(2):
                    dqkv_s[half, :, pc, :, cols] = got[128 * half : 128 * half + 128].reshape(
                        8, 16, 128
                    )
        return 0

    def out_grads():
        for p, places in (
            (1, ((1, 1, 1), (1, 2, 2))), (2, ((0, 2, 0), (1, 0, 3), (1, 1, 4), (1, 2, 5)))
        ):
            at_t = mm_nt(perm_s[p], at_ref[0:512, :]).astype(BF16)
            cols = jnp.concatenate(
                [dbr_ref[:, 128 * g : 128 * g + 128] for _, _, g in places], axis=1
            )
            got = mm(at_t, cols).astype(BF16)
            for n, (which, u, _) in enumerate(places):
                lg_s[which, p, u] = got[:, 128 * n : 128 * n + 128]

    def late_grads(group):
        copies = []
        for p in range(3):
            for which in range(2):
                blocks = LATE[which][group][p]
                made = [n for n in blocks if not isinstance(n, str)]
                if not made:
                    continue
                cols = jnp.concatenate(
                    [
                        dqkv_s[:, :, :, :, 128 * n : 128 * n + 128].reshape(512, 128)
                        for n in made
                    ],
                    axis=1,
                )
                got = mm(hct_s[p], cols).astype(BF16)
                for n, block in enumerate(made):
                    u = 3 if group else blocks.index(block)
                    lg_s[which, p, u] = got[:, 128 * n : 128 * n + 128]
            part = late_part(group)
            sem = 4 + p if group == 0 else (9, 12, 15)[p]
            copies.append(
                remote(
                    lg_s.at[(1 - core, p) + part], prl_s.at[(p,) + part], pair_sem.at[sem, 0],
                    pair_sem.at[sem, 1], other,
                )
            )
            copies[-1].start()
        return copies

    def late_part(group):
        return (3,) if group else (pl.ds(0, 3),)

    def late_first(group, copies):
        out = []
        part = late_part(group)
        for p in range(3):
            copies[p].wait()
            for u in (3,) if group else (0, 1, 2):
                lg_s[core, p, u] = lg_s[core, p, u] + prl_s[p, u]
            out += stage_sends(
                0,
                lambda p, o, a: (
                    lg_s.at[(core, p) + part + (chunk(a, 192),)], r1l.at[(o - 1, p) + part]
                ),
                1 + group, (p,),
            )
        return out

    def late_second(group, copies):
        out = []
        part = late_part(group)
        for p in range(3):
            for copy in copies[3 * p : 3 * p + 3]:
                copy.wait()
            for u in (3,) if group else (0, 1, 2):
                total = lg_s[core, p, u, chunk(spots[0][p], 192), :].astype(F32)
                for o in range(3):
                    total = total + r1l[o, p, u].astype(F32)
                s1l[p, u] = total.astype(BF16)
            out += stage_sends(
                1,
                lambda p, o, b: (
                    s1l.at[(p,) + part + (chunk(b, 48),)], r2l.at[(o - 1, p) + part]
                ),
                1 + group, (p,),
            )
        return out

    def late_third(group, copies):
        out = []
        t3l, r3l = (t3b, r3b) if group else (t3a, r3a)
        for p in range(3):
            for copy in copies[3 * p : 3 * p + 3]:
                copy.wait()
            got = second(s1l, r2l, (3,) if group else (0, 1, 2), p, spots[1][p])
            pad = jnp.zeros((4 if group else 12, 128), F32)
            for c in range(4):
                t3l[p, c] = jnp.concatenate(
                    [v[12 * c : 12 * c + 12] for v in got] + [pad], axis=0
                ).astype(BF16)
            out += stage_sends(
                2, lambda p, o, c: (t3l.at[p, c], r3l.at[o - 1, p]), 1 + group, (p,)
            )
        return out

    def late_total(group, copies):
        t3l, r3l = (t3b, r3b) if group else (t3a, r3a)
        rows = slice(48, 64) if group else slice(0, 48)
        for copy in copies:
            copy.wait()
        for p in range(3):
            total = t3l[p, spots[2][p]].astype(F32)
            for o in range(3):
                total = total + r3l[o, p].astype(F32)
            fl_s[p, rows, :] = total

    spots = [[axis_spot(me, ORDERS[p][stage]) for p in range(3)] for stage in range(3)]
    z_me = axis_spot(me, "z")

    def small_stage(stage, sums, items, kind):
        axis = "zxy"[stage]
        if stage == 0:
            ref = items.at[core, me["y"], me["x"], z_me]
        elif stage == 1:
            ref = items.at[core, me["y"], me["x"]]
        else:
            ref = items.at[core, me["y"]]
        out = []
        for o in (1, 2, 3):
            peer = axis_peer(me, axis, o)
            at = (kind, stage, o - 1)
            out.append(
                remote(sums.at[4 * stage], sums.at[4 * stage + o], sm_send.at[at], sm_recv.at[at], peer)
            )
            out.append(remote(ref, ref, dm_send.at[at], dm_recv.at[at], peer))
        for copy in out:
            copy.start()
        return out

    def small_take(stage, sums, items, kind, copies, last):
        axis = "zxy"[stage]
        for copy in copies:
            copy.wait_send()
        for o in (1, 2, 3):
            at = (kind, stage, o - 1)
            arrived(sums.at[4 * stage + o], sm_recv.at[at])
            there = (axis_spot(me, axis) + 4 - o) & 3
            if stage == 0:
                ref = items.at[core, me["y"], me["x"], there]
            elif stage == 1:
                ref = items.at[core, me["y"], there]
            else:
                ref = items.at[core, there]
            arrived(ref, dm_recv.at[at])
        total = sums[4 * stage].astype(F32)
        for o in (1, 2, 3):
            total = total + sums[4 * stage + o].astype(F32)
        if stage < 2:
            sums[4 * stage + 4] = total.astype(BF16)
        else:
            last[...] = total

    def lane_rows(values, count):
        return [
            values[i : i + 1, 128 * l : 128 * l + 128] for i in range(count) for l in range(6)
        ]

    ends = []

    def spread(done, out, at):
        for copy in (
            pltpu.make_async_copy(done, out.at[core], loc.at[at]),
            remote(done, out.at[core], pair_sem.at[at, 0], pair_sem.at[at, 1], other),
        ):
            copy.start()
            ends.append(copy)

    def second(own, recv, panels, p, here):
        out = []
        for k in panels:
            total = own[p, k, chunk(here, 48), :].astype(F32)
            for o in range(3):
                total = total + recv[o, p, k].astype(F32)
            out.append(total)
        return out

    def finish(copies, own, recv, done, out, at, places):
        for copy in copies:
            copy.wait()
        for p in range(3):
            total = own[p, places[p]].astype(F32)
            for o in range(3):
                total = total + recv[o, p].astype(F32)
            done[p] = total
        spread(done, out, at)

    def pairs_turn(i, _):
        hct_s[i] = mm_nt(perm_s[i], hcg_ref[...]).astype(BF16)
        return pairs(i, 0)

    for load in loads[:7]:
        load.wait()
    lax.fori_loop(0, 1, pairs_turn, 0)
    heard(len(peers))
    loads[7].wait()
    st1x = stage_sends(0, lambda p, o, a: (last_ref.at[p, a], r1x.at[o - 1, p]), 0)
    mp_s[...] = sb_ref[...]
    mp_copy = remote(mp_s, mr_s, pair_sem.at[1, 0], pair_sem.at[1, 1], other)
    mp_copy.start()
    for half in range(2):
        for q in range(2):
            at = D * (2 * half + q)
            se_p[half, 16 * q : 16 * q + 16, :] = s2_ref[:, at : at + D].astype(BF16)
    se_copy = remote(se_p.at[1 - core], se_r, pair_sem.at[2, 0], pair_sem.at[2, 1], other)
    se_copy.start()

    loads[8].wait()
    for b in range(2):
        os_s[b] = mm(home, o_ref[256 * b : 256 * b + 256, :]).astype(BF16)
    give_back(0, lambda make, local: make().start())
    lax.fori_loop(1, 3, pairs_turn, 0)
    out_grads()
    pairs(3, 0)
    late_a = late_grads(0)
    mp_copy.wait()
    item_s[2:6, :] = (mp_s[0:4, :] + mr_s[0:4, :]).astype(BF16).astype(F32)
    time_id = time_ref[zh]
    stamp = jnp.ones((1, 128), F32)
    rows = lane_rows(item_s[2:6, :], 4) + lane_rows(mod_ref[7:8, :], 1)
    rows += [stamp * (time_id // 32).astype(F32), stamp * (time_id % 32).astype(F32)]
    both = jnp.concatenate(rows, axis=0).astype(BF16)
    de_s[core, me["y"], me["x"], z_me] = jnp.where(core == 0, both[0:16], both[16:32])
    se_copy.wait()
    se_s[0] = (se_p[core].astype(F32) + se_r[...].astype(F32)).astype(BF16)
    small = small_stage(0, se_s, de_s, 0)
    lax.fori_loop(4, 6, pairs, 0)
    late_b = late_grads(1)
    loads[9].wait()
    for half in (1, 0):
        got = mm_nt(dqkv_s[half].reshape(256, 3 * D), w_s[...]).astype(BF16)
        dhc_s[half] = got.reshape(8, 2, 16, D)
        if half == 1:
            dhc_copy = remote(
                dhc_s.at[1], dh_s.at[pl.ds(0, 8), 1], pair_sem.at[3, 0], pair_sem.at[3, 1], other
            )
            dhc_copy.start()
    near = [
        pltpu.make_async_copy(dhc_s.at[0], dh_s.at[pl.ds(0, 8), 0], loc.at[7]),
        pltpu.make_async_copy(dhc_s.at[1, 7], dh_s.at[8, 0], loc.at[8]),
    ]
    for copy in near:
        copy.start()
    st1a = late_first(0, late_a)
    st1b = late_first(1, late_b)
    loads[14].wait()
    d_silu = jnp.zeros((8, D), F32)

    def silu_part(i):
        row = jnp.concatenate([item_s[i : i + 1, :]] * 8, axis=0).astype(BF16)
        return mm_nt(row, mw_s[:, D * i : D * i + D])

    for i in range(2, 6):
        d_silu = d_silu + silu_part(i)
    ones = jnp.ones((8, 512), BF16)
    for row, at in ((10, 0), (11, 2 * D)):
        sums = mm(ones, dqkv_s[:, :, :, :, at : at + D].reshape(512, D))
        sv_s[row : row + 1, :] = sums[0:1]
    sv_s[12:14, :] = sb_ref[4:6, :]
    sv_s[14:16, :] = jnp.zeros((2, D), F32)

    dhc_copy.wait()
    for copy in near:
        copy.wait()
    loads[11].wait()
    masks = side_masks()

    def lanes(j, _):
        cols = pl.ds(pl.multiple_of(j * 128, 128), 128)
        taps = tap_ref[:, cols].astype(F32)
        taps = [taps[t : t + 1] for t in range(9)]
        back = [by_core(taps, 8 - t, core) for t in range(9)]
        back = [jnp.broadcast_to(v, (16, 128)).astype(BF16) for v in back]

        def sided_d(l):
            return with_sides_low(
                dh_s[l // 2, l % 2, 0, :, cols], dh_s[l // 2, l % 2, 1, :, cols], masks
            )

        def sided_h(l):
            return with_sides_low(
                h_ref[32 * l : 32 * l + 16, cols], h_ref[32 * l + 16 : 32 * l + 32, cols], masks
            )

        rows = [None, sided_d(0), sided_d(1)]
        rows_h = [None, sided_h(0), sided_h(1)]
        sums = [None] * 9
        held = bias_sum = None
        for l in range(16):
            ge, go = conv_row(rows, back)
            gh_s[32 * l : 32 * l + 16, cols] = ge.astype(F32)
            gh_s[32 * l + 16 : 32 * l + 32, cols] = go.astype(F32)
            de, do = rows[1][0], rows[1][1]
            held = tap_pairs(held if l % 2 else None, rows_h, de, do)
            if l % 2:
                for t in range(9):
                    term = fold8(held[t].astype(F32))
                    sums[t] = term if sums[t] is None else sums[t] + term
            term = fold8(de.astype(F32) + do.astype(F32))
            bias_sum = term if bias_sum is None else bias_sum + term
            if l < 15:
                rows = [rows[1], rows[2], sided_d(l + 2)]
                rows_h = [rows_h[1], rows_h[2], sided_h(l + 2)]
        for t in range(9):
            total = jnp.sum(by_core(sums, t, core), axis=0, keepdims=True)
            sv_s[t : t + 1, cols] = total
        sv_s[9:10, cols] = jnp.sum(bias_sum, axis=0, keepdims=True)
        return 0

    lax.fori_loop(0, D // 128, lanes, 0)
    small_take(0, se_s, de_s, 0, small, se_f)
    small = small_stage(1, se_s, de_s, 0)
    for load in loads[12:14]:
        load.wait()
    scale1 = mod_ref[1:2, :]
    acc_s[...] = jnp.zeros_like(acc_s)

    def rows_n(r, _):
        at = pl.ds(pl.multiple_of(r * 128, 128), 128)
        n1, rs = norm_parts(x_ref[at, :].astype(F32))
        dh = gh_s[at, :]
        g1 = dh * (1.0 + scale1)
        got = dx_ref[at, :] + rs * (
            g1
            - jnp.mean(g1, axis=-1, keepdims=True)
            - n1 * jnp.mean(g1 * n1, axis=-1, keepdims=True)
        )
        ig_s[at, :] = got.astype(BF16)
        acc_s[0] += fold8(dh)
        acc_s[1] += fold8(dh * n1)
        return 0

    lax.fori_loop(0, 4, rows_n, 0)
    mpl_s[...] = jnp.zeros_like(mpl_s)
    for i in range(2):
        mpl_s[i : i + 1, :] = jnp.sum(acc_s[i], axis=0, keepdims=True)
    mpl_copy = remote(mpl_s, mrl_s, pair_sem.at[7, 0], pair_sem.at[7, 1], other)
    mpl_copy.start()
    for half in range(2):
        sl_p[half] = sv_s[:, 384 * half : 384 * half + 384].astype(BF16)
    sl_copy = remote(sl_p.at[1 - core], sl_r, pair_sem.at[8, 0], pair_sem.at[8, 1], other)
    sl_copy.start()
    for b in range(2):
        is_s[b] = mm(home, ig_s[256 * b : 256 * b + 256, :]).astype(BF16)
    mpl_copy.wait()
    item_s[0:2, :] = (mpl_s[0:2, :] + mrl_s[0:2, :]).astype(BF16).astype(F32)
    cond = mod_ref[6:7, :]
    for i in range(2):
        d_silu = d_silu + silu_part(i)
    slope = 1.0 / (1.0 + jnp.exp(-cond))
    d_cond = (slope * (1.0 + cond * (1.0 - slope))) * d_silu[0:1]
    zeros = [jnp.zeros((1, 128), F32)]
    rows_0 = jnp.concatenate(lane_rows(item_s[0:2, :], 2) + zeros * 4, axis=0)
    rows_1 = jnp.concatenate(lane_rows(d_cond, 1) + zeros * 10, axis=0)
    dl_s[core, me["y"], me["x"], z_me] = jnp.where(core == 0, rows_0, rows_1).astype(BF16)
    sl_copy.wait()
    sl_s[0] = (sl_p[core].astype(F32) + sl_r[...].astype(F32)).astype(BF16)
    small_l = small_stage(0, sl_s, dl_s, 1)
    give_back(1, lambda make, local: make().start())
    loads[10].wait()
    for copy in st1x:
        copy.wait()
    for p in range(3):
        here, _peer = early_peer(me, 0, p, 1)
        total = last_ref[p, here].astype(F32)
        for o in range(3):
            total = total + r1x[o, p].astype(F32)
        total = total.astype(BF16)

        @pl.when(core == 0)
        def _():
            s1_s[p, 3] = total

        @pl.when(core == 1)
        def _():
            for c in range(4):
                s1_s[p, c, 144:192] = total[48 * c : 48 * c + 48]

    st2e = stage_sends(1, lambda p, o, b: (s1_s.at[p, :, chunk(b, 48)], r2e.at[o - 1, p]), 0)
    small_take(1, se_s, de_s, 0, small, se_f)
    small = small_stage(2, se_s, de_s, 0)
    st2a = late_second(0, st1a)
    small_take(0, sl_s, dl_s, 1, small_l, sl_f)
    small_l = small_stage(1, sl_s, dl_s, 1)
    st2b = late_second(1, st1b)
    for copy in st2e:
        copy.wait()
    for p in range(3):
        got = second(s1_s, r2e, range(4), p, early_peer(me, 1, p, 1)[0])

        @pl.when(core == 0)
        def _():
            for c in range(4):
                t3e[p, c] = jnp.concatenate(
                    [got[k][12 * c : 12 * c + 12] for k in range(4)], axis=0
                ).astype(BF16)

        @pl.when(core == 1)
        def _():
            for c in range(4):
                t3e[p, c] = got[c].astype(BF16)

    st3e = stage_sends(2, lambda p, o, c: (t3e.at[p, c], r3e.at[o - 1, p]), 0)
    small_take(2, se_s, de_s, 0, small, se_f)
    spread(se_f, se_out, 10)
    spread(de_s.at[core], de_out, 16)
    small_take(1, sl_s, dl_s, 1, small_l, sl_f)
    small_l = small_stage(2, sl_s, dl_s, 1)
    st3a = late_third(0, st2a)
    st3b = late_third(1, st2b)
    finish(st3e, t3e, r3e, fe_s, fe_out, 17, [early_peer(me, 2, p, 1)[0] for p in range(3)])
    late_total(0, st3a)
    late_total(1, st3b)
    spread(fl_s, fl_out, 18)
    small_take(2, sl_s, dl_s, 1, small_l, sl_f)
    spread(sl_f, sl_out, 13)
    spread(dl_s.at[core], dl_out, 14)
    for which in range(2):
        give_back(which, lambda make, local: None if local else make().wait_send())
        for item_slot in range(2):
            out = (oret_out, iret_out)[which]
            arrived(out.at[item_slot], ret_recv.at[which, item_slot])
    for copy in ends:
        copy.wait()


def back_call(
    da, qkv, p, hcg, h, x, dx, mod, times, w, mw, taps, perm, o, s1, last, dbr, at, s2, sb
):
    G = (2, 8, 2, 16)
    shape = jax.ShapeDtypeStruct
    V = pltpu.VMEM
    items = (2, 4, 4, 4, 16, 128)
    DMA = pltpu.SemaphoreType.DMA
    return pl.pallas_call(
        back_kernel,
        in_specs=[
            ANY_SPEC, ANY_SPEC, ANY_SPEC, ANY_SPEC, ANY_SPEC, ANY_SPEC, ANY_SPEC, VMEM_SPEC,
            SMEM_SPEC, ANY_SPEC, ANY_SPEC, VMEM_SPEC, ANY_SPEC, ANY_SPEC, ANY_SPEC, ANY_SPEC,
            ANY_SPEC, ANY_SPEC, VMEM_SPEC, VMEM_SPEC,
        ],
        out_specs=[ANY_SPEC] * 8,
        out_shape=[
            shape((2, 256, D), BF16), shape((2, 256, D), BF16),
            shape((2, 3, 48, 256), F32), shape((2, 3, 64, 128), F32),
            shape((2, 32, D), F32), shape((2, 16, 384), F32),
            shape(items, BF16), shape(items, BF16),
        ],
        scratch_shapes=[
            V(G + (3 * D,), BF16), V((24, 256, 256), BF16), V((D, 3 * D), BF16),
            V(mw.shape, BF16), V((3, D, D), BF16), V(G + (D,), BF16), V(G + (3 * D,), BF16),
            V((3, D, 512), BF16), V(G + (D,), BF16), V((9, 2, 2, 16, D), BF16), V((512, D), F32),
            V((512, D), BF16), V((2, 256, D), BF16), V((2, 256, D), BF16),
            V((2, 3, 4, D, 128), BF16), V((3, 4, D, 128), BF16), V((3, 4, 192, 256), BF16),
            V((3, 3, 192, 256), BF16), V((3, 3, 4, 192, 128), BF16), V((3, 4, 192, 128), BF16),
            V((3, 3, 4, 48, 256), BF16), V((3, 3, 4, 48, 128), BF16), V((3, 4, 48, 256), BF16),
            V((3, 4, 48, 128), BF16), V((3, 4, 16, 128), BF16), V((3, 3, 48, 256), BF16),
            V((3, 3, 48, 128), BF16), V((3, 3, 16, 128), BF16), V((3, 48, 256), F32),
            V((3, 64, 128), F32),
            V((2, 8, D), F32), V((16, D), F32),
            V((2, 32, D), BF16), V((32, D), BF16), V((12, 32, D), BF16), V((32, D), F32),
            V((2, 16, 384), BF16), V((16, 384), BF16), V((12, 16, 384), BF16), V((16, 384), F32),
            V((8, D), F32), V((8, D), F32), V((8, D), F32), V((8, D), F32), V((8, D), F32),
            V(items, BF16), V(items, BF16),
            V((512, D), BF16), V((576, D), BF16), V((576, D), BF16), V((512, D), F32),
            V((512, D), BF16), V((3, 4, 192, 256), BF16), V((512, D), BF16), V((576, D), BF16),
            DMA((35,)), DMA((19, 2)), DMA((2, 2)), DMA((2, 2)), DMA((3, 3, 3, 3)),
            DMA((3, 3, 3, 3)), DMA((2, 3, 3)), DMA((2, 3, 3)), DMA((2, 3, 3)), DMA((2, 3, 3)),
        ],
        compiler_params=pltpu.CompilerParams(
            collective_id=2, has_side_effects=True, vmem_limit_bytes=60 * 2**20
        ),
        name="back",
    )(da, qkv, p, hcg, h, x, dx, mod, times, w, mw, taps, perm, o, s1, last, dbr, at, s2, sb)


def share_kernel(
    out_ref, ig_ref, fe_hbm, fl_hbm, se_hbm, sl_hbm, de_hbm, dl_hbm,
    o_out, ig_out, cond_out, table_out, mw_out, mb_out, aw_out, ab_out, qkv_out, qb_out, vb_out,
    ow_out, ob_out, f1_out, f1b_out, fw_out, fb_out, f2_out, f2b_out,
    ig_s, o_s, igf_s, e_s, l_s, fe_ref, fl_ref, se_ref, sl_ref, de_ref, dl_ref, sem,
):
    me = spot()
    core = me["core"]
    shard = me["dp"] * 4 + me["seq"]
    ig_load = pltpu.make_async_copy(ig_ref, ig_s, sem.at[0])
    o_load = pltpu.make_async_copy(out_ref, o_s, sem.at[9])
    o_move = pltpu.make_async_copy(o_s, o_out, sem.at[1])
    loads = [
        pltpu.make_async_copy(*pair, sem.at[3 + at])
        for at, pair in enumerate((
            (fe_hbm, fe_ref), (fl_hbm, fl_ref), (se_hbm, se_ref), (sl_hbm, sl_ref),
            (de_hbm, de_ref), (dl_hbm, dl_ref),
        ))
    ]
    for load in loads:
        load.start()
    ig_load.start()
    o_load.start()
    o_load.wait()
    o_move.start()
    ig_load.wait()
    igf_s[...] = ig_s[...].astype(F32)
    ig_move = pltpu.make_async_copy(igf_s, ig_out, sem.at[2])
    ig_move.start()
    for load in loads:
        load.wait()
    e_s[...] = de_ref[...].reshape(2048, 128).astype(F32)
    l_s[...] = dl_ref[...].reshape(2048, 128).astype(F32)

    def six(v, at):
        return jnp.where(core == 0, v[at : at + 6], v[at + 6 : at + 12])

    for p in range(3):
        early0, early1 = fe_ref[0, p], fe_ref[1, p]
        for i in range(4):
            at = D * i + 256 * p
            f1_out[:, at : at + 256] = six(early0, 12 * i)
        f2_out[:, 256 * p : 256 * p + 256] = jnp.where(core == 0, early1[0:24], early1[24:48])
        for which in range(2):
            late = fl_ref[which, p]
            for group in range(2):
                for u, block in enumerate(LATE[which][group][p]):
                    got = six(late, 48 if group else 12 * u)
                    if isinstance(block, str):
                        at = 128 * int(block[1])
                        ow_out[:, at : at + 128] = got
                    else:
                        qkv_out[:, 128 * block : 128 * block + 128] = got

    def columns(start, count=D):
        at = lax.broadcasted_iota(jnp.int32, (count, 128), 0)
        to = lax.broadcasted_iota(jnp.int32, (count, 128), 1)
        return at == start + to

    def exact(a, b):
        return lax.dot_general(
            a, b.astype(F32), (((1,), (0,)), ((), ())), preferred_element_type=F32,
            precision=lax.Precision.HIGHEST,
        )

    mine = columns(shard * 6)
    slim = exact(jnp.concatenate((sl_ref[0], sl_ref[1]), axis=1), mine)
    aw_out[...] = slim.T[0:6, 0:9]
    for ref, at in ((ab_out, 9), (qb_out, 10), (vb_out, 11), (ob_out, 12), (f2b_out, 13)):
        ref[...] = slim[at : at + 1, 0:6].reshape(6)
    quarter = shard // 32
    wide = se_ref[quarter // 2, pl.ds(pl.multiple_of(quarter % 2 * 16, 16), 16), :]
    wide = exact(wide, columns(shard % 32 * 24))
    fw_out[...] = wide[0:9, 0:24]
    fb_out[...] = wide[9:10, 0:24].reshape(24)
    f1b_out[...] = wide[10:11, 0:24].reshape(24)

    def item_rows(ref, at):
        return ref[pl.ds(at // 16 * 1024 + at % 16, 64, stride=16), :]

    silu = jnp.concatenate([item_rows(e_s, 24 + l) for l in range(6)], axis=1)
    silu = mm(silu.astype(BF16), mine.astype(BF16)).astype(BF16)
    sums = []
    for at in range(36):
        d_mod = item_rows(l_s, at) if at < 12 else item_rows(e_s, at - 12)
        mw_out[:, 128 * at : 128 * at + 128] = mm_tn(silu, d_mod.astype(BF16))[0:6]
        sums.append(jnp.sum(d_mod, axis=0, keepdims=True))
    total = jnp.concatenate(sums, axis=1)
    total = exact(jnp.concatenate([total] * 8, axis=0), columns(shard * 36, 6 * D))
    mb_out[...] = total[0:1, 0:36].reshape(36)

    cond = jnp.concatenate([item_rows(l_s, 16 + l) for l in range(6)], axis=1).astype(BF16)
    here = lax.broadcasted_iota(jnp.int32, (8, 64), 1)
    slot = lax.broadcasted_iota(jnp.int32, (8, 64), 0)
    own = here == (me["y"] * 4 + me["x"]) * 4 + slot * 2 + me["zl"]
    own = jnp.logical_and(own, slot < 2)
    cond_out[...] = mm(own.astype(BF16), cond)[0:2]
    times = 32.0 * item_rows(e_s, 30) + item_rows(e_s, 31)
    bucket = lax.broadcasted_iota(jnp.int32, (64, 1024), 1).astype(F32)
    hot = (bucket == jnp.concatenate([times] * 8, axis=1)).astype(BF16)
    my_cond = mm(cond, mine.astype(BF16)).astype(BF16)
    table_out[...] = mm_tn(my_cond, hot)[0:6, 0 : table_out.shape[1]]

    ig_move.wait()
    o_move.wait()


def share_call(buckets, *args):
    shapes = [
        ((2, 256, D), BF16), ((2, 256, D), F32), ((2, D), F32), ((6, buckets), F32),
        ((6, 6 * D), F32), ((36,), F32), ((6, 9), F32), ((6,), F32), ((6, 3 * D), F32),
        ((6,), F32), ((6,), F32), ((6, D), F32), ((6,), F32), ((6, FF), F32), ((24,), F32),
        ((9, 24), F32), ((24,), F32), ((24, D), F32), ((6,), F32),
    ]
    return pl.pallas_call(
        share_kernel,
        in_specs=[ANY_SPEC] * 8,
        out_specs=[ANY_SPEC] * 2 + [VMEM_SPEC] * 17,
        out_shape=[jax.ShapeDtypeStruct(*s) for s in shapes],
        scratch_shapes=[
            pltpu.VMEM((2, 256, D), BF16), pltpu.VMEM((2, 256, D), BF16),
            pltpu.VMEM((2, 256, D), F32), pltpu.VMEM((2048, 128), F32), pltpu.VMEM((2048, 128), F32),
            *[pltpu.VMEM(v.shape, v.dtype) for v in args[2:]],
            pltpu.SemaphoreType.DMA((10,)),
        ],
        compiler_params=pltpu.CompilerParams(vmem_limit_bytes=60 * 2**20),
        name="share",
    )(*args)


def perm_matrices():
    at = np.arange(D)
    rows = []
    for order in ORDERS:
        spots = dict(zip(order, (at // 192, at // 48 % 4, at // 12 % 4)))
        x, y, z = spots["x"], spots["y"], spots["z"]
        rows.append((((x * 2 + z % 2) * 4 + y) * 2 + z // 2) * 12 + at % 12)
    return np.stack(rows).astype(np.int32)


def local(
    latents, conditioning, timesteps, item_counts, cotangent, time_table, mod_weight, mod_bias,
    conv_attn_weight, conv_attn_bias, qkv_weight, query_bias, value_bias, out_weight, out_bias,
    fc1_weight, fc1_bias, conv_ffn_weight, conv_ffn_bias, fc2_weight, fc2_bias,
):
    alive = (lax.axis_index("seq") // 2 < item_counts).astype(F32)
    perm = (perm_matrices()[:, :, None] == np.arange(D)[None, None, :]).astype(BF16)
    x, ct, h, hcg, qkv, p, at, mod = attn_call(
        latents.reshape(2, 256, D), cotangent.reshape(2, 256, D), conditioning, timesteps,
        time_table, mod_weight, mod_bias, qkv_weight, query_bias, value_bias, conv_attn_weight,
        conv_attn_bias,
    )
    at = at.reshape(576, D)
    out, s1, last, dbr, da, dx, s2, sb = ffn_call(
        x, at, ct, mod, alive, perm, out_weight, out_bias, fc1_weight, fc1_bias, conv_ffn_weight,
        conv_ffn_bias, fc2_weight, fc2_bias,
    )
    got = back_call(
        da, qkv, p, hcg.reshape(512, D), h, x, dx, mod, timesteps,
        qkv_weight, mod_weight, conv_attn_weight, perm, out, s1, last,
        dbr.reshape(512, D), at, s2, sb,
    )
    outs = list(share_call(time_table.shape[0], *got))
    outs[0], outs[1] = outs[0].reshape(latents.shape), outs[1].reshape(latents.shape)
    outs[3], outs[6] = outs[3].T, outs[6].T
    return tuple(outs)


def solution(mesh):
    return jax.shard_map(
        local,
        mesh=mesh,
        in_specs=(
            P("dp", "seq", None, None),
            P("dp", None),
            P("dp"),
            P("dp"),
            P("dp", "seq", None, None),
            P(),
            P(),
            P(),
            P(),
            P(),
            P(),
            P(),
            P(),
            P(),
            P(),
            P(),
            P(),
            P(),
            P(),
            P(),
            P(),
        ),
        out_specs=(
            P("dp", "seq", None, None),
            P("dp", "seq", None, None),
            P("dp", None),
            P(None, ("dp", "seq")),
            P(("dp", "seq"), None),
            P(("dp", "seq")),
            P(None, ("dp", "seq")),
            P(("dp", "seq")),
            P(("dp", "seq"), None),
            P(("dp", "seq")),
            P(("dp", "seq")),
            P(("dp", "seq"), None),
            P(("dp", "seq")),
            P(("dp", "seq"), None),
            P(("dp", "seq")),
            P(None, ("dp", "seq")),
            P(("dp", "seq")),
            P(("dp", "seq"), None),
            P(("dp", "seq")),
        ),
        check_vma=False,
    )
```
